256 devices in a mesh: img: 8 (over x, z_hi), ori: 32 (over z_lo, y, core).
Axes of the slice: x: 4, y: 4, z: 8 (z_hi: 2, z_lo: 4; z = z_hi * 4 + z_lo), core: 2. Of those that a mesh axis runs over, the one named last changes fastest.
Arguments:
- images: bfloat16 [1024, 2, 8320], P(('img', 'ori')), may hold values from -60 to 60
- projections: bfloat16 [2048, 2, 8320], P('ori'), may hold values from -6 to 6
- ctf_table: float32 [64, 8320], replicated, may hold values from -1 to 1
- noise_weight: float32 [8320], replicated, may hold values from 0.0039663464 to 0.03966346
- shifts: int32 [1024, 4, 2], P(('img', 'ori')), may hold values from -8 to 8, as said below
- defocus: int32 [1024], P(('img', 'ori')), may hold values from 0 to 63, as said below
Outputs:
- log_evidence: float32 [1024], P(('img', 'ori'))
- class_sums: float32 [2048, 2, 8320], P(('ori', 'img'))
The draws below stay inside these ranges and needn't reach their ends.
Inputs may be any that keep to these rules, and one draw needn't show every extreme that they name: `shifts`: both ends of the range occur. `defocus`: every class from 0 to 63 may occur; the first and the last do.
All inputs are finite; a program needn't handle non-finite values.
Results may differ from the reference program's by a relative error of at most 0.011.
Values may be sent and summed in bfloat16 or wider, within the bound.
A program may use at most 128 MiB of HBM per device.

```python
import math
import jax
import jax.numpy as jnp
from jax import lax

KY = 128
KX = 65
PIX = 8320
TRANS = 4
CLASSES = 64
MAX_SHIFT = 8
IMAGES = 1024
PROJECTIONS = 2048
N_IMG = 8


def shared_draws(key):
    base_key = jax.random.fold_in(key, 11)
    key_proj, key_ctf, key_class, key_shift = jax.random.split(base_key, 4)
    projections = jnp.clip(jax.random.normal(key_proj, (PROJECTIONS, 2, PIX), jnp.float32), -6.0, 6.0)
    ctf_values = jax.random.uniform(key_ctf, (CLASSES, PIX), jnp.float32, -1.0, 1.0)
    classes = jax.random.randint(key_class, (IMAGES,), 0, CLASSES).astype(jnp.int32)
    classes = classes.at[0].set(0).at[1].set(CLASSES - 1)
    offsets = jax.random.randint(key_shift, (IMAGES, TRANS, 2), -MAX_SHIFT, MAX_SHIFT + 1).astype(jnp.int32)
    offsets = offsets.at[0, 0, 0].set(-MAX_SHIFT).at[0, 0, 1].set(MAX_SHIFT)
    return (projections, ctf_values, classes, offsets)


def rotated(chosen, offsets, which):
    pixel_index = jnp.arange(PIX, dtype=jnp.int32)
    column = pixel_index % KX
    height = pixel_index // KX
    phase_steps = (column[None, :] * offsets[:, which, 0:1] + height[None, :] * offsets[:, which, 1:2]) % KY
    angles = phase_steps.astype(jnp.float32) * (2.0 * math.pi / KY)
    cosine = jnp.cos(angles)
    sine_part = jnp.sin(angles)
    real_part = chosen[:, 0, :] * cosine - chosen[:, 1, :] * sine_part
    imag_part = chosen[:, 0, :] * sine_part + chosen[:, 1, :] * cosine
    return jnp.stack([real_part, imag_part], axis=1)


def drawn_rows(projections, ctf_values, classes, offsets):
    index = jnp.arange(IMAGES, dtype=jnp.int32)
    target = index * 37 % PROJECTIONS
    strength = (1 + index // 8 % 3).astype(jnp.float32)
    second = 1.0 - 2.0 / (130.0 * strength)
    signs = jnp.sign(ctf_values[classes])
    chosen = projections[target]
    aligned = strength[:, None, None] * signs[:, None, :] * (rotated(chosen, offsets, 0) + second[:, None, None] * rotated(chosen, offsets, 1))
    picked = (index % 8 == 3)[:, None, None]
    return (aligned, picked)


def draw_images(key, part):
    projections, ctf_values, classes, offsets = shared_draws(key)
    aligned, picked = drawn_rows(projections, ctf_values, classes, offsets)
    key = jax.random.fold_in(key, 5)
    key_base = jax.random.fold_in(key, 0)
    base = jnp.clip(jax.random.normal(key_base, (IMAGES, 2, PIX), jnp.float32), -6.0, 6.0)
    return jnp.where(picked, aligned, base).astype(jnp.bfloat16)


def draw_projections(key, part):
    projections, ctf_values, classes, offsets = shared_draws(key)
    return projections.astype(jnp.bfloat16)


def draw_ctf_table(key, part):
    projections, ctf_values, classes, offsets = shared_draws(key)
    return ctf_values


def draw_shifts(key, part):
    projections, ctf_values, classes, offsets = shared_draws(key)
    return offsets


def draw_defocus(key, part):
    projections, ctf_values, classes, offsets = shared_draws(key)
    return classes


def setup_inputs(seed: int = 0) -> dict:
    key_list = jax.random.split(jax.random.key(seed), 7)
    images = draw_images(jax.random.fold_in(key_list[6], 71), 0)
    projections = draw_projections(jax.random.fold_in(key_list[6], 71), 0)
    ctf_table = draw_ctf_table(jax.random.fold_in(key_list[6], 71), 0)
    noise_weight = jnp.clip(jnp.exp(jax.random.uniform(key_list[3], (PIX,), jnp.float32, math.log(0.0039663464), math.log(0.03966346))), 0.0039663464, 0.03966346)
    shifts = draw_shifts(jax.random.fold_in(key_list[6], 71), 0)
    defocus = draw_defocus(jax.random.fold_in(key_list[6], 71), 0)
    return dict(images=images, projections=projections, ctf_table=ctf_table, noise_weight=noise_weight, shifts=shifts, defocus=defocus)


TWO_PI = 2.0 * math.pi


def class_lookup(classes, ctf_table):
    labels = jnp.arange(CLASSES, dtype=jnp.int32)
    onehot = (classes[:, None] == labels[None, :]).astype(jnp.float32)
    rows_ctf = jnp.dot(onehot, ctf_table, precision=lax.Precision.HIGHEST, preferred_element_type=jnp.float32)
    return onehot, rows_ctf


def shifted_weighted(block, offsets, rows_ctf):
    pixel_index = jnp.arange(PIX, dtype=jnp.int32)
    column = pixel_index % KX
    height = pixel_index // KX
    phase_steps = (column[None, None, :] * offsets[:, :, 0:1] + height[None, None, :] * offsets[:, :, 1:2]) % KY
    angles = phase_steps.astype(jnp.float32) * (TWO_PI / KY)
    cosine = jnp.cos(angles)
    sine_part = jnp.sin(angles)
    real_part = block[:, 0, :].astype(jnp.float32)[:, None, :]
    imag_part = block[:, 1, :].astype(jnp.float32)[:, None, :]
    shifted = jnp.stack([real_part * cosine + imag_part * sine_part, imag_part * cosine - real_part * sine_part], axis=2)
    return (shifted * rows_ctf[:, None, None, :]).astype(jnp.bfloat16)


def reference(images, projections, ctf_table, noise_weight, shifts, defocus):
    proj_float = projections.astype(jnp.float32)
    weighted = (proj_float * noise_weight[None, None, :]).astype(jnp.bfloat16).reshape(PROJECTIONS, 2 * PIX)
    power = proj_float[:, 0, :] * proj_float[:, 0, :] + proj_float[:, 1, :] * proj_float[:, 1, :]
    class_norm = 0.5 * jnp.dot(ctf_table * ctf_table * noise_weight[None, :], power.T, precision=lax.Precision.HIGHEST, preferred_element_type=jnp.float32)
    group_rows = IMAGES // N_IMG

    def group_step(running, inputs):
        block, offsets, classes = inputs
        onehot, rows_ctf = class_lookup(classes, ctf_table)
        prepared = shifted_weighted(block, offsets, rows_ctf).reshape(group_rows * TRANS, 2 * PIX)
        cross = jnp.dot(prepared, weighted.T, preferred_element_type=jnp.float32).reshape(group_rows, TRANS, PROJECTIONS)
        norms = jnp.dot(onehot, class_norm, precision=lax.Precision.HIGHEST, preferred_element_type=jnp.float32)
        scores = cross - norms[:, None, :]
        largest = jnp.max(scores, axis=(1, 2))
        totals = jnp.sum(jnp.exp(scores - largest[:, None, None]), axis=(1, 2))
        evidence = largest + jnp.log(totals)
        posterior = (jnp.exp(scores - evidence[:, None, None]) * PROJECTIONS).astype(jnp.bfloat16)
        partial_value = jnp.dot(posterior.reshape(group_rows * TRANS, PROJECTIONS).T, prepared, preferred_element_type=jnp.float32)
        rounded = lax.optimization_barrier(partial_value.astype(jnp.bfloat16))
        return running + rounded.astype(jnp.float32), evidence

    start_sums = jnp.zeros((PROJECTIONS, 2 * PIX), jnp.float32)
    sums, evidence = lax.scan(group_step, start_sums, (images.reshape(N_IMG, group_rows, 2, PIX), shifts.reshape(N_IMG, group_rows, TRANS, 2), defocus.reshape(N_IMG, group_rows)))
    return evidence.reshape(IMAGES), sums.reshape(PROJECTIONS, 2, PIX)
```

```python
import math

import jax
import jax.numpy as jnp
import numpy as np
from jax import lax
from jax.experimental import pallas as pl
from jax.experimental.pallas import tpu as pltpu
from jax.sharding import PartitionSpec as P

KY = 128
KX = 65
LANES = 128
NX, NZ, NY = 4, 4, 4
BLOCKS = NZ * NY
TRANS = 4
TILES = 33
HALF = TILES * LANES
SHIFT = 32 * LANES
HALF_A = 17 * LANES
CHUNKS = 11
CHUNK_TILES = TILES // CHUNKS
CW = CHUNK_TILES * 2 * LANES
OTHERS = [(dz, dy) for dz in range(NZ) for dy in range(NY) if (dz, dy) != (0, 0)]
F32 = jnp.float32
BF16 = jnp.bfloat16
NT = (((1,), (1,)), ((), ()))
HI = lax.Precision.HIGHEST


def kernel(
    img_ref, proj_ref, ctf_ref, noise_ref, trig_ref, shift_ref, class_ref,
    out_ref, ev_ref,
    placed, ometa, pair, pmeta, smeta, gath, praw, ctfh, weights, norms, onehot, ctfrows, vtab, prep,
    score, pscore, stats, post, part, from_a, from_b, from_p, from_m, zsend, zrecv, keep, fin,
    loc_sem, core_s, core_r, meta_s, meta_r, stat_s, stat_r, z_s, z_r,
    yp_s, ym_s, yl_r, yr_r, fa_s, fb_s, fa_r, fb_r, sc_s, sc_r,
    a_s, b_s, a_r, b_r, p_s, m_s, p_r, m_r, w_s, w_r, f_s, f_r,
):
    img = lax.axis_index("img")
    ori = lax.axis_index("ori")
    x, zh = img // 2, img % 2
    core, y, zl = ori % 2, (ori // 2) % 4, ori // 8
    xp, xm, x2 = (x + 1) % 4, (x + 3) % 4, (x + 2) % 4
    yp, ym, y2 = (y + 1) % 4, (y + 3) % 4, (y + 2) % 4
    own = zl * 4 + y

    def dev(x_=x, zh_=zh, zl_=zl, y_=y, core_=core):
        return (x_ * 2 + zh_, (zl_ * 4 + y_) * 2 + core_)

    def send(src, dst, ss, rs, target):
        return pltpu.make_async_remote_copy(
            src_ref=src, dst_ref=dst, send_sem=ss, recv_sem=rs,
            device_id=target, device_id_type=pl.DeviceIdType.MESH,
        )

    peer = dev(core_=1 - core)
    others = [dev(zl_=(zl + dz) % 4, y_=(y + dy) % 4) for dz, dy in OTHERS]
    right, left = dev(x_=xp), dev(x_=xm)
    up, down = dev(y_=yp), dev(y_=ym)
    across = dev(zh_=1 - zh)

    barrier = pltpu.get_barrier_semaphore()
    greeted = [peer, *others, right, left, across]
    for target in greeted:
        pl.semaphore_signal(barrier, inc=1, device_id=target, device_id_type=pl.DeviceIdType.MESH)

    mine = pl.ds(pl.multiple_of(core * SHIFT, LANES), HALF)
    theirs = pl.ds(pl.multiple_of((1 - core) * SHIFT, LANES), HALF)
    ctf_copy = pltpu.make_async_copy(ctf_ref.at[:, mine], ctfh, loc_sem.at[0])
    proj_copy = pltpu.make_async_copy(proj_ref.at[:, mine], praw.at[core], loc_sem.at[1])
    ctf_copy.start()
    proj_copy.start()

    lane = lax.broadcasted_iota(jnp.int32, (8, LANES), 1)
    place = lax.broadcasted_iota(jnp.int32, (8, LANES), 0)
    held_here = (place >= 4) == (core == 1)

    def lay_out(s, carry):
        cols = pl.ds(pl.multiple_of(s * LANES, LANES), LANES)
        straight = img_ref[:, cols].astype(F32)
        swapped = pltpu.roll(straight, 4, 0)
        low = jnp.where(core == 0, straight, swapped)
        high = jnp.where(core == 0, swapped, straight)
        both = jnp.concatenate([low, high], axis=0)
        seen = jnp.concatenate([held_here, held_here], axis=0)
        placed[:, cols] = jnp.where(seen, both, 0.0).astype(BF16)
        return carry

    lax.fori_loop(0, 65, lay_out, 0, unroll=5)
    meta = jnp.zeros((8, LANES), jnp.int32)
    for i in range(4):
        row = place == i + 4 * core
        for t in range(TRANS):
            for k in range(2):
                spot = jnp.logical_and(row, lane == 2 * t + k)
                meta = jnp.where(spot, shift_ref[i, k, t], meta)
        meta = jnp.where(jnp.logical_and(row, lane == 8), class_ref[i], meta)
    meta = meta.astype(F32)
    ometa[...] = jnp.concatenate([meta, jnp.zeros_like(meta)], axis=0).astype(BF16)

    pl.semaphore_wait(barrier, len(greeted))

    pair_copy = send(placed.at[:, theirs], pair, core_s.at[0], core_r.at[0], peer)
    pmeta_copy = send(ometa, pmeta, core_s.at[1], core_r.at[1], peer)
    praw_copy = send(proj_ref.at[:, theirs], praw.at[core], core_s.at[2], core_r.at[2], peer)
    pmeta_copy.start()
    pair_copy.start()
    praw_copy.start()

    pmeta_copy.wait_recv()
    smeta[own] = ometa[...] + pmeta[...]
    meta_copies = [
        send(smeta.at[own], smeta.at[own], meta_s.at[n], meta_r.at[n], target)
        for n, target in enumerate(others)
    ]
    for copy in meta_copies:
        copy.start()

    pair_copy.wait_recv()
    gath[own] = placed[:, mine] + pair[...]

    b0, b1 = zl % 2, zl // 2

    def pick(table):
        low = (1 - b0) * table[0] + b0 * table[1]
        high = (1 - b0) * table[2] + b0 * table[3]
        return (1 - b1) * low + b1 * high

    order = [zl, pick([1, 0, 3, 2]), pick([2, 2, 1, 1]), pick([3, 3, 0, 0])]

    def z_copy(zq, step, target):
        b = zq * 4 + y
        return send(gath.at[b], gath.at[b], z_s.at[step], z_r.at[zq], target)

    z_right = [z_copy(order[q], q, dev(zl_=zl + 1)) for q in range(4)]
    z_left = [z_copy(order[q], 4 + q, dev(zl_=zl - 1)) for q in range(4)]
    goes_right = [zl < 3] + [jnp.logical_and(order[q] < zl, zl < 3) for q in (1, 2, 3)]
    goes_left = [zl > 0] + [jnp.logical_and(order[q] > zl, zl > 0) for q in (1, 2, 3)]
    y_up = [
        send(gath.at[order[q] * 4 + y], gath.at[order[q] * 4 + y], yp_s.at[q], yl_r.at[q], up)
        for q in range(4)
    ]
    y_down = [
        send(gath.at[order[q] * 4 + y], gath.at[order[q] * 4 + y], ym_s.at[q], yr_r.at[q], down)
        for q in range(4)
    ]
    first, second = pl.ds(0, HALF_A), pl.ds(HALF_A, HALF - HALF_A)
    fwd_up, fwd_down = [], []
    for q in range(4):
        low = gath.at[order[q] * 4 + ym, :, first]
        high = gath.at[order[q] * 4 + yp, :, second]
        fwd_up.append(send(low, low, fa_s.at[q], fa_r.at[q], up))
        fwd_down.append(send(high, high, fb_s.at[q], fb_r.at[q], down))

    def launch(q):
        pl.when(goes_right[q])(lambda: z_right[q].start())
        pl.when(goes_left[q])(lambda: z_left[q].start())
        y_up[q].start()
        y_down[q].start()

    launch(0)

    def fill_rows(s, carry):
        p = (s + 32 * core) * LANES + lane
        vtab[s] = lax.shift_right_logical(p * 64528, 22)
        return carry

    lax.fori_loop(0, TILES, fill_rows, 0)

    for copy in meta_copies:
        copy.wait_recv()

    lane2 = lax.broadcasted_iota(jnp.int32, (8, 256), 1)

    def fill_onehot(b, carry):
        classes = smeta[b].astype(F32)[0:8, 8:9].astype(jnp.int32)
        hit = jnp.logical_and(lane2 % 64 == classes, lane2 < 192)
        onehot[pl.ds(pl.multiple_of(b * 8, 8), 8), :] = hit.astype(F32)
        return carry

    lax.fori_loop(0, BLOCKS, fill_onehot, 0)
    ctf_copy.wait()

    def pieces(value):
        one = value.astype(BF16)
        rest = value - one.astype(F32)
        two = rest.astype(BF16)
        three = (rest - two.astype(F32)).astype(BF16)
        return one, two, three

    def fill_ctf(s, carry):
        cols = pl.ds(pl.multiple_of(s * 384, 384), 384)
        one, two, three = pieces(ctfh[:, cols])
        ctfrows[:, cols] = jnp.dot(
            onehot[...].astype(BF16),
            jnp.concatenate([one, two, three, one], axis=0),
            preferred_element_type=F32,
        )
        return carry

    lax.fori_loop(0, TILES // 3, fill_ctf, 0)

    def weigh(s, total):
        cols = pl.ds(pl.multiple_of(s * LANES, LANES), LANES)
        first_ = praw[0, :, cols].astype(F32).reshape(2, 8, 1, 8, LANES)
        second_ = praw[1, :, cols].astype(F32).reshape(2, 8, 1, 8, LANES)
        both = jnp.concatenate([first_, second_], axis=2).reshape(2, 128, LANES)
        counted = 1 - core * (1 - jnp.minimum(s, 1))
        noise = noise_ref[pl.ds(core * 32 + s, 1), :] * counted.astype(F32)
        scaled = (both * noise[None]).astype(BF16)
        weights[:, pl.ds(pl.multiple_of(s * 256, 256), LANES)] = scaled[0]
        weights[:, pl.ds(pl.multiple_of(s * 256 + 128, 128), LANES)] = scaled[1]
        power = both[0] * both[0] + both[1] * both[1]
        ctf = ctfh[:, cols]
        p1, p2, p3 = pieces(power)
        c1, c2, c3 = pieces(ctf * ctf * noise)
        return total + lax.dot_general(
            jnp.concatenate([p1, p2, p3, p1, p2, p1], axis=1),
            jnp.concatenate([c1, c1, c1, c2, c2, c3], axis=1),
            NT, preferred_element_type=F32,
        )

    cosine = trig_ref[0:8, :]
    sine = trig_ref[8:16, :]

    def prepare(b):
        meta = smeta[b].astype(F32)[0:8, :].astype(jnp.int32)
        base, slope = [], []
        for t in range(TRANS):
            sx = meta[:, 2 * t : 2 * t + 1]
            sy = meta[:, 2 * t + 1 : 2 * t + 2]
            base.append(lane * sx)
            slope.append(jnp.broadcast_to(sy - KX * sx, (8, LANES)))

        def body(s, carry):
            cols = pl.ds(pl.multiple_of(s * LANES, LANES), LANES)
            block = gath[b, :, cols].astype(F32)
            ctf = ctfrows[pl.ds(pl.multiple_of(b * 8, 8), 8), cols]
            real, imag = block[0:8] * ctf, block[8:16] * ctf
            height = vtab[s]
            reals, imags = [], []
            for t in range(TRANS):
                index = (base[t] + height * slope[t]) & (KY - 1)
                c = jnp.take_along_axis(cosine, index, axis=1)
                si = jnp.take_along_axis(sine, index, axis=1)
                reals.append(real * c + imag * si)
                imags.append(imag * c - real * si)
            for h in range(2):
                at = pl.ds(pl.multiple_of(b * 32 + h * 16, 16), 16)
                prep[at, pl.ds(pl.multiple_of(s * 256, 256), LANES)] = jnp.concatenate(
                    reals[2 * h : 2 * h + 2], axis=0
                ).astype(BF16)
                prep[at, pl.ds(pl.multiple_of(s * 256 + 128, 128), LANES)] = jnp.concatenate(
                    imags[2 * h : 2 * h + 2], axis=0
                ).astype(BF16)
            return carry

        lax.fori_loop(0, TILES, body, 0, unroll=11)

    def score_group(g):
        rows = pl.ds(pl.multiple_of(g * 128, 128), 128)

        def body(i, total):
            cols = pl.ds(pl.multiple_of(i * 768, 768), 768)
            return total + lax.dot_general(
                weights[:, cols], prep[rows, cols], NT, preferred_element_type=F32
            )

        cross = lax.fori_loop(0, TILES // 3, body, jnp.zeros((128, 128), F32))
        picked = onehot[pl.ds(pl.multiple_of(g * 32, 32), 32), 0:LANES].reshape(4, 1, 8, LANES)
        picked = jnp.concatenate([picked] * TRANS, axis=1).reshape(128, LANES)
        norm = lax.dot_general(
            norms[...], picked[:, :64], NT, precision=HI, preferred_element_type=F32
        )
        score[g] = cross - norm

    sc_copies = [
        send(score.at[order[q]], pscore.at[order[q]], sc_s.at[q], sc_r.at[q], peer)
        for q in range(4)
    ]

    def finish(q):
        fwd_up[q].wait_recv()
        fwd_down[q].wait_recv()
        prepare(order[q] * 4 + y2)
        score_group(order[q])
        sc_copies[q].start()

    def arrive(q):
        z_right[q].wait_recv()
        launch(q)

    def forward(q):
        y_up[q].wait_recv()
        fwd_up[q].start()
        y_down[q].wait_recv()
        fwd_down[q].start()

    def prepare_three(q):
        def three(i, carry):
            prepare(order[q] * 4 + (y + 3 + i) % 4)
            return carry

        lax.fori_loop(0, 3, three, 0)

    arrive(1)
    forward(0)
    prepare_three(0)
    arrive(2)
    forward(1)
    proj_copy.wait()
    praw_copy.wait_recv()
    norms[...] = 0.5 * lax.fori_loop(0, TILES, weigh, jnp.zeros((128, 64), F32), unroll=3)
    arrive(3)
    prepare_three(1)
    forward(2)
    finish(0)
    prepare_three(2)
    forward(3)
    finish(1)
    prepare_three(3)
    finish(2)
    finish(3)

    stats[own] = jnp.zeros((16, LANES), F32)
    for copy in sc_copies:
        copy.wait_recv()
    for g in range(4):
        whole = score[g] + pscore[g]
        pscore[g] = whole
        top = jnp.max(whole, axis=0, keepdims=True)
        stats[own, g : g + 1, :] = top
        stats[own, 8 + g : 9 + g, :] = jnp.sum(jnp.exp(whole - top), axis=0, keepdims=True)
    stat_copies = [
        send(stats.at[own], stats.at[own], stat_s.at[n], stat_r.at[n], target)
        for n, target in enumerate(others)
    ]
    for copy in stat_copies:
        copy.start()
    for copy in stat_copies:
        copy.wait_recv()
    tops = [stats[b, 0:8, :] for b in range(BLOCKS)]
    top = tops[0]
    for b in range(1, BLOCKS):
        top = jnp.maximum(top, tops[b])
    total = jnp.zeros((8, LANES), F32)
    for b in range(BLOCKS):
        total += stats[b, 8:16, :] * jnp.exp(tops[b] - top)
    held = lax.broadcasted_iota(jnp.int32, (8, LANES), 1) % 32

    def turn(value, by):
        inside = pltpu.roll(value, by, 1)
        wrapped = pltpu.roll(value, by + LANES - 32, 1)
        return jnp.where(held >= by, inside, wrapped)

    largest = jnp.maximum(top, turn(top, 8))
    largest = jnp.maximum(largest, turn(largest, 16))
    total = total * jnp.exp(top - largest)
    total = total + turn(total, 8)
    total = total + turn(total, 16)
    evidence = largest + jnp.log(total)
    own_row = jnp.sum(jnp.where(place == zl, evidence, 0.0), axis=0, keepdims=True)
    ev_ref[...] = pltpu.roll(jnp.broadcast_to(own_row, (8, LANES)), 128 - (y * 32 + core * 4), 1)
    for g in range(4):
        post[:, g * 128 : (g + 1) * 128] = (
            jnp.exp(pscore[g] - evidence[g : g + 1, :]) * 2048.0
        ).astype(BF16)

    def copy_a(c):
        return send(part.at[c, 2 * x2], from_a.at[c], a_s.at[c], a_r.at[c], right)

    def copy_b(c):
        return send(part.at[c, 2 * x2 + 1], from_b.at[c], b_s.at[c], b_r.at[c], left)

    def copy_p(c):
        return send(part.at[c, pl.ds(2 * xp, 2)], from_p.at[c], p_s.at[c], p_r.at[c], right)

    def copy_m(c):
        return send(part.at[c, pl.ds(2 * xm, 2)], from_m.at[c], m_s.at[c], m_r.at[c], left)

    def copy_w(c):
        return send(zsend.at[c], zrecv.at[c], w_s.at[c], w_r.at[c], across)

    def copy_f(c):
        other = pl.ds(pl.multiple_of((1 - core) * 8, 8), 8)
        return send(keep.at[c, other], fin.at[c], f_s.at[c], f_r.at[c], peer)

    def write(c, half, value):
        for s in range(CHUNK_TILES):
            at = pl.ds(pl.multiple_of(half * SHIFT + (c * CHUNK_TILES + s) * LANES, LANES), LANES)
            for k in range(2):
                out_ref[k, :, at] = value[:, s * 256 + k * 128 : s * 256 + k * 128 + 128]

    def project(c):
        cols = pl.ds(pl.multiple_of(c * CW, CW), CW)
        sums = jnp.dot(post[...], prep[:, cols], preferred_element_type=F32).astype(BF16)
        for i in range(8):
            part[c, i] = sums[16 * i : 16 * i + 16]
        copy_a(c).start()
        copy_b(c).start()

    def add(into, *others_):
        value = into.astype(F32)
        for other in others_:
            value = value + other.astype(F32)
        return value

    def pass_on(c):
        copy_a(c).wait_recv()
        part[c, 2 * xp] = add(part[c, 2 * xp], from_a[c]).astype(BF16)
        copy_p(c).start()
        copy_b(c).wait_recv()
        part[c, 2 * xm + 1] = add(part[c, 2 * xm + 1], from_b[c]).astype(BF16)
        copy_m(c).start()

    def collect(c):
        copy_p(c).wait_recv()
        copy_m(c).wait_recv()
        far = 1 - zh
        zsend[c] = add(part[c, 2 * x + far], from_p[c, far], from_m[c, far]).astype(BF16)
        copy_w(c).start()
        keep[c] = add(part[c, 2 * x + zh], from_p[c, zh], from_m[c, zh])

    def complete(c):
        copy_w(c).wait_recv()
        keep[c] = keep[c] + zrecv[c].astype(F32)
        copy_f(c).start()
        write(c, core, keep[c, pl.ds(pl.multiple_of(core * 8, 8), 8), :])

    def close(c):
        copy_f(c).wait_recv()
        write(c, 1 - core, fin[c])

    stages = [(0, project), (2, pass_on), (4, collect), (6, complete), (8, close)]

    def step(n, carry):
        for lag, stage in stages:
            here = jnp.logical_and(n >= lag, n < CHUNKS + lag)

            @pl.when(here)
            def _(lag=lag, stage=stage):
                stage(n - lag)

        return carry

    lax.fori_loop(0, CHUNKS + 8, step, 0)

    pmeta_copy.wait_send()
    pair_copy.wait_send()
    praw_copy.wait_send()
    for copy in meta_copies + stat_copies + sc_copies + y_up + y_down + fwd_up + fwd_down:
        copy.wait_send()
    for q in range(4):
        pl.when(goes_right[q])(lambda q=q: z_right[q].wait_send())
        pl.when(goes_left[q])(lambda q=q: z_left[q].wait_send())

    def sent(c, carry):
        for copy in (copy_a, copy_b, copy_p, copy_m, copy_w, copy_f):
            copy(c).wait_send()
        return carry

    lax.fori_loop(0, CHUNKS, sent, 0)


def per_device(images, projections, ctf_table, noise_weight, shifts, defocus):
    local = images.shape[0]
    pixels = images.shape[2]
    rows = images.transpose(1, 0, 2).reshape(2 * local, pixels)
    proj = projections.transpose(1, 0, 2).reshape(128, pixels)
    angles = np.arange(KY) * (2.0 * math.pi / KY)
    trig = np.concatenate([np.tile(np.cos(angles), (8, 1)), np.tile(np.sin(angles), (8, 1))])
    trig = jnp.asarray(trig.astype(np.float32))
    vmem = pl.BlockSpec(memory_space=pltpu.VMEM)
    hbm = pl.BlockSpec(memory_space=pl.ANY)
    smem = pl.BlockSpec(memory_space=pltpu.SMEM)
    dma = pltpu.SemaphoreType.DMA
    sems = [dma((2,)), dma((3,)), dma((3,)), dma((15,)), dma((15,)), dma((15,)), dma((15,))]
    sems += [dma((8,)), dma((4,))] + [dma((4,))] * 10 + [dma((CHUNKS,))] * 12
    sums, evidence = pl.pallas_call(
        kernel,
        out_shape=(
            jax.ShapeDtypeStruct((2, 8, pixels), F32),
            jax.ShapeDtypeStruct((8, LANES), F32),
        ),
        in_specs=[vmem, hbm, hbm, vmem, vmem, smem, smem],
        out_specs=(vmem, vmem),
        scratch_shapes=[
            pltpu.VMEM((16, 65 * LANES), BF16),
            pltpu.VMEM((16, LANES), BF16),
            pltpu.VMEM((16, HALF), BF16),
            pltpu.VMEM((16, LANES), BF16),
            pltpu.VMEM((BLOCKS, 16, LANES), BF16),
            pltpu.VMEM((BLOCKS, 16, HALF), BF16),
            pltpu.VMEM((2, 128, HALF), BF16),
            pltpu.VMEM((64, HALF), F32),
            pltpu.VMEM((128, 2 * HALF), BF16),
            pltpu.VMEM((128, 64), F32),
            pltpu.VMEM((128, 2 * LANES), F32),
            pltpu.VMEM((128, HALF), F32),
            pltpu.VMEM((TILES, 8, LANES), jnp.int32),
            pltpu.VMEM((BLOCKS * 32, 2 * HALF), BF16),
            pltpu.VMEM((4, 128, 128), F32),
            pltpu.VMEM((4, 128, 128), F32),
            pltpu.VMEM((BLOCKS, 16, LANES), F32),
            pltpu.VMEM((128, 512), BF16),
            pltpu.VMEM((CHUNKS, 8, 16, CW), BF16),
            pltpu.VMEM((CHUNKS, 16, CW), BF16),
            pltpu.VMEM((CHUNKS, 16, CW), BF16),
            pltpu.VMEM((CHUNKS, 2, 16, CW), BF16),
            pltpu.VMEM((CHUNKS, 2, 16, CW), BF16),
            pltpu.VMEM((CHUNKS, 16, CW), BF16),
            pltpu.VMEM((CHUNKS, 16, CW), BF16),
            pltpu.VMEM((CHUNKS, 16, CW), F32),
            pltpu.VMEM((CHUNKS, 8, CW), F32),
            *sems,
        ],
        compiler_params=pltpu.CompilerParams(
            collective_id=0, has_side_effects=True, vmem_limit_bytes=56 * 1024 * 1024
        ),
    )(
        rows, proj, ctf_table, noise_weight.reshape(65, LANES), trig,
        shifts.transpose(0, 2, 1), defocus,
    )
    return evidence[0, :local], sums.transpose(1, 0, 2)


def solution(mesh):
    in_specs = (
        P(("img", "ori"), None, None),
        P("ori", None, None),
        P(),
        P(),
        P(("img", "ori"), None, None),
        P(("img", "ori")),
    )
    out_specs = (P(("img", "ori")), P(("ori", "img"), None, None))
    return jax.shard_map(
        per_device, mesh=mesh, in_specs=in_specs, out_specs=out_specs, check_vma=False
    )
```

```python
import math

import jax
import jax.numpy as jnp
import numpy as np
from jax import lax
from jax.experimental import pallas as pl
from jax.experimental.pallas import tpu as pltpu
from jax.sharding import PartitionSpec as P

KY = 128
KX = 65
LANES = 128
NX, NZ, NY = 4, 4, 4
BLOCKS = NZ * NY
TRANS = 4
TILES = 33
HALF = TILES * LANES
SHIFT = 32 * LANES
HALF_A = 17 * LANES
CHUNKS = 11
CHUNK_TILES = TILES // CHUNKS
CW = CHUNK_TILES * 2 * LANES
OTHERS = [(dz, dy) for dz in range(NZ) for dy in range(NY) if (dz, dy) != (0, 0)]
F32 = jnp.float32
BF16 = jnp.bfloat16
HI = lax.Precision.HIGHEST


def kernel(
    img_ref, proj_ref, ctf_ref, noise_ref, trig_ref, shift_ref, class_ref,
    out_ref, ev_ref,
    placed, ometa, pair, pmeta, smeta, gath, praw, ctfh, weights, norms, onehot, ctfrows, vtab, prep,
    score, pscore, stats, post, part, from_a, from_b, from_p, from_m, zsend, zrecv, keep, fin,
    loc_sem, core_s, core_r, meta_s, meta_r, stat_s, stat_r, z_s, z_r,
    yp_s, ym_s, yl_r, yr_r, fa_s, fb_s, fa_r, fb_r, sc_s, sc_r,
    a_s, b_s, a_r, b_r, p_s, m_s, p_r, m_r, w_s, w_r, f_s, f_r,
):
    img = lax.axis_index("img")
    ori = lax.axis_index("ori")
    x, zh = img // 2, img % 2
    core, y, zl = ori % 2, (ori // 2) % 4, ori // 8
    xp, xm, x2 = (x + 1) % 4, (x + 3) % 4, (x + 2) % 4
    yp, ym, y2 = (y + 1) % 4, (y + 3) % 4, (y + 2) % 4
    own = zl * 4 + y

    def dev(x_=x, zh_=zh, zl_=zl, y_=y, core_=core):
        return (x_ * 2 + zh_, (zl_ * 4 + y_) * 2 + core_)

    def send(src, dst, ss, rs, target):
        return pltpu.make_async_remote_copy(
            src_ref=src, dst_ref=dst, send_sem=ss, recv_sem=rs,
            device_id=target, device_id_type=pl.DeviceIdType.MESH,
        )

    peer = dev(core_=1 - core)
    others = [dev(zl_=(zl + dz) % 4, y_=(y + dy) % 4) for dz, dy in OTHERS]
    right, left = dev(x_=xp), dev(x_=xm)
    up, down = dev(y_=yp), dev(y_=ym)
    across = [dev(zh_=1 - zh, core_=k) for k in range(2)]

    barrier = pltpu.get_barrier_semaphore()
    greeted = [peer, *others, right, left, *across]
    for target in greeted:
        pl.semaphore_signal(barrier, inc=1, device_id=target, device_id_type=pl.DeviceIdType.MESH)

    mine = pl.ds(pl.multiple_of(core * SHIFT, LANES), HALF)
    theirs = pl.ds(pl.multiple_of((1 - core) * SHIFT, LANES), HALF)
    ctf_copy = pltpu.make_async_copy(ctf_ref.at[:, mine], ctfh, loc_sem.at[0])
    proj_copy = pltpu.make_async_copy(proj_ref.at[:, mine], praw.at[core], loc_sem.at[1])
    ctf_copy.start()
    proj_copy.start()

    lane = lax.broadcasted_iota(jnp.int32, (8, LANES), 1)
    place = lax.broadcasted_iota(jnp.int32, (8, LANES), 0)
    held_here = (place >= 4) == (core == 1)

    def lay_out(s, carry):
        cols = pl.ds(pl.multiple_of(s * LANES, LANES), LANES)
        straight = img_ref[:, cols].astype(F32)
        swapped = pltpu.roll(straight, 4, 0)
        low = jnp.where(core == 0, straight, swapped)
        high = jnp.where(core == 0, swapped, straight)
        both = jnp.concatenate([low, high], axis=0)
        seen = jnp.concatenate([held_here, held_here], axis=0)
        placed[:, cols] = jnp.where(seen, both, 0.0).astype(BF16)
        return carry

    lax.fori_loop(0, 65, lay_out, 0, unroll=5)
    meta = jnp.zeros((8, LANES), jnp.int32)
    for i in range(4):
        row = place == i + 4 * core
        for t in range(TRANS):
            for k in range(2):
                spot = jnp.logical_and(row, lane == 2 * t + k)
                meta = jnp.where(spot, shift_ref[i, k, t], meta)
        meta = jnp.where(jnp.logical_and(row, lane == 8), class_ref[i], meta)
    meta = meta.astype(F32)
    ometa[...] = jnp.concatenate([meta, jnp.zeros_like(meta)], axis=0).astype(BF16)

    pl.semaphore_wait(barrier, len(greeted))

    pair_copy = send(placed.at[:, theirs], pair, core_s.at[0], core_r.at[0], peer)
    pmeta_copy = send(ometa, pmeta, core_s.at[1], core_r.at[1], peer)
    praw_copy = send(proj_ref.at[:, theirs], praw.at[core], core_s.at[2], core_r.at[2], peer)
    pmeta_copy.start()
    pair_copy.start()
    praw_copy.start()

    pmeta_copy.wait_recv()
    smeta[own] = ometa[...] + pmeta[...]
    meta_copies = [
        send(smeta.at[own], smeta.at[own], meta_s.at[n], meta_r.at[n], target)
        for n, target in enumerate(others)
    ]
    for copy in meta_copies:
        copy.start()

    pair_copy.wait_recv()
    gath[own] = placed[:, mine] + pair[...]

    b0, b1 = zl % 2, zl // 2

    def pick(table):
        low = (1 - b0) * table[0] + b0 * table[1]
        high = (1 - b0) * table[2] + b0 * table[3]
        return (1 - b1) * low + b1 * high

    order = [zl, pick([1, 0, 3, 2]), pick([2, 2, 1, 1]), pick([3, 3, 0, 0])]

    def z_copy(zq, step, target):
        b = zq * 4 + y
        return send(gath.at[b], gath.at[b], z_s.at[step], z_r.at[zq], target)

    z_right = [z_copy(order[q], q, dev(zl_=zl + 1)) for q in range(4)]
    z_left = [z_copy(order[q], 4 + q, dev(zl_=zl - 1)) for q in range(4)]
    goes_right = [zl < 3] + [jnp.logical_and(order[q] < zl, zl < 3) for q in (1, 2, 3)]
    goes_left = [zl > 0] + [jnp.logical_and(order[q] > zl, zl > 0) for q in (1, 2, 3)]
    y_up = [
        send(gath.at[order[q] * 4 + y], gath.at[order[q] * 4 + y], yp_s.at[q], yl_r.at[q], up)
        for q in range(4)
    ]
    y_down = [
        send(gath.at[order[q] * 4 + y], gath.at[order[q] * 4 + y], ym_s.at[q], yr_r.at[q], down)
        for q in range(4)
    ]
    first, second = pl.ds(0, HALF_A), pl.ds(HALF_A, HALF - HALF_A)
    fwd_up, fwd_down = [], []
    for q in range(4):
        low = gath.at[order[q] * 4 + ym, :, first]
        high = gath.at[order[q] * 4 + yp, :, second]
        fwd_up.append(send(low, low, fa_s.at[q], fa_r.at[q], up))
        fwd_down.append(send(high, high, fb_s.at[q], fb_r.at[q], down))

    def launch(q):
        pl.when(goes_right[q])(lambda: z_right[q].start())
        pl.when(goes_left[q])(lambda: z_left[q].start())
        y_up[q].start()
        y_down[q].start()

    launch(0)

    def fill_rows(s, carry):
        p = (s + 32 * core) * LANES + lane
        after = lax.shift_right_logical((p + LANES) * 64528, 22)
        vtab[s] = after - lax.shift_right_logical(p * 64528, 22)
        return carry

    lax.fori_loop(0, TILES, fill_rows, 0)
    top_row = lax.shift_right_logical((32 * core * LANES + lane) * 64528, 22)

    for copy in meta_copies:
        copy.wait_recv()

    lane2 = lax.broadcasted_iota(jnp.int32, (8, 256), 1)

    def fill_onehot(b, carry):
        classes = smeta[b].astype(F32)[0:8, 8:9].astype(jnp.int32)
        hit = jnp.logical_and(lane2 % 64 == classes, lane2 < 192)
        onehot[pl.ds(pl.multiple_of(b * 8, 8), 8), :] = hit.astype(F32)
        return carry

    lax.fori_loop(0, BLOCKS, fill_onehot, 0)
    ctf_copy.wait()

    def pieces(value):
        one = value.astype(BF16)
        rest = value - one.astype(F32)
        two = rest.astype(BF16)
        three = (rest - two.astype(F32)).astype(BF16)
        return one, two, three

    def fill_ctf(s, carry):
        cols = pl.ds(pl.multiple_of(s * 384, 384), 384)
        one, two, three = pieces(ctfh[:, cols])
        ctfrows[:, cols] = jnp.dot(
            onehot[...].astype(BF16),
            jnp.concatenate([one, two, three, one], axis=0),
            preferred_element_type=F32,
        )
        return carry

    lax.fori_loop(0, TILES // 3, fill_ctf, 0)

    def weigh(s, total):
        cols = pl.ds(pl.multiple_of(s * LANES, LANES), LANES)
        first_ = praw[0, :, cols].astype(F32).reshape(2, 8, 1, 8, LANES)
        second_ = praw[1, :, cols].astype(F32).reshape(2, 8, 1, 8, LANES)
        both = jnp.concatenate([first_, second_], axis=2).reshape(2, 128, LANES)
        counted = 1 - core * (1 - jnp.minimum(s, 1))
        noise = noise_ref[pl.ds(core * 32 + s, 1), :] * counted.astype(F32)
        scaled = (both * noise[None]).astype(BF16)
        weights[pl.ds(pl.multiple_of(s * 256, 256), LANES), :] = scaled[0].T
        weights[pl.ds(pl.multiple_of(s * 256 + 128, 128), LANES), :] = scaled[1].T
        power = (both[0] * both[0] + both[1] * both[1]).T
        ctf = ctfh[:, cols]
        p1, p2, p3 = pieces(power)
        c1, c2, c3 = pieces(ctf * ctf * noise)
        return total + jnp.dot(
            jnp.concatenate([c1, c1, c1, c2, c2, c3], axis=1),
            jnp.concatenate([p1, p2, p3, p1, p2, p1], axis=0),
            preferred_element_type=F32,
        )

    cosine = trig_ref[0:8, :]
    sine = trig_ref[8:16, :]

    def prepare(b):
        meta = smeta[b].astype(F32)[0:8, :].astype(jnp.int32)

        def wave(steps):
            index = steps & (KY - 1)
            return (
                jnp.take_along_axis(cosine, index, axis=1),
                jnp.take_along_axis(sine, index, axis=1),
            )

        begin, one_row, two_rows = [], [], []
        for t in range(TRANS):
            sx = meta[:, 2 * t : 2 * t + 1]
            sy = meta[:, 2 * t + 1 : 2 * t + 2]
            slope = jnp.broadcast_to(sy - KX * sx, (8, LANES))
            begin.append(wave(lane * sx + top_row * slope))
            one_row.append(wave(slope))
            two_rows.append(wave(2 * slope))

        def body(s, phases):
            cols = pl.ds(pl.multiple_of(s * LANES, LANES), LANES)
            block = gath[b, :, cols].astype(F32)
            ctf = ctfrows[pl.ds(pl.multiple_of(b * 8, 8), 8), cols]
            real, imag = block[0:8] * ctf, block[8:16] * ctf
            single = vtab[s] == 1
            reals, imags, later = [], [], []
            for t in range(TRANS):
                c, si = phases[t]
                reals.append(real * c + imag * si)
                imags.append(imag * c - real * si)
                mc = jnp.where(single, one_row[t][0], two_rows[t][0])
                ms = jnp.where(single, one_row[t][1], two_rows[t][1])
                later.append((c * mc - si * ms, si * mc + c * ms))
            for h in range(2):
                at = pl.ds(pl.multiple_of(b * 32 + h * 16, 16), 16)
                prep[at, pl.ds(pl.multiple_of(s * 256, 256), LANES)] = jnp.concatenate(
                    reals[2 * h : 2 * h + 2], axis=0
                ).astype(BF16)
                prep[at, pl.ds(pl.multiple_of(s * 256 + 128, 128), LANES)] = jnp.concatenate(
                    imags[2 * h : 2 * h + 2], axis=0
                ).astype(BF16)
            return tuple(later)

        lax.fori_loop(0, TILES, body, tuple(begin), unroll=11)

    def score_group(g):
        rows = pl.ds(pl.multiple_of(g * 128, 128), 128)

        def body(i, total):
            cols = pl.ds(pl.multiple_of(i * 768, 768), 768)
            return total + jnp.dot(
                prep[rows, cols], weights[cols, :], preferred_element_type=F32
            )

        cross = lax.fori_loop(0, TILES // 3, body, jnp.zeros((128, 128), F32))
        picked = onehot[pl.ds(pl.multiple_of(g * 32, 32), 32), 0:LANES].reshape(4, 1, 8, LANES)
        picked = jnp.concatenate([picked] * TRANS, axis=1).reshape(128, LANES)
        norm = jnp.dot(picked[:, :64], norms[...], precision=HI, preferred_element_type=F32)
        score[g] = cross - norm

    sc_copies = [
        send(score.at[order[q]], pscore.at[order[q]], sc_s.at[q], sc_r.at[q], peer)
        for q in range(4)
    ]

    def finish(q):
        fwd_up[q].wait_recv()
        fwd_down[q].wait_recv()
        prepare(order[q] * 4 + y2)
        score_group(order[q])
        sc_copies[q].start()

    def arrive(q):
        z_right[q].wait_recv()
        launch(q)

    def forward(q):
        y_up[q].wait_recv()
        fwd_up[q].start()
        y_down[q].wait_recv()
        fwd_down[q].start()

    def prepare_three(q):
        def three(i, carry):
            prepare(order[q] * 4 + (y + 3 + i) % 4)
            return carry

        lax.fori_loop(0, 3, three, 0)

    arrive(1)
    forward(0)
    prepare_three(0)
    arrive(2)
    forward(1)
    proj_copy.wait()
    praw_copy.wait_recv()
    norms[...] = 0.5 * lax.fori_loop(0, TILES, weigh, jnp.zeros((64, 128), F32), unroll=3)
    arrive(3)
    prepare_three(1)
    forward(2)
    finish(0)
    prepare_three(2)
    forward(3)
    finish(1)
    prepare_three(3)
    finish(2)
    finish(3)

    stats[own] = jnp.zeros((16, LANES), F32)
    for copy in sc_copies:
        copy.wait_recv()
    for g in range(4):
        whole = (score[g] + pscore[g]).T
        pscore[g] = whole
        top = jnp.max(whole, axis=0, keepdims=True)
        stats[own, g : g + 1, :] = top
        stats[own, 8 + g : 9 + g, :] = jnp.sum(jnp.exp(whole - top), axis=0, keepdims=True)
    stat_copies = [
        send(stats.at[own], stats.at[own], stat_s.at[n], stat_r.at[n], target)
        for n, target in enumerate(others)
    ]
    for copy in stat_copies:
        copy.start()
    for copy in stat_copies:
        copy.wait_recv()
    tops = [stats[b, 0:8, :] for b in range(BLOCKS)]
    top = tops[0]
    for b in range(1, BLOCKS):
        top = jnp.maximum(top, tops[b])
    total = jnp.zeros((8, LANES), F32)
    for b in range(BLOCKS):
        total += stats[b, 8:16, :] * jnp.exp(tops[b] - top)
    held = lax.broadcasted_iota(jnp.int32, (8, LANES), 1) % 32

    def turn(value, by):
        inside = pltpu.roll(value, by, 1)
        wrapped = pltpu.roll(value, by + LANES - 32, 1)
        return jnp.where(held >= by, inside, wrapped)

    largest = jnp.maximum(top, turn(top, 8))
    largest = jnp.maximum(largest, turn(largest, 16))
    total = total * jnp.exp(top - largest)
    total = total + turn(total, 8)
    total = total + turn(total, 16)
    evidence = largest + jnp.log(total)
    own_row = jnp.sum(jnp.where(place == zl, evidence, 0.0), axis=0, keepdims=True)
    ev_ref[...] = pltpu.roll(jnp.broadcast_to(own_row, (8, LANES)), 128 - (y * 32 + core * 4), 1)
    for g in range(4):
        post[:, g * 128 : (g + 1) * 128] = (
            jnp.exp(pscore[g] - evidence[g : g + 1, :]) * 2048.0
        ).astype(BF16)

    def copy_a(c):
        return send(part.at[c, 2 * x2], from_a.at[c], a_s.at[c], a_r.at[c], right)

    def copy_b(c):
        return send(part.at[c, 2 * x2 + 1], from_b.at[c], b_s.at[c], b_r.at[c], left)

    def copy_p(c):
        return send(part.at[c, pl.ds(2 * xp, 2)], from_p.at[c], p_s.at[c], p_r.at[c], right)

    def copy_m(c):
        return send(part.at[c, pl.ds(2 * xm, 2)], from_m.at[c], m_s.at[c], m_r.at[c], left)

    def copy_w(c, k):
        return send(zsend.at[c, k], zrecv.at[c, core], w_s.at[c, k], w_r.at[c, core], across[k])

    def arrived_w(c, half):
        return send(zsend.at[c, 0], zrecv.at[c, half], w_s.at[c, 0], w_r.at[c, half], across[0])

    def copy_f(c):
        other = pl.ds(pl.multiple_of((1 - core) * 8, 8), 8)
        return send(keep.at[c, other], fin.at[c], f_s.at[c], f_r.at[c], peer)

    def write(c, half, value):
        for s in range(CHUNK_TILES):
            at = pl.ds(pl.multiple_of(half * SHIFT + (c * CHUNK_TILES + s) * LANES, LANES), LANES)
            for k in range(2):
                out_ref[k, :, at] = value[:, s * 256 + k * 128 : s * 256 + k * 128 + 128]

    def project(c):
        cols = pl.ds(pl.multiple_of(c * CW, CW), CW)
        sums = jnp.dot(post[...], prep[:, cols], preferred_element_type=F32).astype(BF16)
        for i in range(8):
            part[c, i] = sums[16 * i : 16 * i + 16]
        copy_a(c).start()
        copy_b(c).start()

    def add(into, *others_):
        value = into.astype(F32)
        for other in others_:
            value = value + other.astype(F32)
        return value

    def pass_on(c):
        copy_a(c).wait_recv()
        part[c, 2 * xp] = add(part[c, 2 * xp], from_a[c]).astype(BF16)
        copy_p(c).start()
        copy_b(c).wait_recv()
        part[c, 2 * xm + 1] = add(part[c, 2 * xm + 1], from_b[c]).astype(BF16)
        copy_m(c).start()

    def collect(c):
        copy_p(c).wait_recv()
        copy_m(c).wait_recv()
        far = 1 - zh
        away = add(part[c, 2 * x + far], from_p[c, far], from_m[c, far])
        for k in range(2):
            rows = away[8 * k : 8 * k + 8]
            zsend[c, k] = jnp.concatenate([rows[:, : CW // 2], rows[:, CW // 2 :]], axis=0).astype(BF16)
            copy_w(c, k).start()
        keep[c] = add(part[c, 2 * x + zh], from_p[c, zh], from_m[c, zh])
        copy_f(c).start()

    def complete(c):
        for half in range(2):
            arrived_w(c, half).wait_recv()
        copy_f(c).wait_recv()
        here = keep[c, pl.ds(pl.multiple_of(core * 8, 8), 8), :]
        for half, near in ((core, here), (1 - core, fin[c])):
            rows = zrecv[c, half].astype(F32)
            write(c, half, near + jnp.concatenate([rows[0:8], rows[8:16]], axis=1))

    stages = [(0, project), (3, pass_on), (6, collect), (10, complete)]

    def step(n, carry):
        for lag, stage in stages:
            here = jnp.logical_and(n >= lag, n < CHUNKS + lag)

            @pl.when(here)
            def _(lag=lag, stage=stage):
                stage(n - lag)

        return carry

    lax.fori_loop(0, CHUNKS + 10, step, 0)

    pmeta_copy.wait_send()
    pair_copy.wait_send()
    praw_copy.wait_send()
    for copy in meta_copies + stat_copies + sc_copies + y_up + y_down + fwd_up + fwd_down:
        copy.wait_send()
    for q in range(4):
        pl.when(goes_right[q])(lambda q=q: z_right[q].wait_send())
        pl.when(goes_left[q])(lambda q=q: z_left[q].wait_send())

    def sent(c, carry):
        for copy in (copy_a, copy_b, copy_p, copy_m, copy_f):
            copy(c).wait_send()
        for k in range(2):
            copy_w(c, k).wait_send()
        return carry

    lax.fori_loop(0, CHUNKS, sent, 0)


def per_device(images, projections, ctf_table, noise_weight, shifts, defocus):
    local = images.shape[0]
    pixels = images.shape[2]
    rows = images.transpose(1, 0, 2).reshape(2 * local, pixels)
    proj = projections.transpose(1, 0, 2).reshape(128, pixels)
    angles = np.arange(KY) * (2.0 * math.pi / KY)
    trig = np.concatenate([np.tile(np.cos(angles), (8, 1)), np.tile(np.sin(angles), (8, 1))])
    trig = jnp.asarray(trig.astype(np.float32))
    vmem = pl.BlockSpec(memory_space=pltpu.VMEM)
    hbm = pl.BlockSpec(memory_space=pl.ANY)
    smem = pl.BlockSpec(memory_space=pltpu.SMEM)
    dma = pltpu.SemaphoreType.DMA
    sems = [dma((2,)), dma((3,)), dma((3,)), dma((15,)), dma((15,)), dma((15,)), dma((15,))]
    sems += [dma((8,)), dma((4,))] + [dma((4,))] * 10 + [dma((CHUNKS,))] * 8 + [dma((CHUNKS, 2))] * 2 + [dma((CHUNKS,))] * 2
    sums, evidence = pl.pallas_call(
        kernel,
        out_shape=(
            jax.ShapeDtypeStruct((2, 8, pixels), F32),
            jax.ShapeDtypeStruct((8, LANES), F32),
        ),
        in_specs=[vmem, hbm, hbm, vmem, vmem, smem, smem],
        out_specs=(vmem, vmem),
        scratch_shapes=[
            pltpu.VMEM((16, 65 * LANES), BF16),
            pltpu.VMEM((16, LANES), BF16),
            pltpu.VMEM((16, HALF), BF16),
            pltpu.VMEM((16, LANES), BF16),
            pltpu.VMEM((BLOCKS, 16, LANES), BF16),
            pltpu.VMEM((BLOCKS, 16, HALF), BF16),
            pltpu.VMEM((2, 128, HALF), BF16),
            pltpu.VMEM((64, HALF), F32),
            pltpu.VMEM((2 * HALF, 128), BF16),
            pltpu.VMEM((64, 128), F32),
            pltpu.VMEM((128, 2 * LANES), F32),
            pltpu.VMEM((128, HALF), F32),
            pltpu.VMEM((TILES, 8, LANES), jnp.int32),
            pltpu.VMEM((BLOCKS * 32, 2 * HALF), BF16),
            pltpu.VMEM((4, 128, 128), F32),
            pltpu.VMEM((4, 128, 128), F32),
            pltpu.VMEM((BLOCKS, 16, LANES), F32),
            pltpu.VMEM((128, 512), BF16),
            pltpu.VMEM((CHUNKS, 8, 16, CW), BF16),
            pltpu.VMEM((CHUNKS, 16, CW), BF16),
            pltpu.VMEM((CHUNKS, 16, CW), BF16),
            pltpu.VMEM((CHUNKS, 2, 16, CW), BF16),
            pltpu.VMEM((CHUNKS, 2, 16, CW), BF16),
            pltpu.VMEM((CHUNKS, 2, 16, CW // 2), BF16),
            pltpu.VMEM((CHUNKS, 2, 16, CW // 2), BF16),
            pltpu.VMEM((CHUNKS, 16, CW), F32),
            pltpu.VMEM((CHUNKS, 8, CW), F32),
            *sems,
        ],
        compiler_params=pltpu.CompilerParams(
            collective_id=0, has_side_effects=True, vmem_limit_bytes=56 * 1024 * 1024
        ),
    )(
        rows, proj, ctf_table, noise_weight.reshape(65, LANES), trig,
        shifts.transpose(0, 2, 1), defocus,
    )
    return evidence[0, :local], sums.transpose(1, 0, 2)


def solution(mesh):
    in_specs = (
        P(("img", "ori"), None, None),
        P("ori", None, None),
        P(),
        P(),
        P(("img", "ori"), None, None),
        P(("img", "ori")),
    )
    out_specs = (P(("img", "ori")), P(("ori", "img"), None, None))
    return jax.shard_map(
        per_device, mesh=mesh, in_specs=in_specs, out_specs=out_specs, check_vma=False
    )
```

```python
import math

import jax
import jax.numpy as jnp
import numpy as np
from jax import lax
from jax.experimental import pallas as pl
from jax.experimental.pallas import tpu as pltpu
from jax.sharding import PartitionSpec as P

KY = 128
KX = 65
LANES = 128
NX, NZ, NY = 4, 4, 4
BLOCKS = NZ * NY
TRANS = 4
TILES = 33
HALF = TILES * LANES
SHIFT = 32 * LANES
HALF_A = 17 * LANES
CHUNKS = 11
CHUNK_TILES = TILES // CHUNKS
CW = CHUNK_TILES * 2 * LANES
OTHERS = [(dz, dy) for dz in range(NZ) for dy in range(NY) if (dz, dy) != (0, 0)]
F32 = jnp.float32
BF16 = jnp.bfloat16
HI = lax.Precision.HIGHEST


def kernel(
    img_ref, proj_ref, ctf_ref, noise_ref, trig_ref, shift_ref, class_ref,
    out_ref, ev_ref,
    placed, ometa, pair, pmeta, smeta, gath, praw, ctfh, weights, norms, onehot, ctfrows, vtab, prep,
    score, pscore, stats, post, part, from_a, from_b, from_p, from_m, zsend, zrecv, keep, fin,
    loc_sem, core_s, core_r, meta_s, meta_r, stat_s, stat_r, z_s, z_r,
    yp_s, ym_s, yl_r, yr_r, fa_s, fb_s, fa_r, fb_r, sc_s, sc_r,
    a_s, b_s, a_r, b_r, p_s, m_s, p_r, m_r, w_s, w_r, f_s, f_r,
):
    img = lax.axis_index("img")
    ori = lax.axis_index("ori")
    x, zh = img // 2, img % 2
    core, y, zl = ori % 2, (ori // 2) % 4, ori // 8
    xp, xm, x2 = (x + 1) % 4, (x + 3) % 4, (x + 2) % 4
    yp, ym, y2 = (y + 1) % 4, (y + 3) % 4, (y + 2) % 4
    own = zl * 4 + y

    def dev(x_=x, zh_=zh, zl_=zl, y_=y, core_=core):
        return (x_ * 2 + zh_, (zl_ * 4 + y_) * 2 + core_)

    def send(src, dst, ss, rs, target):
        return pltpu.make_async_remote_copy(
            src_ref=src, dst_ref=dst, send_sem=ss, recv_sem=rs,
            device_id=target, device_id_type=pl.DeviceIdType.MESH,
        )

    peer = dev(core_=1 - core)
    others = [dev(zl_=(zl + dz) % 4, y_=(y + dy) % 4) for dz, dy in OTHERS]
    right, left = dev(x_=xp), dev(x_=xm)
    up, down = dev(y_=yp), dev(y_=ym)
    across = [dev(zh_=1 - zh, core_=k) for k in range(2)]

    barrier = pltpu.get_barrier_semaphore()
    greeted = [peer, *others, right, left, *across]
    for target in greeted:
        pl.semaphore_signal(barrier, inc=1, device_id=target, device_id_type=pl.DeviceIdType.MESH)

    mine = pl.ds(pl.multiple_of(core * SHIFT, LANES), HALF)
    theirs = pl.ds(pl.multiple_of((1 - core) * SHIFT, LANES), HALF)
    ctf_copy = pltpu.make_async_copy(ctf_ref.at[:, mine], ctfh, loc_sem.at[0])
    proj_copy = pltpu.make_async_copy(proj_ref.at[:, mine], praw.at[core], loc_sem.at[1])
    ctf_copy.start()
    proj_copy.start()

    lane = lax.broadcasted_iota(jnp.int32, (8, LANES), 1)
    place = lax.broadcasted_iota(jnp.int32, (8, LANES), 0)
    held_here = (place >= 4) == (core == 1)

    def lay_out(s, carry):
        cols = pl.ds(pl.multiple_of(s * LANES, LANES), LANES)
        straight = img_ref[:, cols].astype(F32)
        swapped = pltpu.roll(straight, 4, 0)
        low = jnp.where(core == 0, straight, swapped)
        high = jnp.where(core == 0, swapped, straight)
        both = jnp.concatenate([low, high], axis=0)
        seen = jnp.concatenate([held_here, held_here], axis=0)
        placed[:, cols] = jnp.where(seen, both, 0.0).astype(BF16)
        return carry

    lax.fori_loop(0, 65, lay_out, 0, unroll=5)
    meta = jnp.zeros((8, LANES), jnp.int32)
    for i in range(4):
        row = place == i + 4 * core
        for t in range(TRANS):
            for k in range(2):
                spot = jnp.logical_and(row, lane == 2 * t + k)
                meta = jnp.where(spot, shift_ref[i, k, t], meta)
        meta = jnp.where(jnp.logical_and(row, lane == 8), class_ref[i], meta)
    meta = meta.astype(F32)
    ometa[...] = jnp.concatenate([meta, jnp.zeros_like(meta)], axis=0).astype(BF16)

    pl.semaphore_wait(barrier, len(greeted))

    pair_copy = send(placed.at[:, theirs], pair, core_s.at[0], core_r.at[0], peer)
    pmeta_copy = send(ometa, pmeta, core_s.at[1], core_r.at[1], peer)
    praw_copy = send(proj_ref.at[:, theirs], praw.at[core], core_s.at[2], core_r.at[2], peer)
    pmeta_copy.start()
    pair_copy.start()
    praw_copy.start()

    pmeta_copy.wait_recv()
    smeta[own] = ometa[...] + pmeta[...]
    meta_copies = [
        send(smeta.at[own], smeta.at[own], meta_s.at[n], meta_r.at[n], target)
        for n, target in enumerate(others)
    ]
    for copy in meta_copies:
        copy.start()

    pair_copy.wait_recv()
    gath[own] = placed[:, mine] + pair[...]

    b0, b1 = zl % 2, zl // 2

    def pick(table):
        low = (1 - b0) * table[0] + b0 * table[1]
        high = (1 - b0) * table[2] + b0 * table[3]
        return (1 - b1) * low + b1 * high

    order = [zl, pick([1, 0, 3, 2]), pick([2, 2, 1, 1]), pick([3, 3, 0, 0])]

    def z_copy(zq, step, target):
        b = zq * 4 + y
        return send(gath.at[b], gath.at[b], z_s.at[step], z_r.at[zq], target)

    z_right = [z_copy(order[q], q, dev(zl_=zl + 1)) for q in range(4)]
    z_left = [z_copy(order[q], 4 + q, dev(zl_=zl - 1)) for q in range(4)]
    goes_right = [zl < 3] + [jnp.logical_and(order[q] < zl, zl < 3) for q in (1, 2, 3)]
    goes_left = [zl > 0] + [jnp.logical_and(order[q] > zl, zl > 0) for q in (1, 2, 3)]
    y_up = [
        send(gath.at[order[q] * 4 + y], gath.at[order[q] * 4 + y], yp_s.at[q], yl_r.at[q], up)
        for q in range(4)
    ]
    y_down = [
        send(gath.at[order[q] * 4 + y], gath.at[order[q] * 4 + y], ym_s.at[q], yr_r.at[q], down)
        for q in range(4)
    ]
    first, second = pl.ds(0, HALF_A), pl.ds(HALF_A, HALF - HALF_A)
    fwd_up, fwd_down = [], []
    for q in range(4):
        low = gath.at[order[q] * 4 + ym, :, first]
        high = gath.at[order[q] * 4 + yp, :, second]
        fwd_up.append(send(low, low, fa_s.at[q], fa_r.at[q], up))
        fwd_down.append(send(high, high, fb_s.at[q], fb_r.at[q], down))

    def launch(q):
        pl.when(goes_right[q])(lambda: z_right[q].start())
        pl.when(goes_left[q])(lambda: z_left[q].start())
        y_up[q].start()
        y_down[q].start()

    launch(0)

    def fill_rows(s, carry):
        p = (s + 32 * core) * LANES + lane
        after = lax.shift_right_logical((p + LANES) * 64528, 22)
        vtab[s] = after - lax.shift_right_logical(p * 64528, 22)
        return carry

    lax.fori_loop(0, TILES, fill_rows, 0)
    top_row = lax.shift_right_logical((32 * core * LANES + lane) * 64528, 22)

    for copy in meta_copies:
        copy.wait_recv()

    lane2 = lax.broadcasted_iota(jnp.int32, (8, 256), 1)

    def fill_onehot(b, carry):
        classes = smeta[b].astype(F32)[0:8, 8:9].astype(jnp.int32)
        hit = jnp.logical_and(lane2 % 64 == classes, lane2 < 192)
        onehot[pl.ds(pl.multiple_of(b * 8, 8), 8), :] = hit.astype(F32)
        return carry

    lax.fori_loop(0, BLOCKS, fill_onehot, 0)
    ctf_copy.wait()

    def pieces(value):
        one = value.astype(BF16)
        rest = value - one.astype(F32)
        two = rest.astype(BF16)
        three = (rest - two.astype(F32)).astype(BF16)
        return one, two, three

    def fill_ctf(s, carry):
        cols = pl.ds(pl.multiple_of(s * 384, 384), 384)
        one, two, three = pieces(ctfh[:, cols])
        ctfrows[:, cols] = jnp.dot(
            onehot[...].astype(BF16),
            jnp.concatenate([one, two, three, one], axis=0),
            preferred_element_type=F32,
        )
        return carry

    lax.fori_loop(0, TILES // 3, fill_ctf, 0)

    def weigh(s, total):
        cols = pl.ds(pl.multiple_of(s * LANES, LANES), LANES)
        first_ = praw[0, :, cols].astype(F32).reshape(2, 8, 1, 8, LANES)
        second_ = praw[1, :, cols].astype(F32).reshape(2, 8, 1, 8, LANES)
        both = jnp.concatenate([first_, second_], axis=2).reshape(2, 128, LANES)
        counted = 1 - core * (1 - jnp.minimum(s, 1))
        noise = noise_ref[pl.ds(core * 32 + s, 1), :] * counted.astype(F32)
        scaled = (both * noise[None]).astype(BF16)
        weights[pl.ds(pl.multiple_of(s * 256, 256), LANES), :] = scaled[0].T
        weights[pl.ds(pl.multiple_of(s * 256 + 128, 128), LANES), :] = scaled[1].T
        power = (both[0] * both[0] + both[1] * both[1]).T
        ctf = ctfh[:, cols]
        p1, p2, p3 = pieces(power)
        c1, c2, c3 = pieces(ctf * ctf * noise)
        return total + jnp.dot(
            jnp.concatenate([c1, c1, c1, c2, c2, c3], axis=1),
            jnp.concatenate([p1, p2, p3, p1, p2, p1], axis=0),
            preferred_element_type=F32,
        )

    cosine = trig_ref[0:8, :]
    sine = trig_ref[8:16, :]

    def prepare(b):
        meta = smeta[b].astype(F32)[0:8, :].astype(jnp.int32)

        def wave(steps):
            index = steps & (KY - 1)
            return (
                jnp.take_along_axis(cosine, index, axis=1),
                jnp.take_along_axis(sine, index, axis=1),
            )

        begin, one_row, two_rows = [], [], []
        for t in range(TRANS):
            sx = meta[:, 2 * t : 2 * t + 1]
            sy = meta[:, 2 * t + 1 : 2 * t + 2]
            slope = jnp.broadcast_to(sy - KX * sx, (8, LANES))
            begin.append(wave(lane * sx + top_row * slope))
            one_row.append(wave(slope))
            two_rows.append(wave(2 * slope))

        def body(s, phases):
            cols = pl.ds(pl.multiple_of(s * LANES, LANES), LANES)
            block = gath[b, :, cols].astype(F32)
            ctf = ctfrows[pl.ds(pl.multiple_of(b * 8, 8), 8), cols]
            real, imag = block[0:8] * ctf, block[8:16] * ctf
            single = vtab[s] == 1
            reals, imags, later = [], [], []
            for t in range(TRANS):
                c, si = phases[t]
                reals.append(real * c + imag * si)
                imags.append(imag * c - real * si)
                mc = jnp.where(single, one_row[t][0], two_rows[t][0])
                ms = jnp.where(single, one_row[t][1], two_rows[t][1])
                later.append((c * mc - si * ms, si * mc + c * ms))
            for h in range(2):
                at = pl.ds(pl.multiple_of(b * 32 + h * 16, 16), 16)
                prep[at, pl.ds(pl.multiple_of(s * 256, 256), LANES)] = jnp.concatenate(
                    reals[2 * h : 2 * h + 2], axis=0
                ).astype(BF16)
                prep[at, pl.ds(pl.multiple_of(s * 256 + 128, 128), LANES)] = jnp.concatenate(
                    imags[2 * h : 2 * h + 2], axis=0
                ).astype(BF16)
            return tuple(later)

        lax.fori_loop(0, TILES, body, tuple(begin), unroll=11)

    def score_group(g):
        rows = pl.ds(pl.multiple_of(g * 128, 128), 128)

        def body(i, total):
            cols = pl.ds(pl.multiple_of(i * 768, 768), 768)
            return total + jnp.dot(
                prep[rows, cols], weights[cols, :], preferred_element_type=F32
            )

        cross = lax.fori_loop(0, TILES // 3, body, jnp.zeros((128, 128), F32), unroll=11)
        picked = onehot[pl.ds(pl.multiple_of(g * 32, 32), 32), 0:LANES].reshape(4, 1, 8, LANES)
        picked = jnp.concatenate([picked] * TRANS, axis=1).reshape(128, LANES)
        norm = jnp.dot(picked[:, :64], norms[...], precision=HI, preferred_element_type=F32)
        score[g] = cross - norm

    sc_copies = [
        send(score.at[order[q]], pscore.at[order[q]], sc_s.at[q], sc_r.at[q], peer)
        for q in range(4)
    ]

    stats[own] = jnp.zeros((16, LANES), F32)

    def summarise(q):
        sc_copies[q].wait_recv()
        g = order[q]
        whole = (score[g] + pscore[g]).T
        pscore[g] = whole
        top = jnp.max(whole, axis=0, keepdims=True)
        stats[own, pl.ds(g, 1), :] = top
        stats[own, pl.ds(8 + g, 1), :] = jnp.sum(jnp.exp(whole - top), axis=0, keepdims=True)

    def finish(q):
        fwd_up[q].wait_recv()
        fwd_down[q].wait_recv()
        prepare(order[q] * 4 + y2)
        score_group(order[q])
        sc_copies[q].start()

    def arrive(q):
        z_right[q].wait_recv()
        launch(q)

    def forward(q):
        y_up[q].wait_recv()
        fwd_up[q].start()
        y_down[q].wait_recv()
        fwd_down[q].start()

    def prepare_three(q):
        def three(i, carry):
            prepare(order[q] * 4 + (y + 3 + i) % 4)
            return carry

        lax.fori_loop(0, 3, three, 0)

    arrive(1)
    forward(0)
    prepare_three(0)
    arrive(2)
    forward(1)
    proj_copy.wait()
    praw_copy.wait_recv()
    norms[...] = 0.5 * lax.fori_loop(0, TILES, weigh, jnp.zeros((64, 128), F32), unroll=3)
    arrive(3)
    prepare_three(1)
    forward(2)
    finish(0)
    prepare_three(2)
    forward(3)
    finish(1)
    summarise(0)
    prepare_three(3)
    finish(2)
    summarise(1)
    finish(3)
    summarise(2)
    summarise(3)

    stat_copies = [
        send(stats.at[own], stats.at[own], stat_s.at[n], stat_r.at[n], target)
        for n, target in enumerate(others)
    ]
    for copy in stat_copies:
        copy.start()
    for copy in stat_copies:
        copy.wait_recv()
    tops = [stats[b, 0:8, :] for b in range(BLOCKS)]
    top = tops[0]
    for b in range(1, BLOCKS):
        top = jnp.maximum(top, tops[b])
    total = jnp.zeros((8, LANES), F32)
    for b in range(BLOCKS):
        total += stats[b, 8:16, :] * jnp.exp(tops[b] - top)
    held = lax.broadcasted_iota(jnp.int32, (8, LANES), 1) % 32

    def turn(value, by):
        inside = pltpu.roll(value, by, 1)
        wrapped = pltpu.roll(value, by + LANES - 32, 1)
        return jnp.where(held >= by, inside, wrapped)

    largest = jnp.maximum(top, turn(top, 8))
    largest = jnp.maximum(largest, turn(largest, 16))
    total = total * jnp.exp(top - largest)
    total = total + turn(total, 8)
    total = total + turn(total, 16)
    evidence = largest + jnp.log(total)
    own_row = jnp.sum(jnp.where(place == zl, evidence, 0.0), axis=0, keepdims=True)
    ev_ref[...] = pltpu.roll(jnp.broadcast_to(own_row, (8, LANES)), 128 - (y * 32 + core * 4), 1)
    for g in range(4):
        post[:, g * 128 : (g + 1) * 128] = (
            jnp.exp(pscore[g] - evidence[g : g + 1, :]) * 2048.0
        ).astype(BF16)

    def copy_a(c):
        return send(part.at[c, 2 * x2], from_a.at[c], a_s.at[c], a_r.at[c], right)

    def copy_b(c):
        return send(part.at[c, 2 * x2 + 1], from_b.at[c], b_s.at[c], b_r.at[c], left)

    def copy_p(c):
        return send(part.at[c, pl.ds(2 * xp, 2)], from_p.at[c], p_s.at[c], p_r.at[c], right)

    def copy_m(c):
        return send(part.at[c, pl.ds(2 * xm, 2)], from_m.at[c], m_s.at[c], m_r.at[c], left)

    def copy_w(c, k):
        return send(zsend.at[c, k], zrecv.at[c, core], w_s.at[c, k], w_r.at[c, core], across[k])

    def arrived_w(c, half):
        return send(zsend.at[c, 0], zrecv.at[c, half], w_s.at[c, 0], w_r.at[c, half], across[0])

    def copy_f(c):
        other = pl.ds(pl.multiple_of((1 - core) * 8, 8), 8)
        return send(keep.at[c, other], fin.at[c], f_s.at[c], f_r.at[c], peer)

    def write(c, half, value):
        for s in range(CHUNK_TILES):
            at = pl.ds(pl.multiple_of(half * SHIFT + (c * CHUNK_TILES + s) * LANES, LANES), LANES)
            for k in range(2):
                out_ref[k, :, at] = value[:, s * 256 + k * 128 : s * 256 + k * 128 + 128]

    def project(c):
        cols = pl.ds(pl.multiple_of(c * CW, CW), CW)
        sums = jnp.dot(post[...], prep[:, cols], preferred_element_type=F32).astype(BF16)
        for i in range(8):
            part[c, i] = sums[16 * i : 16 * i + 16]
        copy_a(c).start()
        copy_b(c).start()

    def add(into, *others_):
        value = into.astype(F32)
        for other in others_:
            value = value + other.astype(F32)
        return value

    def pass_on(c):
        copy_a(c).wait_recv()
        part[c, 2 * xp] = add(part[c, 2 * xp], from_a[c]).astype(BF16)
        copy_p(c).start()
        copy_b(c).wait_recv()
        part[c, 2 * xm + 1] = add(part[c, 2 * xm + 1], from_b[c]).astype(BF16)
        copy_m(c).start()

    def collect(c):
        copy_p(c).wait_recv()
        copy_m(c).wait_recv()
        far = 1 - zh
        away = add(part[c, 2 * x + far], from_p[c, far], from_m[c, far])
        for k in range(2):
            rows = away[8 * k : 8 * k + 8]
            zsend[c, k] = jnp.concatenate([rows[:, : CW // 2], rows[:, CW // 2 :]], axis=0).astype(BF16)
            copy_w(c, k).start()
        keep[c] = add(part[c, 2 * x + zh], from_p[c, zh], from_m[c, zh])
        copy_f(c).start()

    def complete(c):
        for half in range(2):
            arrived_w(c, half).wait_recv()
        copy_f(c).wait_recv()
        here = keep[c, pl.ds(pl.multiple_of(core * 8, 8), 8), :]
        for half, near in ((core, here), (1 - core, fin[c])):
            rows = zrecv[c, half].astype(F32)
            write(c, half, near + jnp.concatenate([rows[0:8], rows[8:16]], axis=1))

    stages = [(0, project), (3, pass_on), (6, collect), (10, complete)]

    def step(n, carry):
        for lag, stage in stages:
            here = jnp.logical_and(n >= lag, n < CHUNKS + lag)

            @pl.when(here)
            def _(lag=lag, stage=stage):
                stage(n - lag)

        return carry

    lax.fori_loop(0, CHUNKS + 10, step, 0)

    pmeta_copy.wait_send()
    pair_copy.wait_send()
    praw_copy.wait_send()
    for copy in meta_copies + stat_copies + sc_copies + y_up + y_down + fwd_up + fwd_down:
        copy.wait_send()
    for q in range(4):
        pl.when(goes_right[q])(lambda q=q: z_right[q].wait_send())
        pl.when(goes_left[q])(lambda q=q: z_left[q].wait_send())

    def sent(c, carry):
        for copy in (copy_a, copy_b, copy_p, copy_m, copy_f):
            copy(c).wait_send()
        for k in range(2):
            copy_w(c, k).wait_send()
        return carry

    lax.fori_loop(0, CHUNKS, sent, 0)


def per_device(images, projections, ctf_table, noise_weight, shifts, defocus):
    local = images.shape[0]
    pixels = images.shape[2]
    rows = images.transpose(1, 0, 2).reshape(2 * local, pixels)
    proj = projections.transpose(1, 0, 2).reshape(128, pixels)
    angles = np.arange(KY) * (2.0 * math.pi / KY)
    trig = np.concatenate([np.tile(np.cos(angles), (8, 1)), np.tile(np.sin(angles), (8, 1))])
    trig = jnp.asarray(trig.astype(np.float32))
    vmem = pl.BlockSpec(memory_space=pltpu.VMEM)
    hbm = pl.BlockSpec(memory_space=pl.ANY)
    smem = pl.BlockSpec(memory_space=pltpu.SMEM)
    dma = pltpu.SemaphoreType.DMA
    sems = [dma((2,)), dma((3,)), dma((3,)), dma((15,)), dma((15,)), dma((15,)), dma((15,))]
    sems += [dma((8,)), dma((4,))] + [dma((4,))] * 10 + [dma((CHUNKS,))] * 8 + [dma((CHUNKS, 2))] * 2 + [dma((CHUNKS,))] * 2
    sums, evidence = pl.pallas_call(
        kernel,
        out_shape=(
            jax.ShapeDtypeStruct((2, 8, pixels), F32),
            jax.ShapeDtypeStruct((8, LANES), F32),
        ),
        in_specs=[vmem, hbm, hbm, vmem, vmem, smem, smem],
        out_specs=(vmem, vmem),
        scratch_shapes=[
            pltpu.VMEM((16, 65 * LANES), BF16),
            pltpu.VMEM((16, LANES), BF16),
            pltpu.VMEM((16, HALF), BF16),
            pltpu.VMEM((16, LANES), BF16),
            pltpu.VMEM((BLOCKS, 16, LANES), BF16),
            pltpu.VMEM((BLOCKS, 16, HALF), BF16),
            pltpu.VMEM((2, 128, HALF), BF16),
            pltpu.VMEM((64, HALF), F32),
            pltpu.VMEM((2 * HALF, 128), BF16),
            pltpu.VMEM((64, 128), F32),
            pltpu.VMEM((128, 2 * LANES), F32),
            pltpu.VMEM((128, HALF), F32),
            pltpu.VMEM((TILES, 8, LANES), jnp.int32),
            pltpu.VMEM((BLOCKS * 32, 2 * HALF), BF16),
            pltpu.VMEM((4, 128, 128), F32),
            pltpu.VMEM((4, 128, 128), F32),
            pltpu.VMEM((BLOCKS, 16, LANES), F32),
            pltpu.VMEM((128, 512), BF16),
            pltpu.VMEM((CHUNKS, 8, 16, CW), BF16),
            pltpu.VMEM((CHUNKS, 16, CW), BF16),
            pltpu.VMEM((CHUNKS, 16, CW), BF16),
            pltpu.VMEM((CHUNKS, 2, 16, CW), BF16),
            pltpu.VMEM((CHUNKS, 2, 16, CW), BF16),
            pltpu.VMEM((CHUNKS, 2, 16, CW // 2), BF16),
            pltpu.VMEM((CHUNKS, 2, 16, CW // 2), BF16),
            pltpu.VMEM((CHUNKS, 16, CW), F32),
            pltpu.VMEM((CHUNKS, 8, CW), F32),
            *sems,
        ],
        compiler_params=pltpu.CompilerParams(
            collective_id=0, has_side_effects=True, vmem_limit_bytes=56 * 1024 * 1024
        ),
    )(
        rows, proj, ctf_table, noise_weight.reshape(65, LANES), trig,
        shifts.transpose(0, 2, 1), defocus,
    )
    return evidence[0, :local], sums.transpose(1, 0, 2)


def solution(mesh):
    in_specs = (
        P(("img", "ori"), None, None),
        P("ori", None, None),
        P(),
        P(),
        P(("img", "ori"), None, None),
        P(("img", "ori")),
    )
    out_specs = (P(("img", "ori")), P(("ori", "img"), None, None))
    return jax.shard_map(
        per_device, mesh=mesh, in_specs=in_specs, out_specs=out_specs, check_vma=False
    )
```

```python
import math

import jax
import jax.numpy as jnp
import numpy as np
from jax import lax
from jax.experimental import pallas as pl
from jax.experimental.pallas import tpu as pltpu
from jax.sharding import PartitionSpec as P

KY = 128
KX = 65
LANES = 128
NX, NZ, NY = 4, 4, 4
BLOCKS = NZ * NY
TRANS = 4
TILES = 33
HALF = TILES * LANES
SHIFT = 32 * LANES
HALF_A = 17 * LANES
CHUNKS = 11
CHUNK_TILES = TILES // CHUNKS
CW = CHUNK_TILES * 2 * LANES
OTHERS = [(dz, dy) for dz in range(NZ) for dy in range(NY) if (dz, dy) != (0, 0)]
F32 = jnp.float32
BF16 = jnp.bfloat16
HI = lax.Precision.HIGHEST


def kernel(
    img_ref, proj_ref, ctf_ref, noise_ref, trig_ref, shift_ref, class_ref,
    out_ref, ev_ref,
    placed, ometa, pair, pmeta, smeta, gath, praw, ctfh, weights, norms, onehot, ctfrows, vtab, prep,
    score, pscore, stats, post, part, from_a, from_b, from_p, from_m, zsend, zmid, zrecv, keep, fin,
    loc_sem, core_s, core_r, meta_s, meta_r, stat_s, stat_r, z_s, z_r,
    yp_s, ym_s, yl_r, yr_r, fa_s, fb_s, fa_r, fb_r, sc_s, sc_r,
    a_s, b_s, a_r, b_r, p_s, m_s, p_r, m_r, v_s, v_r, w_s, w_r, f_s, f_r,
):
    img = lax.axis_index("img")
    ori = lax.axis_index("ori")
    x, zh = img // 2, img % 2
    core, y, zl = ori % 2, (ori // 2) % 4, ori // 8
    xp, xm, x2 = (x + 1) % 4, (x + 3) % 4, (x + 2) % 4
    yp, ym, y2 = (y + 1) % 4, (y + 3) % 4, (y + 2) % 4
    own = zl * 4 + y

    def dev(x_=x, zh_=zh, zl_=zl, y_=y, core_=core):
        return (x_ * 2 + zh_, (zl_ * 4 + y_) * 2 + core_)

    def send(src, dst, ss, rs, target):
        return pltpu.make_async_remote_copy(
            src_ref=src, dst_ref=dst, send_sem=ss, recv_sem=rs,
            device_id=target, device_id_type=pl.DeviceIdType.MESH,
        )

    peer = dev(core_=1 - core)
    others = [dev(zl_=(zl + dz) % 4, y_=(y + dy) % 4) for dz, dy in OTHERS]
    right, left = dev(x_=xp), dev(x_=xm)
    up, down = dev(y_=yp), dev(y_=ym)
    z = zh * 4 + zl

    def along(steps, core_=core):
        there = (z + steps) % 8
        return dev(zh_=there // 4, zl_=there % 4, core_=core_)


    barrier = pltpu.get_barrier_semaphore()
    greeted = [peer, *others, right, left]
    greeted += [along(steps, k) for steps in (2, 6) for k in range(2)]
    for target in greeted:
        pl.semaphore_signal(barrier, inc=1, device_id=target, device_id_type=pl.DeviceIdType.MESH)

    mine = pl.ds(pl.multiple_of(core * SHIFT, LANES), HALF)
    theirs = pl.ds(pl.multiple_of((1 - core) * SHIFT, LANES), HALF)
    ctf_copy = pltpu.make_async_copy(ctf_ref.at[:, mine], ctfh, loc_sem.at[0])
    proj_copy = pltpu.make_async_copy(proj_ref.at[:, mine], praw.at[core], loc_sem.at[1])
    ctf_copy.start()
    proj_copy.start()

    lane = lax.broadcasted_iota(jnp.int32, (8, LANES), 1)
    place = lax.broadcasted_iota(jnp.int32, (8, LANES), 0)
    held_here = (place >= 4) == (core == 1)

    def lay_out(s, carry):
        cols = pl.ds(pl.multiple_of(s * LANES, LANES), LANES)
        straight = img_ref[:, cols].astype(F32)
        swapped = pltpu.roll(straight, 4, 0)
        low = jnp.where(core == 0, straight, swapped)
        high = jnp.where(core == 0, swapped, straight)
        both = jnp.concatenate([low, high], axis=0)
        seen = jnp.concatenate([held_here, held_here], axis=0)
        placed[:, cols] = jnp.where(seen, both, 0.0).astype(BF16)
        return carry

    lax.fori_loop(0, 65, lay_out, 0, unroll=5)
    meta = jnp.zeros((8, LANES), jnp.int32)
    for i in range(4):
        row = place == i + 4 * core
        for t in range(TRANS):
            for k in range(2):
                spot = jnp.logical_and(row, lane == 2 * t + k)
                meta = jnp.where(spot, shift_ref[i, k, t], meta)
        meta = jnp.where(jnp.logical_and(row, lane == 8), class_ref[i], meta)
    meta = meta.astype(F32)
    ometa[...] = jnp.concatenate([meta, jnp.zeros_like(meta)], axis=0).astype(BF16)

    pl.semaphore_wait(barrier, len(greeted))

    pair_copy = send(placed.at[:, theirs], pair, core_s.at[0], core_r.at[0], peer)
    pmeta_copy = send(ometa, pmeta, core_s.at[1], core_r.at[1], peer)
    praw_copy = send(proj_ref.at[:, theirs], praw.at[core], core_s.at[2], core_r.at[2], peer)
    pmeta_copy.start()
    pair_copy.start()
    praw_copy.start()

    pmeta_copy.wait_recv()
    smeta[own] = ometa[...] + pmeta[...]
    meta_copies = [
        send(smeta.at[own], smeta.at[own], meta_s.at[n], meta_r.at[n], target)
        for n, target in enumerate(others)
    ]
    for copy in meta_copies:
        copy.start()

    pair_copy.wait_recv()
    gath[own] = placed[:, mine] + pair[...]

    b0, b1 = zl % 2, zl // 2

    def pick(table):
        low = (1 - b0) * table[0] + b0 * table[1]
        high = (1 - b0) * table[2] + b0 * table[3]
        return (1 - b1) * low + b1 * high

    order = [zl, pick([1, 0, 3, 2]), pick([2, 2, 1, 1]), pick([3, 3, 0, 0])]

    def z_copy(zq, step, target):
        b = zq * 4 + y
        return send(gath.at[b], gath.at[b], z_s.at[step], z_r.at[zq], target)

    z_right = [z_copy(order[q], q, dev(zl_=zl + 1)) for q in range(4)]
    z_left = [z_copy(order[q], 4 + q, dev(zl_=zl - 1)) for q in range(4)]
    goes_right = [zl < 3] + [jnp.logical_and(order[q] < zl, zl < 3) for q in (1, 2, 3)]
    goes_left = [zl > 0] + [jnp.logical_and(order[q] > zl, zl > 0) for q in (1, 2, 3)]
    y_up = [
        send(gath.at[order[q] * 4 + y], gath.at[order[q] * 4 + y], yp_s.at[q], yl_r.at[q], up)
        for q in range(4)
    ]
    y_down = [
        send(gath.at[order[q] * 4 + y], gath.at[order[q] * 4 + y], ym_s.at[q], yr_r.at[q], down)
        for q in range(4)
    ]
    first, second = pl.ds(0, HALF_A), pl.ds(HALF_A, HALF - HALF_A)
    fwd_up, fwd_down = [], []
    for q in range(4):
        low = gath.at[order[q] * 4 + ym, :, first]
        high = gath.at[order[q] * 4 + yp, :, second]
        fwd_up.append(send(low, low, fa_s.at[q], fa_r.at[q], up))
        fwd_down.append(send(high, high, fb_s.at[q], fb_r.at[q], down))

    def launch(q):
        pl.when(goes_right[q])(lambda: z_right[q].start())
        pl.when(goes_left[q])(lambda: z_left[q].start())
        y_up[q].start()
        y_down[q].start()

    launch(0)

    def fill_rows(s, carry):
        p = (s + 32 * core) * LANES + lane
        after = lax.shift_right_logical((p + LANES) * 64528, 22)
        vtab[s] = after - lax.shift_right_logical(p * 64528, 22)
        return carry

    lax.fori_loop(0, TILES, fill_rows, 0)
    top_row = lax.shift_right_logical((32 * core * LANES + lane) * 64528, 22)

    for copy in meta_copies:
        copy.wait_recv()

    lane2 = lax.broadcasted_iota(jnp.int32, (8, 256), 1)

    def fill_onehot(b, carry):
        classes = smeta[b].astype(F32)[0:8, 8:9].astype(jnp.int32)
        hit = jnp.logical_and(lane2 % 64 == classes, lane2 < 192)
        onehot[pl.ds(pl.multiple_of(b * 8, 8), 8), :] = hit.astype(F32)
        return carry

    lax.fori_loop(0, BLOCKS, fill_onehot, 0)
    ctf_copy.wait()

    def pieces(value):
        one = value.astype(BF16)
        rest = value - one.astype(F32)
        two = rest.astype(BF16)
        three = (rest - two.astype(F32)).astype(BF16)
        return one, two, three

    def fill_ctf(s, carry):
        cols = pl.ds(pl.multiple_of(s * 384, 384), 384)
        one, two, three = pieces(ctfh[:, cols])
        ctfrows[:, cols] = jnp.dot(
            onehot[...].astype(BF16),
            jnp.concatenate([one, two, three, one], axis=0),
            preferred_element_type=F32,
        )
        return carry

    lax.fori_loop(0, TILES // 3, fill_ctf, 0)

    def weigh(s, total):
        cols = pl.ds(pl.multiple_of(s * LANES, LANES), LANES)
        first_ = praw[0, :, cols].astype(F32).reshape(2, 8, 1, 8, LANES)
        second_ = praw[1, :, cols].astype(F32).reshape(2, 8, 1, 8, LANES)
        both = jnp.concatenate([first_, second_], axis=2).reshape(2, 128, LANES)
        counted = 1 - core * (1 - jnp.minimum(s, 1))
        noise = noise_ref[pl.ds(core * 32 + s, 1), :] * counted.astype(F32)
        scaled = (both * noise[None]).astype(BF16)
        weights[pl.ds(pl.multiple_of(s * 256, 256), LANES), :] = scaled[0].T
        weights[pl.ds(pl.multiple_of(s * 256 + 128, 128), LANES), :] = scaled[1].T
        power = (both[0] * both[0] + both[1] * both[1]).T
        ctf = ctfh[:, cols]
        p1, p2, p3 = pieces(power)
        c1, c2, c3 = pieces(ctf * ctf * noise)
        return total + jnp.dot(
            jnp.concatenate([c1, c1, c1, c2, c2, c3], axis=1),
            jnp.concatenate([p1, p2, p3, p1, p2, p1], axis=0),
            preferred_element_type=F32,
        )

    cosine = trig_ref[0:8, :]
    sine = trig_ref[8:16, :]

    def prepare(b):
        meta = smeta[b].astype(F32)[0:8, :].astype(jnp.int32)

        def wave(steps):
            index = steps & (KY - 1)
            return (
                jnp.take_along_axis(cosine, index, axis=1),
                jnp.take_along_axis(sine, index, axis=1),
            )

        begin, one_row, two_rows = [], [], []
        for t in range(TRANS):
            sx = meta[:, 2 * t : 2 * t + 1]
            sy = meta[:, 2 * t + 1 : 2 * t + 2]
            slope = jnp.broadcast_to(sy - KX * sx, (8, LANES))
            begin.append(wave(lane * sx + top_row * slope))
            one_row.append(wave(slope))
            two_rows.append(wave(2 * slope))

        def body(s, phases):
            cols = pl.ds(pl.multiple_of(s * LANES, LANES), LANES)
            block = gath[b, :, cols].astype(F32)
            ctf = ctfrows[pl.ds(pl.multiple_of(b * 8, 8), 8), cols]
            real, imag = block[0:8] * ctf, block[8:16] * ctf
            single = vtab[s] == 1
            reals, imags, later = [], [], []
            for t in range(TRANS):
                c, si = phases[t]
                reals.append(real * c + imag * si)
                imags.append(imag * c - real * si)
                mc = jnp.where(single, one_row[t][0], two_rows[t][0])
                ms = jnp.where(single, one_row[t][1], two_rows[t][1])
                later.append((c * mc - si * ms, si * mc + c * ms))
            for h in range(2):
                at = pl.ds(pl.multiple_of(b * 32 + h * 16, 16), 16)
                prep[at, pl.ds(pl.multiple_of(s * 256, 256), LANES)] = jnp.concatenate(
                    reals[2 * h : 2 * h + 2], axis=0
                ).astype(BF16)
                prep[at, pl.ds(pl.multiple_of(s * 256 + 128, 128), LANES)] = jnp.concatenate(
                    imags[2 * h : 2 * h + 2], axis=0
                ).astype(BF16)
            return tuple(later)

        lax.fori_loop(0, TILES, body, tuple(begin), unroll=11)

    def score_group(g):
        rows = pl.ds(pl.multiple_of(g * 128, 128), 128)

        def body(i, total):
            cols = pl.ds(pl.multiple_of(i * 768, 768), 768)
            return total + jnp.dot(
                prep[rows, cols], weights[cols, :], preferred_element_type=F32
            )

        cross = lax.fori_loop(0, TILES // 3, body, jnp.zeros((128, 128), F32), unroll=11)
        picked = onehot[pl.ds(pl.multiple_of(g * 32, 32), 32), 0:LANES].reshape(4, 1, 8, LANES)
        picked = jnp.concatenate([picked] * TRANS, axis=1).reshape(128, LANES)
        norm = jnp.dot(picked[:, :64], norms[...], precision=HI, preferred_element_type=F32)
        score[g] = cross - norm

    sc_copies = [
        send(score.at[order[q]], pscore.at[order[q]], sc_s.at[q], sc_r.at[q], peer)
        for q in range(4)
    ]

    stats[own] = jnp.zeros((16, LANES), F32)

    def summarise(q):
        sc_copies[q].wait_recv()
        g = order[q]
        whole = (score[g] + pscore[g]).T
        pscore[g] = whole
        top = jnp.max(whole, axis=0, keepdims=True)
        stats[own, pl.ds(g, 1), :] = top
        stats[own, pl.ds(8 + g, 1), :] = jnp.sum(jnp.exp(whole - top), axis=0, keepdims=True)

    def finish(q):
        fwd_up[q].wait_recv()
        fwd_down[q].wait_recv()
        prepare(order[q] * 4 + y2)
        score_group(order[q])
        sc_copies[q].start()

    def arrive(q):
        z_right[q].wait_recv()
        launch(q)

    def forward(q):
        y_up[q].wait_recv()
        fwd_up[q].start()
        y_down[q].wait_recv()
        fwd_down[q].start()

    def prepare_three(q):
        def three(i, carry):
            prepare(order[q] * 4 + (y + 3 + i) % 4)
            return carry

        lax.fori_loop(0, 3, three, 0)

    arrive(1)
    forward(0)
    prepare_three(0)
    arrive(2)
    forward(1)
    proj_copy.wait()
    praw_copy.wait_recv()
    norms[...] = 0.5 * lax.fori_loop(0, TILES, weigh, jnp.zeros((64, 128), F32), unroll=3)
    arrive(3)
    prepare_three(1)
    forward(2)
    finish(0)
    prepare_three(2)
    forward(3)
    finish(1)
    summarise(0)
    prepare_three(3)
    finish(2)
    summarise(1)
    finish(3)
    summarise(2)
    summarise(3)

    stat_copies = [
        send(stats.at[own], stats.at[own], stat_s.at[n], stat_r.at[n], target)
        for n, target in enumerate(others)
    ]
    for copy in stat_copies:
        copy.start()
    for copy in stat_copies:
        copy.wait_recv()
    tops = [stats[b, 0:8, :] for b in range(BLOCKS)]
    top = tops[0]
    for b in range(1, BLOCKS):
        top = jnp.maximum(top, tops[b])
    total = jnp.zeros((8, LANES), F32)
    for b in range(BLOCKS):
        total += stats[b, 8:16, :] * jnp.exp(tops[b] - top)
    held = lax.broadcasted_iota(jnp.int32, (8, LANES), 1) % 32

    def turn(value, by):
        inside = pltpu.roll(value, by, 1)
        wrapped = pltpu.roll(value, by + LANES - 32, 1)
        return jnp.where(held >= by, inside, wrapped)

    largest = jnp.maximum(top, turn(top, 8))
    largest = jnp.maximum(largest, turn(largest, 16))
    total = total * jnp.exp(top - largest)
    total = total + turn(total, 8)
    total = total + turn(total, 16)
    evidence = largest + jnp.log(total)
    own_row = jnp.sum(jnp.where(place == zl, evidence, 0.0), axis=0, keepdims=True)
    ev_ref[...] = pltpu.roll(jnp.broadcast_to(own_row, (8, LANES)), 128 - (y * 32 + core * 4), 1)
    for g in range(4):
        post[:, g * 128 : (g + 1) * 128] = (
            jnp.exp(pscore[g] - evidence[g : g + 1, :]) * 2048.0
        ).astype(BF16)

    def copy_a(c):
        return send(part.at[c, 2 * x2], from_a.at[c], a_s.at[c], a_r.at[c], right)

    def copy_b(c):
        return send(part.at[c, 2 * x2 + 1], from_b.at[c], b_s.at[c], b_r.at[c], left)

    def copy_p(c):
        return send(part.at[c, pl.ds(2 * xp, 2)], from_p.at[c], p_s.at[c], p_r.at[c], right)

    def copy_m(c):
        return send(part.at[c, pl.ds(2 * xm, 2)], from_m.at[c], m_s.at[c], m_r.at[c], left)

    def copy_v(c):
        return send(zsend.at[c], zmid.at[c], v_s.at[c], v_r.at[c], along(2 + 4 * (c % 2)))

    def copy_w(c, k):
        return send(
            zmid.at[c, k], zrecv.at[c, core], w_s.at[c, k], w_r.at[c, core],
            along(2 + 4 * (c % 2), k),
        )

    def arrived_w(c, half):
        return send(zmid.at[c, 0], zrecv.at[c, half], w_s.at[c, 0], w_r.at[c, half], along(2))

    def copy_f(c):
        other = pl.ds(pl.multiple_of((1 - core) * 8, 8), 8)
        return send(keep.at[c, other], fin.at[c], f_s.at[c], f_r.at[c], peer)

    def write(c, half, value):
        for s in range(CHUNK_TILES):
            at = pl.ds(pl.multiple_of(half * SHIFT + (c * CHUNK_TILES + s) * LANES, LANES), LANES)
            for k in range(2):
                out_ref[k, :, at] = value[:, s * 256 + k * 128 : s * 256 + k * 128 + 128]

    def project(c):
        cols = pl.ds(pl.multiple_of(c * CW, CW), CW)
        sums = jnp.dot(post[...], prep[:, cols], preferred_element_type=F32).astype(BF16)
        for i in range(8):
            part[c, i] = sums[16 * i : 16 * i + 16]
        copy_a(c).start()
        copy_b(c).start()

    def add(into, *others_):
        value = into.astype(F32)
        for other in others_:
            value = value + other.astype(F32)
        return value

    def pass_on(c):
        copy_a(c).wait_recv()
        part[c, 2 * xp] = add(part[c, 2 * xp], from_a[c]).astype(BF16)
        copy_p(c).start()
        copy_b(c).wait_recv()
        part[c, 2 * xm + 1] = add(part[c, 2 * xm + 1], from_b[c]).astype(BF16)
        copy_m(c).start()

    def collect(c):
        copy_p(c).wait_recv()
        copy_m(c).wait_recv()
        far = 1 - zh
        away = add(part[c, 2 * x + far], from_p[c, far], from_m[c, far])
        for k in range(2):
            rows = away[8 * k : 8 * k + 8]
            zsend[c, k] = jnp.concatenate([rows[:, : CW // 2], rows[:, CW // 2 :]], axis=0).astype(BF16)
        copy_v(c).start()
        keep[c] = add(part[c, 2 * x + zh], from_p[c, zh], from_m[c, zh])
        copy_f(c).start()

    def relay(c):
        copy_v(c).wait_recv()
        for k in range(2):
            copy_w(c, k).start()

    def complete(c):
        for half in range(2):
            arrived_w(c, half).wait_recv()
        copy_f(c).wait_recv()
        here = keep[c, pl.ds(pl.multiple_of(core * 8, 8), 8), :]
        for half, near in ((core, here), (1 - core, fin[c])):
            rows = zrecv[c, half].astype(F32)
            write(c, half, near + jnp.concatenate([rows[0:8], rows[8:16]], axis=1))

    stages = [(0, project), (3, pass_on), (6, collect), (8, relay), (11, complete)]

    def step(n, carry):
        for lag, stage in stages:
            here = jnp.logical_and(n >= lag, n < CHUNKS + lag)

            @pl.when(here)
            def _(lag=lag, stage=stage):
                stage(n - lag)

        return carry

    lax.fori_loop(0, CHUNKS + 11, step, 0)

    pmeta_copy.wait_send()
    pair_copy.wait_send()
    praw_copy.wait_send()
    for copy in meta_copies + stat_copies + sc_copies + y_up + y_down + fwd_up + fwd_down:
        copy.wait_send()
    for q in range(4):
        pl.when(goes_right[q])(lambda q=q: z_right[q].wait_send())
        pl.when(goes_left[q])(lambda q=q: z_left[q].wait_send())

    def sent(c, carry):
        for copy in (copy_a, copy_b, copy_p, copy_m, copy_v, copy_f):
            copy(c).wait_send()
        for k in range(2):
            copy_w(c, k).wait_send()
        return carry

    lax.fori_loop(0, CHUNKS, sent, 0)


def per_device(images, projections, ctf_table, noise_weight, shifts, defocus):
    local = images.shape[0]
    pixels = images.shape[2]
    rows = images.transpose(1, 0, 2).reshape(2 * local, pixels)
    proj = projections.transpose(1, 0, 2).reshape(128, pixels)
    angles = np.arange(KY) * (2.0 * math.pi / KY)
    trig = np.concatenate([np.tile(np.cos(angles), (8, 1)), np.tile(np.sin(angles), (8, 1))])
    trig = jnp.asarray(trig.astype(np.float32))
    vmem = pl.BlockSpec(memory_space=pltpu.VMEM)
    hbm = pl.BlockSpec(memory_space=pl.ANY)
    smem = pl.BlockSpec(memory_space=pltpu.SMEM)
    dma = pltpu.SemaphoreType.DMA
    sems = [dma((2,)), dma((3,)), dma((3,)), dma((15,)), dma((15,)), dma((15,)), dma((15,))]
    sems += [dma((8,)), dma((4,))] + [dma((4,))] * 10 + [dma((CHUNKS,))] * 10 + [dma((CHUNKS, 2))] * 2 + [dma((CHUNKS,))] * 2
    sums, evidence = pl.pallas_call(
        kernel,
        out_shape=(
            jax.ShapeDtypeStruct((2, 8, pixels), F32),
            jax.ShapeDtypeStruct((8, LANES), F32),
        ),
        in_specs=[vmem, hbm, hbm, vmem, vmem, smem, smem],
        out_specs=(vmem, vmem),
        scratch_shapes=[
            pltpu.VMEM((16, 65 * LANES), BF16),
            pltpu.VMEM((16, LANES), BF16),
            pltpu.VMEM((16, HALF), BF16),
            pltpu.VMEM((16, LANES), BF16),
            pltpu.VMEM((BLOCKS, 16, LANES), BF16),
            pltpu.VMEM((BLOCKS, 16, HALF), BF16),
            pltpu.VMEM((2, 128, HALF), BF16),
            pltpu.VMEM((64, HALF), F32),
            pltpu.VMEM((2 * HALF, 128), BF16),
            pltpu.VMEM((64, 128), F32),
            pltpu.VMEM((128, 2 * LANES), F32),
            pltpu.VMEM((128, HALF), F32),
            pltpu.VMEM((TILES, 8, LANES), jnp.int32),
            pltpu.VMEM((BLOCKS * 32, 2 * HALF), BF16),
            pltpu.VMEM((4, 128, 128), F32),
            pltpu.VMEM((4, 128, 128), F32),
            pltpu.VMEM((BLOCKS, 16, LANES), F32),
            pltpu.VMEM((128, 512), BF16),
            pltpu.VMEM((CHUNKS, 8, 16, CW), BF16),
            pltpu.VMEM((CHUNKS, 16, CW), BF16),
            pltpu.VMEM((CHUNKS, 16, CW), BF16),
            pltpu.VMEM((CHUNKS, 2, 16, CW), BF16),
            pltpu.VMEM((CHUNKS, 2, 16, CW), BF16),
            pltpu.VMEM((CHUNKS, 2, 16, CW // 2), BF16),
            pltpu.VMEM((CHUNKS, 2, 16, CW // 2), BF16),
            pltpu.VMEM((CHUNKS, 2, 16, CW // 2), BF16),
            pltpu.VMEM((CHUNKS, 16, CW), F32),
            pltpu.VMEM((CHUNKS, 8, CW), F32),
            *sems,
        ],
        compiler_params=pltpu.CompilerParams(
            collective_id=0, has_side_effects=True, vmem_limit_bytes=56 * 1024 * 1024
        ),
    )(
        rows, proj, ctf_table, noise_weight.reshape(65, LANES), trig,
        shifts.transpose(0, 2, 1), defocus,
    )
    return evidence[0, :local], sums.transpose(1, 0, 2)


def solution(mesh):
    in_specs = (
        P(("img", "ori"), None, None),
        P("ori", None, None),
        P(),
        P(),
        P(("img", "ori"), None, None),
        P(("img", "ori")),
    )
    out_specs = (P(("img", "ori")), P(("ori", "img"), None, None))
    return jax.shard_map(
        per_device, mesh=mesh, in_specs=in_specs, out_specs=out_specs, check_vma=False
    )
```

```python
import math

import jax
import jax.numpy as jnp
import numpy as np
from jax import lax
from jax.experimental import pallas as pl
from jax.experimental.pallas import tpu as pltpu
from jax.sharding import PartitionSpec as P

KY = 128
KX = 65
LANES = 128
NX, NZ, NY = 4, 4, 4
BLOCKS = NZ * NY
TRANS = 4
TILES = 33
HALF = TILES * LANES
SHIFT = 32 * LANES
HALF_A = 17 * LANES
SIZES = (5, 7, 8, 8, 5)
STARTS = (0, 5, 12, 20, 28, 33)
CHUNKS = len(SIZES)
OTHERS = [(dz, dy) for dz in range(NZ) for dy in range(NY) if (dz, dy) != (0, 0)]
F32 = jnp.float32
BF16 = jnp.bfloat16
HI = lax.Precision.HIGHEST


def kernel(
    img_ref, proj_ref, ctf_ref, noise_ref, trig_ref, shift_ref, class_ref,
    out_ref, ev_ref,
    placed, ometa, pair, pmeta, smeta, gath, praw, ctfh, weights, norms, onehot, ctfrows, vtab, prep,
    score, pscore, stats, post, part, from_a, from_b, from_p, from_m, zsend, zrecv, keep, fin,
    loc_sem, core_s, core_r, meta_s, meta_r, stat_s, stat_r, z_s, z_r,
    yp_s, ym_s, yl_r, yr_r, fa_s, fb_s, fa_r, fb_r, sc_s, sc_r,
    a_s, b_s, a_r, b_r, p_s, m_s, p_r, m_r, w_s, w_r, f_s, f_r,
):
    img = lax.axis_index("img")
    ori = lax.axis_index("ori")
    x, zh = img // 2, img % 2
    core, y, zl = ori % 2, (ori // 2) % 4, ori // 8
    xp, xm, x2 = (x + 1) % 4, (x + 3) % 4, (x + 2) % 4
    yp, ym, y2 = (y + 1) % 4, (y + 3) % 4, (y + 2) % 4
    own = zl * 4 + y

    def dev(x_=x, zh_=zh, zl_=zl, y_=y, core_=core):
        return (x_ * 2 + zh_, (zl_ * 4 + y_) * 2 + core_)

    def send(src, dst, ss, rs, target):
        return pltpu.make_async_remote_copy(
            src_ref=src, dst_ref=dst, send_sem=ss, recv_sem=rs,
            device_id=target, device_id_type=pl.DeviceIdType.MESH,
        )

    peer = dev(core_=1 - core)
    others = [dev(zl_=(zl + dz) % 4, y_=(y + dy) % 4) for dz, dy in OTHERS]
    right, left = dev(x_=xp), dev(x_=xm)
    up, down = dev(y_=yp), dev(y_=ym)
    across = [dev(zh_=1 - zh, core_=k) for k in range(2)]

    barrier = pltpu.get_barrier_semaphore()
    greeted = [peer, *others, right, left, *across]
    for target in greeted:
        pl.semaphore_signal(barrier, inc=1, device_id=target, device_id_type=pl.DeviceIdType.MESH)

    mine = pl.ds(pl.multiple_of(core * SHIFT, LANES), HALF)
    theirs = pl.ds(pl.multiple_of((1 - core) * SHIFT, LANES), HALF)
    ctf_copy = pltpu.make_async_copy(ctf_ref.at[:, mine], ctfh, loc_sem.at[0])
    proj_copy = pltpu.make_async_copy(proj_ref.at[:, mine], praw.at[core], loc_sem.at[1])
    ctf_copy.start()
    proj_copy.start()

    lane = lax.broadcasted_iota(jnp.int32, (8, LANES), 1)
    place = lax.broadcasted_iota(jnp.int32, (8, LANES), 0)
    held_here = (place >= 4) == (core == 1)

    def lay_out(s, carry):
        cols = pl.ds(pl.multiple_of(s * LANES, LANES), LANES)
        straight = img_ref[:, cols].astype(F32)
        swapped = pltpu.roll(straight, 4, 0)
        low = jnp.where(core == 0, straight, swapped)
        high = jnp.where(core == 0, swapped, straight)
        both = jnp.concatenate([low, high], axis=0)
        seen = jnp.concatenate([held_here, held_here], axis=0)
        placed[:, cols] = jnp.where(seen, both, 0.0).astype(BF16)
        return carry

    lax.fori_loop(0, 65, lay_out, 0, unroll=5)
    meta = jnp.zeros((8, LANES), jnp.int32)
    for i in range(4):
        row = place == i + 4 * core
        for t in range(TRANS):
            for k in range(2):
                spot = jnp.logical_and(row, lane == 2 * t + k)
                meta = jnp.where(spot, shift_ref[i, k, t], meta)
        meta = jnp.where(jnp.logical_and(row, lane == 8), class_ref[i], meta)
    meta = meta.astype(F32)
    ometa[...] = jnp.concatenate([meta, jnp.zeros_like(meta)], axis=0).astype(BF16)

    pl.semaphore_wait(barrier, len(greeted))

    pair_copy = send(placed.at[:, theirs], pair, core_s.at[0], core_r.at[0], peer)
    pmeta_copy = send(ometa, pmeta, core_s.at[1], core_r.at[1], peer)
    praw_copy = send(proj_ref.at[:, theirs], praw.at[core], core_s.at[2], core_r.at[2], peer)
    pmeta_copy.start()
    pair_copy.start()
    praw_copy.start()

    pmeta_copy.wait_recv()
    smeta[own] = ometa[...] + pmeta[...]
    meta_copies = [
        send(smeta.at[own], smeta.at[own], meta_s.at[n], meta_r.at[n], target)
        for n, target in enumerate(others)
    ]
    for copy in meta_copies:
        copy.start()

    pair_copy.wait_recv()
    gath[own] = placed[:, mine] + pair[...]

    b0, b1 = zl % 2, zl // 2

    def pick(table):
        low = (1 - b0) * table[0] + b0 * table[1]
        high = (1 - b0) * table[2] + b0 * table[3]
        return (1 - b1) * low + b1 * high

    order = [zl, pick([1, 0, 3, 2]), pick([2, 2, 1, 1]), pick([3, 3, 0, 0])]

    def z_copy(zq, step, target):
        b = zq * 4 + y
        return send(gath.at[b], gath.at[b], z_s.at[step], z_r.at[zq], target)

    z_right = [z_copy(order[q], q, dev(zl_=zl + 1)) for q in range(4)]
    z_left = [z_copy(order[q], 4 + q, dev(zl_=zl - 1)) for q in range(4)]
    goes_right = [zl < 3] + [jnp.logical_and(order[q] < zl, zl < 3) for q in (1, 2, 3)]
    goes_left = [zl > 0] + [jnp.logical_and(order[q] > zl, zl > 0) for q in (1, 2, 3)]
    y_up = [
        send(gath.at[order[q] * 4 + y], gath.at[order[q] * 4 + y], yp_s.at[q], yl_r.at[q], up)
        for q in range(4)
    ]
    y_down = [
        send(gath.at[order[q] * 4 + y], gath.at[order[q] * 4 + y], ym_s.at[q], yr_r.at[q], down)
        for q in range(4)
    ]
    first, second = pl.ds(0, HALF_A), pl.ds(HALF_A, HALF - HALF_A)
    fwd_up, fwd_down = [], []
    for q in range(4):
        low = gath.at[order[q] * 4 + ym, :, first]
        high = gath.at[order[q] * 4 + yp, :, second]
        fwd_up.append(send(low, low, fa_s.at[q], fa_r.at[q], up))
        fwd_down.append(send(high, high, fb_s.at[q], fb_r.at[q], down))

    def launch(q):
        pl.when(goes_right[q])(lambda: z_right[q].start())
        pl.when(goes_left[q])(lambda: z_left[q].start())
        y_up[q].start()
        y_down[q].start()

    launch(0)

    def fill_rows(s, carry):
        p = (s + 32 * core) * LANES + lane
        after = lax.shift_right_logical((p + LANES) * 64528, 22)
        vtab[s] = after - lax.shift_right_logical(p * 64528, 22)
        return carry

    lax.fori_loop(0, TILES, fill_rows, 0)
    top_row = lax.shift_right_logical((32 * core * LANES + lane) * 64528, 22)

    def pieces(value):
        one = value.astype(BF16)
        rest = value - one.astype(F32)
        two = rest.astype(BF16)
        three = (rest - two.astype(F32)).astype(BF16)
        return one, two, three

    def fill_ctf(s, carry):
        cols = pl.ds(pl.multiple_of(s * 1408, 1408), 1408)
        one, two, three = pieces(ctfh[:, cols])
        ctfrows[:, cols] = jnp.dot(
            onehot[...].astype(BF16),
            jnp.concatenate([one, two, three, one], axis=0),
            preferred_element_type=F32,
        )
        return carry


    def weigh(n, total):
        wide = pl.ds(pl.multiple_of(n * 384, 384), 384)
        raw = [praw[0, :, wide], praw[1, :, wide]]
        ctfs = ctfh[:, wide]
        noises = [noise_ref[pl.ds(core * 32 + 3 * n + i, 1), :] for i in range(3)]
        counted = 1 - core * (1 - jnp.minimum(n, 1))
        noises[0] = noises[0] * counted.astype(F32)
        turned = []
        for i in range(3):
            tile = slice(i * LANES, (i + 1) * LANES)
            parts = [r[:, tile].astype(F32).reshape(2, 8, 1, 8, LANES) for r in raw]
            both = jnp.concatenate(parts, axis=2).reshape(2, 128, LANES)
            scaled = (both * noises[i][None]).astype(BF16)
            turned += [scaled[0].T, scaled[1].T]
            power = (both[0] * both[0] + both[1] * both[1]).T
            ctf = ctfs[:, tile]
            p1, p2, p3 = pieces(power)
            c1, c2, c3 = pieces(ctf * ctf * noises[i])
            total = total + jnp.dot(
                jnp.concatenate([c1, c1, c1, c2, c2, c3], axis=1),
                jnp.concatenate([p1, p2, p3, p1, p2, p1], axis=0),
                preferred_element_type=F32,
            )
        weights[pl.ds(pl.multiple_of(n * 768, 768), 768), :] = jnp.concatenate(turned, axis=0)
        return total

    cosine = trig_ref[0:8, :]
    sine = trig_ref[8:16, :]

    def prepare(b):
        meta = smeta[b].astype(F32)[0:8, :].astype(jnp.int32)

        def wave(steps):
            index = steps & (KY - 1)
            return (
                jnp.take_along_axis(cosine, index, axis=1),
                jnp.take_along_axis(sine, index, axis=1),
            )

        begin, one_row, two_rows = [], [], []
        for t in range(TRANS):
            sx = meta[:, 2 * t : 2 * t + 1]
            sy = meta[:, 2 * t + 1 : 2 * t + 2]
            slope = jnp.broadcast_to(sy - KX * sx, (8, LANES))
            begin.append(wave(lane * sx + top_row * slope))
            one_row.append(wave(slope))
            two_rows.append(wave(2 * slope))

        def body(n, phases):
            wide = pl.ds(pl.multiple_of(n * 384, 384), 384)
            blocks = gath[b, :, wide].astype(F32)
            ctfs = ctfrows[pl.ds(pl.multiple_of(b * 8, 8), 8), wide]
            singles = [vtab[3 * n + i] == 1 for i in range(3)]
            rows = [[], []]
            for i in range(3):
                tile = slice(i * LANES, (i + 1) * LANES)
                ctf = ctfs[:, tile]
                real, imag = blocks[0:8, tile] * ctf, blocks[8:16, tile] * ctf
                reals, imags, later = [], [], []
                for t in range(TRANS):
                    c, si = phases[t]
                    reals.append(real * c + imag * si)
                    imags.append(imag * c - real * si)
                    mc = jnp.where(singles[i], one_row[t][0], two_rows[t][0])
                    ms = jnp.where(singles[i], one_row[t][1], two_rows[t][1])
                    later.append((c * mc - si * ms, si * mc + c * ms))
                phases = tuple(later)
                for h in range(2):
                    for values in (reals, imags):
                        pair_ = jnp.concatenate(values[2 * h : 2 * h + 2], axis=0)
                        rows[h].append(pair_.astype(BF16))
            for h in range(2):
                at = pl.ds(pl.multiple_of(b * 32 + h * 16, 16), 16)
                prep[at, pl.ds(pl.multiple_of(n * 768, 768), 768)] = jnp.concatenate(
                    rows[h], axis=1
                )
            return phases

        lax.fori_loop(0, TILES // 3, body, tuple(begin), unroll=11)

    def score_group(g):
        rows = pl.ds(pl.multiple_of(g * 128, 128), 128)

        def body(i, total):
            cols = pl.ds(pl.multiple_of(i * 768, 768), 768)
            return total + jnp.dot(
                prep[rows, cols], weights[cols, :], preferred_element_type=F32
            )

        cross = lax.fori_loop(0, TILES // 3, body, jnp.zeros((128, 128), F32), unroll=11)
        picked = onehot[pl.ds(pl.multiple_of(g * 32, 32), 32), 0:LANES].reshape(4, 1, 8, LANES)
        picked = jnp.concatenate([picked] * TRANS, axis=1).reshape(128, LANES)
        norm = jnp.dot(picked[:, :64], norms[...], precision=HI, preferred_element_type=F32)
        score[g] = cross - norm

    sc_copies = [
        send(score.at[order[q]], pscore.at[order[q]], sc_s.at[q], sc_r.at[q], peer)
        for q in range(4)
    ]

    stats[own] = jnp.zeros((16, LANES), F32)

    def summarise(q):
        sc_copies[q].wait_recv()
        g = order[q]
        whole = (score[g] + pscore[g]).T
        pscore[g] = whole
        top = jnp.max(whole, axis=0, keepdims=True)
        stats[own, pl.ds(g, 1), :] = top
        stats[own, pl.ds(8 + g, 1), :] = jnp.sum(jnp.exp(whole - top), axis=0, keepdims=True)

    def finish(q):
        fwd_up[q].wait_recv()
        fwd_down[q].wait_recv()
        prepare(order[q] * 4 + y2)
        score_group(order[q])
        sc_copies[q].start()

    def arrive(q):
        z_right[q].wait_recv()
        launch(q)

    def forward(q):
        y_up[q].wait_recv()
        fwd_up[q].start()
        y_down[q].wait_recv()
        fwd_down[q].start()

    def prepare_three(q):
        def three(i, carry):
            prepare(order[q] * 4 + (y + 3 + i) % 4)
            return carry

        lax.fori_loop(0, 3, three, 0)

    ctf_copy.wait()
    proj_copy.wait()
    praw_copy.wait_recv()
    half_norms = lax.fori_loop(0, 4, weigh, jnp.zeros((64, 128), F32))

    for copy in meta_copies:
        copy.wait_recv()

    lane2 = lax.broadcasted_iota(jnp.int32, (8, 256), 1)

    def fill_onehot(b, carry):
        classes = smeta[b].astype(F32)[0:8, 8:9].astype(jnp.int32)
        hit = jnp.logical_and(lane2 % 64 == classes, lane2 < 192)
        onehot[pl.ds(pl.multiple_of(b * 8, 8), 8), :] = hit.astype(F32)
        return carry

    lax.fori_loop(0, BLOCKS, fill_onehot, 0)
    lax.fori_loop(0, 3, fill_ctf, 0)

    arrive(1)
    forward(0)
    half_norms = lax.fori_loop(4, 8, weigh, half_norms)
    arrive(2)
    prepare_three(0)
    forward(1)
    norms[...] = 0.5 * lax.fori_loop(8, 11, weigh, half_norms)
    arrive(3)
    prepare_three(1)
    forward(2)
    finish(0)
    prepare_three(2)
    forward(3)
    finish(1)
    summarise(0)
    prepare_three(3)
    finish(2)
    summarise(1)
    finish(3)
    summarise(2)
    summarise(3)

    stat_copies = [
        send(stats.at[own], stats.at[own], stat_s.at[n], stat_r.at[n], target)
        for n, target in enumerate(others)
    ]
    for copy in stat_copies:
        copy.start()
    for copy in stat_copies:
        copy.wait_recv()
    tops = [stats[b, 0:8, :] for b in range(BLOCKS)]
    top = tops[0]
    for b in range(1, BLOCKS):
        top = jnp.maximum(top, tops[b])
    total = jnp.zeros((8, LANES), F32)
    for b in range(BLOCKS):
        total += stats[b, 8:16, :] * jnp.exp(tops[b] - top)
    held = lax.broadcasted_iota(jnp.int32, (8, LANES), 1) % 32

    def turn(value, by):
        inside = pltpu.roll(value, by, 1)
        wrapped = pltpu.roll(value, by + LANES - 32, 1)
        return jnp.where(held >= by, inside, wrapped)

    largest = jnp.maximum(top, turn(top, 8))
    largest = jnp.maximum(largest, turn(largest, 16))
    total = total * jnp.exp(top - largest)
    total = total + turn(total, 8)
    total = total + turn(total, 16)
    evidence = largest + jnp.log(total)
    own_row = jnp.sum(jnp.where(place == zl, evidence, 0.0), axis=0, keepdims=True)
    ev_ref[...] = pltpu.roll(jnp.broadcast_to(own_row, (8, LANES)), 128 - (y * 32 + core * 4), 1)
    for g in range(4):
        post[:, g * 128 : (g + 1) * 128] = (
            jnp.exp(pscore[g] - evidence[g : g + 1, :]) * 2048.0
        ).astype(BF16)

    def copy_a(c):
        return send(part[c].at[2 * x2], from_a[c], a_s.at[c], a_r.at[c], right)

    def copy_b(c):
        return send(part[c].at[2 * x2 + 1], from_b[c], b_s.at[c], b_r.at[c], left)

    def copy_p(c):
        return send(part[c].at[pl.ds(2 * xp, 2)], from_p[c], p_s.at[c], p_r.at[c], right)

    def copy_m(c):
        return send(part[c].at[pl.ds(2 * xm, 2)], from_m[c], m_s.at[c], m_r.at[c], left)

    def copy_w(c, k):
        return send(
            zsend[c].at[k], zrecv[c].at[core], w_s.at[c, k], w_r.at[c, core], across[k]
        )

    def arrived_w(c, half):
        return send(zsend[c].at[0], zrecv[c].at[half], w_s.at[c, 0], w_r.at[c, half], across[0])

    def copy_f(c):
        other = pl.ds(pl.multiple_of((1 - core) * 8, 8), 8)
        return send(keep[c].at[other], fin[c], f_s.at[c], f_r.at[c], peer)

    def project(c):
        sums = jnp.dot(
            post[...], prep[:, STARTS[c] * 256 : STARTS[c + 1] * 256], preferred_element_type=F32
        ).astype(BF16)
        for i in range(8):
            part[c][i] = sums[16 * i : 16 * i + 16]
        copy_a(c).start()
        copy_b(c).start()

    def add(into, *others_):
        value = into.astype(F32)
        for other in others_:
            value = value + other.astype(F32)
        return value

    def pass_on(c):
        copy_a(c).wait_recv()
        part[c][2 * xp] = add(part[c][2 * xp], from_a[c][...]).astype(BF16)
        copy_p(c).start()
        copy_b(c).wait_recv()
        part[c][2 * xm + 1] = add(part[c][2 * xm + 1], from_b[c][...]).astype(BF16)
        copy_m(c).start()

    def collect(c):
        half = SIZES[c] * LANES
        copy_p(c).wait_recv()
        copy_m(c).wait_recv()
        far = 1 - zh
        away = add(part[c][2 * x + far], from_p[c][far], from_m[c][far])
        for k in range(2):
            rows = away[8 * k : 8 * k + 8]
            zsend[c][k] = jnp.concatenate([rows[:, :half], rows[:, half:]], axis=0).astype(BF16)
            copy_w(c, k).start()
        keep[c][...] = add(part[c][2 * x + zh], from_p[c][zh], from_m[c][zh])
        copy_f(c).start()

    def complete(c):
        for half in range(2):
            arrived_w(c, half).wait_recv()
        copy_f(c).wait_recv()
        here = keep[c][pl.ds(pl.multiple_of(core * 8, 8), 8), :]
        for half, near in ((core, here), (1 - core, fin[c][...])):
            rows = zrecv[c][half].astype(F32)
            value = near + jnp.concatenate([rows[0:8], rows[8:16]], axis=1)
            for s in range(SIZES[c]):
                at = pl.multiple_of(half * SHIFT + (STARTS[c] + s) * LANES, LANES)
                for k in range(2):
                    out_ref[k, :, pl.ds(at, LANES)] = value[
                        :, s * 256 + k * 128 : s * 256 + k * 128 + 128
                    ]

    for n in range(CHUNKS + 4):
        for lag, stage in ((0, project), (1, pass_on), (2, collect), (4, complete)):
            if 0 <= n - lag < CHUNKS:
                stage(n - lag)

    pmeta_copy.wait_send()
    pair_copy.wait_send()
    praw_copy.wait_send()
    for copy in meta_copies + stat_copies + sc_copies + y_up + y_down + fwd_up + fwd_down:
        copy.wait_send()
    for q in range(4):
        pl.when(goes_right[q])(lambda q=q: z_right[q].wait_send())
        pl.when(goes_left[q])(lambda q=q: z_left[q].wait_send())

    for c in range(CHUNKS):
        for copy in (copy_a, copy_b, copy_p, copy_m, copy_f):
            copy(c).wait_send()
        for k in range(2):
            copy_w(c, k).wait_send()


def per_device(images, projections, ctf_table, noise_weight, shifts, defocus):
    local = images.shape[0]
    pixels = images.shape[2]
    rows = images.transpose(1, 0, 2).reshape(2 * local, pixels)
    proj = projections.transpose(1, 0, 2).reshape(128, pixels)
    angles = np.arange(KY) * (2.0 * math.pi / KY)
    trig = np.concatenate([np.tile(np.cos(angles), (8, 1)), np.tile(np.sin(angles), (8, 1))])
    trig = jnp.asarray(trig.astype(np.float32))
    vmem = pl.BlockSpec(memory_space=pltpu.VMEM)
    hbm = pl.BlockSpec(memory_space=pl.ANY)
    smem = pl.BlockSpec(memory_space=pltpu.SMEM)
    dma = pltpu.SemaphoreType.DMA
    sems = [dma((2,)), dma((3,)), dma((3,)), dma((15,)), dma((15,)), dma((15,)), dma((15,))]
    sems += [dma((8,)), dma((4,))] + [dma((4,))] * 10 + [dma((CHUNKS,))] * 8 + [dma((CHUNKS, 2))] * 2 + [dma((CHUNKS,))] * 2
    sums, evidence = pl.pallas_call(
        kernel,
        out_shape=(
            jax.ShapeDtypeStruct((2, 8, pixels), F32),
            jax.ShapeDtypeStruct((8, LANES), F32),
        ),
        in_specs=[vmem, hbm, hbm, vmem, vmem, smem, smem],
        out_specs=(vmem, vmem),
        scratch_shapes=[
            pltpu.VMEM((16, 65 * LANES), BF16),
            pltpu.VMEM((16, LANES), BF16),
            pltpu.VMEM((16, HALF), BF16),
            pltpu.VMEM((16, LANES), BF16),
            pltpu.VMEM((BLOCKS, 16, LANES), BF16),
            pltpu.VMEM((BLOCKS, 16, HALF), BF16),
            pltpu.VMEM((2, 128, HALF), BF16),
            pltpu.VMEM((64, HALF), F32),
            pltpu.VMEM((2 * HALF, 128), BF16),
            pltpu.VMEM((64, 128), F32),
            pltpu.VMEM((128, 2 * LANES), F32),
            pltpu.VMEM((128, HALF), F32),
            pltpu.VMEM((TILES, 8, LANES), jnp.int32),
            pltpu.VMEM((BLOCKS * 32, 2 * HALF), BF16),
            pltpu.VMEM((4, 128, 128), F32),
            pltpu.VMEM((4, 128, 128), F32),
            pltpu.VMEM((BLOCKS, 16, LANES), F32),
            pltpu.VMEM((128, 512), BF16),
            [pltpu.VMEM((8, 16, 256 * t), BF16) for t in SIZES],
            [pltpu.VMEM((16, 256 * t), BF16) for t in SIZES],
            [pltpu.VMEM((16, 256 * t), BF16) for t in SIZES],
            [pltpu.VMEM((2, 16, 256 * t), BF16) for t in SIZES],
            [pltpu.VMEM((2, 16, 256 * t), BF16) for t in SIZES],
            [pltpu.VMEM((2, 16, 128 * t), BF16) for t in SIZES],
            [pltpu.VMEM((2, 16, 128 * t), BF16) for t in SIZES],
            [pltpu.VMEM((16, 256 * t), F32) for t in SIZES],
            [pltpu.VMEM((8, 256 * t), F32) for t in SIZES],
            *sems,
        ],
        compiler_params=pltpu.CompilerParams(
            collective_id=0, has_side_effects=True, vmem_limit_bytes=56 * 1024 * 1024
        ),
    )(
        rows, proj, ctf_table, noise_weight.reshape(65, LANES), trig,
        shifts.transpose(0, 2, 1), defocus,
    )
    return evidence[0, :local], sums.transpose(1, 0, 2)


def solution(mesh):
    in_specs = (
        P(("img", "ori"), None, None),
        P("ori", None, None),
        P(),
        P(),
        P(("img", "ori"), None, None),
        P(("img", "ori")),
    )
    out_specs = (P(("img", "ori")), P(("ori", "img"), None, None))
    return jax.shard_map(
        per_device, mesh=mesh, in_specs=in_specs, out_specs=out_specs, check_vma=False
    )
```

```python
import math

import jax
import jax.numpy as jnp
import numpy as np
from jax import lax
from jax.experimental import pallas as pl
from jax.experimental.pallas import tpu as pltpu
from jax.sharding import PartitionSpec as P

KY = 128
KX = 65
LANES = 128
NX, NZ, NY = 4, 4, 4
BLOCKS = NZ * NY
TRANS = 4
TILES = 33
HALF = TILES * LANES
SHIFT = 32 * LANES
HALF_A = 17 * LANES
SIZES = (5, 7, 8, 8, 5)
STARTS = (0, 5, 12, 20, 28, 33)
CHUNKS = len(SIZES)
OTHERS = [(dz, dy) for dz in range(NZ) for dy in range(NY) if (dz, dy) != (0, 0)]
F32 = jnp.float32
BF16 = jnp.bfloat16
HI = lax.Precision.HIGHEST


def kernel(
    img_ref, proj_ref, ctf_ref, noise_ref, trig_ref, shift_ref, class_ref,
    out_ref, ev_ref,
    placed, ometa, pair, pmeta, smeta, gath, praw, ctfh, weights, norms, onehot, ctfrows, vtab, prep,
    score, pscore, stats, post, part, from_a, from_b, from_p, from_m, zsend, zrecv, keep, fin,
    loc_sem, core_s, core_r, meta_s, meta_r, stat_s, stat_r, z_s, z_r,
    yp_s, ym_s, yl_r, yr_r, fa_s, fb_s, fa_r, fb_r, sc_s, sc_r,
    a_s, b_s, a_r, b_r, p_s, m_s, p_r, m_r, w_s, w_r, f_s, f_r,
):
    img = lax.axis_index("img")
    ori = lax.axis_index("ori")
    x, zh = img // 2, img % 2
    core, y, zl = ori % 2, (ori // 2) % 4, ori // 8
    xp, xm, x2 = (x + 1) % 4, (x + 3) % 4, (x + 2) % 4
    yp, ym, y2 = (y + 1) % 4, (y + 3) % 4, (y + 2) % 4
    own = zl * 4 + y

    def dev(x_=x, zh_=zh, zl_=zl, y_=y, core_=core):
        return (x_ * 2 + zh_, (zl_ * 4 + y_) * 2 + core_)

    def send(src, dst, ss, rs, target):
        return pltpu.make_async_remote_copy(
            src_ref=src, dst_ref=dst, send_sem=ss, recv_sem=rs,
            device_id=target, device_id_type=pl.DeviceIdType.MESH,
        )

    peer = dev(core_=1 - core)
    others = [dev(zl_=(zl + dz) % 4, y_=(y + dy) % 4) for dz, dy in OTHERS]
    right, left = dev(x_=xp), dev(x_=xm)
    up, down = dev(y_=yp), dev(y_=ym)
    across = [dev(zh_=1 - zh, core_=k) for k in range(2)]

    barrier = pltpu.get_barrier_semaphore()
    greeted = [peer, *others, right, left, *across]
    for target in greeted:
        pl.semaphore_signal(barrier, inc=1, device_id=target, device_id_type=pl.DeviceIdType.MESH)

    mine = pl.ds(pl.multiple_of(core * SHIFT, LANES), HALF)
    theirs = pl.ds(pl.multiple_of((1 - core) * SHIFT, LANES), HALF)
    ctf_copy = pltpu.make_async_copy(ctf_ref.at[:, mine], ctfh, loc_sem.at[0])
    proj_copy = pltpu.make_async_copy(proj_ref.at[:, mine], praw.at[core], loc_sem.at[1])
    ctf_copy.start()
    proj_copy.start()

    lane = lax.broadcasted_iota(jnp.int32, (8, LANES), 1)
    place = lax.broadcasted_iota(jnp.int32, (8, LANES), 0)

    def lay_out(s, carry):
        cols = pl.ds(pl.multiple_of(s * 5 * LANES, LANES), 5 * LANES)
        at = lax.broadcasted_iota(jnp.int32, (8, 5 * LANES), 0)
        real = jnp.zeros((8, 5 * LANES), F32)
        imag = jnp.zeros((8, 5 * LANES), F32)
        for i in range(4):
            both = img_ref[i, :, cols].astype(F32)
            here = at == i + 4 * core
            real = jnp.where(here, both[0:1], real)
            imag = jnp.where(here, both[1:2], imag)
        placed[:, cols] = jnp.concatenate([real, imag], axis=0).astype(BF16)
        return carry

    lax.fori_loop(0, 13, lay_out, 0)
    meta = jnp.zeros((8, LANES), jnp.int32)
    for i in range(4):
        row = place == i + 4 * core
        for t in range(TRANS):
            for k in range(2):
                spot = jnp.logical_and(row, lane == 2 * t + k)
                meta = jnp.where(spot, shift_ref[i, k, t], meta)
        meta = jnp.where(jnp.logical_and(row, lane == 8), class_ref[i], meta)
    meta = meta.astype(F32)
    ometa[...] = jnp.concatenate([meta, jnp.zeros_like(meta)], axis=0).astype(BF16)

    pl.semaphore_wait(barrier, len(greeted))

    pair_copy = send(placed.at[:, theirs], pair, core_s.at[0], core_r.at[0], peer)
    pmeta_copy = send(ometa, pmeta, core_s.at[1], core_r.at[1], peer)
    praw_copy = send(proj_ref.at[:, theirs], praw.at[core], core_s.at[2], core_r.at[2], peer)
    pmeta_copy.start()
    pair_copy.start()
    praw_copy.start()

    pmeta_copy.wait_recv()
    smeta[own] = ometa[...] + pmeta[...]
    meta_copies = [
        send(smeta.at[own], smeta.at[own], meta_s.at[n], meta_r.at[n], target)
        for n, target in enumerate(others)
    ]
    for copy in meta_copies:
        copy.start()

    pair_copy.wait_recv()
    gath[own] = placed[:, mine] + pair[...]

    b0, b1 = zl % 2, zl // 2

    def pick(table):
        low = (1 - b0) * table[0] + b0 * table[1]
        high = (1 - b0) * table[2] + b0 * table[3]
        return (1 - b1) * low + b1 * high

    order = [zl, pick([1, 0, 3, 2]), pick([2, 2, 1, 1]), pick([3, 3, 0, 0])]

    def z_copy(zq, step, target):
        b = zq * 4 + y
        return send(gath.at[b], gath.at[b], z_s.at[step], z_r.at[zq], target)

    z_right = [z_copy(order[q], q, dev(zl_=zl + 1)) for q in range(4)]
    z_left = [z_copy(order[q], 4 + q, dev(zl_=zl - 1)) for q in range(4)]
    goes_right = [zl < 3] + [jnp.logical_and(order[q] < zl, zl < 3) for q in (1, 2, 3)]
    goes_left = [zl > 0] + [jnp.logical_and(order[q] > zl, zl > 0) for q in (1, 2, 3)]
    y_up = [
        send(gath.at[order[q] * 4 + y], gath.at[order[q] * 4 + y], yp_s.at[q], yl_r.at[q], up)
        for q in range(4)
    ]
    y_down = [
        send(gath.at[order[q] * 4 + y], gath.at[order[q] * 4 + y], ym_s.at[q], yr_r.at[q], down)
        for q in range(4)
    ]
    first, second = pl.ds(0, HALF_A), pl.ds(HALF_A, HALF - HALF_A)
    fwd_up, fwd_down = [], []
    for q in range(4):
        low = gath.at[order[q] * 4 + ym, :, first]
        high = gath.at[order[q] * 4 + yp, :, second]
        fwd_up.append(send(low, low, fa_s.at[q], fa_r.at[q], up))
        fwd_down.append(send(high, high, fb_s.at[q], fb_r.at[q], down))

    def launch(q):
        pl.when(goes_right[q])(lambda: z_right[q].start())
        pl.when(goes_left[q])(lambda: z_left[q].start())
        y_up[q].start()
        y_down[q].start()

    launch(0)

    def fill_rows(s, carry):
        p = (s + 32 * core) * LANES + lane
        after = lax.shift_right_logical((p + LANES) * 64528, 22)
        vtab[s] = after - lax.shift_right_logical(p * 64528, 22)
        return carry

    lax.fori_loop(0, TILES, fill_rows, 0)
    top_row = lax.shift_right_logical((32 * core * LANES + lane) * 64528, 22)

    def pieces(value):
        one = value.astype(BF16)
        rest = value - one.astype(F32)
        two = rest.astype(BF16)
        three = (rest - two.astype(F32)).astype(BF16)
        return one, two, three

    def fill_ctf(s, carry):
        cols = pl.ds(pl.multiple_of(s * 1408, 1408), 1408)
        one, two, three = pieces(ctfh[:, cols])
        ctfrows[:, cols] = jnp.dot(
            onehot[...].astype(BF16),
            jnp.concatenate([one, two, three, one], axis=0),
            preferred_element_type=F32,
        )
        return carry


    def weigh(n, total):
        wide = pl.ds(pl.multiple_of(n * 384, 384), 384)
        raw = [praw[0, :, wide], praw[1, :, wide]]
        ctfs = ctfh[:, wide]
        noises = [noise_ref[pl.ds(core * 32 + 3 * n + i, 1), :] for i in range(3)]
        counted = 1 - core * (1 - jnp.minimum(n, 1))
        noises[0] = noises[0] * counted.astype(F32)
        turned = []
        for i in range(3):
            tile = slice(i * LANES, (i + 1) * LANES)
            parts = [r[:, tile].astype(F32).reshape(2, 8, 1, 8, LANES) for r in raw]
            both = jnp.concatenate(parts, axis=2).reshape(2, 128, LANES)
            scaled = (both * noises[i][None]).astype(BF16)
            turned += [scaled[0].T, scaled[1].T]
            power = (both[0] * both[0] + both[1] * both[1]).T
            ctf = ctfs[:, tile]
            p1, p2, p3 = pieces(power)
            c1, c2, c3 = pieces(ctf * ctf * noises[i])
            total = total + jnp.dot(
                jnp.concatenate([c1, c1, c1, c2, c2, c3], axis=1),
                jnp.concatenate([p1, p2, p3, p1, p2, p1], axis=0),
                preferred_element_type=F32,
            )
        weights[pl.ds(pl.multiple_of(n * 768, 768), 768), :] = jnp.concatenate(turned, axis=0)
        return total

    cosine = trig_ref[0:8, :]
    sine = trig_ref[8:16, :]

    def prepare(b):
        meta = smeta[b].astype(F32)[0:8, :].astype(jnp.int32)

        def wave(steps):
            index = steps & (KY - 1)
            return (
                jnp.take_along_axis(cosine, index, axis=1),
                jnp.take_along_axis(sine, index, axis=1),
            )

        begin, one_row, two_rows = [], [], []
        for t in range(TRANS):
            sx = meta[:, 2 * t : 2 * t + 1]
            sy = meta[:, 2 * t + 1 : 2 * t + 2]
            slope = jnp.broadcast_to(sy - KX * sx, (8, LANES))
            begin.append(wave(lane * sx + top_row * slope))
            one_row.append(wave(slope))
            two_rows.append(wave(2 * slope))

        def body(n, phases):
            wide = pl.ds(pl.multiple_of(n * 384, 384), 384)
            blocks = gath[b, :, wide].astype(F32)
            ctfs = ctfrows[pl.ds(pl.multiple_of(b * 8, 8), 8), wide]
            singles = [vtab[3 * n + i] == 1 for i in range(3)]
            rows = [[], []]
            for i in range(3):
                tile = slice(i * LANES, (i + 1) * LANES)
                ctf = ctfs[:, tile]
                real, imag = blocks[0:8, tile] * ctf, blocks[8:16, tile] * ctf
                reals, imags, later = [], [], []
                for t in range(TRANS):
                    c, si = phases[t]
                    reals.append(real * c + imag * si)
                    imags.append(imag * c - real * si)
                    mc = jnp.where(singles[i], one_row[t][0], two_rows[t][0])
                    ms = jnp.where(singles[i], one_row[t][1], two_rows[t][1])
                    later.append((c * mc - si * ms, si * mc + c * ms))
                phases = tuple(later)
                for h in range(2):
                    for values in (reals, imags):
                        pair_ = jnp.concatenate(values[2 * h : 2 * h + 2], axis=0)
                        rows[h].append(pair_.astype(BF16))
            for h in range(2):
                at = pl.ds(pl.multiple_of(b * 32 + h * 16, 16), 16)
                prep[at, pl.ds(pl.multiple_of(n * 768, 768), 768)] = jnp.concatenate(
                    rows[h], axis=1
                )
            return phases

        lax.fori_loop(0, TILES // 3, body, tuple(begin), unroll=11)

    def score_group(g):
        rows = pl.ds(pl.multiple_of(g * 128, 128), 128)

        def body(i, total):
            cols = pl.ds(pl.multiple_of(i * 768, 768), 768)
            return total + jnp.dot(
                prep[rows, cols], weights[cols, :], preferred_element_type=F32
            )

        cross = lax.fori_loop(0, TILES // 3, body, jnp.zeros((128, 128), F32), unroll=11)
        picked = onehot[pl.ds(pl.multiple_of(g * 32, 32), 32), 0:LANES].reshape(4, 1, 8, LANES)
        picked = jnp.concatenate([picked] * TRANS, axis=1).reshape(128, LANES)
        norm = jnp.dot(picked[:, :64], norms[...], precision=HI, preferred_element_type=F32)
        score[g] = cross - norm

    sc_copies = [
        send(score.at[order[q]], pscore.at[order[q]], sc_s.at[q], sc_r.at[q], peer)
        for q in range(4)
    ]

    stats[own] = jnp.zeros((16, LANES), F32)

    def summarise(q):
        sc_copies[q].wait_recv()
        g = order[q]
        whole = (score[g] + pscore[g]).T
        pscore[g] = whole
        top = jnp.max(whole, axis=0, keepdims=True)
        stats[own, pl.ds(g, 1), :] = top
        stats[own, pl.ds(8 + g, 1), :] = jnp.sum(jnp.exp(whole - top), axis=0, keepdims=True)

    def finish(q):
        fwd_up[q].wait_recv()
        fwd_down[q].wait_recv()
        prepare(order[q] * 4 + y2)
        score_group(order[q])
        sc_copies[q].start()

    def arrive(q):
        z_right[q].wait_recv()
        launch(q)

    def forward(q):
        y_up[q].wait_recv()
        fwd_up[q].start()
        y_down[q].wait_recv()
        fwd_down[q].start()

    def prepare_three(q):
        def three(i, carry):
            prepare(order[q] * 4 + (y + 3 + i) % 4)
            return carry

        lax.fori_loop(0, 3, three, 0)

    ctf_copy.wait()
    proj_copy.wait()
    praw_copy.wait_recv()
    half_norms = lax.fori_loop(0, 4, weigh, jnp.zeros((64, 128), F32))

    for copy in meta_copies:
        copy.wait_recv()

    lane2 = lax.broadcasted_iota(jnp.int32, (8, 256), 1)

    def fill_onehot(b, carry):
        classes = smeta[b].astype(F32)[0:8, 8:9].astype(jnp.int32)
        hit = jnp.logical_and(lane2 % 64 == classes, lane2 < 192)
        onehot[pl.ds(pl.multiple_of(b * 8, 8), 8), :] = hit.astype(F32)
        return carry

    lax.fori_loop(0, BLOCKS, fill_onehot, 0)
    lax.fori_loop(0, 3, fill_ctf, 0)

    arrive(1)
    forward(0)
    half_norms = lax.fori_loop(4, 8, weigh, half_norms)
    arrive(2)
    prepare_three(0)
    forward(1)
    norms[...] = 0.5 * lax.fori_loop(8, 11, weigh, half_norms)
    arrive(3)
    prepare_three(1)
    forward(2)
    finish(0)
    prepare_three(2)
    forward(3)
    finish(1)
    summarise(0)
    prepare_three(3)
    finish(2)
    summarise(1)
    finish(3)
    summarise(2)
    summarise(3)

    stat_copies = [
        send(stats.at[own], stats.at[own], stat_s.at[n], stat_r.at[n], target)
        for n, target in enumerate(others)
    ]
    for copy in stat_copies:
        copy.start()
    for copy in stat_copies:
        copy.wait_recv()
    tops = [stats[b, 0:8, :] for b in range(BLOCKS)]
    top = tops[0]
    for b in range(1, BLOCKS):
        top = jnp.maximum(top, tops[b])
    total = jnp.zeros((8, LANES), F32)
    for b in range(BLOCKS):
        total += stats[b, 8:16, :] * jnp.exp(tops[b] - top)
    held = lax.broadcasted_iota(jnp.int32, (8, LANES), 1) % 32

    def turn(value, by):
        inside = pltpu.roll(value, by, 1)
        wrapped = pltpu.roll(value, by + LANES - 32, 1)
        return jnp.where(held >= by, inside, wrapped)

    largest = jnp.maximum(top, turn(top, 8))
    largest = jnp.maximum(largest, turn(largest, 16))
    total = total * jnp.exp(top - largest)
    total = total + turn(total, 8)
    total = total + turn(total, 16)
    evidence = largest + jnp.log(total)
    for i in range(4):
        spot = jnp.logical_and(place == zl, lane == y * 32 + core * 4 + i)
        ev_ref[i] = jnp.sum(jnp.where(spot, evidence, 0.0))
    for g in range(4):
        post[:, g * 128 : (g + 1) * 128] = (
            jnp.exp(pscore[g] - evidence[g : g + 1, :]) * 2048.0
        ).astype(BF16)

    def copy_a(c):
        return send(part[c].at[2 * x2], from_a[c], a_s.at[c], a_r.at[c], right)

    def copy_b(c):
        return send(part[c].at[2 * x2 + 1], from_b[c], b_s.at[c], b_r.at[c], left)

    def copy_p(c):
        return send(part[c].at[pl.ds(2 * xp, 2)], from_p[c], p_s.at[c], p_r.at[c], right)

    def copy_m(c):
        return send(part[c].at[pl.ds(2 * xm, 2)], from_m[c], m_s.at[c], m_r.at[c], left)

    def copy_w(c, k):
        return send(
            zsend[c].at[k], zrecv[c].at[core], w_s.at[c, k], w_r.at[c, core], across[k]
        )

    def arrived_w(c, half):
        return send(zsend[c].at[0], zrecv[c].at[half], w_s.at[c, 0], w_r.at[c, half], across[0])

    def copy_f(c):
        other = pl.ds(pl.multiple_of((1 - core) * 8, 8), 8)
        return send(keep[c].at[other], fin[c], f_s.at[c], f_r.at[c], peer)

    def project(c):
        sums = jnp.dot(
            post[...], prep[:, STARTS[c] * 256 : STARTS[c + 1] * 256], preferred_element_type=F32
        ).astype(BF16)
        for i in range(8):
            part[c][i] = sums[16 * i : 16 * i + 16]
        copy_a(c).start()
        copy_b(c).start()

    def add(into, *others_):
        value = into.astype(F32)
        for other in others_:
            value = value + other.astype(F32)
        return value

    def pass_on(c):
        copy_a(c).wait_recv()
        part[c][2 * xp] = add(part[c][2 * xp], from_a[c][...]).astype(BF16)
        copy_p(c).start()
        copy_b(c).wait_recv()
        part[c][2 * xm + 1] = add(part[c][2 * xm + 1], from_b[c][...]).astype(BF16)
        copy_m(c).start()

    def collect(c):
        half = SIZES[c] * LANES
        copy_p(c).wait_recv()
        copy_m(c).wait_recv()
        far = 1 - zh
        away = add(part[c][2 * x + far], from_p[c][far], from_m[c][far])
        for k in range(2):
            rows = away[8 * k : 8 * k + 8]
            zsend[c][k] = jnp.concatenate([rows[:, :half], rows[:, half:]], axis=0).astype(BF16)
            copy_w(c, k).start()
        keep[c][...] = add(part[c][2 * x + zh], from_p[c][zh], from_m[c][zh])
        copy_f(c).start()

    def complete(c):
        for half in range(2):
            arrived_w(c, half).wait_recv()
        copy_f(c).wait_recv()
        here = keep[c][pl.ds(pl.multiple_of(core * 8, 8), 8), :]
        for half, near in ((core, here), (1 - core, fin[c][...])):
            rows = zrecv[c][half].astype(F32)
            value = near + jnp.concatenate([rows[0:8], rows[8:16]], axis=1)
            for s in range(SIZES[c]):
                at = pl.multiple_of(half * SHIFT + (STARTS[c] + s) * LANES, LANES)
                for k in range(2):
                    out_ref[:, k, pl.ds(at, LANES)] = value[
                        :, s * 256 + k * 128 : s * 256 + k * 128 + 128
                    ]

    for n in range(CHUNKS + 4):
        for lag, stage in ((0, project), (1, pass_on), (2, collect), (4, complete)):
            if 0 <= n - lag < CHUNKS:
                stage(n - lag)

    pmeta_copy.wait_send()
    pair_copy.wait_send()
    praw_copy.wait_send()
    for copy in meta_copies + stat_copies + sc_copies + y_up + y_down + fwd_up + fwd_down:
        copy.wait_send()
    for q in range(4):
        pl.when(goes_right[q])(lambda q=q: z_right[q].wait_send())
        pl.when(goes_left[q])(lambda q=q: z_left[q].wait_send())

    for c in range(CHUNKS):
        for copy in (copy_a, copy_b, copy_p, copy_m, copy_f):
            copy(c).wait_send()
        for k in range(2):
            copy_w(c, k).wait_send()


def per_device(images, projections, ctf_table, noise_weight, shifts, defocus):
    local = images.shape[0]
    pixels = images.shape[2]
    proj = projections.transpose(1, 0, 2).reshape(128, pixels)
    angles = np.arange(KY) * (2.0 * math.pi / KY)
    trig = np.concatenate([np.tile(np.cos(angles), (8, 1)), np.tile(np.sin(angles), (8, 1))])
    trig = jnp.asarray(trig.astype(np.float32))
    vmem = pl.BlockSpec(memory_space=pltpu.VMEM)
    hbm = pl.BlockSpec(memory_space=pl.ANY)
    smem = pl.BlockSpec(memory_space=pltpu.SMEM)
    dma = pltpu.SemaphoreType.DMA
    sems = [dma((2,)), dma((3,)), dma((3,)), dma((15,)), dma((15,)), dma((15,)), dma((15,))]
    sems += [dma((8,)), dma((4,))] + [dma((4,))] * 10 + [dma((CHUNKS,))] * 8 + [dma((CHUNKS, 2))] * 2 + [dma((CHUNKS,))] * 2
    sums, evidence = pl.pallas_call(
        kernel,
        out_shape=(
            jax.ShapeDtypeStruct((8, 2, pixels), F32),
            jax.ShapeDtypeStruct((local,), F32),
        ),
        in_specs=[vmem, hbm, hbm, vmem, vmem, smem, smem],
        out_specs=(vmem, smem),
        scratch_shapes=[
            pltpu.VMEM((16, 65 * LANES), BF16),
            pltpu.VMEM((16, LANES), BF16),
            pltpu.VMEM((16, HALF), BF16),
            pltpu.VMEM((16, LANES), BF16),
            pltpu.VMEM((BLOCKS, 16, LANES), BF16),
            pltpu.VMEM((BLOCKS, 16, HALF), BF16),
            pltpu.VMEM((2, 128, HALF), BF16),
            pltpu.VMEM((64, HALF), F32),
            pltpu.VMEM((2 * HALF, 128), BF16),
            pltpu.VMEM((64, 128), F32),
            pltpu.VMEM((128, 2 * LANES), F32),
            pltpu.VMEM((128, HALF), F32),
            pltpu.VMEM((TILES, 8, LANES), jnp.int32),
            pltpu.VMEM((BLOCKS * 32, 2 * HALF), BF16),
            pltpu.VMEM((4, 128, 128), F32),
            pltpu.VMEM((4, 128, 128), F32),
            pltpu.VMEM((BLOCKS, 16, LANES), F32),
            pltpu.VMEM((128, 512), BF16),
            [pltpu.VMEM((8, 16, 256 * t), BF16) for t in SIZES],
            [pltpu.VMEM((16, 256 * t), BF16) for t in SIZES],
            [pltpu.VMEM((16, 256 * t), BF16) for t in SIZES],
            [pltpu.VMEM((2, 16, 256 * t), BF16) for t in SIZES],
            [pltpu.VMEM((2, 16, 256 * t), BF16) for t in SIZES],
            [pltpu.VMEM((2, 16, 128 * t), BF16) for t in SIZES],
            [pltpu.VMEM((2, 16, 128 * t), BF16) for t in SIZES],
            [pltpu.VMEM((16, 256 * t), F32) for t in SIZES],
            [pltpu.VMEM((8, 256 * t), F32) for t in SIZES],
            *sems,
        ],
        compiler_params=pltpu.CompilerParams(
            collective_id=0, has_side_effects=True, vmem_limit_bytes=56 * 1024 * 1024
        ),
    )(
        images, proj, ctf_table, noise_weight.reshape(65, LANES), trig,
        shifts.transpose(0, 2, 1), defocus,
    )
    return evidence, sums


def solution(mesh):
    in_specs = (
        P(("img", "ori"), None, None),
        P("ori", None, None),
        P(),
        P(),
        P(("img", "ori"), None, None),
        P(("img", "ori")),
    )
    out_specs = (P(("img", "ori")), P(("ori", "img"), None, None))
    return jax.shard_map(
        per_device, mesh=mesh, in_specs=in_specs, out_specs=out_specs, check_vma=False
    )
```

```python
import math

import jax
import jax.numpy as jnp
import numpy as np
from jax import lax
from jax.experimental import pallas as pl
from jax.experimental.pallas import tpu as pltpu
from jax.sharding import PartitionSpec as P

KY = 128
KX = 65
LANES = 128
NX, NZ, NY = 4, 4, 4
BLOCKS = NZ * NY
TRANS = 4
TILES = 33
HALF = TILES * LANES
SHIFT = 32 * LANES
HALF_A = 17 * LANES
SIZES = (5, 7, 8, 8, 5)
STARTS = (0, 5, 12, 20, 28, 33)
CHUNKS = len(SIZES)
OTHERS = [(dz, dy) for dz in range(NZ) for dy in range(NY) if (dz, dy) != (0, 0)]
ORDERS = ((0, 1, 2, 3), (1, 0, 2, 3), (2, 3, 1, 0), (3, 2, 1, 0))
STEP_OF = (0, 0, 0, 1, 1, 1, 0, 2, 2, 2, 1, 3, 3, 3, 2, 3)
AHEAD_OF = (3, 0, 1, 3, 0, 1, 2, 3, 0, 1, 2, 3, 0, 1, 2, 2)
F32 = jnp.float32
BF16 = jnp.bfloat16
HI = lax.Precision.HIGHEST


def kernel(
    img_ref, proj_ref, ctf_ref, noise_ref, trig_ref, shift_ref, class_ref,
    out_ref, ev_ref,
    placed, ometa, pair, pmeta, smeta, gath, praw, ctfh, weights, norms, onehot, ctfrows, vtab, prep,
    score, pscore, stats, post, part, from_a, from_b, from_p, from_m, zsend, zrecv, keep, fin,
    loc_sem, core_s, core_r, meta_s, meta_r, stat_s, stat_r, z_s, z_r,
    yp_s, ym_s, yl_r, yr_r, fa_s, fb_s, fa_r, fb_r, sc_s, sc_r,
    a_s, b_s, a_r, b_r, p_s, m_s, p_r, m_r, w_s, w_r, f_s, f_r,
):
    img = lax.axis_index("img")
    ori = lax.axis_index("ori")
    x, zh = img // 2, img % 2
    core, y, zl = ori % 2, (ori // 2) % 4, ori // 8
    xp, xm, x2 = (x + 1) % 4, (x + 3) % 4, (x + 2) % 4
    yp, ym, y2 = (y + 1) % 4, (y + 3) % 4, (y + 2) % 4
    own = zl * 4 + y

    def dev(x_=x, zh_=zh, zl_=zl, y_=y, core_=core):
        return (x_ * 2 + zh_, (zl_ * 4 + y_) * 2 + core_)

    def send(src, dst, ss, rs, target):
        return pltpu.make_async_remote_copy(
            src_ref=src, dst_ref=dst, send_sem=ss, recv_sem=rs,
            device_id=target, device_id_type=pl.DeviceIdType.MESH,
        )

    peer = dev(core_=1 - core)
    others = [dev(zl_=(zl + dz) % 4, y_=(y + dy) % 4) for dz, dy in OTHERS]
    right, left = dev(x_=xp), dev(x_=xm)
    up, down = dev(y_=yp), dev(y_=ym)
    across = [dev(zh_=1 - zh, core_=k) for k in range(2)]

    barrier = pltpu.get_barrier_semaphore()
    greeted = [peer, *others, right, left, *across]
    for target in greeted:
        pl.semaphore_signal(barrier, inc=1, device_id=target, device_id_type=pl.DeviceIdType.MESH)

    mine = pl.ds(pl.multiple_of(core * SHIFT, LANES), HALF)
    theirs = pl.ds(pl.multiple_of((1 - core) * SHIFT, LANES), HALF)
    ctf_copy = pltpu.make_async_copy(ctf_ref.at[:, mine], ctfh, loc_sem.at[0])
    proj_copy = pltpu.make_async_copy(proj_ref.at[:, mine], praw.at[core], loc_sem.at[1])
    ctf_copy.start()
    proj_copy.start()

    lane = lax.broadcasted_iota(jnp.int32, (8, LANES), 1)
    place = lax.broadcasted_iota(jnp.int32, (8, LANES), 0)

    def lay_out(s, carry):
        cols = pl.ds(pl.multiple_of(s * 5 * LANES, LANES), 5 * LANES)
        at = lax.broadcasted_iota(jnp.int32, (8, 5 * LANES), 0)
        real = jnp.zeros((8, 5 * LANES), F32)
        imag = jnp.zeros((8, 5 * LANES), F32)
        for i in range(4):
            both = img_ref[i, :, cols].astype(F32)
            here = at == i + 4 * core
            real = jnp.where(here, both[0:1], real)
            imag = jnp.where(here, both[1:2], imag)
        placed[:, cols] = jnp.concatenate([real, imag], axis=0).astype(BF16)
        return carry

    lax.fori_loop(0, 13, lay_out, 0)
    meta = jnp.zeros((8, LANES), jnp.int32)
    for i in range(4):
        row = place == i + 4 * core
        for t in range(TRANS):
            for k in range(2):
                spot = jnp.logical_and(row, lane == 2 * t + k)
                meta = jnp.where(spot, shift_ref[i, k, t], meta)
        meta = jnp.where(jnp.logical_and(row, lane == 8), class_ref[i], meta)
    meta = meta.astype(F32)
    ometa[...] = jnp.concatenate([meta, jnp.zeros_like(meta)], axis=0).astype(BF16)

    pl.semaphore_wait(barrier, len(greeted))

    pair_copy = send(placed.at[:, theirs], pair, core_s.at[0], core_r.at[0], peer)
    pmeta_copy = send(ometa, pmeta, core_s.at[1], core_r.at[1], peer)
    praw_copy = send(proj_ref.at[:, theirs], praw.at[core], core_s.at[2], core_r.at[2], peer)
    pmeta_copy.start()
    pair_copy.start()
    praw_copy.start()

    pmeta_copy.wait_recv()
    smeta[own] = ometa[...] + pmeta[...]
    meta_copies = [
        send(smeta.at[own], smeta.at[own], meta_s.at[n], meta_r.at[n], target)
        for n, target in enumerate(others)
    ]
    for copy in meta_copies:
        copy.start()

    pair_copy.wait_recv()
    gath[own] = placed[:, mine] + pair[...]

    b0, b1 = zl % 2, zl // 2

    def pick(table):
        low = (1 - b0) * table[0] + b0 * table[1]
        high = (1 - b0) * table[2] + b0 * table[3]
        return (1 - b1) * low + b1 * high

    order = [pick([row[q] for row in ORDERS]) for q in range(4)]

    def z_copy(zq, step, target):
        b = zq * 4 + y
        return send(gath.at[b], gath.at[b], z_s.at[step], z_r.at[zq], target)

    z_right = [z_copy(order[q], q, dev(zl_=zl + 1)) for q in range(4)]
    z_left = [z_copy(order[q], 4 + q, dev(zl_=zl - 1)) for q in range(4)]
    goes_right = [zl < 3] + [jnp.logical_and(order[q] < zl, zl < 3) for q in (1, 2, 3)]
    goes_left = [zl > 0] + [jnp.logical_and(order[q] > zl, zl > 0) for q in (1, 2, 3)]
    y_up = [
        send(gath.at[order[q] * 4 + y], gath.at[order[q] * 4 + y], yp_s.at[q], yl_r.at[q], up)
        for q in range(4)
    ]
    y_down = [
        send(gath.at[order[q] * 4 + y], gath.at[order[q] * 4 + y], ym_s.at[q], yr_r.at[q], down)
        for q in range(4)
    ]
    first, second = pl.ds(0, HALF_A), pl.ds(HALF_A, HALF - HALF_A)
    fwd_up, fwd_down = [], []
    for q in range(4):
        low = gath.at[order[q] * 4 + ym, :, first]
        high = gath.at[order[q] * 4 + yp, :, second]
        fwd_up.append(send(low, low, fa_s.at[q], fa_r.at[q], up))
        fwd_down.append(send(high, high, fb_s.at[q], fb_r.at[q], down))

    def launch(q):
        pl.when(goes_right[q])(lambda: z_right[q].start())
        pl.when(goes_left[q])(lambda: z_left[q].start())
        y_up[q].start()
        y_down[q].start()

    launch(0)

    def fill_rows(s, carry):
        p = (s + 32 * core) * LANES + lane
        after = lax.shift_right_logical((p + LANES) * 64528, 22)
        vtab[s] = after - lax.shift_right_logical(p * 64528, 22)
        return carry

    lax.fori_loop(0, TILES, fill_rows, 0)
    top_row = lax.shift_right_logical((32 * core * LANES + lane) * 64528, 22)

    def pieces(value):
        one = value.astype(BF16)
        rest = value - one.astype(F32)
        two = rest.astype(BF16)
        three = (rest - two.astype(F32)).astype(BF16)
        return one, two, three

    def fill_ctf(s, carry):
        cols = pl.ds(pl.multiple_of(s * 1408, 1408), 1408)
        one, two, three = pieces(ctfh[:, cols])
        ctfrows[:, cols] = jnp.dot(
            onehot[...].astype(BF16),
            jnp.concatenate([one, two, three, one], axis=0),
            preferred_element_type=F32,
        )
        return carry


    def weigh(n):
        total = norms[...]
        wide = pl.ds(pl.multiple_of(n * 384, 384), 384)
        raw = [praw[0, :, wide], praw[1, :, wide]]
        ctfs = ctfh[:, wide]
        noises = [noise_ref[pl.ds(core * 32 + 3 * n + i, 1), :] for i in range(3)]
        counted = 1 - core * (1 - jnp.minimum(n, 1))
        noises[0] = noises[0] * counted.astype(F32)
        turned = []
        for i in range(3):
            tile = slice(i * LANES, (i + 1) * LANES)
            parts = [r[:, tile].astype(F32).reshape(2, 8, 1, 8, LANES) for r in raw]
            both = jnp.concatenate(parts, axis=2).reshape(2, 128, LANES)
            scaled = (both * noises[i][None]).astype(BF16)
            turned += [scaled[0].T, scaled[1].T]
            power = (both[0] * both[0] + both[1] * both[1]).T
            ctf = ctfs[:, tile]
            p1, p2, p3 = pieces(power)
            c1, c2, c3 = pieces(0.5 * ctf * ctf * noises[i])
            total = total + jnp.dot(
                jnp.concatenate([c1, c1, c1, c2, c2, c3], axis=1),
                jnp.concatenate([p1, p2, p3, p1, p2, p1], axis=0),
                preferred_element_type=F32,
            )
        weights[pl.ds(pl.multiple_of(n * 768, 768), 768), :] = jnp.concatenate(turned, axis=0)
        norms[...] = total

    cosine = trig_ref[0:8, :]
    sine = trig_ref[8:16, :]

    def prepare(b):
        meta = smeta[b].astype(F32)[0:8, :].astype(jnp.int32)

        def wave(steps):
            index = steps & (KY - 1)
            return (
                jnp.take_along_axis(cosine, index, axis=1),
                jnp.take_along_axis(sine, index, axis=1),
            )

        begin, one_row, two_rows = [], [], []
        for t in range(TRANS):
            sx = meta[:, 2 * t : 2 * t + 1]
            sy = meta[:, 2 * t + 1 : 2 * t + 2]
            slope = jnp.broadcast_to(sy - KX * sx, (8, LANES))
            begin.append(wave(lane * sx + top_row * slope))
            one_row.append(wave(slope))
            two_rows.append(wave(2 * slope))

        def body(n, phases):
            wide = pl.ds(pl.multiple_of(n * 384, 384), 384)
            blocks = gath[b, :, wide].astype(F32)
            ctfs = ctfrows[pl.ds(pl.multiple_of(b * 8, 8), 8), wide]
            singles = [vtab[3 * n + i] == 1 for i in range(3)]
            rows = [[], []]
            for i in range(3):
                tile = slice(i * LANES, (i + 1) * LANES)
                ctf = ctfs[:, tile]
                real, imag = blocks[0:8, tile] * ctf, blocks[8:16, tile] * ctf
                reals, imags, later = [], [], []
                for t in range(TRANS):
                    c, si = phases[t]
                    reals.append(real * c + imag * si)
                    imags.append(imag * c - real * si)
                    mc = jnp.where(singles[i], one_row[t][0], two_rows[t][0])
                    ms = jnp.where(singles[i], one_row[t][1], two_rows[t][1])
                    later.append((c * mc - si * ms, si * mc + c * ms))
                phases = tuple(later)
                for h in range(2):
                    for values in (reals, imags):
                        pair_ = jnp.concatenate(values[2 * h : 2 * h + 2], axis=0)
                        rows[h].append(pair_.astype(BF16))
            for h in range(2):
                at = pl.ds(pl.multiple_of(b * 32 + h * 16, 16), 16)
                prep[at, pl.ds(pl.multiple_of(n * 768, 768), 768)] = jnp.concatenate(
                    rows[h], axis=1
                )
            return phases

        lax.fori_loop(0, TILES // 3, body, tuple(begin), unroll=11)

    def score_group(g):
        rows = pl.ds(pl.multiple_of(g * 128, 128), 128)

        def body(i, total):
            cols = pl.ds(pl.multiple_of(i * 768, 768), 768)
            return total + jnp.dot(
                prep[rows, cols], weights[cols, :], preferred_element_type=F32
            )

        cross = lax.fori_loop(0, TILES // 3, body, jnp.zeros((128, 128), F32), unroll=11)
        picked = onehot[pl.ds(pl.multiple_of(g * 32, 32), 32), 0:LANES].reshape(4, 1, 8, LANES)
        picked = jnp.concatenate([picked] * TRANS, axis=1).reshape(128, LANES)
        norm = jnp.dot(picked[:, :64], norms[...], precision=HI, preferred_element_type=F32)
        score[g] = cross - norm

    packed = pick([sum(o << (2 * k) for k, o in enumerate(row)) for row in ORDERS])

    def order_at(q):
        return lax.shift_right_logical(packed, 2 * q) & 3

    def sc_copy(q):
        g = order_at(q)
        return send(score.at[g], pscore.at[g], sc_s.at[q], sc_r.at[q], peer)

    stats[own] = jnp.zeros((16, LANES), F32)

    def summarise(q):
        sc_copy(q).wait_recv()
        g = order_at(q)
        whole = (score[g] + pscore[g]).T
        pscore[g] = whole
        top = jnp.max(whole, axis=0, keepdims=True)
        stats[own, pl.ds(g, 1), :] = top
        stats[own, pl.ds(8 + g, 1), :] = jnp.sum(jnp.exp(whole - top), axis=0, keepdims=True)

    def arrive(q):
        z_right[q].wait_recv()
        launch(q)

    def forward(q):
        y_up[q].wait_recv()
        fwd_up[q].start()
        y_down[q].wait_recv()
        fwd_down[q].start()

    def know():
        for copy in meta_copies:
            copy.wait_recv()
        lane2 = lax.broadcasted_iota(jnp.int32, (8, 256), 1)

        def fill_onehot(b, carry):
            classes = smeta[b].astype(F32)[0:8, 8:9].astype(jnp.int32)
            hit = jnp.logical_and(lane2 % 64 == classes, lane2 < 192)
            onehot[pl.ds(pl.multiple_of(b * 8, 8), 8), :] = hit.astype(F32)
            return carry

        lax.fori_loop(0, BLOCKS, fill_onehot, 0)
        lax.fori_loop(0, 3, fill_ctf, 0)

    ctf_copy.wait()
    proj_copy.wait()
    praw_copy.wait_recv()
    norms[...] = jnp.zeros((64, 128), F32)

    def weighing(n, carry):
        @pl.when(n == 4)
        def _():
            know()
            arrive(1)
            forward(0)

        pl.when(n == 8)(lambda: arrive(2))
        weigh(n)
        return carry

    lax.fori_loop(0, TILES // 3, weighing, 0)

    def look_up(table, n):
        low, high = (sum(v << (2 * k) for k, v in enumerate(table[i : i + 8])) for i in (0, 8))
        return lax.shift_right_logical(low + (n // 8) * (high - low), 2 * (n % 8)) & 3

    def blocks(n, carry):
        q, ahead = look_up(STEP_OF, n), look_up(AHEAD_OF, n)
        pl.when(n == 1)(lambda: forward(1))
        pl.when(n == 3)(lambda: arrive(3))
        pl.when(n == 6)(lambda: forward(2))
        pl.when(n == 10)(lambda: forward(3))

        @pl.when(ahead == 2)
        def _():
            b = order_at(q) * 4 + y2
            low, high = gath.at[b, :, first], gath.at[b, :, second]
            send(low, low, fa_s.at[q], fa_r.at[q], up).wait_recv()
            send(high, high, fb_s.at[q], fb_r.at[q], down).wait_recv()

        prepare(order_at(q) * 4 + (y + ahead) % 4)

        @pl.when(ahead == 2)
        def _():
            score_group(order_at(q))
            sc_copy(q).start()
            pl.when(q >= 1)(lambda: summarise(q - 1))

        return carry

    lax.fori_loop(0, BLOCKS, blocks, 0)
    summarise(3)

    stat_copies = [
        send(stats.at[own], stats.at[own], stat_s.at[n], stat_r.at[n], target)
        for n, target in enumerate(others)
    ]
    for copy in stat_copies:
        copy.start()
    for copy in stat_copies:
        copy.wait_recv()
    tops = [stats[b, 0:8, :] for b in range(BLOCKS)]
    top = tops[0]
    for b in range(1, BLOCKS):
        top = jnp.maximum(top, tops[b])
    total = jnp.zeros((8, LANES), F32)
    for b in range(BLOCKS):
        total += stats[b, 8:16, :] * jnp.exp(tops[b] - top)
    held = lax.broadcasted_iota(jnp.int32, (8, LANES), 1) % 32

    def turn(value, by):
        inside = pltpu.roll(value, by, 1)
        wrapped = pltpu.roll(value, by + LANES - 32, 1)
        return jnp.where(held >= by, inside, wrapped)

    largest = jnp.maximum(top, turn(top, 8))
    largest = jnp.maximum(largest, turn(largest, 16))
    total = total * jnp.exp(top - largest)
    total = total + turn(total, 8)
    total = total + turn(total, 16)
    evidence = largest + jnp.log(total)
    for i in range(4):
        spot = jnp.logical_and(place == zl, lane == y * 32 + core * 4 + i)
        ev_ref[i] = jnp.sum(jnp.where(spot, evidence, 0.0))
    for g in range(4):
        post[:, g * 128 : (g + 1) * 128] = (
            jnp.exp(pscore[g] - evidence[g : g + 1, :]) * 2048.0
        ).astype(BF16)

    def copy_a(c):
        return send(part[c].at[2 * x2], from_a[c], a_s.at[c], a_r.at[c], right)

    def copy_b(c):
        return send(part[c].at[2 * x2 + 1], from_b[c], b_s.at[c], b_r.at[c], left)

    def copy_p(c):
        return send(part[c].at[pl.ds(2 * xp, 2)], from_p[c], p_s.at[c], p_r.at[c], right)

    def copy_m(c):
        return send(part[c].at[pl.ds(2 * xm, 2)], from_m[c], m_s.at[c], m_r.at[c], left)

    def copy_w(c, k):
        return send(
            zsend[c].at[k], zrecv[c].at[core], w_s.at[c, k], w_r.at[c, core], across[k]
        )

    def arrived_w(c, half):
        return send(zsend[c].at[0], zrecv[c].at[half], w_s.at[c, 0], w_r.at[c, half], across[0])

    def copy_f(c):
        other = pl.ds(pl.multiple_of((1 - core) * 8, 8), 8)
        return send(keep[c].at[other], fin[c], f_s.at[c], f_r.at[c], peer)

    def project(c):
        sums = jnp.dot(
            post[...], prep[:, STARTS[c] * 256 : STARTS[c + 1] * 256], preferred_element_type=F32
        ).astype(BF16)
        for i in range(8):
            part[c][i] = sums[16 * i : 16 * i + 16]
        copy_a(c).start()
        copy_b(c).start()

    def add(into, *others_):
        value = into.astype(F32)
        for other in others_:
            value = value + other.astype(F32)
        return value

    def pass_on(c):
        copy_a(c).wait_recv()
        part[c][2 * xp] = add(part[c][2 * xp], from_a[c][...]).astype(BF16)
        copy_p(c).start()
        copy_b(c).wait_recv()
        part[c][2 * xm + 1] = add(part[c][2 * xm + 1], from_b[c][...]).astype(BF16)
        copy_m(c).start()

    def collect(c):
        half = SIZES[c] * LANES
        copy_p(c).wait_recv()
        copy_m(c).wait_recv()
        far = 1 - zh
        away = add(part[c][2 * x + far], from_p[c][far], from_m[c][far])
        for k in range(2):
            rows = away[8 * k : 8 * k + 8]
            zsend[c][k] = jnp.concatenate([rows[:, :half], rows[:, half:]], axis=0).astype(BF16)
            copy_w(c, k).start()
        keep[c][...] = add(part[c][2 * x + zh], from_p[c][zh], from_m[c][zh])
        copy_f(c).start()

    def complete(c):
        for half in range(2):
            arrived_w(c, half).wait_recv()
        copy_f(c).wait_recv()
        here = keep[c][pl.ds(pl.multiple_of(core * 8, 8), 8), :]
        for half, near in ((core, here), (1 - core, fin[c][...])):
            rows = zrecv[c][half].astype(F32)
            value = near + jnp.concatenate([rows[0:8], rows[8:16]], axis=1)
            for s in range(SIZES[c]):
                at = pl.multiple_of(half * SHIFT + (STARTS[c] + s) * LANES, LANES)
                for k in range(2):
                    out_ref[:, k, pl.ds(at, LANES)] = value[
                        :, s * 256 + k * 128 : s * 256 + k * 128 + 128
                    ]

    for n in range(CHUNKS + 4):
        for lag, stage in ((0, project), (1, pass_on), (2, collect), (4, complete)):
            if 0 <= n - lag < CHUNKS:
                stage(n - lag)

    pmeta_copy.wait_send()
    pair_copy.wait_send()
    praw_copy.wait_send()
    for copy in meta_copies + stat_copies + [sc_copy(q) for q in range(4)] + y_up + y_down + fwd_up + fwd_down:
        copy.wait_send()
    for q in range(4):
        pl.when(goes_right[q])(lambda q=q: z_right[q].wait_send())
        pl.when(goes_left[q])(lambda q=q: z_left[q].wait_send())

    for c in range(CHUNKS):
        for copy in (copy_a, copy_b, copy_p, copy_m, copy_f):
            copy(c).wait_send()
        for k in range(2):
            copy_w(c, k).wait_send()


def per_device(images, projections, ctf_table, noise_weight, shifts, defocus):
    local = images.shape[0]
    pixels = images.shape[2]
    proj = projections.transpose(1, 0, 2).reshape(128, pixels)
    angles = np.arange(KY) * (2.0 * math.pi / KY)
    trig = np.concatenate([np.tile(np.cos(angles), (8, 1)), np.tile(np.sin(angles), (8, 1))])
    trig = jnp.asarray(trig.astype(np.float32))
    vmem = pl.BlockSpec(memory_space=pltpu.VMEM)
    hbm = pl.BlockSpec(memory_space=pl.ANY)
    smem = pl.BlockSpec(memory_space=pltpu.SMEM)
    dma = pltpu.SemaphoreType.DMA
    sems = [dma((2,)), dma((3,)), dma((3,)), dma((15,)), dma((15,)), dma((15,)), dma((15,))]
    sems += [dma((8,)), dma((4,))] + [dma((4,))] * 10 + [dma((CHUNKS,))] * 8 + [dma((CHUNKS, 2))] * 2 + [dma((CHUNKS,))] * 2
    sums, evidence = pl.pallas_call(
        kernel,
        out_shape=(
            jax.ShapeDtypeStruct((8, 2, pixels), F32),
            jax.ShapeDtypeStruct((local,), F32),
        ),
        in_specs=[vmem, hbm, hbm, vmem, vmem, smem, smem],
        out_specs=(vmem, smem),
        scratch_shapes=[
            pltpu.VMEM((16, 65 * LANES), BF16),
            pltpu.VMEM((16, LANES), BF16),
            pltpu.VMEM((16, HALF), BF16),
            pltpu.VMEM((16, LANES), BF16),
            pltpu.VMEM((BLOCKS, 16, LANES), BF16),
            pltpu.VMEM((BLOCKS, 16, HALF), BF16),
            pltpu.VMEM((2, 128, HALF), BF16),
            pltpu.VMEM((64, HALF), F32),
            pltpu.VMEM((2 * HALF, 128), BF16),
            pltpu.VMEM((64, 128), F32),
            pltpu.VMEM((128, 2 * LANES), F32),
            pltpu.VMEM((128, HALF), F32),
            pltpu.VMEM((TILES, 8, LANES), jnp.int32),
            pltpu.VMEM((BLOCKS * 32, 2 * HALF), BF16),
            pltpu.VMEM((4, 128, 128), F32),
            pltpu.VMEM((4, 128, 128), F32),
            pltpu.VMEM((BLOCKS, 16, LANES), F32),
            pltpu.VMEM((128, 512), BF16),
            [pltpu.VMEM((8, 16, 256 * t), BF16) for t in SIZES],
            [pltpu.VMEM((16, 256 * t), BF16) for t in SIZES],
            [pltpu.VMEM((16, 256 * t), BF16) for t in SIZES],
            [pltpu.VMEM((2, 16, 256 * t), BF16) for t in SIZES],
            [pltpu.VMEM((2, 16, 256 * t), BF16) for t in SIZES],
            [pltpu.VMEM((2, 16, 128 * t), BF16) for t in SIZES],
            [pltpu.VMEM((2, 16, 128 * t), BF16) for t in SIZES],
            [pltpu.VMEM((16, 256 * t), F32) for t in SIZES],
            [pltpu.VMEM((8, 256 * t), F32) for t in SIZES],
            *sems,
        ],
        compiler_params=pltpu.CompilerParams(
            collective_id=0, has_side_effects=True, vmem_limit_bytes=56 * 1024 * 1024
        ),
    )(
        images, proj, ctf_table, noise_weight.reshape(65, LANES), trig,
        shifts.transpose(0, 2, 1), defocus,
    )
    return evidence, sums


def solution(mesh):
    in_specs = (
        P(("img", "ori"), None, None),
        P("ori", None, None),
        P(),
        P(),
        P(("img", "ori"), None, None),
        P(("img", "ori")),
    )
    out_specs = (P(("img", "ori")), P(("ori", "img"), None, None))
    return jax.shard_map(
        per_device, mesh=mesh, in_specs=in_specs, out_specs=out_specs, check_vma=False
    )
```

```python
import math

import jax
import jax.numpy as jnp
import numpy as np
from jax import lax
from jax.experimental import pallas as pl
from jax.experimental.pallas import tpu as pltpu
from jax.sharding import PartitionSpec as P

KY = 128
KX = 65
LANES = 128
NX, NZ, NY = 4, 4, 4
BLOCKS = NZ * NY
TRANS = 4
TILES = 33
HALF = TILES * LANES
SHIFT = 32 * LANES
HALF_A = 17 * LANES
SIZES = (5, 7, 8, 8, 5)
STARTS = (0, 5, 12, 20, 28, 33)
CHUNKS = len(SIZES)
OTHERS = [(dz, dy) for dz in range(NZ) for dy in range(NY) if (dz, dy) != (0, 0)]
F32 = jnp.float32
BF16 = jnp.bfloat16
HI = lax.Precision.HIGHEST


def kernel(
    img_ref, proj_ref, ctf_ref, noise_ref, trig_ref, shift_ref, class_ref,
    out_ref, ev_ref,
    placed, ometa, pair, pmeta, smeta, gath, praw, ctfh, weights, norms, normrows, onehot, ctfrows, vtab, prep,
    score, pscore, stats, post, part, from_a, from_b, from_p, from_m, zsend, zrecv, keep, fin,
    loc_sem, core_s, core_r, meta_s, meta_r, stat_s, stat_r, z_s, z_r,
    yp_s, ym_s, yl_r, yr_r, fa_s, fb_s, fa_r, fb_r, sc_s, sc_r,
    a_s, b_s, a_r, b_r, p_s, m_s, p_r, m_r, w_s, w_r, f_s, f_r,
):
    img = lax.axis_index("img")
    ori = lax.axis_index("ori")
    x, zh = img // 2, img % 2
    core, y, zl = ori % 2, (ori // 2) % 4, ori // 8
    xp, xm, x2 = (x + 1) % 4, (x + 3) % 4, (x + 2) % 4
    yp, ym, y2 = (y + 1) % 4, (y + 3) % 4, (y + 2) % 4
    own = zl * 4 + y

    def dev(x_=x, zh_=zh, zl_=zl, y_=y, core_=core):
        return (x_ * 2 + zh_, (zl_ * 4 + y_) * 2 + core_)

    def send(src, dst, ss, rs, target):
        return pltpu.make_async_remote_copy(
            src_ref=src, dst_ref=dst, send_sem=ss, recv_sem=rs,
            device_id=target, device_id_type=pl.DeviceIdType.MESH,
        )

    peer = dev(core_=1 - core)
    others = [dev(zl_=(zl + dz) % 4, y_=(y + dy) % 4) for dz, dy in OTHERS]
    right, left = dev(x_=xp), dev(x_=xm)
    up, down = dev(y_=yp), dev(y_=ym)
    across = [dev(zh_=1 - zh, core_=k) for k in range(2)]

    barrier = pltpu.get_barrier_semaphore()
    greeted = [peer, *others, right, left, *across]
    for target in greeted:
        pl.semaphore_signal(barrier, inc=1, device_id=target, device_id_type=pl.DeviceIdType.MESH)

    mine = pl.ds(pl.multiple_of(core * SHIFT, LANES), HALF)
    theirs = pl.ds(pl.multiple_of((1 - core) * SHIFT, LANES), HALF)
    ctf_copy = pltpu.make_async_copy(ctf_ref.at[:, mine], ctfh, loc_sem.at[0])
    proj_copy = pltpu.make_async_copy(proj_ref.at[:, mine], praw.at[core], loc_sem.at[1])
    ctf_copy.start()
    proj_copy.start()

    lane = lax.broadcasted_iota(jnp.int32, (8, LANES), 1)
    place = lax.broadcasted_iota(jnp.int32, (8, LANES), 0)

    def lay_out(s, carry):
        cols = pl.ds(pl.multiple_of(s * 5 * LANES, LANES), 5 * LANES)
        at = lax.broadcasted_iota(jnp.int32, (8, 5 * LANES), 0)
        real = jnp.zeros((8, 5 * LANES), F32)
        imag = jnp.zeros((8, 5 * LANES), F32)
        for i in range(4):
            both = img_ref[i, :, cols].astype(F32)
            here = at == i + 4 * core
            real = jnp.where(here, both[0:1], real)
            imag = jnp.where(here, both[1:2], imag)
        placed[:, cols] = jnp.concatenate([real, imag], axis=0).astype(BF16)
        return carry

    lax.fori_loop(0, 13, lay_out, 0)
    meta = jnp.zeros((8, LANES), jnp.int32)
    for i in range(4):
        row = place == i + 4 * core
        for t in range(TRANS):
            for k in range(2):
                spot = jnp.logical_and(row, lane == 2 * t + k)
                meta = jnp.where(spot, shift_ref[i, k, t], meta)
        meta = jnp.where(jnp.logical_and(row, lane == 8), class_ref[i], meta)
    meta = meta.astype(F32)
    ometa[...] = jnp.concatenate([meta, jnp.zeros_like(meta)], axis=0).astype(BF16)

    pl.semaphore_wait(barrier, len(greeted))

    pair_copy = send(placed.at[:, theirs], pair, core_s.at[0], core_r.at[0], peer)
    pmeta_copy = send(ometa, pmeta, core_s.at[1], core_r.at[1], peer)
    praw_copy = send(proj_ref.at[:, theirs], praw.at[core], core_s.at[2], core_r.at[2], peer)
    pmeta_copy.start()
    pair_copy.start()
    praw_copy.start()

    pmeta_copy.wait_recv()
    smeta[own] = ometa[...] + pmeta[...]
    meta_copies = [
        send(smeta.at[own], smeta.at[own], meta_s.at[n], meta_r.at[n], target)
        for n, target in enumerate(others)
    ]
    for copy in meta_copies:
        copy.start()

    pair_copy.wait_recv()
    gath[own] = placed[:, mine] + pair[...]

    b0, b1 = zl % 2, zl // 2

    def pick(table):
        low = (1 - b0) * table[0] + b0 * table[1]
        high = (1 - b0) * table[2] + b0 * table[3]
        return (1 - b1) * low + b1 * high

    order = [zl, pick([1, 0, 3, 2]), pick([2, 2, 1, 1]), pick([3, 3, 0, 0])]

    def z_copy(zq, step, target):
        b = zq * 4 + y
        return send(gath.at[b], gath.at[b], z_s.at[step], z_r.at[zq], target)

    z_right = [z_copy(order[q], q, dev(zl_=zl + 1)) for q in range(4)]
    z_left = [z_copy(order[q], 4 + q, dev(zl_=zl - 1)) for q in range(4)]
    goes_right = [zl < 3] + [jnp.logical_and(order[q] < zl, zl < 3) for q in (1, 2, 3)]
    goes_left = [zl > 0] + [jnp.logical_and(order[q] > zl, zl > 0) for q in (1, 2, 3)]
    y_up = [
        send(gath.at[order[q] * 4 + y], gath.at[order[q] * 4 + y], yp_s.at[q], yl_r.at[q], up)
        for q in range(4)
    ]
    y_down = [
        send(gath.at[order[q] * 4 + y], gath.at[order[q] * 4 + y], ym_s.at[q], yr_r.at[q], down)
        for q in range(4)
    ]
    first, second = pl.ds(0, HALF_A), pl.ds(HALF_A, HALF - HALF_A)
    fwd_up, fwd_down = [], []
    for q in range(4):
        low = gath.at[order[q] * 4 + ym, :, first]
        high = gath.at[order[q] * 4 + yp, :, second]
        fwd_up.append(send(low, low, fa_s.at[q], fa_r.at[q], up))
        fwd_down.append(send(high, high, fb_s.at[q], fb_r.at[q], down))

    def launch(q):
        pl.when(goes_right[q])(lambda: z_right[q].start())
        pl.when(goes_left[q])(lambda: z_left[q].start())
        y_up[q].start()
        y_down[q].start()

    launch(0)

    def fill_rows(s, carry):
        p = (s + 32 * core) * LANES + lane
        after = lax.shift_right_logical((p + LANES) * 64528, 22)
        vtab[s] = after - lax.shift_right_logical(p * 64528, 22)
        return carry

    lax.fori_loop(0, TILES, fill_rows, 0)
    top_row = lax.shift_right_logical((32 * core * LANES + lane) * 64528, 22)

    def pieces(value):
        one = value.astype(BF16)
        rest = value - one.astype(F32)
        two = rest.astype(BF16)
        three = (rest - two.astype(F32)).astype(BF16)
        return one, two, three

    def fill_ctf(s, carry):
        cols = pl.ds(pl.multiple_of(s * 1408, 1408), 1408)
        one, two, three = pieces(ctfh[:, cols])
        ctfrows[:, cols] = jnp.dot(
            onehot[...].astype(BF16),
            jnp.concatenate([one, two, three, one], axis=0),
            preferred_element_type=F32,
        )
        return carry


    def weigh(n, total):
        wide = pl.ds(pl.multiple_of(n * 384, 384), 384)
        raw = [praw[0, :, wide], praw[1, :, wide]]
        ctfs = ctfh[:, wide]
        noises = [noise_ref[pl.ds(core * 32 + 3 * n + i, 1), :] for i in range(3)]
        counted = 1 - core * (1 - jnp.minimum(n, 1))
        noises[0] = noises[0] * counted.astype(F32)
        turned = []
        for i in range(3):
            tile = slice(i * LANES, (i + 1) * LANES)
            parts = [r[:, tile].astype(F32).reshape(2, 8, 1, 8, LANES) for r in raw]
            both = jnp.concatenate(parts, axis=2).reshape(2, 128, LANES)
            scaled = (both * noises[i][None]).astype(BF16)
            turned += [scaled[0].T, scaled[1].T]
            power = (both[0] * both[0] + both[1] * both[1]).T
            ctf = ctfs[:, tile]
            p1, p2, p3 = pieces(power)
            c1, c2, c3 = pieces(ctf * ctf * noises[i])
            total = total + jnp.dot(
                jnp.concatenate([c1, c1, c1, c2, c2, c3], axis=1),
                jnp.concatenate([p1, p2, p3, p1, p2, p1], axis=0),
                preferred_element_type=F32,
            )
        weights[pl.ds(pl.multiple_of(n * 768, 768), 768), :] = jnp.concatenate(turned, axis=0)
        return total

    cosine = trig_ref[0:8, :]
    sine = trig_ref[8:16, :]

    def prepare(b):
        meta = smeta[b].astype(F32)[0:8, :].astype(jnp.int32)

        def wave(steps):
            index = steps & (KY - 1)
            return (
                jnp.take_along_axis(cosine, index, axis=1),
                jnp.take_along_axis(sine, index, axis=1),
            )

        begin, one_row, two_rows = [], [], []
        for t in range(TRANS):
            sx = meta[:, 2 * t : 2 * t + 1]
            sy = meta[:, 2 * t + 1 : 2 * t + 2]
            slope = jnp.broadcast_to(sy - KX * sx, (8, LANES))
            begin.append(wave(lane * sx + top_row * slope))
            one_row.append(wave(slope))
            two_rows.append(wave(2 * slope))

        def body(n, carry):
            phases, total = carry
            wide = pl.ds(pl.multiple_of(n * 384, 384), 384)
            blocks = gath[b, :, wide].astype(F32)
            ctfs = ctfrows[pl.ds(pl.multiple_of(b * 8, 8), 8), wide]
            singles = [vtab[3 * n + i] == 1 for i in range(3)]
            rows = [[], []]
            for i in range(3):
                tile = slice(i * LANES, (i + 1) * LANES)
                ctf = ctfs[:, tile]
                real, imag = blocks[0:8, tile] * ctf, blocks[8:16, tile] * ctf
                reals, imags, later = [], [], []
                for t in range(TRANS):
                    c, si = phases[t]
                    reals.append(real * c + imag * si)
                    imags.append(imag * c - real * si)
                    mc = jnp.where(singles[i], one_row[t][0], two_rows[t][0])
                    ms = jnp.where(singles[i], one_row[t][1], two_rows[t][1])
                    later.append((c * mc - si * ms, si * mc + c * ms))
                phases = tuple(later)
                for h in range(2):
                    for values in (reals, imags):
                        pair_ = jnp.concatenate(values[2 * h : 2 * h + 2], axis=0)
                        rows[h].append(pair_.astype(BF16))
            steps = pl.ds(pl.multiple_of(n * 768, 768), 768)
            made = jnp.concatenate([jnp.concatenate(r, axis=1) for r in rows], axis=0)
            total = total + jnp.dot(made, weights[steps, :], preferred_element_type=F32)
            prep[pl.ds(pl.multiple_of(b * 32, 32), 32), steps] = made
            return phases, total

        start = (tuple(begin), jnp.zeros((32, LANES), F32))
        _, cross = lax.fori_loop(0, TILES // 3, body, start, unroll=11)
        norm = normrows[pl.ds(pl.multiple_of(b * 8, 8), 8), :]
        at = pl.ds(pl.multiple_of((b % 4) * 32, 32), 32)
        score[b // 4, at, :] = cross - jnp.concatenate([norm] * TRANS, axis=0)

    sc_copies = [
        send(score.at[order[q]], pscore.at[order[q]], sc_s.at[q], sc_r.at[q], peer)
        for q in range(4)
    ]

    stats[own] = jnp.zeros((16, LANES), F32)

    def summarise(q):
        sc_copies[q].wait_recv()
        g = order[q]
        whole = (score[g] + pscore[g]).T
        pscore[g] = whole
        top = jnp.max(whole, axis=0, keepdims=True)
        stats[own, pl.ds(g, 1), :] = top
        stats[own, pl.ds(8 + g, 1), :] = jnp.sum(jnp.exp(whole - top), axis=0, keepdims=True)

    def finish(q):
        fwd_up[q].wait_recv()
        fwd_down[q].wait_recv()
        prepare(order[q] * 4 + y2)
        sc_copies[q].start()

    def arrive(q):
        z_right[q].wait_recv()
        launch(q)

    def forward(q):
        y_up[q].wait_recv()
        fwd_up[q].start()
        y_down[q].wait_recv()
        fwd_down[q].start()

    def prepare_three(q):
        def three(i, carry):
            prepare(order[q] * 4 + (y + 3 + i) % 4)
            return carry

        lax.fori_loop(0, 3, three, 0)

    ctf_copy.wait()
    proj_copy.wait()
    praw_copy.wait_recv()
    half_norms = lax.fori_loop(0, 4, weigh, jnp.zeros((64, 128), F32))

    for copy in meta_copies:
        copy.wait_recv()

    lane2 = lax.broadcasted_iota(jnp.int32, (8, 256), 1)

    def fill_onehot(b, carry):
        classes = smeta[b].astype(F32)[0:8, 8:9].astype(jnp.int32)
        hit = jnp.logical_and(lane2 % 64 == classes, lane2 < 192)
        onehot[pl.ds(pl.multiple_of(b * 8, 8), 8), :] = hit.astype(F32)
        return carry

    lax.fori_loop(0, BLOCKS, fill_onehot, 0)
    lax.fori_loop(0, 3, fill_ctf, 0)

    arrive(1)
    forward(0)
    half_norms = lax.fori_loop(4, 11, weigh, half_norms)
    norms[...] = 0.5 * half_norms
    normrows[...] = jnp.dot(
        onehot[:, 0:64], norms[...], precision=HI, preferred_element_type=F32
    )
    arrive(2)
    prepare_three(0)
    forward(1)
    arrive(3)
    prepare_three(1)
    forward(2)
    finish(0)
    prepare_three(2)
    forward(3)
    finish(1)
    summarise(0)
    prepare_three(3)
    finish(2)
    summarise(1)
    finish(3)
    summarise(2)
    summarise(3)

    stat_copies = [
        send(stats.at[own], stats.at[own], stat_s.at[n], stat_r.at[n], target)
        for n, target in enumerate(others)
    ]
    for copy in stat_copies:
        copy.start()
    for copy in stat_copies:
        copy.wait_recv()
    tops = [stats[b, 0:8, :] for b in range(BLOCKS)]
    top = tops[0]
    for b in range(1, BLOCKS):
        top = jnp.maximum(top, tops[b])
    total = jnp.zeros((8, LANES), F32)
    for b in range(BLOCKS):
        total += stats[b, 8:16, :] * jnp.exp(tops[b] - top)
    held = lax.broadcasted_iota(jnp.int32, (8, LANES), 1) % 32

    def turn(value, by):
        inside = pltpu.roll(value, by, 1)
        wrapped = pltpu.roll(value, by + LANES - 32, 1)
        return jnp.where(held >= by, inside, wrapped)

    largest = jnp.maximum(top, turn(top, 8))
    largest = jnp.maximum(largest, turn(largest, 16))
    total = total * jnp.exp(top - largest)
    total = total + turn(total, 8)
    total = total + turn(total, 16)
    evidence = largest + jnp.log(total)
    for i in range(4):
        spot = jnp.logical_and(place == zl, lane == y * 32 + core * 4 + i)
        ev_ref[i] = jnp.sum(jnp.where(spot, evidence, 0.0))
    for g in range(4):
        post[:, g * 128 : (g + 1) * 128] = (
            jnp.exp(pscore[g] - evidence[g : g + 1, :]) * 2048.0
        ).astype(BF16)

    def copy_a(c):
        return send(part[c].at[2 * x2], from_a[c], a_s.at[c], a_r.at[c], right)

    def copy_b(c):
        return send(part[c].at[2 * x2 + 1], from_b[c], b_s.at[c], b_r.at[c], left)

    def copy_p(c):
        return send(part[c].at[pl.ds(2 * xp, 2)], from_p[c], p_s.at[c], p_r.at[c], right)

    def copy_m(c):
        return send(part[c].at[pl.ds(2 * xm, 2)], from_m[c], m_s.at[c], m_r.at[c], left)

    def copy_w(c, k):
        return send(
            zsend[c].at[k], zrecv[c].at[core], w_s.at[c, k], w_r.at[c, core], across[k]
        )

    def arrived_w(c, half):
        return send(zsend[c].at[0], zrecv[c].at[half], w_s.at[c, 0], w_r.at[c, half], across[0])

    def copy_f(c):
        other = pl.ds(pl.multiple_of((1 - core) * 8, 8), 8)
        return send(keep[c].at[other], fin[c], f_s.at[c], f_r.at[c], peer)

    def project(c):
        sums = jnp.dot(
            post[...], prep[:, STARTS[c] * 256 : STARTS[c + 1] * 256], preferred_element_type=F32
        ).astype(BF16)
        for i in range(8):
            part[c][i] = sums[16 * i : 16 * i + 16]
        copy_a(c).start()
        copy_b(c).start()

    def add(into, *others_):
        value = into.astype(F32)
        for other in others_:
            value = value + other.astype(F32)
        return value

    def pass_on(c):
        copy_a(c).wait_recv()
        part[c][2 * xp] = add(part[c][2 * xp], from_a[c][...]).astype(BF16)
        copy_p(c).start()
        copy_b(c).wait_recv()
        part[c][2 * xm + 1] = add(part[c][2 * xm + 1], from_b[c][...]).astype(BF16)
        copy_m(c).start()

    def collect(c):
        half = SIZES[c] * LANES
        copy_p(c).wait_recv()
        copy_m(c).wait_recv()
        far = 1 - zh
        away = add(part[c][2 * x + far], from_p[c][far], from_m[c][far])
        for k in range(2):
            rows = away[8 * k : 8 * k + 8]
            zsend[c][k] = jnp.concatenate([rows[:, :half], rows[:, half:]], axis=0).astype(BF16)
            copy_w(c, k).start()
        keep[c][...] = add(part[c][2 * x + zh], from_p[c][zh], from_m[c][zh])
        copy_f(c).start()

    def complete(c):
        for half in range(2):
            arrived_w(c, half).wait_recv()
        copy_f(c).wait_recv()
        here = keep[c][pl.ds(pl.multiple_of(core * 8, 8), 8), :]
        for half, near in ((core, here), (1 - core, fin[c][...])):
            rows = zrecv[c][half].astype(F32)
            value = near + jnp.concatenate([rows[0:8], rows[8:16]], axis=1)
            for s in range(SIZES[c]):
                at = pl.multiple_of(half * SHIFT + (STARTS[c] + s) * LANES, LANES)
                for k in range(2):
                    out_ref[:, k, pl.ds(at, LANES)] = value[
                        :, s * 256 + k * 128 : s * 256 + k * 128 + 128
                    ]

    for n in range(CHUNKS + 4):
        for lag, stage in ((0, project), (1, pass_on), (2, collect), (4, complete)):
            if 0 <= n - lag < CHUNKS:
                stage(n - lag)

    pmeta_copy.wait_send()
    pair_copy.wait_send()
    praw_copy.wait_send()
    for copy in meta_copies + stat_copies + sc_copies + y_up + y_down + fwd_up + fwd_down:
        copy.wait_send()
    for q in range(4):
        pl.when(goes_right[q])(lambda q=q: z_right[q].wait_send())
        pl.when(goes_left[q])(lambda q=q: z_left[q].wait_send())

    for c in range(CHUNKS):
        for copy in (copy_a, copy_b, copy_p, copy_m, copy_f):
            copy(c).wait_send()
        for k in range(2):
            copy_w(c, k).wait_send()


def per_device(images, projections, ctf_table, noise_weight, shifts, defocus):
    local = images.shape[0]
    pixels = images.shape[2]
    proj = projections.transpose(1, 0, 2).reshape(128, pixels)
    angles = np.arange(KY) * (2.0 * math.pi / KY)
    trig = np.concatenate([np.tile(np.cos(angles), (8, 1)), np.tile(np.sin(angles), (8, 1))])
    trig = jnp.asarray(trig.astype(np.float32))
    vmem = pl.BlockSpec(memory_space=pltpu.VMEM)
    hbm = pl.BlockSpec(memory_space=pl.ANY)
    smem = pl.BlockSpec(memory_space=pltpu.SMEM)
    dma = pltpu.SemaphoreType.DMA
    sems = [dma((2,)), dma((3,)), dma((3,)), dma((15,)), dma((15,)), dma((15,)), dma((15,))]
    sems += [dma((8,)), dma((4,))] + [dma((4,))] * 10 + [dma((CHUNKS,))] * 8 + [dma((CHUNKS, 2))] * 2 + [dma((CHUNKS,))] * 2
    sums, evidence = pl.pallas_call(
        kernel,
        out_shape=(
            jax.ShapeDtypeStruct((8, 2, pixels), F32),
            jax.ShapeDtypeStruct((local,), F32),
        ),
        in_specs=[vmem, hbm, hbm, vmem, vmem, smem, smem],
        out_specs=(vmem, smem),
        scratch_shapes=[
            pltpu.VMEM((16, 65 * LANES), BF16),
            pltpu.VMEM((16, LANES), BF16),
            pltpu.VMEM((16, HALF), BF16),
            pltpu.VMEM((16, LANES), BF16),
            pltpu.VMEM((BLOCKS, 16, LANES), BF16),
            pltpu.VMEM((BLOCKS, 16, HALF), BF16),
            pltpu.VMEM((2, 128, HALF), BF16),
            pltpu.VMEM((64, HALF), F32),
            pltpu.VMEM((2 * HALF, 128), BF16),
            pltpu.VMEM((64, 128), F32),
            pltpu.VMEM((128, 128), F32),
            pltpu.VMEM((128, 2 * LANES), F32),
            pltpu.VMEM((128, HALF), F32),
            pltpu.VMEM((TILES, 8, LANES), jnp.int32),
            pltpu.VMEM((BLOCKS * 32, 2 * HALF), BF16),
            pltpu.VMEM((4, 128, 128), F32),
            pltpu.VMEM((4, 128, 128), F32),
            pltpu.VMEM((BLOCKS, 16, LANES), F32),
            pltpu.VMEM((128, 512), BF16),
            [pltpu.VMEM((8, 16, 256 * t), BF16) for t in SIZES],
            [pltpu.VMEM((16, 256 * t), BF16) for t in SIZES],
            [pltpu.VMEM((16, 256 * t), BF16) for t in SIZES],
            [pltpu.VMEM((2, 16, 256 * t), BF16) for t in SIZES],
            [pltpu.VMEM((2, 16, 256 * t), BF16) for t in SIZES],
            [pltpu.VMEM((2, 16, 128 * t), BF16) for t in SIZES],
            [pltpu.VMEM((2, 16, 128 * t), BF16) for t in SIZES],
            [pltpu.VMEM((16, 256 * t), F32) for t in SIZES],
            [pltpu.VMEM((8, 256 * t), F32) for t in SIZES],
            *sems,
        ],
        compiler_params=pltpu.CompilerParams(
            collective_id=0, has_side_effects=True, vmem_limit_bytes=56 * 1024 * 1024
        ),
    )(
        images, proj, ctf_table, noise_weight.reshape(65, LANES), trig,
        shifts.transpose(0, 2, 1), defocus,
    )
    return evidence, sums


def solution(mesh):
    in_specs = (
        P(("img", "ori"), None, None),
        P("ori", None, None),
        P(),
        P(),
        P(("img", "ori"), None, None),
        P(("img", "ori")),
    )
    out_specs = (P(("img", "ori")), P(("ori", "img"), None, None))
    return jax.shard_map(
        per_device, mesh=mesh, in_specs=in_specs, out_specs=out_specs, check_vma=False
    )
```

```python
import math

import jax
import jax.numpy as jnp
import numpy as np
from jax import lax
from jax.experimental import pallas as pl
from jax.experimental.pallas import tpu as pltpu
from jax.sharding import PartitionSpec as P

KY = 128
KX = 65
LANES = 128
NX, NZ, NY = 4, 4, 4
BLOCKS = NZ * NY
TRANS = 4
TILES = 33
HALF = TILES * LANES
SHIFT = 32 * LANES
HALF_A = 17 * LANES
SIZES = (5, 7, 8, 8, 5)
STARTS = (0, 5, 12, 20, 28, 33)
CHUNKS = len(SIZES)
F32 = jnp.float32
BF16 = jnp.bfloat16
HI = lax.Precision.HIGHEST


def kernel(
    img_ref, proj_ref, ctf_ref, noise_ref, trig_ref, shift_ref, class_ref,
    out_ref, ev_ref,
    placed, ometa, pair, pmeta, smeta, gath, praw, ctfh, weights, norms, normrows, onehot, ctfrows, vtab, prep,
    score, pscore, stats, zstats, post, part, from_a, from_b, from_p, from_m, zsend, zrecv, keep, fin,
    loc_sem, core_s, core_r, meta_s, meta_r, stat_s, stat_r, z_s, z_r,
    yp_s, ym_s, yl_r, yr_r, fa_s, fb_s, fa_r, fb_r, sc_s, sc_r,
    a_s, b_s, a_r, b_r, p_s, m_s, p_r, m_r, w_s, w_r, f_s, f_r,
):
    img = lax.axis_index("img")
    ori = lax.axis_index("ori")
    x, zh = img // 2, img % 2
    core, y, zl = ori % 2, (ori // 2) % 4, ori // 8
    xp, xm, x2 = (x + 1) % 4, (x + 3) % 4, (x + 2) % 4
    yp, ym, y2 = (y + 1) % 4, (y + 3) % 4, (y + 2) % 4
    own = zl * 4 + y

    def dev(x_=x, zh_=zh, zl_=zl, y_=y, core_=core):
        return (x_ * 2 + zh_, (zl_ * 4 + y_) * 2 + core_)

    def send(src, dst, ss, rs, target):
        return pltpu.make_async_remote_copy(
            src_ref=src, dst_ref=dst, send_sem=ss, recv_sem=rs,
            device_id=target, device_id_type=pl.DeviceIdType.MESH,
        )

    peer = dev(core_=1 - core)
    along_y = [dev(y_=(y + d) % 4) for d in (1, 2, 3)]
    along_z = [dev(zl_=(zl + d) % 4) for d in (1, 2, 3)]
    right, left = dev(x_=xp), dev(x_=xm)
    up, down = dev(y_=yp), dev(y_=ym)
    across = [dev(zh_=1 - zh, core_=k) for k in range(2)]

    barrier = pltpu.get_barrier_semaphore()
    greeted = [peer, *along_y, *along_z, right, left, *across]
    for target in greeted:
        pl.semaphore_signal(barrier, inc=1, device_id=target, device_id_type=pl.DeviceIdType.MESH)

    mine = pl.ds(pl.multiple_of(core * SHIFT, LANES), HALF)
    theirs = pl.ds(pl.multiple_of((1 - core) * SHIFT, LANES), HALF)
    ctf_copy = pltpu.make_async_copy(ctf_ref.at[:, mine], ctfh, loc_sem.at[0])
    proj_copy = pltpu.make_async_copy(proj_ref.at[:, mine], praw.at[core], loc_sem.at[1])
    ctf_copy.start()
    proj_copy.start()

    lane = lax.broadcasted_iota(jnp.int32, (8, LANES), 1)
    place = lax.broadcasted_iota(jnp.int32, (8, LANES), 0)

    def lay_out(s, carry):
        cols = pl.ds(pl.multiple_of(s * 5 * LANES, LANES), 5 * LANES)
        at = lax.broadcasted_iota(jnp.int32, (8, 5 * LANES), 0)
        real = jnp.zeros((8, 5 * LANES), F32)
        imag = jnp.zeros((8, 5 * LANES), F32)
        for i in range(4):
            both = img_ref[i, :, cols].astype(F32)
            here = at == i + 4 * core
            real = jnp.where(here, both[0:1], real)
            imag = jnp.where(here, both[1:2], imag)
        placed[:, cols] = jnp.concatenate([real, imag], axis=0).astype(BF16)
        return carry

    lax.fori_loop(0, 13, lay_out, 0)
    meta = jnp.zeros((8, LANES), jnp.int32)
    for i in range(4):
        row = place == i + 4 * core
        for t in range(TRANS):
            for k in range(2):
                spot = jnp.logical_and(row, lane == 2 * t + k)
                meta = jnp.where(spot, shift_ref[i, k, t], meta)
        meta = jnp.where(jnp.logical_and(row, lane == 8), class_ref[i], meta)
    meta = meta.astype(F32)
    ometa[...] = jnp.concatenate([meta, jnp.zeros_like(meta)], axis=0).astype(BF16)

    pl.semaphore_wait(barrier, len(greeted))

    pair_copy = send(placed.at[:, theirs], pair, core_s.at[0], core_r.at[0], peer)
    pmeta_copy = send(ometa, pmeta, core_s.at[1], core_r.at[1], peer)
    praw_copy = send(proj_ref.at[:, theirs], praw.at[core], core_s.at[2], core_r.at[2], peer)
    pmeta_copy.start()
    pair_copy.start()
    praw_copy.start()

    pmeta_copy.wait_recv()
    smeta[own] = ometa[...] + pmeta[...]
    meta_y = [
        send(smeta.at[own], smeta.at[own], meta_s.at[n], meta_r.at[n], target)
        for n, target in enumerate(along_y)
    ]
    column = pl.ds(zl * 4, 4)
    meta_z = [
        send(smeta.at[column], smeta.at[column], meta_s.at[3 + n], meta_r.at[3 + n], target)
        for n, target in enumerate(along_z)
    ]
    for copy in meta_y:
        copy.start()

    pair_copy.wait_recv()
    gath[own] = placed[:, mine] + pair[...]

    b0, b1 = zl % 2, zl // 2

    def pick(table):
        low = (1 - b0) * table[0] + b0 * table[1]
        high = (1 - b0) * table[2] + b0 * table[3]
        return (1 - b1) * low + b1 * high

    order = [zl, pick([1, 0, 3, 2]), pick([2, 2, 1, 1]), pick([3, 3, 0, 0])]

    def z_copy(zq, step, target):
        b = zq * 4 + y
        return send(gath.at[b], gath.at[b], z_s.at[step], z_r.at[zq], target)

    z_right = [z_copy(order[q], q, dev(zl_=zl + 1)) for q in range(4)]
    z_left = [z_copy(order[q], 4 + q, dev(zl_=zl - 1)) for q in range(4)]
    goes_right = [zl < 3] + [jnp.logical_and(order[q] < zl, zl < 3) for q in (1, 2, 3)]
    goes_left = [zl > 0] + [jnp.logical_and(order[q] > zl, zl > 0) for q in (1, 2, 3)]
    y_up = [
        send(gath.at[order[q] * 4 + y], gath.at[order[q] * 4 + y], yp_s.at[q], yl_r.at[q], up)
        for q in range(4)
    ]
    y_down = [
        send(gath.at[order[q] * 4 + y], gath.at[order[q] * 4 + y], ym_s.at[q], yr_r.at[q], down)
        for q in range(4)
    ]
    first, second = pl.ds(0, HALF_A), pl.ds(HALF_A, HALF - HALF_A)
    fwd_up, fwd_down = [], []
    for q in range(4):
        low = gath.at[order[q] * 4 + ym, :, first]
        high = gath.at[order[q] * 4 + yp, :, second]
        fwd_up.append(send(low, low, fa_s.at[q], fa_r.at[q], up))
        fwd_down.append(send(high, high, fb_s.at[q], fb_r.at[q], down))

    def launch(q):
        pl.when(goes_right[q])(lambda: z_right[q].start())
        pl.when(goes_left[q])(lambda: z_left[q].start())
        y_up[q].start()
        y_down[q].start()

    launch(0)

    def fill_rows(s, carry):
        p = (s + 32 * core) * LANES + lane
        after = lax.shift_right_logical((p + LANES) * 64528, 22)
        vtab[s] = after - lax.shift_right_logical(p * 64528, 22)
        return carry

    lax.fori_loop(0, TILES, fill_rows, 0)
    top_row = lax.shift_right_logical((32 * core * LANES + lane) * 64528, 22)

    def pieces(value):
        one = value.astype(BF16)
        rest = value - one.astype(F32)
        two = rest.astype(BF16)
        three = (rest - two.astype(F32)).astype(BF16)
        return one, two, three

    def fill_ctf(s, carry):
        cols = pl.ds(pl.multiple_of(s * 1408, 1408), 1408)
        one, two, three = pieces(ctfh[:, cols])
        ctfrows[:, cols] = jnp.dot(
            onehot[...].astype(BF16),
            jnp.concatenate([one, two, three, one], axis=0),
            preferred_element_type=F32,
        )
        return carry


    def weigh(n, total):
        wide = pl.ds(pl.multiple_of(n * 384, 384), 384)
        raw = [praw[0, :, wide], praw[1, :, wide]]
        ctfs = ctfh[:, wide]
        noises = [noise_ref[pl.ds(core * 32 + 3 * n + i, 1), :] for i in range(3)]
        counted = 1 - core * (1 - jnp.minimum(n, 1))
        noises[0] = noises[0] * counted.astype(F32)
        turned = []
        for i in range(3):
            tile = slice(i * LANES, (i + 1) * LANES)
            parts = [r[:, tile].astype(F32).reshape(2, 8, 1, 8, LANES) for r in raw]
            both = jnp.concatenate(parts, axis=2).reshape(2, 128, LANES)
            scaled = (both * noises[i][None]).astype(BF16)
            turned += [scaled[0].T, scaled[1].T]
            power = (both[0] * both[0] + both[1] * both[1]).T
            ctf = ctfs[:, tile]
            p1, p2, p3 = pieces(power)
            c1, c2, c3 = pieces(ctf * ctf * noises[i])
            total = total + jnp.dot(
                jnp.concatenate([c1, c1, c1, c2, c2, c3], axis=1),
                jnp.concatenate([p1, p2, p3, p1, p2, p1], axis=0),
                preferred_element_type=F32,
            )
        weights[pl.ds(pl.multiple_of(n * 768, 768), 768), :] = jnp.concatenate(turned, axis=0)
        return total

    cosine = trig_ref[0:8, :]
    sine = trig_ref[8:16, :]

    def prepare(b):
        meta = smeta[b].astype(F32)[0:8, :].astype(jnp.int32)

        def wave(steps):
            index = steps & (KY - 1)
            return (
                jnp.take_along_axis(cosine, index, axis=1),
                jnp.take_along_axis(sine, index, axis=1),
            )

        begin, one_row, two_rows = [], [], []
        for t in range(TRANS):
            sx = meta[:, 2 * t : 2 * t + 1]
            sy = meta[:, 2 * t + 1 : 2 * t + 2]
            slope = jnp.broadcast_to(sy - KX * sx, (8, LANES))
            begin.append(wave(lane * sx + top_row * slope))
            one_row.append(wave(slope))
            two_rows.append(wave(2 * slope))

        def body(n, carry):
            phases, total = carry
            wide = pl.ds(pl.multiple_of(n * 384, 384), 384)
            blocks = gath[b, :, wide].astype(F32)
            ctfs = ctfrows[pl.ds(pl.multiple_of(b * 8, 8), 8), wide]
            singles = [vtab[3 * n + i] == 1 for i in range(3)]
            rows = [[], []]
            for i in range(3):
                tile = slice(i * LANES, (i + 1) * LANES)
                ctf = ctfs[:, tile]
                real, imag = blocks[0:8, tile] * ctf, blocks[8:16, tile] * ctf
                reals, imags, later = [], [], []
                for t in range(TRANS):
                    c, si = phases[t]
                    reals.append(real * c + imag * si)
                    imags.append(imag * c - real * si)
                    mc = jnp.where(singles[i], one_row[t][0], two_rows[t][0])
                    ms = jnp.where(singles[i], one_row[t][1], two_rows[t][1])
                    later.append((c * mc - si * ms, si * mc + c * ms))
                phases = tuple(later)
                for h in range(2):
                    for values in (reals, imags):
                        pair_ = jnp.concatenate(values[2 * h : 2 * h + 2], axis=0)
                        rows[h].append(pair_.astype(BF16))
            steps = pl.ds(pl.multiple_of(n * 768, 768), 768)
            made = jnp.concatenate([jnp.concatenate(r, axis=1) for r in rows], axis=0)
            total = total + jnp.dot(made, weights[steps, :], preferred_element_type=F32)
            prep[pl.ds(pl.multiple_of(b * 32, 32), 32), steps] = made
            return phases, total

        start = (tuple(begin), jnp.zeros((32, LANES), F32))
        _, cross = lax.fori_loop(0, TILES // 3, body, start, unroll=11)
        norm = normrows[pl.ds(pl.multiple_of(b * 8, 8), 8), :]
        at = pl.ds(pl.multiple_of((b % 4) * 32, 32), 32)
        score[b // 4, at, :] = cross - jnp.concatenate([norm] * TRANS, axis=0)

    sc_copies = [
        send(score.at[order[q]], pscore.at[order[q]], sc_s.at[q], sc_r.at[q], peer)
        for q in range(4)
    ]

    stats[own] = jnp.zeros((16, LANES), F32)

    def summarise(q):
        sc_copies[q].wait_recv()
        g = order[q]
        whole = (score[g] + pscore[g]).T
        pscore[g] = whole
        top = jnp.max(whole, axis=0, keepdims=True)
        stats[own, pl.ds(g, 1), :] = top
        stats[own, pl.ds(8 + g, 1), :] = jnp.sum(jnp.exp(whole - top), axis=0, keepdims=True)

    def finish(q):
        fwd_up[q].wait_recv()
        fwd_down[q].wait_recv()
        prepare(order[q] * 4 + y2)
        sc_copies[q].start()

    def arrive(q):
        z_right[q].wait_recv()
        launch(q)

    def forward(q):
        y_up[q].wait_recv()
        fwd_up[q].start()
        y_down[q].wait_recv()
        fwd_down[q].start()

    def prepare_three(q):
        def three(i, carry):
            prepare(order[q] * 4 + (y + 3 + i) % 4)
            return carry

        lax.fori_loop(0, 3, three, 0)

    for copy in meta_y:
        copy.wait_recv()
    for copy in meta_z:
        copy.start()
    ctf_copy.wait()
    proj_copy.wait()
    praw_copy.wait_recv()
    half_norms = lax.fori_loop(0, 4, weigh, jnp.zeros((64, 128), F32))

    for copy in meta_z:
        copy.wait_recv()

    lane2 = lax.broadcasted_iota(jnp.int32, (8, 256), 1)

    def fill_onehot(b, carry):
        classes = smeta[b].astype(F32)[0:8, 8:9].astype(jnp.int32)
        hit = jnp.logical_and(lane2 % 64 == classes, lane2 < 192)
        onehot[pl.ds(pl.multiple_of(b * 8, 8), 8), :] = hit.astype(F32)
        return carry

    lax.fori_loop(0, BLOCKS, fill_onehot, 0)
    lax.fori_loop(0, 3, fill_ctf, 0)

    arrive(1)
    forward(0)
    half_norms = lax.fori_loop(4, 11, weigh, half_norms)
    norms[...] = 0.5 * half_norms
    normrows[...] = jnp.dot(
        onehot[:, 0:64], norms[...], precision=HI, preferred_element_type=F32
    )
    arrive(2)
    prepare_three(0)
    forward(1)
    arrive(3)
    prepare_three(1)
    forward(2)
    finish(0)
    prepare_three(2)
    forward(3)
    finish(1)
    summarise(0)
    prepare_three(3)
    finish(2)
    summarise(1)
    finish(3)
    summarise(2)
    summarise(3)

    def merge(values):
        peak = values[0][0:8]
        for value in values[1:]:
            peak = jnp.maximum(peak, value[0:8])
        return peak, sum(value[8:16] * jnp.exp(value[0:8] - peak) for value in values)

    stat_y = [
        send(stats.at[own], stats.at[own], stat_s.at[n], stat_r.at[n], target)
        for n, target in enumerate(along_y)
    ]
    for copy in stat_y:
        copy.start()
    for copy in stat_y:
        copy.wait_recv()
    zstats[zl] = jnp.concatenate(merge([stats[zl * 4 + k] for k in range(4)]), axis=0)
    stat_z = [
        send(zstats.at[zl], zstats.at[zl], stat_s.at[3 + n], stat_r.at[3 + n], target)
        for n, target in enumerate(along_z)
    ]
    for copy in stat_z:
        copy.start()
    for copy in stat_z:
        copy.wait_recv()
    top, total = merge([zstats[k] for k in range(4)])
    held = lax.broadcasted_iota(jnp.int32, (8, LANES), 1) % 32

    def turn(value, by):
        inside = pltpu.roll(value, by, 1)
        wrapped = pltpu.roll(value, by + LANES - 32, 1)
        return jnp.where(held >= by, inside, wrapped)

    largest = jnp.maximum(top, turn(top, 8))
    largest = jnp.maximum(largest, turn(largest, 16))
    total = total * jnp.exp(top - largest)
    total = total + turn(total, 8)
    total = total + turn(total, 16)
    evidence = largest + jnp.log(total)
    for i in range(4):
        spot = jnp.logical_and(place == zl, lane == y * 32 + core * 4 + i)
        ev_ref[i] = jnp.sum(jnp.where(spot, evidence, 0.0))
    for g in range(4):
        post[:, g * 128 : (g + 1) * 128] = (
            jnp.exp(pscore[g] - evidence[g : g + 1, :]) * 2048.0
        ).astype(BF16)

    def copy_a(c):
        return send(part[c].at[2 * x2], from_a[c], a_s.at[c], a_r.at[c], right)

    def copy_b(c):
        return send(part[c].at[2 * x2 + 1], from_b[c], b_s.at[c], b_r.at[c], left)

    def copy_p(c):
        return send(part[c].at[pl.ds(2 * xp, 2)], from_p[c], p_s.at[c], p_r.at[c], right)

    def copy_m(c):
        return send(part[c].at[pl.ds(2 * xm, 2)], from_m[c], m_s.at[c], m_r.at[c], left)

    def copy_w(c, k):
        return send(
            zsend[c].at[k], zrecv[c].at[core], w_s.at[c, k], w_r.at[c, core], across[k]
        )

    def arrived_w(c, half):
        return send(zsend[c].at[0], zrecv[c].at[half], w_s.at[c, 0], w_r.at[c, half], across[0])

    def copy_f(c):
        other = pl.ds(pl.multiple_of((1 - core) * 8, 8), 8)
        return send(keep[c].at[other], fin[c], f_s.at[c], f_r.at[c], peer)

    def project(c):
        sums = jnp.dot(
            post[...], prep[:, STARTS[c] * 256 : STARTS[c + 1] * 256], preferred_element_type=F32
        ).astype(BF16)
        for i in range(8):
            part[c][i] = sums[16 * i : 16 * i + 16]
        copy_a(c).start()
        copy_b(c).start()

    def add(into, *others_):
        value = into.astype(F32)
        for other in others_:
            value = value + other.astype(F32)
        return value

    def pass_on(c):
        copy_a(c).wait_recv()
        part[c][2 * xp] = add(part[c][2 * xp], from_a[c][...]).astype(BF16)
        copy_p(c).start()
        copy_b(c).wait_recv()
        part[c][2 * xm + 1] = add(part[c][2 * xm + 1], from_b[c][...]).astype(BF16)
        copy_m(c).start()

    def collect(c):
        half = SIZES[c] * LANES
        copy_p(c).wait_recv()
        copy_m(c).wait_recv()
        far = 1 - zh
        away = add(part[c][2 * x + far], from_p[c][far], from_m[c][far])
        for k in range(2):
            rows = away[8 * k : 8 * k + 8]
            zsend[c][k] = jnp.concatenate([rows[:, :half], rows[:, half:]], axis=0).astype(BF16)
            copy_w(c, k).start()
        keep[c][...] = add(part[c][2 * x + zh], from_p[c][zh], from_m[c][zh])
        copy_f(c).start()

    def complete(c):
        for half in range(2):
            arrived_w(c, half).wait_recv()
        copy_f(c).wait_recv()
        here = keep[c][pl.ds(pl.multiple_of(core * 8, 8), 8), :]
        for half, near in ((core, here), (1 - core, fin[c][...])):
            rows = zrecv[c][half].astype(F32)
            value = near + jnp.concatenate([rows[0:8], rows[8:16]], axis=1)
            for s in range(SIZES[c]):
                at = pl.multiple_of(half * SHIFT + (STARTS[c] + s) * LANES, LANES)
                for k in range(2):
                    out_ref[:, k, pl.ds(at, LANES)] = value[
                        :, s * 256 + k * 128 : s * 256 + k * 128 + 128
                    ]

    for n in range(CHUNKS + 4):
        for lag, stage in ((0, project), (1, pass_on), (2, collect), (4, complete)):
            if 0 <= n - lag < CHUNKS:
                stage(n - lag)

    pmeta_copy.wait_send()
    pair_copy.wait_send()
    praw_copy.wait_send()
    for copy in meta_y + meta_z + stat_y + stat_z + sc_copies + y_up + y_down + fwd_up + fwd_down:
        copy.wait_send()
    for q in range(4):
        pl.when(goes_right[q])(lambda q=q: z_right[q].wait_send())
        pl.when(goes_left[q])(lambda q=q: z_left[q].wait_send())

    for c in range(CHUNKS):
        for copy in (copy_a, copy_b, copy_p, copy_m, copy_f):
            copy(c).wait_send()
        for k in range(2):
            copy_w(c, k).wait_send()


def per_device(images, projections, ctf_table, noise_weight, shifts, defocus):
    local = images.shape[0]
    pixels = images.shape[2]
    proj = projections.transpose(1, 0, 2).reshape(128, pixels)
    angles = np.arange(KY) * (2.0 * math.pi / KY)
    trig = np.concatenate([np.tile(np.cos(angles), (8, 1)), np.tile(np.sin(angles), (8, 1))])
    trig = jnp.asarray(trig.astype(np.float32))
    vmem = pl.BlockSpec(memory_space=pltpu.VMEM)
    hbm = pl.BlockSpec(memory_space=pl.ANY)
    smem = pl.BlockSpec(memory_space=pltpu.SMEM)
    dma = pltpu.SemaphoreType.DMA
    sems = [dma((2,)), dma((3,)), dma((3,)), dma((6,)), dma((6,)), dma((6,)), dma((6,))]
    sems += [dma((8,)), dma((4,))] + [dma((4,))] * 10 + [dma((CHUNKS,))] * 8 + [dma((CHUNKS, 2))] * 2 + [dma((CHUNKS,))] * 2
    sums, evidence = pl.pallas_call(
        kernel,
        out_shape=(
            jax.ShapeDtypeStruct((8, 2, pixels), F32),
            jax.ShapeDtypeStruct((local,), F32),
        ),
        in_specs=[vmem, hbm, hbm, vmem, vmem, smem, smem],
        out_specs=(vmem, smem),
        scratch_shapes=[
            pltpu.VMEM((16, 65 * LANES), BF16),
            pltpu.VMEM((16, LANES), BF16),
            pltpu.VMEM((16, HALF), BF16),
            pltpu.VMEM((16, LANES), BF16),
            pltpu.VMEM((BLOCKS, 16, LANES), BF16),
            pltpu.VMEM((BLOCKS, 16, HALF), BF16),
            pltpu.VMEM((2, 128, HALF), BF16),
            pltpu.VMEM((64, HALF), F32),
            pltpu.VMEM((2 * HALF, 128), BF16),
            pltpu.VMEM((64, 128), F32),
            pltpu.VMEM((128, 128), F32),
            pltpu.VMEM((128, 2 * LANES), F32),
            pltpu.VMEM((128, HALF), F32),
            pltpu.VMEM((TILES, 8, LANES), jnp.int32),
            pltpu.VMEM((BLOCKS * 32, 2 * HALF), BF16),
            pltpu.VMEM((4, 128, 128), F32),
            pltpu.VMEM((4, 128, 128), F32),
            pltpu.VMEM((BLOCKS, 16, LANES), F32),
            pltpu.VMEM((NZ, 16, LANES), F32),
            pltpu.VMEM((128, 512), BF16),
            [pltpu.VMEM((8, 16, 256 * t), BF16) for t in SIZES],
            [pltpu.VMEM((16, 256 * t), BF16) for t in SIZES],
            [pltpu.VMEM((16, 256 * t), BF16) for t in SIZES],
            [pltpu.VMEM((2, 16, 256 * t), BF16) for t in SIZES],
            [pltpu.VMEM((2, 16, 256 * t), BF16) for t in SIZES],
            [pltpu.VMEM((2, 16, 128 * t), BF16) for t in SIZES],
            [pltpu.VMEM((2, 16, 128 * t), BF16) for t in SIZES],
            [pltpu.VMEM((16, 256 * t), F32) for t in SIZES],
            [pltpu.VMEM((8, 256 * t), F32) for t in SIZES],
            *sems,
        ],
        compiler_params=pltpu.CompilerParams(
            collective_id=0, has_side_effects=True, vmem_limit_bytes=56 * 1024 * 1024
        ),
    )(
        images, proj, ctf_table, noise_weight.reshape(65, LANES), trig,
        shifts.transpose(0, 2, 1), defocus,
    )
    return evidence, sums


def solution(mesh):
    in_specs = (
        P(("img", "ori"), None, None),
        P("ori", None, None),
        P(),
        P(),
        P(("img", "ori"), None, None),
        P(("img", "ori")),
    )
    out_specs = (P(("img", "ori")), P(("ori", "img"), None, None))
    return jax.shard_map(
        per_device, mesh=mesh, in_specs=in_specs, out_specs=out_specs, check_vma=False
    )
```

```python
import math

import jax
import jax.numpy as jnp
import numpy as np
from jax import lax
from jax.experimental import pallas as pl
from jax.experimental.pallas import tpu as pltpu
from jax.sharding import PartitionSpec as P

KY = 128
KX = 65
LANES = 128
NX, NZ, NY = 4, 4, 4
BLOCKS = NZ * NY
TRANS = 4
TILES = 33
HALF = TILES * LANES
SHIFT = 32 * LANES
HALF_A = 17 * LANES
SIZES = (5, 7, 8, 8, 5)
STARTS = (0, 5, 12, 20, 28, 33)
CHUNKS = len(SIZES)
OTHERS = [(dz, dy) for dz in range(NZ) for dy in range(NY) if (dz, dy) != (0, 0)]
F32 = jnp.float32
BF16 = jnp.bfloat16
HI = lax.Precision.HIGHEST


def kernel(
    img_ref, proj_ref, ctf_ref, noise_ref, trig_ref, shift_ref, class_ref,
    out_ref, ev_ref,
    placed, ometa, pair, pmeta, smeta, gath, praw, ctfh, weights, norms, normrows, onehot, ctfrows, vtab, prep,
    score, pscore, stats, post, part, from_a, from_b, from_p, from_m, zsend, zrecv, keep, fin,
    loc_sem, core_s, core_r, meta_s, meta_r, stat_s, stat_r, z_s, z_r,
    yp_s, ym_s, yl_r, yr_r, fa_s, fb_s, fa_r, fb_r, sc_s, sc_r,
    a_s, b_s, a_r, b_r, p_s, m_s, p_r, m_r, w_s, w_r, f_s, f_r,
):
    img = lax.axis_index("img")
    ori = lax.axis_index("ori")
    x, zh = img // 2, img % 2
    core, y, zl = ori % 2, (ori // 2) % 4, ori // 8
    xp, xm, x2 = (x + 1) % 4, (x + 3) % 4, (x + 2) % 4
    yp, ym, y2 = (y + 1) % 4, (y + 3) % 4, (y + 2) % 4
    own = zl * 4 + y

    def dev(x_=x, zh_=zh, zl_=zl, y_=y, core_=core):
        return (x_ * 2 + zh_, (zl_ * 4 + y_) * 2 + core_)

    def send(src, dst, ss, rs, target):
        return pltpu.make_async_remote_copy(
            src_ref=src, dst_ref=dst, send_sem=ss, recv_sem=rs,
            device_id=target, device_id_type=pl.DeviceIdType.MESH,
        )

    peer = dev(core_=1 - core)
    others = [dev(zl_=(zl + dz) % 4, y_=(y + dy) % 4) for dz, dy in OTHERS]
    right, left = dev(x_=xp), dev(x_=xm)
    up, down = dev(y_=yp), dev(y_=ym)
    across = [dev(zh_=1 - zh, core_=k) for k in range(2)]

    barrier = pltpu.get_barrier_semaphore()
    greeted = [peer, *others, right, left, *across]
    for target in greeted:
        pl.semaphore_signal(barrier, inc=1, device_id=target, device_id_type=pl.DeviceIdType.MESH)

    mine = pl.ds(pl.multiple_of(core * SHIFT, LANES), HALF)
    theirs = pl.ds(pl.multiple_of((1 - core) * SHIFT, LANES), HALF)
    ctf_copy = pltpu.make_async_copy(ctf_ref.at[:, mine], ctfh, loc_sem.at[0])
    proj_copy = pltpu.make_async_copy(proj_ref.at[:, mine], praw.at[core], loc_sem.at[1])
    ctf_copy.start()
    proj_copy.start()

    lane = lax.broadcasted_iota(jnp.int32, (8, LANES), 1)
    place = lax.broadcasted_iota(jnp.int32, (8, LANES), 0)

    def lay_out(s, carry):
        cols = pl.ds(pl.multiple_of(s * 5 * LANES, LANES), 5 * LANES)
        at = lax.broadcasted_iota(jnp.int32, (8, 5 * LANES), 0)
        real = jnp.zeros((8, 5 * LANES), F32)
        imag = jnp.zeros((8, 5 * LANES), F32)
        for i in range(4):
            both = img_ref[i, :, cols].astype(F32)
            here = at == i + 4 * core
            real = jnp.where(here, both[0:1], real)
            imag = jnp.where(here, both[1:2], imag)
        placed[:, cols] = jnp.concatenate([real, imag], axis=0).astype(BF16)
        return carry

    lax.fori_loop(0, 13, lay_out, 0)
    meta = jnp.zeros((8, LANES), jnp.int32)
    for i in range(4):
        row = place == i + 4 * core
        for t in range(TRANS):
            for k in range(2):
                spot = jnp.logical_and(row, lane == 2 * t + k)
                meta = jnp.where(spot, shift_ref[i, k, t], meta)
        meta = jnp.where(jnp.logical_and(row, lane == 8), class_ref[i], meta)
    meta = meta.astype(F32)
    ometa[...] = jnp.concatenate([meta, jnp.zeros_like(meta)], axis=0).astype(BF16)

    pl.semaphore_wait(barrier, len(greeted))

    pair_copy = send(placed.at[:, theirs], pair, core_s.at[0], core_r.at[0], peer)
    pmeta_copy = send(ometa, pmeta, core_s.at[1], core_r.at[1], peer)
    praw_copy = send(proj_ref.at[:, theirs], praw.at[core], core_s.at[2], core_r.at[2], peer)
    pmeta_copy.start()
    pair_copy.start()
    praw_copy.start()

    pmeta_copy.wait_recv()
    smeta[own] = ometa[...] + pmeta[...]
    meta_copies = [
        send(smeta.at[own], smeta.at[own], meta_s.at[n], meta_r.at[n], target)
        for n, target in enumerate(others)
    ]
    for copy in meta_copies:
        copy.start()

    pair_copy.wait_recv()
    gath[own] = placed[:, mine] + pair[...]

    b0, b1 = zl % 2, zl // 2

    def pick(table):
        low = (1 - b0) * table[0] + b0 * table[1]
        high = (1 - b0) * table[2] + b0 * table[3]
        return (1 - b1) * low + b1 * high

    order = [zl, pick([1, 0, 3, 2]), pick([2, 2, 1, 1]), pick([3, 3, 0, 0])]

    def z_copy(zq, step, target):
        b = zq * 4 + y
        return send(gath.at[b], gath.at[b], z_s.at[step], z_r.at[zq], target)

    z_right = [z_copy(order[q], q, dev(zl_=zl + 1)) for q in range(4)]
    z_left = [z_copy(order[q], 4 + q, dev(zl_=zl - 1)) for q in range(4)]
    goes_right = [zl < 3] + [jnp.logical_and(order[q] < zl, zl < 3) for q in (1, 2, 3)]
    goes_left = [zl > 0] + [jnp.logical_and(order[q] > zl, zl > 0) for q in (1, 2, 3)]
    y_up = [
        send(gath.at[order[q] * 4 + y], gath.at[order[q] * 4 + y], yp_s.at[q], yl_r.at[q], up)
        for q in range(4)
    ]
    y_down = [
        send(gath.at[order[q] * 4 + y], gath.at[order[q] * 4 + y], ym_s.at[q], yr_r.at[q], down)
        for q in range(4)
    ]
    first, second = pl.ds(0, HALF_A), pl.ds(HALF_A, HALF - HALF_A)
    fwd_up, fwd_down = [], []
    for q in range(4):
        low = gath.at[order[q] * 4 + ym, :, first]
        high = gath.at[order[q] * 4 + yp, :, second]
        fwd_up.append(send(low, low, fa_s.at[q], fa_r.at[q], up))
        fwd_down.append(send(high, high, fb_s.at[q], fb_r.at[q], down))

    def launch(q):
        pl.when(goes_right[q])(lambda: z_right[q].start())
        pl.when(goes_left[q])(lambda: z_left[q].start())
        y_up[q].start()
        y_down[q].start()

    launch(0)

    def fill_rows(s, carry):
        p = (s + 32 * core) * LANES + lane
        after = lax.shift_right_logical((p + LANES) * 64528, 22)
        vtab[s] = after - lax.shift_right_logical(p * 64528, 22)
        return carry

    lax.fori_loop(0, TILES, fill_rows, 0)
    top_row = lax.shift_right_logical((32 * core * LANES + lane) * 64528, 22)

    def pieces(value):
        one = value.astype(BF16)
        rest = value - one.astype(F32)
        two = rest.astype(BF16)
        three = (rest - two.astype(F32)).astype(BF16)
        return one, two, three

    def fill_ctf(s, carry):
        cols = pl.ds(pl.multiple_of(s * 1408, 1408), 1408)
        one, two, three = pieces(ctfh[:, cols])
        ctfrows[:, cols] = jnp.dot(
            onehot[...].astype(BF16),
            jnp.concatenate([one, two, three, one], axis=0),
            preferred_element_type=F32,
        )
        return carry


    def weigh(n, total):
        wide = pl.ds(pl.multiple_of(n * 384, 384), 384)
        raw = [praw[0, :, wide], praw[1, :, wide]]
        ctfs = ctfh[:, wide]
        noises = [noise_ref[pl.ds(core * 32 + 3 * n + i, 1), :] for i in range(3)]
        counted = 1 - core * (1 - jnp.minimum(n, 1))
        noises[0] = noises[0] * counted.astype(F32)
        turned = []
        for i in range(3):
            tile = slice(i * LANES, (i + 1) * LANES)
            parts = [r[:, tile].astype(F32).reshape(2, 8, 1, 8, LANES) for r in raw]
            both = jnp.concatenate(parts, axis=2).reshape(2, 128, LANES)
            scaled = (both * noises[i][None]).astype(BF16)
            turned += [scaled[0].T, scaled[1].T]
            power = (both[0] * both[0] + both[1] * both[1]).T
            ctf = ctfs[:, tile]
            p1, p2, p3 = pieces(power)
            c1, c2, c3 = pieces(ctf * ctf * noises[i])
            total = total + jnp.dot(
                jnp.concatenate([c1, c1, c1, c2, c2, c3], axis=1),
                jnp.concatenate([p1, p2, p3, p1, p2, p1], axis=0),
                preferred_element_type=F32,
            )
        weights[pl.ds(pl.multiple_of(n * 768, 768), 768), :] = jnp.concatenate(turned, axis=0)
        return total

    cosine = trig_ref[0:8, :]
    sine = trig_ref[8:16, :]

    def prepare(b):
        meta = smeta[b].astype(F32)[0:8, :].astype(jnp.int32)

        def wave(steps):
            index = steps & (KY - 1)
            return (
                jnp.take_along_axis(cosine, index, axis=1),
                jnp.take_along_axis(sine, index, axis=1),
            )

        begin, one_row, two_rows = [], [], []
        for t in range(TRANS):
            sx = meta[:, 2 * t : 2 * t + 1]
            sy = meta[:, 2 * t + 1 : 2 * t + 2]
            slope = jnp.broadcast_to(sy - KX * sx, (8, LANES))
            begin.append(wave(lane * sx + top_row * slope))
            one_row.append(wave(slope))
            two_rows.append(wave(2 * slope))

        def body(n, carry):
            phases, total = carry
            wide = pl.ds(pl.multiple_of(n * 384, 384), 384)
            blocks = gath[b, :, wide].astype(F32)
            ctfs = ctfrows[pl.ds(pl.multiple_of(b * 8, 8), 8), wide]
            singles = [vtab[3 * n + i] == 1 for i in range(3)]
            rows = [[], []]
            for i in range(3):
                tile = slice(i * LANES, (i + 1) * LANES)
                ctf = ctfs[:, tile]
                real, imag = blocks[0:8, tile] * ctf, blocks[8:16, tile] * ctf
                reals, imags, later = [], [], []
                for t in range(TRANS):
                    c, si = phases[t]
                    reals.append(real * c + imag * si)
                    imags.append(imag * c - real * si)
                    mc = jnp.where(singles[i], one_row[t][0], two_rows[t][0])
                    ms = jnp.where(singles[i], one_row[t][1], two_rows[t][1])
                    later.append((c * mc - si * ms, si * mc + c * ms))
                phases = tuple(later)
                for h in range(2):
                    for values in (reals, imags):
                        pair_ = jnp.concatenate(values[2 * h : 2 * h + 2], axis=0)
                        rows[h].append(pair_.astype(BF16))
            steps = pl.ds(pl.multiple_of(n * 768, 768), 768)
            made = jnp.concatenate([jnp.concatenate(r, axis=1) for r in rows], axis=0)
            total = total + jnp.dot(made, weights[steps, :], preferred_element_type=F32)
            prep[pl.ds(pl.multiple_of(b * 32, 32), 32), steps] = made
            return phases, total

        start = (tuple(begin), jnp.zeros((32, LANES), F32))
        _, cross = lax.fori_loop(0, TILES // 3, body, start, unroll=11)
        norm = normrows[pl.ds(pl.multiple_of(b * 8, 8), 8), :]
        at = pl.ds(pl.multiple_of((b % 4) * 32, 32), 32)
        score[b // 4, at, :] = cross - jnp.concatenate([norm] * TRANS, axis=0)

    sc_copies = [
        send(score.at[order[q]], pscore.at[order[q]], sc_s.at[q], sc_r.at[q], peer)
        for q in range(4)
    ]

    stats[own] = jnp.zeros((16, LANES), F32)

    def summarise(q):
        sc_copies[q].wait_recv()
        g = order[q]
        whole = (score[g] + pscore[g]).T
        pscore[g] = whole
        top = jnp.max(whole, axis=0, keepdims=True)
        stats[own, pl.ds(g, 1), :] = top
        stats[own, pl.ds(8 + g, 1), :] = jnp.sum(jnp.exp(whole - top), axis=0, keepdims=True)

    def finish(q):
        fwd_up[q].wait_recv()
        fwd_down[q].wait_recv()
        prepare(order[q] * 4 + y2)
        sc_copies[q].start()

    def arrive(q):
        z_right[q].wait_recv()
        launch(q)

    def forward(q):
        y_up[q].wait_recv()
        fwd_up[q].start()
        y_down[q].wait_recv()
        fwd_down[q].start()

    def prepare_three(q):
        def three(i, carry):
            prepare(order[q] * 4 + (y + 3 + i) % 4)
            return carry

        lax.fori_loop(0, 3, three, 0)

    ctf_copy.wait()
    proj_copy.wait()
    praw_copy.wait_recv()
    half_norms = lax.fori_loop(0, 4, weigh, jnp.zeros((64, 128), F32))

    for copy in meta_copies:
        copy.wait_recv()

    lane2 = lax.broadcasted_iota(jnp.int32, (8, 256), 1)

    def fill_onehot(b, carry):
        classes = smeta[b].astype(F32)[0:8, 8:9].astype(jnp.int32)
        hit = jnp.logical_and(lane2 % 64 == classes, lane2 < 192)
        onehot[pl.ds(pl.multiple_of(b * 8, 8), 8), :] = hit.astype(F32)
        return carry

    lax.fori_loop(0, BLOCKS, fill_onehot, 0)
    lax.fori_loop(0, 3, fill_ctf, 0)

    arrive(1)
    forward(0)
    half_norms = lax.fori_loop(4, 11, weigh, half_norms)
    norms[...] = 0.5 * half_norms
    normrows[...] = jnp.dot(
        onehot[:, 0:64], norms[...], precision=HI, preferred_element_type=F32
    )
    arrive(2)
    prepare_three(0)
    forward(1)
    arrive(3)
    prepare_three(1)
    forward(2)
    finish(0)
    prepare_three(2)
    forward(3)
    finish(1)
    summarise(0)
    prepare_three(3)
    finish(2)
    summarise(1)
    finish(3)
    summarise(2)
    summarise(3)

    stat_copies = [
        send(stats.at[own], stats.at[own], stat_s.at[n], stat_r.at[n], target)
        for n, target in enumerate(others)
    ]
    for copy in stat_copies:
        copy.start()
    for copy in stat_copies:
        copy.wait_recv()
    tops = [stats[b, 0:8, :] for b in range(BLOCKS)]
    top = tops[0]
    for b in range(1, BLOCKS):
        top = jnp.maximum(top, tops[b])
    total = jnp.zeros((8, LANES), F32)
    for b in range(BLOCKS):
        total += stats[b, 8:16, :] * jnp.exp(tops[b] - top)
    held = lax.broadcasted_iota(jnp.int32, (8, LANES), 1) % 32

    def turn(value, by):
        inside = pltpu.roll(value, by, 1)
        wrapped = pltpu.roll(value, by + LANES - 32, 1)
        return jnp.where(held >= by, inside, wrapped)

    largest = jnp.maximum(top, turn(top, 8))
    largest = jnp.maximum(largest, turn(largest, 16))
    total = total * jnp.exp(top - largest)
    total = total + turn(total, 8)
    total = total + turn(total, 16)
    evidence = largest + jnp.log(total)
    for i in range(4):
        spot = jnp.logical_and(place == zl, lane == y * 32 + core * 4 + i)
        ev_ref[i] = jnp.sum(jnp.where(spot, evidence, 0.0))
    for g in range(4):
        post[:, g * 128 : (g + 1) * 128] = (
            jnp.exp(pscore[g] - evidence[g : g + 1, :]) * 2048.0
        ).astype(BF16)

    def copy_a(c):
        return send(part[c].at[2 * x2], from_a[c], a_s.at[c], a_r.at[c], right)

    def copy_b(c):
        return send(part[c].at[2 * x2 + 1], from_b[c], b_s.at[c], b_r.at[c], left)

    def copy_p(c):
        return send(part[c].at[pl.ds(2 * xp, 2)], from_p[c], p_s.at[c], p_r.at[c], right)

    def copy_m(c):
        return send(part[c].at[pl.ds(2 * xm, 2)], from_m[c], m_s.at[c], m_r.at[c], left)

    def copy_w(c, k):
        return send(
            zsend[c].at[k], zrecv[c].at[core], w_s.at[c, k], w_r.at[c, core], across[k]
        )

    def arrived_w(c, half):
        return send(zsend[c].at[0], zrecv[c].at[half], w_s.at[c, 0], w_r.at[c, half], across[0])

    def copy_f(c):
        other = pl.ds(pl.multiple_of((1 - core) * 8, 8), 8)
        return send(keep[c].at[other], fin[c], f_s.at[c], f_r.at[c], peer)

    def project(c):
        sums = jnp.dot(
            post[...], prep[:, STARTS[c] * 256 : STARTS[c + 1] * 256], preferred_element_type=F32
        ).astype(BF16)
        for i in range(8):
            part[c][i] = sums[16 * i : 16 * i + 16]
        copy_a(c).start()
        copy_b(c).start()

    def add(into, *others_):
        value = into.astype(F32)
        for other in others_:
            value = value + other.astype(F32)
        return value

    def pass_on(c):
        copy_a(c).wait_recv()
        part[c][2 * xp] = add(part[c][2 * xp], from_a[c][...]).astype(BF16)
        copy_p(c).start()
        copy_b(c).wait_recv()
        part[c][2 * xm + 1] = add(part[c][2 * xm + 1], from_b[c][...]).astype(BF16)
        copy_m(c).start()

    def collect(c):
        half = SIZES[c] * LANES
        copy_p(c).wait_recv()
        copy_m(c).wait_recv()
        far = 1 - zh
        away = add(part[c][2 * x + far], from_p[c][far], from_m[c][far])
        for k in range(2):
            rows = away[8 * k : 8 * k + 8]
            zsend[c][k] = jnp.concatenate([rows[:, :half], rows[:, half:]], axis=0).astype(BF16)
            copy_w(c, k).start()
        keep[c][...] = add(part[c][2 * x + zh], from_p[c][zh], from_m[c][zh])
        copy_f(c).start()

    def complete(c):
        for half in range(2):
            arrived_w(c, half).wait_recv()
        copy_f(c).wait_recv()
        here = keep[c][pl.ds(pl.multiple_of(core * 8, 8), 8), :]
        for half, near in ((core, here), (1 - core, fin[c][...])):
            rows = zrecv[c][half].astype(F32)
            value = near + jnp.concatenate([rows[0:8], rows[8:16]], axis=1)
            for s in range(SIZES[c]):
                at = pl.multiple_of(half * SHIFT + (STARTS[c] + s) * LANES, LANES)
                for k in range(2):
                    out_ref[:, k, pl.ds(at, LANES)] = value[
                        :, s * 256 + k * 128 : s * 256 + k * 128 + 128
                    ]

    for c in range(CHUNKS):
        project(c)
    for c in range(CHUNKS):
        pass_on(c)
    for c in range(CHUNKS):
        collect(c)
        if c >= 2:
            complete(c - 2)
    complete(CHUNKS - 2)
    complete(CHUNKS - 1)

    pmeta_copy.wait_send()
    pair_copy.wait_send()
    praw_copy.wait_send()
    for copy in meta_copies + stat_copies + sc_copies + y_up + y_down + fwd_up + fwd_down:
        copy.wait_send()
    for q in range(4):
        pl.when(goes_right[q])(lambda q=q: z_right[q].wait_send())
        pl.when(goes_left[q])(lambda q=q: z_left[q].wait_send())

    for c in range(CHUNKS):
        for copy in (copy_a, copy_b, copy_p, copy_m, copy_f):
            copy(c).wait_send()
        for k in range(2):
            copy_w(c, k).wait_send()


def per_device(images, projections, ctf_table, noise_weight, shifts, defocus):
    local = images.shape[0]
    pixels = images.shape[2]
    proj = projections.transpose(1, 0, 2).reshape(128, pixels)
    angles = np.arange(KY) * (2.0 * math.pi / KY)
    trig = np.concatenate([np.tile(np.cos(angles), (8, 1)), np.tile(np.sin(angles), (8, 1))])
    trig = jnp.asarray(trig.astype(np.float32))
    vmem = pl.BlockSpec(memory_space=pltpu.VMEM)
    hbm = pl.BlockSpec(memory_space=pl.ANY)
    smem = pl.BlockSpec(memory_space=pltpu.SMEM)
    dma = pltpu.SemaphoreType.DMA
    sems = [dma((2,)), dma((3,)), dma((3,)), dma((15,)), dma((15,)), dma((15,)), dma((15,))]
    sems += [dma((8,)), dma((4,))] + [dma((4,))] * 10 + [dma((CHUNKS,))] * 8 + [dma((CHUNKS, 2))] * 2 + [dma((CHUNKS,))] * 2
    sums, evidence = pl.pallas_call(
        kernel,
        out_shape=(
            jax.ShapeDtypeStruct((8, 2, pixels), F32),
            jax.ShapeDtypeStruct((local,), F32),
        ),
        in_specs=[vmem, hbm, hbm, vmem, vmem, smem, smem],
        out_specs=(vmem, smem),
        scratch_shapes=[
            pltpu.VMEM((16, 65 * LANES), BF16),
            pltpu.VMEM((16, LANES), BF16),
            pltpu.VMEM((16, HALF), BF16),
            pltpu.VMEM((16, LANES), BF16),
            pltpu.VMEM((BLOCKS, 16, LANES), BF16),
            pltpu.VMEM((BLOCKS, 16, HALF), BF16),
            pltpu.VMEM((2, 128, HALF), BF16),
            pltpu.VMEM((64, HALF), F32),
            pltpu.VMEM((2 * HALF, 128), BF16),
            pltpu.VMEM((64, 128), F32),
            pltpu.VMEM((128, 128), F32),
            pltpu.VMEM((128, 2 * LANES), F32),
            pltpu.VMEM((128, HALF), F32),
            pltpu.VMEM((TILES, 8, LANES), jnp.int32),
            pltpu.VMEM((BLOCKS * 32, 2 * HALF), BF16),
            pltpu.VMEM((4, 128, 128), F32),
            pltpu.VMEM((4, 128, 128), F32),
            pltpu.VMEM((BLOCKS, 16, LANES), F32),
            pltpu.VMEM((128, 512), BF16),
            [pltpu.VMEM((8, 16, 256 * t), BF16) for t in SIZES],
            [pltpu.VMEM((16, 256 * t), BF16) for t in SIZES],
            [pltpu.VMEM((16, 256 * t), BF16) for t in SIZES],
            [pltpu.VMEM((2, 16, 256 * t), BF16) for t in SIZES],
            [pltpu.VMEM((2, 16, 256 * t), BF16) for t in SIZES],
            [pltpu.VMEM((2, 16, 128 * t), BF16) for t in SIZES],
            [pltpu.VMEM((2, 16, 128 * t), BF16) for t in SIZES],
            [pltpu.VMEM((16, 256 * t), F32) for t in SIZES],
            [pltpu.VMEM((8, 256 * t), F32) for t in SIZES],
            *sems,
        ],
        compiler_params=pltpu.CompilerParams(
            collective_id=0, has_side_effects=True, vmem_limit_bytes=56 * 1024 * 1024
        ),
    )(
        images, proj, ctf_table, noise_weight.reshape(65, LANES), trig,
        shifts.transpose(0, 2, 1), defocus,
    )
    return evidence, sums


def solution(mesh):
    in_specs = (
        P(("img", "ori"), None, None),
        P("ori", None, None),
        P(),
        P(),
        P(("img", "ori"), None, None),
        P(("img", "ori")),
    )
    out_specs = (P(("img", "ori")), P(("ori", "img"), None, None))
    return jax.shard_map(
        per_device, mesh=mesh, in_specs=in_specs, out_specs=out_specs, check_vma=False
    )
```

```python
import math

import jax
import jax.numpy as jnp
import numpy as np
from jax import lax
from jax.experimental import pallas as pl
from jax.experimental.pallas import tpu as pltpu
from jax.sharding import PartitionSpec as P

KY = 128
KX = 65
LANES = 128
NX, NZ, NY = 4, 4, 4
BLOCKS = NZ * NY
TRANS = 4
TILES = 33
HALF = TILES * LANES
SHIFT = 32 * LANES
HALF_A = 17 * LANES
SIZES = (5, 7, 8, 8, 5)
STARTS = (0, 5, 12, 20, 28, 33)
CHUNKS = len(SIZES)
OTHERS = [(dz, dy) for dz in range(NZ) for dy in range(NY) if (dz, dy) != (0, 0)]
F32 = jnp.float32
BF16 = jnp.bfloat16
HI = lax.Precision.HIGHEST


def kernel(
    img_ref, proj_ref, ctf_ref, noise_ref, trig_ref, shift_ref, class_ref,
    out_ref, ev_ref,
    placed, ometa, pair, pmeta, smeta, gath, praw, ctfh, weights, norms, normrows, onehot, ctfrows, vtab, prep,
    score, pscore, stats, post, part, from_a, from_b, from_p, from_m, zsend, zrecv, keep, fin,
    loc_sem, core_s, core_r, meta_s, meta_r, stat_s, stat_r, z_s, z_r,
    yp_s, ym_s, yl_r, yr_r, fa_s, fb_s, fa_r, fb_r, sc_s, sc_r,
    a_s, b_s, a_r, b_r, p_s, m_s, p_r, m_r, w_s, w_r, f_s, f_r,
):
    img = lax.axis_index("img")
    ori = lax.axis_index("ori")
    x, zh = img // 2, img % 2
    core, y, zl = ori % 2, (ori // 2) % 4, ori // 8
    xp, xm, x2 = (x + 1) % 4, (x + 3) % 4, (x + 2) % 4
    yp, ym, y2 = (y + 1) % 4, (y + 3) % 4, (y + 2) % 4
    own = zl * 4 + y

    def dev(x_=x, zh_=zh, zl_=zl, y_=y, core_=core):
        return (x_ * 2 + zh_, (zl_ * 4 + y_) * 2 + core_)

    def send(src, dst, ss, rs, target):
        return pltpu.make_async_remote_copy(
            src_ref=src, dst_ref=dst, send_sem=ss, recv_sem=rs,
            device_id=target, device_id_type=pl.DeviceIdType.MESH,
        )

    peer = dev(core_=1 - core)
    others = [dev(zl_=(zl + dz) % 4, y_=(y + dy) % 4) for dz, dy in OTHERS]
    right, left = dev(x_=xp), dev(x_=xm)
    up, down = dev(y_=yp), dev(y_=ym)
    across = [dev(zh_=1 - zh, core_=k) for k in range(2)]

    barrier = pltpu.get_barrier_semaphore()
    greeted = [peer, *others, right, left, *across]
    for target in greeted:
        pl.semaphore_signal(barrier, inc=1, device_id=target, device_id_type=pl.DeviceIdType.MESH)

    mine = pl.ds(pl.multiple_of(core * SHIFT, LANES), HALF)
    theirs = pl.ds(pl.multiple_of((1 - core) * SHIFT, LANES), HALF)
    ctf_copy = pltpu.make_async_copy(ctf_ref.at[:, mine], ctfh, loc_sem.at[0])
    proj_copy = pltpu.make_async_copy(proj_ref.at[:, mine], praw.at[core], loc_sem.at[1])
    ctf_copy.start()
    proj_copy.start()

    lane = lax.broadcasted_iota(jnp.int32, (8, LANES), 1)
    place = lax.broadcasted_iota(jnp.int32, (8, LANES), 0)

    def lay_out(s, carry):
        cols = pl.ds(pl.multiple_of(s * 5 * LANES, LANES), 5 * LANES)
        at = lax.broadcasted_iota(jnp.int32, (8, 5 * LANES), 0)
        real = jnp.zeros((8, 5 * LANES), F32)
        imag = jnp.zeros((8, 5 * LANES), F32)
        for i in range(4):
            both = img_ref[i, :, cols].astype(F32)
            here = at == i + 4 * core
            real = jnp.where(here, both[0:1], real)
            imag = jnp.where(here, both[1:2], imag)
        placed[:, cols] = jnp.concatenate([real, imag], axis=0).astype(BF16)
        return carry

    lax.fori_loop(0, 13, lay_out, 0)
    meta = jnp.zeros((8, LANES), jnp.int32)
    for i in range(4):
        row = place == i + 4 * core
        for t in range(TRANS):
            for k in range(2):
                spot = jnp.logical_and(row, lane == 2 * t + k)
                meta = jnp.where(spot, shift_ref[i, k, t], meta)
        meta = jnp.where(jnp.logical_and(row, lane == 8), class_ref[i], meta)
    meta = meta.astype(F32)
    ometa[...] = jnp.concatenate([meta, jnp.zeros_like(meta)], axis=0).astype(BF16)

    pl.semaphore_wait(barrier, len(greeted))

    pair_copy = send(placed.at[:, theirs], pair, core_s.at[0], core_r.at[0], peer)
    pmeta_copy = send(ometa, pmeta, core_s.at[1], core_r.at[1], peer)
    praw_copy = send(proj_ref.at[:, theirs], praw.at[core], core_s.at[2], core_r.at[2], peer)
    pmeta_copy.start()
    pair_copy.start()
    praw_copy.start()

    pmeta_copy.wait_recv()
    smeta[own] = ometa[...] + pmeta[...]
    meta_copies = [
        send(smeta.at[own], smeta.at[own], meta_s.at[n], meta_r.at[n], target)
        for n, target in enumerate(others)
    ]
    for copy in meta_copies:
        copy.start()

    pair_copy.wait_recv()
    gath[own] = placed[:, mine] + pair[...]

    b0, b1 = zl % 2, zl // 2

    def pick(table):
        low = (1 - b0) * table[0] + b0 * table[1]
        high = (1 - b0) * table[2] + b0 * table[3]
        return (1 - b1) * low + b1 * high

    order = [zl, pick([1, 0, 3, 2]), pick([2, 2, 1, 1]), pick([3, 3, 0, 0])]

    halves = (pl.ds(0, HALF_A), pl.ds(HALF_A, HALF - HALF_A))

    def same(b, h, ss, rs, target):
        ref = gath.at[b, :, halves[h]]
        return send(ref, ref, ss, rs, target)

    above, below = dev(zl_=zl + 1), dev(zl_=zl - 1)
    goes_right = [zl < 3] + [jnp.logical_and(order[q] < zl, zl < 3) for q in (1, 2, 3)]
    goes_left = [zl > 0] + [jnp.logical_and(order[q] > zl, zl > 0) for q in (1, 2, 3)]
    z_right, z_left, y_up, y_down, fwd_up, fwd_down = [], [], [], [], [], []
    for q in range(4):
        for h in range(2):
            n, came = 2 * q + h, z_r.at[order[q] * 2 + h]
            b = order[q] * 4 + y
            z_right.append(same(b, h, z_s.at[n], came, above))
            z_left.append(same(b, h, z_s.at[8 + n], came, below))
            y_up.append(same(b, h, yp_s.at[n], yl_r.at[n], up))
            y_down.append(same(b, h, ym_s.at[n], yr_r.at[n], down))
        fwd_up.append(same(order[q] * 4 + ym, 0, fa_s.at[q], fa_r.at[q], up))
        fwd_down.append(same(order[q] * 4 + yp, 1, fb_s.at[q], fb_r.at[q], down))

    def launch(q, h):
        n = 2 * q + h
        pl.when(goes_right[q])(lambda: z_right[n].start())
        pl.when(goes_left[q])(lambda: z_left[n].start())
        y_up[n].start()
        y_down[n].start()

    launch(0, 0)
    launch(0, 1)

    def fill_rows(s, carry):
        p = (s + 32 * core) * LANES + lane
        after = lax.shift_right_logical((p + LANES) * 64528, 22)
        vtab[s] = after - lax.shift_right_logical(p * 64528, 22)
        return carry

    lax.fori_loop(0, TILES, fill_rows, 0)
    top_row = lax.shift_right_logical((32 * core * LANES + lane) * 64528, 22)

    def pieces(value):
        one = value.astype(BF16)
        rest = value - one.astype(F32)
        two = rest.astype(BF16)
        three = (rest - two.astype(F32)).astype(BF16)
        return one, two, three

    def fill_ctf(s, carry):
        cols = pl.ds(pl.multiple_of(s * 1408, 1408), 1408)
        one, two, three = pieces(ctfh[:, cols])
        ctfrows[:, cols] = jnp.dot(
            onehot[...].astype(BF16),
            jnp.concatenate([one, two, three, one], axis=0),
            preferred_element_type=F32,
        )
        return carry


    def weigh(n, total):
        wide = pl.ds(pl.multiple_of(n * 384, 384), 384)
        raw = [praw[0, :, wide], praw[1, :, wide]]
        ctfs = ctfh[:, wide]
        noises = [noise_ref[pl.ds(core * 32 + 3 * n + i, 1), :] for i in range(3)]
        counted = 1 - core * (1 - jnp.minimum(n, 1))
        noises[0] = noises[0] * counted.astype(F32)
        turned = []
        for i in range(3):
            tile = slice(i * LANES, (i + 1) * LANES)
            parts = [r[:, tile].astype(F32).reshape(2, 8, 1, 8, LANES) for r in raw]
            both = jnp.concatenate(parts, axis=2).reshape(2, 128, LANES)
            scaled = (both * noises[i][None]).astype(BF16)
            turned += [scaled[0].T, scaled[1].T]
            power = (both[0] * both[0] + both[1] * both[1]).T
            ctf = ctfs[:, tile]
            p1, p2, p3 = pieces(power)
            c1, c2, c3 = pieces(ctf * ctf * noises[i])
            total = total + jnp.dot(
                jnp.concatenate([c1, c1, c1, c2, c2, c3], axis=1),
                jnp.concatenate([p1, p2, p3, p1, p2, p1], axis=0),
                preferred_element_type=F32,
            )
        weights[pl.ds(pl.multiple_of(n * 768, 768), 768), :] = jnp.concatenate(turned, axis=0)
        return total

    cosine = trig_ref[0:8, :]
    sine = trig_ref[8:16, :]

    def prepare(b):
        meta = smeta[b].astype(F32)[0:8, :].astype(jnp.int32)

        def wave(steps):
            index = steps & (KY - 1)
            return (
                jnp.take_along_axis(cosine, index, axis=1),
                jnp.take_along_axis(sine, index, axis=1),
            )

        begin, one_row, two_rows = [], [], []
        for t in range(TRANS):
            sx = meta[:, 2 * t : 2 * t + 1]
            sy = meta[:, 2 * t + 1 : 2 * t + 2]
            slope = jnp.broadcast_to(sy - KX * sx, (8, LANES))
            begin.append(wave(lane * sx + top_row * slope))
            one_row.append(wave(slope))
            two_rows.append(wave(2 * slope))

        def body(n, carry):
            phases, total = carry
            wide = pl.ds(pl.multiple_of(n * 384, 384), 384)
            blocks = gath[b, :, wide].astype(F32)
            ctfs = ctfrows[pl.ds(pl.multiple_of(b * 8, 8), 8), wide]
            singles = [vtab[3 * n + i] == 1 for i in range(3)]
            rows = [[], []]
            for i in range(3):
                tile = slice(i * LANES, (i + 1) * LANES)
                ctf = ctfs[:, tile]
                real, imag = blocks[0:8, tile] * ctf, blocks[8:16, tile] * ctf
                reals, imags, later = [], [], []
                for t in range(TRANS):
                    c, si = phases[t]
                    reals.append(real * c + imag * si)
                    imags.append(imag * c - real * si)
                    mc = jnp.where(singles[i], one_row[t][0], two_rows[t][0])
                    ms = jnp.where(singles[i], one_row[t][1], two_rows[t][1])
                    later.append((c * mc - si * ms, si * mc + c * ms))
                phases = tuple(later)
                for h in range(2):
                    for values in (reals, imags):
                        pair_ = jnp.concatenate(values[2 * h : 2 * h + 2], axis=0)
                        rows[h].append(pair_.astype(BF16))
            steps = pl.ds(pl.multiple_of(n * 768, 768), 768)
            made = jnp.concatenate([jnp.concatenate(r, axis=1) for r in rows], axis=0)
            total = total + jnp.dot(made, weights[steps, :], preferred_element_type=F32)
            prep[pl.ds(pl.multiple_of(b * 32, 32), 32), steps] = made
            return phases, total

        start = (tuple(begin), jnp.zeros((32, LANES), F32))
        _, cross = lax.fori_loop(0, TILES // 3, body, start, unroll=11)
        norm = normrows[pl.ds(pl.multiple_of(b * 8, 8), 8), :]
        at = pl.ds(pl.multiple_of((b % 4) * 32, 32), 32)
        score[b // 4, at, :] = cross - jnp.concatenate([norm] * TRANS, axis=0)

    sc_copies = [
        send(score.at[order[q]], pscore.at[order[q]], sc_s.at[q], sc_r.at[q], peer)
        for q in range(4)
    ]

    stats[own] = jnp.zeros((16, LANES), F32)

    def summarise(q):
        sc_copies[q].wait_recv()
        g = order[q]
        whole = (score[g] + pscore[g]).T
        pscore[g] = whole
        top = jnp.max(whole, axis=0, keepdims=True)
        stats[own, pl.ds(g, 1), :] = top
        stats[own, pl.ds(8 + g, 1), :] = jnp.sum(jnp.exp(whole - top), axis=0, keepdims=True)

    def finish(q):
        fwd_up[q].wait_recv()
        fwd_down[q].wait_recv()
        prepare(order[q] * 4 + y2)
        sc_copies[q].start()

    def arrive(q, h):
        z_right[2 * q + h].wait_recv()
        launch(q, h)

    def forward(q, h):
        if h == 0:
            y_up[2 * q].wait_recv()
            fwd_up[q].start()
        else:
            y_down[2 * q + 1].wait_recv()
            fwd_down[q].start()

    def prepare_three(q):
        y_up[2 * q + 1].wait_recv()
        y_down[2 * q].wait_recv()

        def three(i, carry):
            prepare(order[q] * 4 + (y + 3 + i) % 4)
            return carry

        lax.fori_loop(0, 3, three, 0)

    ctf_copy.wait()
    proj_copy.wait()
    praw_copy.wait_recv()
    half_norms = lax.fori_loop(0, 4, weigh, jnp.zeros((64, 128), F32))
    arrive(1, 0)
    forward(0, 0)
    half_norms = lax.fori_loop(4, 6, weigh, half_norms)
    arrive(1, 1)
    forward(0, 1)

    for copy in meta_copies:
        copy.wait_recv()

    lane2 = lax.broadcasted_iota(jnp.int32, (8, 256), 1)

    def fill_onehot(b, carry):
        classes = smeta[b].astype(F32)[0:8, 8:9].astype(jnp.int32)
        hit = jnp.logical_and(lane2 % 64 == classes, lane2 < 192)
        onehot[pl.ds(pl.multiple_of(b * 8, 8), 8), :] = hit.astype(F32)
        return carry

    lax.fori_loop(0, BLOCKS, fill_onehot, 0)
    lax.fori_loop(0, 3, fill_ctf, 0)

    arrive(2, 0)
    half_norms = lax.fori_loop(6, 9, weigh, half_norms)
    arrive(2, 1)
    forward(1, 0)
    half_norms = lax.fori_loop(9, 11, weigh, half_norms)
    norms[...] = 0.5 * half_norms
    normrows[...] = jnp.dot(
        onehot[:, 0:64], norms[...], precision=HI, preferred_element_type=F32
    )
    forward(1, 1)
    prepare_three(0)
    arrive(3, 0)
    finish(0)
    arrive(3, 1)
    forward(2, 0)
    prepare_three(1)
    forward(2, 1)
    forward(3, 0)
    finish(1)
    summarise(0)
    prepare_three(2)
    forward(3, 1)
    finish(2)
    summarise(1)
    prepare_three(3)
    finish(3)
    summarise(2)
    summarise(3)

    stat_copies = [
        send(stats.at[own], stats.at[own], stat_s.at[n], stat_r.at[n], target)
        for n, target in enumerate(others)
    ]
    for copy in stat_copies:
        copy.start()
    for copy in stat_copies:
        copy.wait_recv()
    tops = [stats[b, 0:8, :] for b in range(BLOCKS)]
    top = tops[0]
    for b in range(1, BLOCKS):
        top = jnp.maximum(top, tops[b])
    total = jnp.zeros((8, LANES), F32)
    for b in range(BLOCKS):
        total += stats[b, 8:16, :] * jnp.exp(tops[b] - top)
    held = lax.broadcasted_iota(jnp.int32, (8, LANES), 1) % 32

    def turn(value, by):
        inside = pltpu.roll(value, by, 1)
        wrapped = pltpu.roll(value, by + LANES - 32, 1)
        return jnp.where(held >= by, inside, wrapped)

    largest = jnp.maximum(top, turn(top, 8))
    largest = jnp.maximum(largest, turn(largest, 16))
    total = total * jnp.exp(top - largest)
    total = total + turn(total, 8)
    total = total + turn(total, 16)
    evidence = largest + jnp.log(total)
    for i in range(4):
        spot = jnp.logical_and(place == zl, lane == y * 32 + core * 4 + i)
        ev_ref[i] = jnp.sum(jnp.where(spot, evidence, 0.0))
    for g in range(4):
        post[:, g * 128 : (g + 1) * 128] = (
            jnp.exp(pscore[g] - evidence[g : g + 1, :]) * 2048.0
        ).astype(BF16)

    def copy_a(c):
        return send(part[c].at[2 * x2], from_a[c], a_s.at[c], a_r.at[c], right)

    def copy_b(c):
        return send(part[c].at[2 * x2 + 1], from_b[c], b_s.at[c], b_r.at[c], left)

    def copy_p(c):
        return send(part[c].at[pl.ds(2 * xp, 2)], from_p[c], p_s.at[c], p_r.at[c], right)

    def copy_m(c):
        return send(part[c].at[pl.ds(2 * xm, 2)], from_m[c], m_s.at[c], m_r.at[c], left)

    def copy_w(c, k):
        return send(
            zsend[c].at[k], zrecv[c].at[core], w_s.at[c, k], w_r.at[c, core], across[k]
        )

    def arrived_w(c, half):
        return send(zsend[c].at[0], zrecv[c].at[half], w_s.at[c, 0], w_r.at[c, half], across[0])

    def copy_f(c):
        other = pl.ds(pl.multiple_of((1 - core) * 8, 8), 8)
        return send(keep[c].at[other], fin[c], f_s.at[c], f_r.at[c], peer)

    def project(c):
        sums = jnp.dot(
            post[...], prep[:, STARTS[c] * 256 : STARTS[c + 1] * 256], preferred_element_type=F32
        ).astype(BF16)
        for i in range(8):
            part[c][i] = sums[16 * i : 16 * i + 16]
        copy_a(c).start()
        copy_b(c).start()

    def add(into, *others_):
        value = into.astype(F32)
        for other in others_:
            value = value + other.astype(F32)
        return value

    def pass_on(c):
        copy_a(c).wait_recv()
        part[c][2 * xp] = add(part[c][2 * xp], from_a[c][...]).astype(BF16)
        copy_p(c).start()
        copy_b(c).wait_recv()
        part[c][2 * xm + 1] = add(part[c][2 * xm + 1], from_b[c][...]).astype(BF16)
        copy_m(c).start()

    def collect(c):
        half = SIZES[c] * LANES
        copy_p(c).wait_recv()
        copy_m(c).wait_recv()
        far = 1 - zh
        away = add(part[c][2 * x + far], from_p[c][far], from_m[c][far])
        for k in range(2):
            rows = away[8 * k : 8 * k + 8]
            zsend[c][k] = jnp.concatenate([rows[:, :half], rows[:, half:]], axis=0).astype(BF16)
            copy_w(c, k).start()
        keep[c][...] = add(part[c][2 * x + zh], from_p[c][zh], from_m[c][zh])
        copy_f(c).start()

    def complete(c):
        for half in range(2):
            arrived_w(c, half).wait_recv()
        copy_f(c).wait_recv()
        here = keep[c][pl.ds(pl.multiple_of(core * 8, 8), 8), :]
        for half, near in ((core, here), (1 - core, fin[c][...])):
            rows = zrecv[c][half].astype(F32)
            value = near + jnp.concatenate([rows[0:8], rows[8:16]], axis=1)
            for s in range(SIZES[c]):
                at = pl.multiple_of(half * SHIFT + (STARTS[c] + s) * LANES, LANES)
                for k in range(2):
                    out_ref[:, k, pl.ds(at, LANES)] = value[
                        :, s * 256 + k * 128 : s * 256 + k * 128 + 128
                    ]

    for c in range(CHUNKS):
        project(c)
    for c in range(CHUNKS):
        pass_on(c)
    for c in range(CHUNKS):
        collect(c)
        if c >= 2:
            complete(c - 2)
    complete(CHUNKS - 2)
    complete(CHUNKS - 1)

    pmeta_copy.wait_send()
    pair_copy.wait_send()
    praw_copy.wait_send()
    for copy in meta_copies + stat_copies + sc_copies + y_up + y_down + fwd_up + fwd_down:
        copy.wait_send()
    for n in range(8):
        pl.when(goes_right[n // 2])(lambda n=n: z_right[n].wait_send())
        pl.when(goes_left[n // 2])(lambda n=n: z_left[n].wait_send())

    for c in range(CHUNKS):
        for copy in (copy_a, copy_b, copy_p, copy_m, copy_f):
            copy(c).wait_send()
        for k in range(2):
            copy_w(c, k).wait_send()


def per_device(images, projections, ctf_table, noise_weight, shifts, defocus):
    local = images.shape[0]
    pixels = images.shape[2]
    proj = projections.transpose(1, 0, 2).reshape(128, pixels)
    angles = np.arange(KY) * (2.0 * math.pi / KY)
    trig = np.concatenate([np.tile(np.cos(angles), (8, 1)), np.tile(np.sin(angles), (8, 1))])
    trig = jnp.asarray(trig.astype(np.float32))
    vmem = pl.BlockSpec(memory_space=pltpu.VMEM)
    hbm = pl.BlockSpec(memory_space=pl.ANY)
    smem = pl.BlockSpec(memory_space=pltpu.SMEM)
    dma = pltpu.SemaphoreType.DMA
    sems = [dma((2,)), dma((3,)), dma((3,)), dma((15,)), dma((15,)), dma((15,)), dma((15,))]
    sems += [dma((16,)), dma((8,))] + [dma((8,))] * 4 + [dma((4,))] * 6 + [dma((CHUNKS,))] * 8 + [dma((CHUNKS, 2))] * 2 + [dma((CHUNKS,))] * 2
    sums, evidence = pl.pallas_call(
        kernel,
        out_shape=(
            jax.ShapeDtypeStruct((8, 2, pixels), F32),
            jax.ShapeDtypeStruct((local,), F32),
        ),
        in_specs=[vmem, hbm, hbm, vmem, vmem, smem, smem],
        out_specs=(vmem, smem),
        scratch_shapes=[
            pltpu.VMEM((16, 65 * LANES), BF16),
            pltpu.VMEM((16, LANES), BF16),
            pltpu.VMEM((16, HALF), BF16),
            pltpu.VMEM((16, LANES), BF16),
            pltpu.VMEM((BLOCKS, 16, LANES), BF16),
            pltpu.VMEM((BLOCKS, 16, HALF), BF16),
            pltpu.VMEM((2, 128, HALF), BF16),
            pltpu.VMEM((64, HALF), F32),
            pltpu.VMEM((2 * HALF, 128), BF16),
            pltpu.VMEM((64, 128), F32),
            pltpu.VMEM((128, 128), F32),
            pltpu.VMEM((128, 2 * LANES), F32),
            pltpu.VMEM((128, HALF), F32),
            pltpu.VMEM((TILES, 8, LANES), jnp.int32),
            pltpu.VMEM((BLOCKS * 32, 2 * HALF), BF16),
            pltpu.VMEM((4, 128, 128), F32),
            pltpu.VMEM((4, 128, 128), F32),
            pltpu.VMEM((BLOCKS, 16, LANES), F32),
            pltpu.VMEM((128, 512), BF16),
            [pltpu.VMEM((8, 16, 256 * t), BF16) for t in SIZES],
            [pltpu.VMEM((16, 256 * t), BF16) for t in SIZES],
            [pltpu.VMEM((16, 256 * t), BF16) for t in SIZES],
            [pltpu.VMEM((2, 16, 256 * t), BF16) for t in SIZES],
            [pltpu.VMEM((2, 16, 256 * t), BF16) for t in SIZES],
            [pltpu.VMEM((2, 16, 128 * t), BF16) for t in SIZES],
            [pltpu.VMEM((2, 16, 128 * t), BF16) for t in SIZES],
            [pltpu.VMEM((16, 256 * t), F32) for t in SIZES],
            [pltpu.VMEM((8, 256 * t), F32) for t in SIZES],
            *sems,
        ],
        compiler_params=pltpu.CompilerParams(
            collective_id=0, has_side_effects=True, vmem_limit_bytes=56 * 1024 * 1024
        ),
    )(
        images, proj, ctf_table, noise_weight.reshape(65, LANES), trig,
        shifts.transpose(0, 2, 1), defocus,
    )
    return evidence, sums


def solution(mesh):
    in_specs = (
        P(("img", "ori"), None, None),
        P("ori", None, None),
        P(),
        P(),
        P(("img", "ori"), None, None),
        P(("img", "ori")),
    )
    out_specs = (P(("img", "ori")), P(("ori", "img"), None, None))
    return jax.shard_map(
        per_device, mesh=mesh, in_specs=in_specs, out_specs=out_specs, check_vma=False
    )
```

```python
import math

import jax
import jax.numpy as jnp
import numpy as np
from jax import lax
from jax.experimental import pallas as pl
from jax.experimental.pallas import tpu as pltpu
from jax.sharding import PartitionSpec as P

KY = 128
KX = 65
LANES = 128
NX, NZ, NY = 4, 4, 4
BLOCKS = NZ * NY
TRANS = 4
TILES = 33
HALF = TILES * LANES
SHIFT = 32 * LANES
HALF_A = 17 * LANES
SIZES = (5, 7, 8, 8, 5)
STARTS = (0, 5, 12, 20, 28, 33)
CHUNKS = len(SIZES)
OTHERS = [(dz, dy) for dz in range(NZ) for dy in range(NY) if (dz, dy) != (0, 0)]
F32 = jnp.float32
BF16 = jnp.bfloat16
HI = lax.Precision.HIGHEST


def kernel(
    img_hbm, proj_ref, ctf_ref, noise_hbm, trig_hbm, shift_ref, class_ref,
    out_hbm, ev_ref,
    img_ref, noise_ref, trig_ref, out_ref,
    placed, ometa, pair, pmeta, smeta, gath, praw, ctfh, weights, norms, normrows, onehot, ctfrows, vtab, prep,
    score, pscore, stats, post, part, from_a, from_b, from_p, from_m, zsend, zrecv, keep, fin,
    loc_sem, core_s, core_r, meta_s, meta_r, stat_s, stat_r, z_s, z_r,
    yp_s, ym_s, yl_r, yr_r, fa_s, fb_s, fa_r, fb_r, sc_s, sc_r,
    a_s, b_s, a_r, b_r, p_s, m_s, p_r, m_r, w_s, w_r, f_s, f_r, out_sem,
):
    img = lax.axis_index("img")
    ori = lax.axis_index("ori")
    x, zh = img // 2, img % 2
    core, y, zl = ori % 2, (ori // 2) % 4, ori // 8
    xp, xm, x2 = (x + 1) % 4, (x + 3) % 4, (x + 2) % 4
    yp, ym, y2 = (y + 1) % 4, (y + 3) % 4, (y + 2) % 4
    own = zl * 4 + y

    def dev(x_=x, zh_=zh, zl_=zl, y_=y, core_=core):
        return (x_ * 2 + zh_, (zl_ * 4 + y_) * 2 + core_)

    def send(src, dst, ss, rs, target):
        return pltpu.make_async_remote_copy(
            src_ref=src, dst_ref=dst, send_sem=ss, recv_sem=rs,
            device_id=target, device_id_type=pl.DeviceIdType.MESH,
        )

    peer = dev(core_=1 - core)
    others = [dev(zl_=(zl + dz) % 4, y_=(y + dy) % 4) for dz, dy in OTHERS]
    right, left = dev(x_=xp), dev(x_=xm)
    up, down = dev(y_=yp), dev(y_=ym)
    across = [dev(zh_=1 - zh, core_=k) for k in range(2)]

    img_copy = pltpu.make_async_copy(img_hbm, img_ref, loc_sem.at[2])
    noise_copy = pltpu.make_async_copy(noise_hbm, noise_ref, loc_sem.at[3])
    trig_copy = pltpu.make_async_copy(trig_hbm, trig_ref, loc_sem.at[4])
    img_copy.start()
    barrier = pltpu.get_barrier_semaphore()
    greeted = [peer, *others, right, left, *across]
    for target in greeted:
        pl.semaphore_signal(barrier, inc=1, device_id=target, device_id_type=pl.DeviceIdType.MESH)

    mine = pl.ds(pl.multiple_of(core * SHIFT, LANES), HALF)
    theirs = pl.ds(pl.multiple_of((1 - core) * SHIFT, LANES), HALF)
    ctf_copy = pltpu.make_async_copy(ctf_ref.at[:, mine], ctfh, loc_sem.at[0])
    proj_copy = pltpu.make_async_copy(proj_ref.at[:, mine], praw.at[core], loc_sem.at[1])
    ctf_copy.start()
    proj_copy.start()
    noise_copy.start()
    trig_copy.start()

    lane = lax.broadcasted_iota(jnp.int32, (8, LANES), 1)
    place = lax.broadcasted_iota(jnp.int32, (8, LANES), 0)

    def lay_out(s, carry):
        cols = pl.ds(pl.multiple_of(s * 5 * LANES, LANES), 5 * LANES)
        at = lax.broadcasted_iota(jnp.int32, (8, 5 * LANES), 0)
        real = jnp.zeros((8, 5 * LANES), F32)
        imag = jnp.zeros((8, 5 * LANES), F32)
        for i in range(4):
            both = img_ref[i, :, cols].astype(F32)
            here = at == i + 4 * core
            real = jnp.where(here, both[0:1], real)
            imag = jnp.where(here, both[1:2], imag)
        placed[:, cols] = jnp.concatenate([real, imag], axis=0).astype(BF16)
        return carry

    img_copy.wait()
    lax.fori_loop(0, 13, lay_out, 0)
    meta = jnp.zeros((8, LANES), jnp.int32)
    for i in range(4):
        row = place == i + 4 * core
        for t in range(TRANS):
            for k in range(2):
                spot = jnp.logical_and(row, lane == 2 * t + k)
                meta = jnp.where(spot, shift_ref[i, k, t], meta)
        meta = jnp.where(jnp.logical_and(row, lane == 8), class_ref[i], meta)
    meta = meta.astype(F32)
    ometa[...] = jnp.concatenate([meta, jnp.zeros_like(meta)], axis=0).astype(BF16)

    pl.semaphore_wait(barrier, len(greeted))

    pair_copy = send(placed.at[:, theirs], pair, core_s.at[0], core_r.at[0], peer)
    pmeta_copy = send(ometa, pmeta, core_s.at[1], core_r.at[1], peer)
    praw_copy = send(proj_ref.at[:, theirs], praw.at[core], core_s.at[2], core_r.at[2], peer)
    pmeta_copy.start()
    pair_copy.start()
    praw_copy.start()

    pmeta_copy.wait_recv()
    smeta[own] = ometa[...] + pmeta[...]
    meta_copies = [
        send(smeta.at[own], smeta.at[own], meta_s.at[n], meta_r.at[n], target)
        for n, target in enumerate(others)
    ]
    for copy in meta_copies:
        copy.start()

    pair_copy.wait_recv()
    gath[own] = placed[:, mine] + pair[...]

    b0, b1 = zl % 2, zl // 2

    def pick(table):
        low = (1 - b0) * table[0] + b0 * table[1]
        high = (1 - b0) * table[2] + b0 * table[3]
        return (1 - b1) * low + b1 * high

    order = [zl, pick([1, 0, 3, 2]), pick([2, 2, 1, 1]), pick([3, 3, 0, 0])]

    halves = (pl.ds(0, HALF_A), pl.ds(HALF_A, HALF - HALF_A))

    def same(b, h, ss, rs, target):
        ref = gath.at[b, :, halves[h]]
        return send(ref, ref, ss, rs, target)

    above, below = dev(zl_=zl + 1), dev(zl_=zl - 1)
    goes_right = [zl < 3] + [jnp.logical_and(order[q] < zl, zl < 3) for q in (1, 2, 3)]
    goes_left = [zl > 0] + [jnp.logical_and(order[q] > zl, zl > 0) for q in (1, 2, 3)]
    z_right, z_left, y_up, y_down, fwd_up, fwd_down = [], [], [], [], [], []
    for q in range(4):
        for h in range(2):
            n, came = 2 * q + h, z_r.at[order[q] * 2 + h]
            b = order[q] * 4 + y
            z_right.append(same(b, h, z_s.at[n], came, above))
            z_left.append(same(b, h, z_s.at[8 + n], came, below))
            y_up.append(same(b, h, yp_s.at[n], yl_r.at[n], up))
            y_down.append(same(b, h, ym_s.at[n], yr_r.at[n], down))
        fwd_up.append(same(order[q] * 4 + ym, 0, fa_s.at[q], fa_r.at[q], up))
        fwd_down.append(same(order[q] * 4 + yp, 1, fb_s.at[q], fb_r.at[q], down))

    def launch(q, h):
        n = 2 * q + h
        pl.when(goes_right[q])(lambda: z_right[n].start())
        pl.when(goes_left[q])(lambda: z_left[n].start())
        y_up[n].start()
        y_down[n].start()

    launch(0, 0)
    launch(0, 1)

    def fill_rows(s, carry):
        p = (s + 32 * core) * LANES + lane
        after = lax.shift_right_logical((p + LANES) * 64528, 22)
        vtab[s] = after - lax.shift_right_logical(p * 64528, 22)
        return carry

    lax.fori_loop(0, TILES, fill_rows, 0)
    top_row = lax.shift_right_logical((32 * core * LANES + lane) * 64528, 22)

    def pieces(value):
        one = value.astype(BF16)
        rest = value - one.astype(F32)
        two = rest.astype(BF16)
        three = (rest - two.astype(F32)).astype(BF16)
        return one, two, three

    def fill_ctf(s, carry):
        cols = pl.ds(pl.multiple_of(s * 1408, 1408), 1408)
        one, two, three = pieces(ctfh[:, cols])
        ctfrows[:, cols] = jnp.dot(
            onehot[...].astype(BF16),
            jnp.concatenate([one, two, three, one], axis=0),
            preferred_element_type=F32,
        )
        return carry


    def weigh(n, total):
        wide = pl.ds(pl.multiple_of(n * 384, 384), 384)
        raw = [praw[0, :, wide], praw[1, :, wide]]
        ctfs = ctfh[:, wide]
        noises = [noise_ref[pl.ds(core * 32 + 3 * n + i, 1), :] for i in range(3)]
        counted = 1 - core * (1 - jnp.minimum(n, 1))
        noises[0] = noises[0] * counted.astype(F32)
        turned = []
        for i in range(3):
            tile = slice(i * LANES, (i + 1) * LANES)
            parts = [r[:, tile].astype(F32).reshape(2, 8, 1, 8, LANES) for r in raw]
            both = jnp.concatenate(parts, axis=2).reshape(2, 128, LANES)
            scaled = (both * noises[i][None]).astype(BF16)
            turned += [scaled[0].T, scaled[1].T]
            power = (both[0] * both[0] + both[1] * both[1]).T
            ctf = ctfs[:, tile]
            p1, p2, p3 = pieces(power)
            c1, c2, c3 = pieces(ctf * ctf * noises[i])
            total = total + jnp.dot(
                jnp.concatenate([c1, c1, c1, c2, c2, c3], axis=1),
                jnp.concatenate([p1, p2, p3, p1, p2, p1], axis=0),
                preferred_element_type=F32,
            )
        weights[pl.ds(pl.multiple_of(n * 768, 768), 768), :] = jnp.concatenate(turned, axis=0)
        return total

    def prepare(b):
        meta = smeta[b].astype(F32)[0:8, :].astype(jnp.int32)

        cosine, sine = trig_ref[0:8, :], trig_ref[8:16, :]

        def wave(steps):
            index = steps & (KY - 1)
            return (
                jnp.take_along_axis(cosine, index, axis=1),
                jnp.take_along_axis(sine, index, axis=1),
            )

        begin, one_row, two_rows = [], [], []
        for t in range(TRANS):
            sx = meta[:, 2 * t : 2 * t + 1]
            sy = meta[:, 2 * t + 1 : 2 * t + 2]
            slope = jnp.broadcast_to(sy - KX * sx, (8, LANES))
            begin.append(wave(lane * sx + top_row * slope))
            one_row.append(wave(slope))
            two_rows.append(wave(2 * slope))

        def body(n, carry):
            phases, total = carry
            wide = pl.ds(pl.multiple_of(n * 384, 384), 384)
            blocks = gath[b, :, wide].astype(F32)
            ctfs = ctfrows[pl.ds(pl.multiple_of(b * 8, 8), 8), wide]
            singles = [vtab[3 * n + i] == 1 for i in range(3)]
            rows = [[], []]
            for i in range(3):
                tile = slice(i * LANES, (i + 1) * LANES)
                ctf = ctfs[:, tile]
                real, imag = blocks[0:8, tile] * ctf, blocks[8:16, tile] * ctf
                reals, imags, later = [], [], []
                for t in range(TRANS):
                    c, si = phases[t]
                    reals.append(real * c + imag * si)
                    imags.append(imag * c - real * si)
                    mc = jnp.where(singles[i], one_row[t][0], two_rows[t][0])
                    ms = jnp.where(singles[i], one_row[t][1], two_rows[t][1])
                    later.append((c * mc - si * ms, si * mc + c * ms))
                phases = tuple(later)
                for h in range(2):
                    for values in (reals, imags):
                        pair_ = jnp.concatenate(values[2 * h : 2 * h + 2], axis=0)
                        rows[h].append(pair_.astype(BF16))
            steps = pl.ds(pl.multiple_of(n * 768, 768), 768)
            made = jnp.concatenate([jnp.concatenate(r, axis=1) for r in rows], axis=0)
            total = total + jnp.dot(made, weights[steps, :], preferred_element_type=F32)
            prep[pl.ds(pl.multiple_of(b * 32, 32), 32), steps] = made
            return phases, total

        start = (tuple(begin), jnp.zeros((32, LANES), F32))
        _, cross = lax.fori_loop(0, TILES // 3, body, start, unroll=11)
        norm = normrows[pl.ds(pl.multiple_of(b * 8, 8), 8), :]
        at = pl.ds(pl.multiple_of((b % 4) * 32, 32), 32)
        score[b // 4, at, :] = cross - jnp.concatenate([norm] * TRANS, axis=0)

    sc_copies = [
        send(score.at[order[q]], pscore.at[order[q]], sc_s.at[q], sc_r.at[q], peer)
        for q in range(4)
    ]

    stats[own] = jnp.zeros((16, LANES), F32)

    def summarise(q):
        sc_copies[q].wait_recv()
        g = order[q]
        whole = (score[g] + pscore[g]).T
        pscore[g] = whole
        top = jnp.max(whole, axis=0, keepdims=True)
        stats[own, pl.ds(g, 1), :] = top
        stats[own, pl.ds(8 + g, 1), :] = jnp.sum(jnp.exp(whole - top), axis=0, keepdims=True)

    def finish(q):
        fwd_up[q].wait_recv()
        fwd_down[q].wait_recv()
        prepare(order[q] * 4 + y2)
        sc_copies[q].start()

    def arrive(q, h):
        z_right[2 * q + h].wait_recv()
        launch(q, h)

    def forward(q, h):
        if h == 0:
            y_up[2 * q].wait_recv()
            fwd_up[q].start()
        else:
            y_down[2 * q + 1].wait_recv()
            fwd_down[q].start()

    def prepare_three(q):
        y_up[2 * q + 1].wait_recv()
        y_down[2 * q].wait_recv()

        def three(i, carry):
            prepare(order[q] * 4 + (y + 3 + i) % 4)
            return carry

        lax.fori_loop(0, 3, three, 0)

    ctf_copy.wait()
    noise_copy.wait()
    trig_copy.wait()
    proj_copy.wait()
    praw_copy.wait_recv()
    half_norms = lax.fori_loop(0, 4, weigh, jnp.zeros((64, 128), F32), unroll=4)
    arrive(1, 0)
    forward(0, 0)
    half_norms = lax.fori_loop(4, 6, weigh, half_norms, unroll=2)
    arrive(1, 1)
    forward(0, 1)

    for copy in meta_copies:
        copy.wait_recv()

    lane2 = lax.broadcasted_iota(jnp.int32, (8, 256), 1)

    def fill_onehot(b, carry):
        classes = smeta[b].astype(F32)[0:8, 8:9].astype(jnp.int32)
        hit = jnp.logical_and(lane2 % 64 == classes, lane2 < 192)
        onehot[pl.ds(pl.multiple_of(b * 8, 8), 8), :] = hit.astype(F32)
        return carry

    lax.fori_loop(0, BLOCKS, fill_onehot, 0)
    lax.fori_loop(0, 3, fill_ctf, 0)

    arrive(2, 0)
    half_norms = lax.fori_loop(6, 9, weigh, half_norms, unroll=3)
    arrive(2, 1)
    forward(1, 0)
    half_norms = lax.fori_loop(9, 11, weigh, half_norms, unroll=2)
    norms[...] = 0.5 * half_norms
    normrows[...] = jnp.dot(
        onehot[:, 0:64], norms[...], precision=HI, preferred_element_type=F32
    )
    forward(1, 1)
    prepare_three(0)
    arrive(3, 0)
    finish(0)
    arrive(3, 1)
    forward(2, 0)
    prepare_three(1)
    forward(2, 1)
    forward(3, 0)
    finish(1)
    summarise(0)
    prepare_three(2)
    forward(3, 1)
    finish(2)
    summarise(1)
    prepare_three(3)
    finish(3)
    summarise(2)
    summarise(3)

    stat_copies = [
        send(stats.at[own], stats.at[own], stat_s.at[n], stat_r.at[n], target)
        for n, target in enumerate(others)
    ]
    for copy in stat_copies:
        copy.start()
    for copy in stat_copies:
        copy.wait_recv()
    tops = [stats[b, 0:8, :] for b in range(BLOCKS)]
    top = tops[0]
    for b in range(1, BLOCKS):
        top = jnp.maximum(top, tops[b])
    total = jnp.zeros((8, LANES), F32)
    for b in range(BLOCKS):
        total += stats[b, 8:16, :] * jnp.exp(tops[b] - top)
    held = lax.broadcasted_iota(jnp.int32, (8, LANES), 1) % 32

    def turn(value, by):
        inside = pltpu.roll(value, by, 1)
        wrapped = pltpu.roll(value, by + LANES - 32, 1)
        return jnp.where(held >= by, inside, wrapped)

    largest = jnp.maximum(top, turn(top, 8))
    largest = jnp.maximum(largest, turn(largest, 16))
    total = total * jnp.exp(top - largest)
    total = total + turn(total, 8)
    total = total + turn(total, 16)
    evidence = largest + jnp.log(total)
    for i in range(4):
        spot = jnp.logical_and(place == zl, lane == y * 32 + core * 4 + i)
        ev_ref[i] = jnp.sum(jnp.where(spot, evidence, 0.0))
    for g in range(4):
        post[:, g * 128 : (g + 1) * 128] = (
            jnp.exp(pscore[g] - evidence[g : g + 1, :]) * 2048.0
        ).astype(BF16)

    def copy_a(c):
        return send(part[c].at[2 * x2], from_a[c], a_s.at[c], a_r.at[c], right)

    def copy_b(c):
        return send(part[c].at[2 * x2 + 1], from_b[c], b_s.at[c], b_r.at[c], left)

    def copy_p(c):
        return send(part[c].at[pl.ds(2 * xp, 2)], from_p[c], p_s.at[c], p_r.at[c], right)

    def copy_m(c):
        return send(part[c].at[pl.ds(2 * xm, 2)], from_m[c], m_s.at[c], m_r.at[c], left)

    def copy_w(c, k):
        return send(
            zsend[c].at[k], zrecv[c].at[core], w_s.at[c, k], w_r.at[c, core], across[k]
        )

    def arrived_w(c, half):
        return send(zsend[c].at[0], zrecv[c].at[half], w_s.at[c, 0], w_r.at[c, half], across[0])

    def copy_f(c):
        other = pl.ds(pl.multiple_of((1 - core) * 8, 8), 8)
        return send(keep[c].at[other], fin[c], f_s.at[c], f_r.at[c], peer)

    def project(c):
        sums = jnp.dot(
            post[...], prep[:, STARTS[c] * 256 : STARTS[c + 1] * 256], preferred_element_type=F32
        ).astype(BF16)
        for i in range(8):
            part[c][i] = sums[16 * i : 16 * i + 16]
        copy_a(c).start()
        copy_b(c).start()

    def add(into, *others_):
        value = into.astype(F32)
        for other in others_:
            value = value + other.astype(F32)
        return value

    def pass_on(c):
        copy_a(c).wait_recv()
        part[c][2 * xp] = add(part[c][2 * xp], from_a[c][...]).astype(BF16)
        copy_p(c).start()
        copy_b(c).wait_recv()
        part[c][2 * xm + 1] = add(part[c][2 * xm + 1], from_b[c][...]).astype(BF16)
        copy_m(c).start()

    def collect(c):
        half = SIZES[c] * LANES
        copy_p(c).wait_recv()
        copy_m(c).wait_recv()
        far = 1 - zh
        away = add(part[c][2 * x + far], from_p[c][far], from_m[c][far])
        for k in range(2):
            rows = away[8 * k : 8 * k + 8]
            zsend[c][k] = jnp.concatenate([rows[:, :half], rows[:, half:]], axis=0).astype(BF16)
            copy_w(c, k).start()
        keep[c][...] = add(part[c][2 * x + zh], from_p[c][zh], from_m[c][zh])
        copy_f(c).start()

    def complete(c):
        for half in range(2):
            arrived_w(c, half).wait_recv()
        copy_f(c).wait_recv()
        here = keep[c][pl.ds(pl.multiple_of(core * 8, 8), 8), :]
        for half, near in ((core, here), (1 - core, fin[c][...])):
            rows = zrecv[c][half].astype(F32)
            value = near + jnp.concatenate([rows[0:8], rows[8:16]], axis=1)
            for s in range(SIZES[c]):
                at = pl.ds((STARTS[c] + s) * LANES, LANES)
                for k in range(2):
                    out_ref[half, :, k, at] = value[:, s * 256 + k * 128 : s * 256 + k * 128 + 128]
            out_copy(c, half).start()

    def out_copy(c, half):
        skip = 1 if c == 0 else 0
        count = (SIZES[c] - skip) * LANES
        start = (STARTS[c] + skip) * LANES
        return pltpu.make_async_copy(
            out_ref.at[half, :, :, pl.ds(start, count)],
            out_hbm.at[:, :, pl.ds(pl.multiple_of(half * SHIFT + start, LANES), count)],
            out_sem.at[half, c],
        )

    first_tile = pltpu.make_async_copy(
        out_ref.at[0, :, :, pl.ds(0, LANES)], out_hbm.at[:, :, pl.ds(0, LANES)], loc_sem.at[5]
    )

    for c in range(CHUNKS):
        project(c)
    for c in range(CHUNKS):
        pass_on(c)
    for c in range(CHUNKS):
        collect(c)
        if c >= 2:
            complete(c - 2)
        if c == 2:
            first_tile.start()
    complete(CHUNKS - 2)
    complete(CHUNKS - 1)

    first_tile.wait()
    for c in range(CHUNKS):
        for half in range(2):
            out_copy(c, half).wait()

    pmeta_copy.wait_send()
    pair_copy.wait_send()
    praw_copy.wait_send()
    for copy in meta_copies + stat_copies + sc_copies + y_up + y_down + fwd_up + fwd_down:
        copy.wait_send()
    for n in range(8):
        pl.when(goes_right[n // 2])(lambda n=n: z_right[n].wait_send())
        pl.when(goes_left[n // 2])(lambda n=n: z_left[n].wait_send())

    for c in range(CHUNKS):
        for copy in (copy_a, copy_b, copy_p, copy_m, copy_f):
            copy(c).wait_send()
        for k in range(2):
            copy_w(c, k).wait_send()


def per_device(images, projections, ctf_table, noise_weight, shifts, defocus):
    local = images.shape[0]
    pixels = images.shape[2]
    proj = projections.transpose(1, 0, 2).reshape(128, pixels)
    angles = np.arange(KY) * (2.0 * math.pi / KY)
    trig = np.concatenate([np.tile(np.cos(angles), (8, 1)), np.tile(np.sin(angles), (8, 1))])
    trig = jnp.asarray(trig.astype(np.float32))
    hbm = pl.BlockSpec(memory_space=pl.ANY)
    smem = pl.BlockSpec(memory_space=pltpu.SMEM)
    dma = pltpu.SemaphoreType.DMA
    sems = [dma((6,)), dma((3,)), dma((3,)), dma((15,)), dma((15,)), dma((15,)), dma((15,))]
    sems += [dma((16,)), dma((8,))] + [dma((8,))] * 4 + [dma((4,))] * 6 + [dma((CHUNKS,))] * 8 + [dma((CHUNKS, 2))] * 2 + [dma((CHUNKS,))] * 2
    sems += [dma((2, CHUNKS))]
    sums, evidence = pl.pallas_call(
        kernel,
        out_shape=(
            jax.ShapeDtypeStruct((8, 2, pixels), F32),
            jax.ShapeDtypeStruct((local,), F32),
        ),
        in_specs=[hbm, hbm, hbm, hbm, hbm, smem, smem],
        out_specs=(hbm, smem),
        scratch_shapes=[
            pltpu.VMEM((local, 2, pixels), BF16),
            pltpu.VMEM((65, LANES), F32),
            pltpu.VMEM((16, LANES), F32),
            pltpu.VMEM((2, 8, 2, HALF), F32),
            pltpu.VMEM((16, 65 * LANES), BF16),
            pltpu.VMEM((16, LANES), BF16),
            pltpu.VMEM((16, HALF), BF16),
            pltpu.VMEM((16, LANES), BF16),
            pltpu.VMEM((BLOCKS, 16, LANES), BF16),
            pltpu.VMEM((BLOCKS, 16, HALF), BF16),
            pltpu.VMEM((2, 128, HALF), BF16),
            pltpu.VMEM((64, HALF), F32),
            pltpu.VMEM((2 * HALF, 128), BF16),
            pltpu.VMEM((64, 128), F32),
            pltpu.VMEM((128, 128), F32),
            pltpu.VMEM((128, 2 * LANES), F32),
            pltpu.VMEM((128, HALF), F32),
            pltpu.VMEM((TILES, 8, LANES), jnp.int32),
            pltpu.VMEM((BLOCKS * 32, 2 * HALF), BF16),
            pltpu.VMEM((4, 128, 128), F32),
            pltpu.VMEM((4, 128, 128), F32),
            pltpu.VMEM((BLOCKS, 16, LANES), F32),
            pltpu.VMEM((128, 512), BF16),
            [pltpu.VMEM((8, 16, 256 * t), BF16) for t in SIZES],
            [pltpu.VMEM((16, 256 * t), BF16) for t in SIZES],
            [pltpu.VMEM((16, 256 * t), BF16) for t in SIZES],
            [pltpu.VMEM((2, 16, 256 * t), BF16) for t in SIZES],
            [pltpu.VMEM((2, 16, 256 * t), BF16) for t in SIZES],
            [pltpu.VMEM((2, 16, 128 * t), BF16) for t in SIZES],
            [pltpu.VMEM((2, 16, 128 * t), BF16) for t in SIZES],
            [pltpu.VMEM((16, 256 * t), F32) for t in SIZES],
            [pltpu.VMEM((8, 256 * t), F32) for t in SIZES],
            *sems,
        ],
        compiler_params=pltpu.CompilerParams(
            collective_id=0, has_side_effects=True, vmem_limit_bytes=56 * 1024 * 1024
        ),
    )(
        images, proj, ctf_table, noise_weight.reshape(65, LANES), trig,
        shifts.transpose(0, 2, 1), defocus,
    )
    return evidence, sums


def solution(mesh):
    in_specs = (
        P(("img", "ori"), None, None),
        P("ori", None, None),
        P(),
        P(),
        P(("img", "ori"), None, None),
        P(("img", "ori")),
    )
    out_specs = (P(("img", "ori")), P(("ori", "img"), None, None))
    return jax.shard_map(
        per_device, mesh=mesh, in_specs=in_specs, out_specs=out_specs, check_vma=False
    )
```

```python
import math

import jax
import jax.numpy as jnp
import numpy as np
from jax import lax
from jax.experimental import pallas as pl
from jax.experimental.pallas import tpu as pltpu
from jax.sharding import PartitionSpec as P

KY = 128
KX = 65
LANES = 128
NX, NZ, NY = 4, 4, 4
BLOCKS = NZ * NY
TRANS = 4
TILES = 33
HALF = TILES * LANES
SHIFT = 32 * LANES
HALF_A = 17 * LANES
SIZES = (5, 7, 8, 8, 5)
STARTS = (0, 5, 12, 20, 28, 33)
CHUNKS = len(SIZES)
OTHERS = [(dz, dy) for dz in range(NZ) for dy in range(NY) if (dz, dy) != (0, 0)]
F32 = jnp.float32
BF16 = jnp.bfloat16
HI = lax.Precision.HIGHEST


def kernel(
    img_hbm, proj_ref, ctf_ref, noise_hbm, trig_hbm, shift_ref, class_ref,
    out_hbm, ev_ref,
    img_ref, noise_ref, trig_ref, out_ref,
    placed, ometa, pair, pmeta, smeta, gath, praw, ctfh, weights, norms, normrows, onehot, ctfrows, vtab, prep,
    score, pscore, stats, post, part, from_a, from_b, from_p, from_m, zsend, zrecv, keep, fsend, fin,
    loc_sem, core_s, core_r, meta_s, meta_r, stat_s, stat_r, z_s, z_r,
    yp_s, ym_s, yl_r, yr_r, fa_s, fb_s, fa_r, fb_r, sc_s, sc_r,
    a_s, b_s, a_r, b_r, p_s, m_s, p_r, m_r, w_s, w_r, f_s, f_r, out_sem,
):
    img = lax.axis_index("img")
    ori = lax.axis_index("ori")
    x, zh = img // 2, img % 2
    core, y, zl = ori % 2, (ori // 2) % 4, ori // 8
    xp, xm, x2 = (x + 1) % 4, (x + 3) % 4, (x + 2) % 4
    yp, ym, y2 = (y + 1) % 4, (y + 3) % 4, (y + 2) % 4
    own = zl * 4 + y

    def dev(x_=x, zh_=zh, zl_=zl, y_=y, core_=core):
        return (x_ * 2 + zh_, (zl_ * 4 + y_) * 2 + core_)

    def send(src, dst, ss, rs, target):
        return pltpu.make_async_remote_copy(
            src_ref=src, dst_ref=dst, send_sem=ss, recv_sem=rs,
            device_id=target, device_id_type=pl.DeviceIdType.MESH,
        )

    peer = dev(core_=1 - core)
    others = [dev(zl_=(zl + dz) % 4, y_=(y + dy) % 4) for dz, dy in OTHERS]
    right, left = dev(x_=xp), dev(x_=xm)
    up, down = dev(y_=yp), dev(y_=ym)
    across = [dev(zh_=1 - zh, core_=k) for k in range(2)]

    img_copy = pltpu.make_async_copy(img_hbm, img_ref, loc_sem.at[2])
    noise_copy = pltpu.make_async_copy(noise_hbm, noise_ref, loc_sem.at[3])
    trig_copy = pltpu.make_async_copy(trig_hbm, trig_ref, loc_sem.at[4])
    img_copy.start()
    barrier = pltpu.get_barrier_semaphore()
    greeted = [peer, *others, right, left, *across]
    for target in greeted:
        pl.semaphore_signal(barrier, inc=1, device_id=target, device_id_type=pl.DeviceIdType.MESH)

    mine = pl.ds(pl.multiple_of(core * SHIFT, LANES), HALF)
    theirs = pl.ds(pl.multiple_of((1 - core) * SHIFT, LANES), HALF)
    ctf_copy = pltpu.make_async_copy(ctf_ref.at[:, mine], ctfh, loc_sem.at[0])
    proj_copy = pltpu.make_async_copy(proj_ref.at[:, mine], praw.at[core], loc_sem.at[1])
    ctf_copy.start()
    proj_copy.start()
    noise_copy.start()
    trig_copy.start()

    lane = lax.broadcasted_iota(jnp.int32, (8, LANES), 1)
    place = lax.broadcasted_iota(jnp.int32, (8, LANES), 0)

    def lay_out(s, carry):
        cols = pl.ds(pl.multiple_of(s * 5 * LANES, LANES), 5 * LANES)
        at = lax.broadcasted_iota(jnp.int32, (8, 5 * LANES), 0)
        real = jnp.zeros((8, 5 * LANES), F32)
        imag = jnp.zeros((8, 5 * LANES), F32)
        for i in range(4):
            both = img_ref[i, :, cols].astype(F32)
            here = at == i + 4 * core
            real = jnp.where(here, both[0:1], real)
            imag = jnp.where(here, both[1:2], imag)
        placed[:, cols] = jnp.concatenate([real, imag], axis=0).astype(BF16)
        return carry

    img_copy.wait()
    lax.fori_loop(0, 13, lay_out, 0)
    meta = jnp.zeros((8, LANES), jnp.int32)
    for i in range(4):
        row = place == i + 4 * core
        for t in range(TRANS):
            for k in range(2):
                spot = jnp.logical_and(row, lane == 2 * t + k)
                meta = jnp.where(spot, shift_ref[i, k, t], meta)
        meta = jnp.where(jnp.logical_and(row, lane == 8), class_ref[i], meta)
    meta = meta.astype(F32)
    ometa[...] = jnp.concatenate([meta, jnp.zeros_like(meta)], axis=0).astype(BF16)

    pl.semaphore_wait(barrier, len(greeted))

    pair_copy = send(placed.at[:, theirs], pair, core_s.at[0], core_r.at[0], peer)
    pmeta_copy = send(ometa, pmeta, core_s.at[1], core_r.at[1], peer)
    praw_copy = send(proj_ref.at[:, theirs], praw.at[core], core_s.at[2], core_r.at[2], peer)
    pmeta_copy.start()
    pair_copy.start()

    pmeta_copy.wait_recv()
    smeta[own] = ometa[...] + pmeta[...]
    meta_copies = [
        send(smeta.at[own], smeta.at[own], meta_s.at[n], meta_r.at[n], target)
        for n, target in enumerate(others)
    ]
    for copy in meta_copies:
        copy.start()

    pair_copy.wait_recv()
    gath[own] = placed[:, mine] + pair[...]

    b0, b1 = zl % 2, zl // 2

    def pick(table):
        low = (1 - b0) * table[0] + b0 * table[1]
        high = (1 - b0) * table[2] + b0 * table[3]
        return (1 - b1) * low + b1 * high

    order = [zl, pick([1, 0, 3, 2]), pick([2, 2, 1, 1]), pick([3, 3, 0, 0])]

    halves = (pl.ds(0, HALF_A), pl.ds(HALF_A, HALF - HALF_A))

    def same(b, h, ss, rs, target):
        ref = gath.at[b, :, halves[h]]
        return send(ref, ref, ss, rs, target)

    above, below = dev(zl_=zl + 1), dev(zl_=zl - 1)
    goes_right = [zl < 3] + [jnp.logical_and(order[q] < zl, zl < 3) for q in (1, 2, 3)]
    goes_left = [zl > 0] + [jnp.logical_and(order[q] > zl, zl > 0) for q in (1, 2, 3)]
    z_right, z_left, y_up, y_down, fwd_up, fwd_down = [], [], [], [], [], []
    for q in range(4):
        for h in range(2):
            n, came = 2 * q + h, z_r.at[order[q] * 2 + h]
            b = order[q] * 4 + y
            z_right.append(same(b, h, z_s.at[n], came, above))
            z_left.append(same(b, h, z_s.at[8 + n], came, below))
            y_up.append(same(b, h, yp_s.at[n], yl_r.at[n], up))
            y_down.append(same(b, h, ym_s.at[n], yr_r.at[n], down))
        fwd_up.append(same(order[q] * 4 + ym, 0, fa_s.at[q], fa_r.at[q], up))
        fwd_down.append(same(order[q] * 4 + yp, 1, fb_s.at[q], fb_r.at[q], down))

    def launch(q, h):
        n = 2 * q + h
        pl.when(goes_right[q])(lambda: z_right[n].start())
        pl.when(goes_left[q])(lambda: z_left[n].start())
        y_up[n].start()
        y_down[n].start()

    launch(0, 0)
    launch(0, 1)
    praw_copy.start()

    def fill_rows(s, carry):
        p = (s + 32 * core) * LANES + lane
        after = lax.shift_right_logical((p + LANES) * 64528, 22)
        vtab[s] = after - lax.shift_right_logical(p * 64528, 22)
        return carry

    lax.fori_loop(0, TILES, fill_rows, 0)
    top_row = lax.shift_right_logical((32 * core * LANES + lane) * 64528, 22)

    def pieces(value):
        one = value.astype(BF16)
        rest = value - one.astype(F32)
        two = rest.astype(BF16)
        three = (rest - two.astype(F32)).astype(BF16)
        return one, two, three

    def fill_ctf(s, carry):
        cols = pl.ds(pl.multiple_of(s * 1408, 1408), 1408)
        one, two, three = pieces(ctfh[:, cols])
        ctfrows[:, cols] = jnp.dot(
            onehot[...].astype(BF16),
            jnp.concatenate([one, two, three, one], axis=0),
            preferred_element_type=F32,
        )
        return carry


    def weigh(n, total):
        wide = pl.ds(pl.multiple_of(n * 384, 384), 384)
        raw = [praw[0, :, wide], praw[1, :, wide]]
        ctfs = ctfh[:, wide]
        noises = [noise_ref[pl.ds(core * 32 + 3 * n + i, 1), :] for i in range(3)]
        counted = 1 - core * (1 - jnp.minimum(n, 1))
        noises[0] = noises[0] * counted.astype(F32)
        turned = []
        for i in range(3):
            tile = slice(i * LANES, (i + 1) * LANES)
            parts = [r[:, tile].astype(F32).reshape(2, 8, 1, 8, LANES) for r in raw]
            both = jnp.concatenate(parts, axis=2).reshape(2, 128, LANES)
            scaled = (both * noises[i][None]).astype(BF16)
            turned += [scaled[0].T, scaled[1].T]
            power = (both[0] * both[0] + both[1] * both[1]).T
            ctf = ctfs[:, tile]
            p1, p2, p3 = pieces(power)
            c1, c2, c3 = pieces(ctf * ctf * noises[i])
            total = total + jnp.dot(
                jnp.concatenate([c1, c1, c1, c2, c2, c3], axis=1),
                jnp.concatenate([p1, p2, p3, p1, p2, p1], axis=0),
                preferred_element_type=F32,
            )
        weights[pl.ds(pl.multiple_of(n * 768, 768), 768), :] = jnp.concatenate(turned, axis=0)
        return total

    def prepare(b):
        meta = smeta[b].astype(F32)[0:8, :].astype(jnp.int32)

        cosine, sine = trig_ref[0:8, :], trig_ref[8:16, :]

        def wave(steps):
            index = steps & (KY - 1)
            return (
                jnp.take_along_axis(cosine, index, axis=1),
                jnp.take_along_axis(sine, index, axis=1),
            )

        begin, one_row, two_rows = [], [], []
        for t in range(TRANS):
            sx = meta[:, 2 * t : 2 * t + 1]
            sy = meta[:, 2 * t + 1 : 2 * t + 2]
            slope = jnp.broadcast_to(sy - KX * sx, (8, LANES))
            begin.append(wave(lane * sx + top_row * slope))
            one_row.append(wave(slope))
            two_rows.append(wave(2 * slope))

        def body(n, carry):
            phases, total = carry
            wide = pl.ds(pl.multiple_of(n * 384, 384), 384)
            blocks = gath[b, :, wide].astype(F32)
            ctfs = ctfrows[pl.ds(pl.multiple_of(b * 8, 8), 8), wide]
            singles = [vtab[3 * n + i] == 1 for i in range(3)]
            rows = [[], []]
            for i in range(3):
                tile = slice(i * LANES, (i + 1) * LANES)
                ctf = ctfs[:, tile]
                real, imag = blocks[0:8, tile] * ctf, blocks[8:16, tile] * ctf
                reals, imags, later = [], [], []
                for t in range(TRANS):
                    c, si = phases[t]
                    reals.append(real * c + imag * si)
                    imags.append(imag * c - real * si)
                    mc = jnp.where(singles[i], one_row[t][0], two_rows[t][0])
                    ms = jnp.where(singles[i], one_row[t][1], two_rows[t][1])
                    later.append((c * mc - si * ms, si * mc + c * ms))
                phases = tuple(later)
                for h in range(2):
                    for values in (reals, imags):
                        pair_ = jnp.concatenate(values[2 * h : 2 * h + 2], axis=0)
                        rows[h].append(pair_.astype(BF16))
            steps = pl.ds(pl.multiple_of(n * 768, 768), 768)
            made = jnp.concatenate([jnp.concatenate(r, axis=1) for r in rows], axis=0)
            total = total + jnp.dot(made, weights[steps, :], preferred_element_type=F32)
            prep[pl.ds(pl.multiple_of(b * 32, 32), 32), steps] = made
            return phases, total

        start = (tuple(begin), jnp.zeros((32, LANES), F32))
        _, cross = lax.fori_loop(0, TILES // 3, body, start, unroll=11)
        norm = normrows[pl.ds(pl.multiple_of(b * 8, 8), 8), :]
        at = pl.ds(pl.multiple_of((b % 4) * 32, 32), 32)
        score[b // 4, at, :] = cross - jnp.concatenate([norm] * TRANS, axis=0)

    sc_copies = [
        send(score.at[order[q]], pscore.at[order[q]], sc_s.at[q], sc_r.at[q], peer)
        for q in range(4)
    ]

    stats[own] = jnp.zeros((16, LANES), F32)

    def summarise(q):
        sc_copies[q].wait_recv()
        g = order[q]
        whole = (score[g] + pscore[g]).T
        pscore[g] = whole
        top = jnp.max(whole, axis=0, keepdims=True)
        stats[own, pl.ds(g, 1), :] = top
        stats[own, pl.ds(8 + g, 1), :] = jnp.sum(jnp.exp(whole - top), axis=0, keepdims=True)

    def finish(q):
        fwd_up[q].wait_recv()
        fwd_down[q].wait_recv()
        prepare(order[q] * 4 + y2)
        sc_copies[q].start()

    def arrive(q, h):
        z_right[2 * q + h].wait_recv()
        launch(q, h)

    def forward(q, h):
        if h == 0:
            y_up[2 * q].wait_recv()
            fwd_up[q].start()
        else:
            y_down[2 * q + 1].wait_recv()
            fwd_down[q].start()

    def prepare_three(q):
        y_up[2 * q + 1].wait_recv()
        y_down[2 * q].wait_recv()

        def three(i, carry):
            prepare(order[q] * 4 + (y + 3 + i) % 4)
            return carry

        lax.fori_loop(0, 3, three, 0)

    ctf_copy.wait()
    for copy in meta_copies:
        copy.wait_recv()

    lane2 = lax.broadcasted_iota(jnp.int32, (8, 256), 1)

    def fill_onehot(b, carry):
        classes = smeta[b].astype(F32)[0:8, 8:9].astype(jnp.int32)
        hit = jnp.logical_and(lane2 % 64 == classes, lane2 < 192)
        onehot[pl.ds(pl.multiple_of(b * 8, 8), 8), :] = hit.astype(F32)
        return carry

    lax.fori_loop(0, BLOCKS, fill_onehot, 0)
    lax.fori_loop(0, 3, fill_ctf, 0)

    arrive(1, 0)
    forward(0, 0)
    noise_copy.wait()
    trig_copy.wait()
    proj_copy.wait()
    praw_copy.wait_recv()
    half_norms = lax.fori_loop(0, 4, weigh, jnp.zeros((64, 128), F32), unroll=4)
    arrive(1, 1)
    forward(0, 1)
    half_norms = lax.fori_loop(4, 6, weigh, half_norms, unroll=2)
    arrive(2, 0)
    half_norms = lax.fori_loop(6, 9, weigh, half_norms, unroll=3)
    arrive(2, 1)
    forward(1, 0)
    half_norms = lax.fori_loop(9, 11, weigh, half_norms, unroll=2)
    norms[...] = 0.5 * half_norms
    normrows[...] = jnp.dot(
        onehot[:, 0:64], norms[...], precision=HI, preferred_element_type=F32
    )
    forward(1, 1)
    prepare_three(0)
    arrive(3, 0)
    finish(0)
    arrive(3, 1)
    forward(2, 0)
    prepare_three(1)
    forward(2, 1)
    forward(3, 0)
    finish(1)
    summarise(0)
    prepare_three(2)
    forward(3, 1)
    finish(2)
    summarise(1)
    prepare_three(3)
    finish(3)
    summarise(2)
    summarise(3)

    stat_copies = [
        send(stats.at[own], stats.at[own], stat_s.at[n], stat_r.at[n], target)
        for n, target in enumerate(others)
    ]
    for copy in stat_copies:
        copy.start()
    for copy in stat_copies:
        copy.wait_recv()
    tops = [stats[b, 0:8, :] for b in range(BLOCKS)]
    top = tops[0]
    for b in range(1, BLOCKS):
        top = jnp.maximum(top, tops[b])
    total = jnp.zeros((8, LANES), F32)
    for b in range(BLOCKS):
        total += stats[b, 8:16, :] * jnp.exp(tops[b] - top)
    held = lax.broadcasted_iota(jnp.int32, (8, LANES), 1) % 32

    def turn(value, by):
        inside = pltpu.roll(value, by, 1)
        wrapped = pltpu.roll(value, by + LANES - 32, 1)
        return jnp.where(held >= by, inside, wrapped)

    largest = jnp.maximum(top, turn(top, 8))
    largest = jnp.maximum(largest, turn(largest, 16))
    total = total * jnp.exp(top - largest)
    total = total + turn(total, 8)
    total = total + turn(total, 16)
    evidence = largest + jnp.log(total)
    for i in range(4):
        spot = jnp.logical_and(place == zl, lane == y * 32 + core * 4 + i)
        ev_ref[i] = jnp.sum(jnp.where(spot, evidence, 0.0))
    for g in range(4):
        post[:, g * 128 : (g + 1) * 128] = (
            jnp.exp(pscore[g] - evidence[g : g + 1, :]) * 2048.0
        ).astype(BF16)

    def copy_a(c):
        return send(part[c].at[2 * x2], from_a[c], a_s.at[c], a_r.at[c], right)

    def copy_b(c):
        return send(part[c].at[2 * x2 + 1], from_b[c], b_s.at[c], b_r.at[c], left)

    def copy_p(c):
        return send(part[c].at[pl.ds(2 * xp, 2)], from_p[c], p_s.at[c], p_r.at[c], right)

    def copy_m(c):
        return send(part[c].at[pl.ds(2 * xm, 2)], from_m[c], m_s.at[c], m_r.at[c], left)

    def copy_w(c, k):
        return send(
            zsend[c].at[k], zrecv[c].at[core], w_s.at[c, k], w_r.at[c, core], across[k]
        )

    def arrived_w(c, half):
        return send(zsend[c].at[0], zrecv[c].at[half], w_s.at[c, 0], w_r.at[c, half], across[0])

    def copy_f(c):
        return send(fsend[c], fin[c], f_s.at[c], f_r.at[c], peer)

    def project(c):
        sums = jnp.dot(
            post[...], prep[:, STARTS[c] * 256 : STARTS[c + 1] * 256], preferred_element_type=F32
        ).astype(BF16)
        for i in range(8):
            part[c][i] = sums[16 * i : 16 * i + 16]
        copy_a(c).start()
        copy_b(c).start()

    def add(into, *others_):
        value = into.astype(F32)
        for other in others_:
            value = value + other.astype(F32)
        return value

    def pass_on(c):
        copy_a(c).wait_recv()
        part[c][2 * xp] = add(part[c][2 * xp], from_a[c][...]).astype(BF16)
        copy_p(c).start()
        copy_b(c).wait_recv()
        part[c][2 * xm + 1] = add(part[c][2 * xm + 1], from_b[c][...]).astype(BF16)
        copy_m(c).start()

    def collect(c):
        half = SIZES[c] * LANES
        copy_p(c).wait_recv()
        copy_m(c).wait_recv()
        far = 1 - zh
        away = add(part[c][2 * x + far], from_p[c][far], from_m[c][far])
        for k in range(2):
            rows = away[8 * k : 8 * k + 8]
            zsend[c][k] = jnp.concatenate([rows[:, :half], rows[:, half:]], axis=0).astype(BF16)
            copy_w(c, k).start()
        near = add(part[c][2 * x + zh], from_p[c][zh], from_m[c][zh])
        keep[c][...] = near
        rows = jnp.where(core == 0, near[8:16], near[0:8])
        fsend[c][...] = jnp.concatenate([rows[:, :half], rows[:, half:]], axis=0).astype(BF16)
        copy_f(c).start()

    def complete(c):
        for half in range(2):
            arrived_w(c, half).wait_recv()
        copy_f(c).wait_recv()
        here = keep[c][pl.ds(pl.multiple_of(core * 8, 8), 8), :]
        def unfold(rows):
            rows = rows.astype(F32)
            return jnp.concatenate([rows[0:8], rows[8:16]], axis=1)

        for half, near in ((core, here), (1 - core, unfold(fin[c][...]))):
            value = near + unfold(zrecv[c][half])
            for s in range(SIZES[c]):
                at = pl.ds((STARTS[c] + s) * LANES, LANES)
                for k in range(2):
                    out_ref[half, :, k, at] = value[:, s * 256 + k * 128 : s * 256 + k * 128 + 128]
            out_copy(c, half).start()

    def out_copy(c, half):
        skip = 1 if c == 0 else 0
        count = (SIZES[c] - skip) * LANES
        start = (STARTS[c] + skip) * LANES
        return pltpu.make_async_copy(
            out_ref.at[half, :, :, pl.ds(start, count)],
            out_hbm.at[:, :, pl.ds(pl.multiple_of(half * SHIFT + start, LANES), count)],
            out_sem.at[half, c],
        )

    first_tile = pltpu.make_async_copy(
        out_ref.at[0, :, :, pl.ds(0, LANES)], out_hbm.at[:, :, pl.ds(0, LANES)], loc_sem.at[5]
    )

    for c in range(CHUNKS):
        project(c)
    for c in range(CHUNKS):
        pass_on(c)
    for c in range(CHUNKS):
        collect(c)
        if c >= 2:
            complete(c - 2)
        if c == 2:
            first_tile.start()
    complete(CHUNKS - 2)
    complete(CHUNKS - 1)

    first_tile.wait()
    for c in range(CHUNKS):
        for half in range(2):
            out_copy(c, half).wait()

    pmeta_copy.wait_send()
    pair_copy.wait_send()
    praw_copy.wait_send()
    for copy in meta_copies + stat_copies + sc_copies + y_up + y_down + fwd_up + fwd_down:
        copy.wait_send()
    for n in range(8):
        pl.when(goes_right[n // 2])(lambda n=n: z_right[n].wait_send())
        pl.when(goes_left[n // 2])(lambda n=n: z_left[n].wait_send())

    for c in range(CHUNKS):
        for copy in (copy_a, copy_b, copy_p, copy_m, copy_f):
            copy(c).wait_send()
        for k in range(2):
            copy_w(c, k).wait_send()


def per_device(images, projections, ctf_table, noise_weight, shifts, defocus):
    local = images.shape[0]
    pixels = images.shape[2]
    proj = projections.transpose(1, 0, 2).reshape(128, pixels)
    angles = np.arange(KY) * (2.0 * math.pi / KY)
    trig = np.concatenate([np.tile(np.cos(angles), (8, 1)), np.tile(np.sin(angles), (8, 1))])
    trig = jnp.asarray(trig.astype(np.float32))
    hbm = pl.BlockSpec(memory_space=pl.ANY)
    smem = pl.BlockSpec(memory_space=pltpu.SMEM)
    dma = pltpu.SemaphoreType.DMA
    sems = [dma((6,)), dma((3,)), dma((3,)), dma((15,)), dma((15,)), dma((15,)), dma((15,))]
    sems += [dma((16,)), dma((8,))] + [dma((8,))] * 4 + [dma((4,))] * 6 + [dma((CHUNKS,))] * 8 + [dma((CHUNKS, 2))] * 2 + [dma((CHUNKS,))] * 2
    sems += [dma((2, CHUNKS))]
    sums, evidence = pl.pallas_call(
        kernel,
        out_shape=(
            jax.ShapeDtypeStruct((8, 2, pixels), F32),
            jax.ShapeDtypeStruct((local,), F32),
        ),
        in_specs=[hbm, hbm, hbm, hbm, hbm, smem, smem],
        out_specs=(hbm, smem),
        scratch_shapes=[
            pltpu.VMEM((local, 2, pixels), BF16),
            pltpu.VMEM((65, LANES), F32),
            pltpu.VMEM((16, LANES), F32),
            pltpu.VMEM((2, 8, 2, HALF), F32),
            pltpu.VMEM((16, 65 * LANES), BF16),
            pltpu.VMEM((16, LANES), BF16),
            pltpu.VMEM((16, HALF), BF16),
            pltpu.VMEM((16, LANES), BF16),
            pltpu.VMEM((BLOCKS, 16, LANES), BF16),
            pltpu.VMEM((BLOCKS, 16, HALF), BF16),
            pltpu.VMEM((2, 128, HALF), BF16),
            pltpu.VMEM((64, HALF), F32),
            pltpu.VMEM((2 * HALF, 128), BF16),
            pltpu.VMEM((64, 128), F32),
            pltpu.VMEM((128, 128), F32),
            pltpu.VMEM((128, 2 * LANES), F32),
            pltpu.VMEM((128, HALF), F32),
            pltpu.VMEM((TILES, 8, LANES), jnp.int32),
            pltpu.VMEM((BLOCKS * 32, 2 * HALF), BF16),
            pltpu.VMEM((4, 128, 128), F32),
            pltpu.VMEM((4, 128, 128), F32),
            pltpu.VMEM((BLOCKS, 16, LANES), F32),
            pltpu.VMEM((128, 512), BF16),
            [pltpu.VMEM((8, 16, 256 * t), BF16) for t in SIZES],
            [pltpu.VMEM((16, 256 * t), BF16) for t in SIZES],
            [pltpu.VMEM((16, 256 * t), BF16) for t in SIZES],
            [pltpu.VMEM((2, 16, 256 * t), BF16) for t in SIZES],
            [pltpu.VMEM((2, 16, 256 * t), BF16) for t in SIZES],
            [pltpu.VMEM((2, 16, 128 * t), BF16) for t in SIZES],
            [pltpu.VMEM((2, 16, 128 * t), BF16) for t in SIZES],
            [pltpu.VMEM((16, 256 * t), F32) for t in SIZES],
            [pltpu.VMEM((16, 128 * t), BF16) for t in SIZES],
            [pltpu.VMEM((16, 128 * t), BF16) for t in SIZES],
            *sems,
        ],
        compiler_params=pltpu.CompilerParams(
            collective_id=0, has_side_effects=True, vmem_limit_bytes=56 * 1024 * 1024
        ),
    )(
        images, proj, ctf_table, noise_weight.reshape(65, LANES), trig,
        shifts.transpose(0, 2, 1), defocus,
    )
    return evidence, sums


def solution(mesh):
    in_specs = (
        P(("img", "ori"), None, None),
        P("ori", None, None),
        P(),
        P(),
        P(("img", "ori"), None, None),
        P(("img", "ori")),
    )
    out_specs = (P(("img", "ori")), P(("ori", "img"), None, None))
    return jax.shard_map(
        per_device, mesh=mesh, in_specs=in_specs, out_specs=out_specs, check_vma=False
    )
```

```python
import math

import jax
import jax.numpy as jnp
import numpy as np
from jax import lax
from jax.experimental import pallas as pl
from jax.experimental.pallas import tpu as pltpu
from jax.sharding import PartitionSpec as P

KY = 128
KX = 65
LANES = 128
NX, NZ, NY = 4, 4, 4
BLOCKS = NZ * NY
TRANS = 4
TILES = 33
HALF = TILES * LANES
SHIFT = 32 * LANES
HALF_A = 17 * LANES
SIZES = (5, 7, 8, 8, 5)
STARTS = (0, 5, 12, 20, 28, 33)
CHUNKS = len(SIZES)
OTHERS = [(dz, dy) for dz in range(NZ) for dy in range(NY) if (dz, dy) != (0, 0)]
F32 = jnp.float32
BF16 = jnp.bfloat16
HI = lax.Precision.HIGHEST


def kernel(
    img_ref, proj_ref, ctf_ref, noise_ref, trig_ref, shift_ref, class_ref,
    out_ref, ev_ref,
    placed, ometa, pair, pmeta, smeta, gath, praw, ctfh, weights, norms, normrows, onehot, ctfrows, vtab, prep,
    score, pscore, stats, post, part, from_a, from_b, from_p, from_m, zsend, zrecv, keep, fin,
    loc_sem, core_s, core_r, meta_s, meta_r, stat_s, stat_r, z_s, z_r,
    yp_s, ym_s, yl_r, yr_r, fa_s, fb_s, fa_r, fb_r, sc_s, sc_r,
    a_s, b_s, a_r, b_r, p_s, m_s, p_r, m_r, w_s, w_r, f_s, f_r,
):
    img = lax.axis_index("img")
    ori = lax.axis_index("ori")
    x, zh = img // 2, img % 2
    core, y, zl = ori % 2, (ori // 2) % 4, ori // 8
    xp, xm, x2 = (x + 1) % 4, (x + 3) % 4, (x + 2) % 4
    yp, ym, y2 = (y + 1) % 4, (y + 3) % 4, (y + 2) % 4
    own = zl * 4 + y

    def dev(x_=x, zh_=zh, zl_=zl, y_=y, core_=core):
        return (x_ * 2 + zh_, (zl_ * 4 + y_) * 2 + core_)

    def send(src, dst, ss, rs, target):
        return pltpu.make_async_remote_copy(
            src_ref=src, dst_ref=dst, send_sem=ss, recv_sem=rs,
            device_id=target, device_id_type=pl.DeviceIdType.MESH,
        )

    peer = dev(core_=1 - core)
    others = [dev(zl_=(zl + dz) % 4, y_=(y + dy) % 4) for dz, dy in OTHERS]
    right, left = dev(x_=xp), dev(x_=xm)
    up, down = dev(y_=yp), dev(y_=ym)
    across = [dev(zh_=1 - zh, core_=k) for k in range(2)]

    barrier = pltpu.get_barrier_semaphore()
    greeted = [peer, *others, right, left, *across]
    for target in greeted:
        pl.semaphore_signal(barrier, inc=1, device_id=target, device_id_type=pl.DeviceIdType.MESH)

    mine = pl.ds(pl.multiple_of(core * SHIFT, LANES), HALF)
    theirs = pl.ds(pl.multiple_of((1 - core) * SHIFT, LANES), HALF)
    ctf_copy = pltpu.make_async_copy(ctf_ref.at[:, mine], ctfh, loc_sem.at[0])
    proj_copy = pltpu.make_async_copy(proj_ref.at[:, mine], praw.at[core], loc_sem.at[1])
    ctf_copy.start()
    proj_copy.start()

    lane = lax.broadcasted_iota(jnp.int32, (8, LANES), 1)
    place = lax.broadcasted_iota(jnp.int32, (8, LANES), 0)

    def lay_out(s, carry):
        cols = pl.ds(pl.multiple_of(s * 5 * LANES, LANES), 5 * LANES)
        at = lax.broadcasted_iota(jnp.int32, (8, 5 * LANES), 0)
        real = jnp.zeros((8, 5 * LANES), F32)
        imag = jnp.zeros((8, 5 * LANES), F32)
        for i in range(4):
            both = img_ref[i, :, cols].astype(F32)
            here = at == i + 4 * core
            real = jnp.where(here, both[0:1], real)
            imag = jnp.where(here, both[1:2], imag)
        placed[:, cols] = jnp.concatenate([real, imag], axis=0).astype(BF16)
        return carry

    lax.fori_loop(0, 13, lay_out, 0)
    meta = jnp.zeros((8, LANES), jnp.int32)
    for i in range(4):
        row = place == i + 4 * core
        for t in range(TRANS):
            for k in range(2):
                spot = jnp.logical_and(row, lane == 2 * t + k)
                meta = jnp.where(spot, shift_ref[i, k, t], meta)
        meta = jnp.where(jnp.logical_and(row, lane == 8), class_ref[i], meta)
    meta = meta.astype(F32)
    ometa[...] = jnp.concatenate([meta, jnp.zeros_like(meta)], axis=0).astype(BF16)

    pl.semaphore_wait(barrier, len(greeted))

    pair_copy = send(placed.at[:, theirs], pair, core_s.at[0], core_r.at[0], peer)
    pmeta_copy = send(ometa, pmeta, core_s.at[1], core_r.at[1], peer)
    praw_copy = send(proj_ref.at[:, theirs], praw.at[core], core_s.at[2], core_r.at[2], peer)
    pmeta_copy.start()
    pair_copy.start()
    praw_copy.start()

    pmeta_copy.wait_recv()
    smeta[own] = ometa[...] + pmeta[...]
    meta_copies = [
        send(smeta.at[own], smeta.at[own], meta_s.at[n], meta_r.at[n], target)
        for n, target in enumerate(others)
    ]
    for copy in meta_copies:
        copy.start()

    pair_copy.wait_recv()
    gath[own] = placed[:, mine] + pair[...]

    b0, b1 = zl % 2, zl // 2

    def pick(table):
        low = (1 - b0) * table[0] + b0 * table[1]
        high = (1 - b0) * table[2] + b0 * table[3]
        return (1 - b1) * low + b1 * high

    order = [zl, pick([1, 0, 3, 2]), pick([2, 2, 1, 1]), pick([3, 3, 0, 0])]

    halves = (pl.ds(0, HALF_A), pl.ds(HALF_A, HALF - HALF_A))

    def same(b, h, ss, rs, target):
        ref = gath.at[b, :, halves[h]]
        return send(ref, ref, ss, rs, target)

    above, below = dev(zl_=zl + 1), dev(zl_=zl - 1)
    goes_right = [zl < 3] + [jnp.logical_and(order[q] < zl, zl < 3) for q in (1, 2, 3)]
    goes_left = [zl > 0] + [jnp.logical_and(order[q] > zl, zl > 0) for q in (1, 2, 3)]
    z_right, z_left, y_up, y_down, fwd_up, fwd_down = [], [], [], [], [], []
    for q in range(4):
        for h in range(2):
            n, came = 2 * q + h, z_r.at[order[q] * 2 + h]
            b = order[q] * 4 + y
            z_right.append(same(b, h, z_s.at[n], came, above))
            z_left.append(same(b, h, z_s.at[8 + n], came, below))
            y_up.append(same(b, h, yp_s.at[n], yl_r.at[n], up))
            y_down.append(same(b, h, ym_s.at[n], yr_r.at[n], down))
        fwd_up.append(same(order[q] * 4 + ym, 0, fa_s.at[q], fa_r.at[q], up))
        fwd_down.append(same(order[q] * 4 + yp, 1, fb_s.at[q], fb_r.at[q], down))

    def launch(q, h):
        n = 2 * q + h
        pl.when(goes_right[q])(lambda: z_right[n].start())
        pl.when(goes_left[q])(lambda: z_left[n].start())
        y_up[n].start()
        y_down[n].start()

    launch(0, 0)
    launch(0, 1)

    def fill_rows(s, carry):
        p = (s + 32 * core) * LANES + lane
        after = lax.shift_right_logical((p + LANES) * 64528, 22)
        vtab[s] = after - lax.shift_right_logical(p * 64528, 22)
        return carry

    lax.fori_loop(0, TILES, fill_rows, 0)
    top_row = lax.shift_right_logical((32 * core * LANES + lane) * 64528, 22)

    def pieces(value):
        one = value.astype(BF16)
        rest = value - one.astype(F32)
        two = rest.astype(BF16)
        three = (rest - two.astype(F32)).astype(BF16)
        return one, two, three

    def fill_ctf(s, carry):
        cols = pl.ds(pl.multiple_of(s * 1408, 1408), 1408)
        one, two, three = pieces(ctfh[:, cols])
        ctfrows[:, cols] = jnp.dot(
            onehot[...].astype(BF16),
            jnp.concatenate([one, two, three, one], axis=0),
            preferred_element_type=F32,
        )
        return carry


    def weigh(n, total):
        wide = pl.ds(pl.multiple_of(n * 384, 384), 384)
        raw = [praw[0, :, wide], praw[1, :, wide]]
        ctfs = ctfh[:, wide]
        noises = [noise_ref[pl.ds(core * 32 + 3 * n + i, 1), :] for i in range(3)]
        counted = 1 - core * (1 - jnp.minimum(n, 1))
        noises[0] = noises[0] * counted.astype(F32)
        turned = []
        for i in range(3):
            tile = slice(i * LANES, (i + 1) * LANES)
            parts = [r[:, tile].astype(F32).reshape(2, 8, 1, 8, LANES) for r in raw]
            both = jnp.concatenate(parts, axis=2).reshape(2, 128, LANES)
            scaled = (both * noises[i][None]).astype(BF16)
            turned += [scaled[0].T, scaled[1].T]
            power = (both[0] * both[0] + both[1] * both[1]).T
            ctf = ctfs[:, tile]
            p1, p2, p3 = pieces(power)
            c1, c2, c3 = pieces(ctf * ctf * noises[i])
            total = total + jnp.dot(
                jnp.concatenate([c1, c1, c1, c2, c2, c3], axis=1),
                jnp.concatenate([p1, p2, p3, p1, p2, p1], axis=0),
                preferred_element_type=F32,
            )
        weights[pl.ds(pl.multiple_of(n * 768, 768), 768), :] = jnp.concatenate(turned, axis=0)
        return total

    def prepare(*bs):
        cosine, sine = trig_ref[0:8, :], trig_ref[8:16, :]

        def wave(steps):
            index = steps & (KY - 1)
            return (
                jnp.take_along_axis(cosine, index, axis=1),
                jnp.take_along_axis(sine, index, axis=1),
            )

        begin, one_row, two_rows = [], [], []
        for b in bs:
            meta = smeta[b].astype(F32)[0:8, :].astype(jnp.int32)
            first_, one, two = [], [], []
            for t in range(TRANS):
                sx = meta[:, 2 * t : 2 * t + 1]
                sy = meta[:, 2 * t + 1 : 2 * t + 2]
                slope = jnp.broadcast_to(sy - KX * sx, (8, LANES))
                first_.append(wave(lane * sx + top_row * slope))
                one.append(wave(slope))
                two.append(wave(2 * slope))
            begin.append(tuple(first_))
            one_row.append(one)
            two_rows.append(two)

        def body(n, carry):
            every, total = carry
            wide = pl.ds(pl.multiple_of(n * 384, 384), 384)
            steps = pl.ds(pl.multiple_of(n * 768, 768), 768)
            singles = [vtab[3 * n + i] == 1 for i in range(3)]
            loaded = [
                (gath[b, :, wide].astype(F32), ctfrows[pl.ds(pl.multiple_of(b * 8, 8), 8), wide])
                for b in bs
            ]
            after, made = [], []
            for k, phases in enumerate(every):
                blocks, ctfs = loaded[k]
                rows = [[], []]
                for i in range(3):
                    tile = slice(i * LANES, (i + 1) * LANES)
                    ctf = ctfs[:, tile]
                    real, imag = blocks[0:8, tile] * ctf, blocks[8:16, tile] * ctf
                    reals, imags, later = [], [], []
                    for t in range(TRANS):
                        c, si = phases[t]
                        reals.append(real * c + imag * si)
                        imags.append(imag * c - real * si)
                        mc = jnp.where(singles[i], one_row[k][t][0], two_rows[k][t][0])
                        ms = jnp.where(singles[i], one_row[k][t][1], two_rows[k][t][1])
                        later.append((c * mc - si * ms, si * mc + c * ms))
                    phases = tuple(later)
                    for h in range(2):
                        for values in (reals, imags):
                            pair_ = jnp.concatenate(values[2 * h : 2 * h + 2], axis=0)
                            rows[h].append(pair_.astype(BF16))
                after.append(phases)
                made += [jnp.concatenate(r, axis=1) for r in rows]
            for k, b in enumerate(bs):
                at = pl.ds(pl.multiple_of(b * 32, 32), 32)
                prep[at, steps] = jnp.concatenate(made[2 * k : 2 * k + 2], axis=0)
            total = total + jnp.dot(
                jnp.concatenate(made, axis=0), weights[steps, :], preferred_element_type=F32
            )
            return tuple(after), total

        start = (tuple(begin), jnp.zeros((32 * len(bs), LANES), F32))
        _, cross = lax.fori_loop(0, TILES // 3, body, start, unroll=11)
        for k, b in enumerate(bs):
            norm = normrows[pl.ds(pl.multiple_of(b * 8, 8), 8), :]
            at = pl.ds(pl.multiple_of((b % 4) * 32, 32), 32)
            score[b // 4, at, :] = cross[32 * k : 32 * k + 32] - jnp.concatenate(
                [norm] * TRANS, axis=0
            )

    sc_copies = [
        send(score.at[order[q]], pscore.at[order[q]], sc_s.at[q], sc_r.at[q], peer)
        for q in range(4)
    ]

    stats[own] = jnp.zeros((16, LANES), F32)

    def summarise(q):
        sc_copies[q].wait_recv()
        g = order[q]
        whole = (score[g] + pscore[g]).T
        pscore[g] = whole
        top = jnp.max(whole, axis=0, keepdims=True)
        stats[own, pl.ds(g, 1), :] = top
        stats[own, pl.ds(8 + g, 1), :] = jnp.sum(jnp.exp(whole - top), axis=0, keepdims=True)

    def sides(q):
        y_up[2 * q + 1].wait_recv()
        y_down[2 * q].wait_recv()
        prepare(order[q] * 4 + ym, order[q] * 4 + yp)

    def farthest(q):
        fwd_up[q].wait_recv()
        fwd_down[q].wait_recv()
        return order[q] * 4 + y2

    def arrive(q, h):
        z_right[2 * q + h].wait_recv()
        launch(q, h)

    def forward(q, h):
        if h == 0:
            y_up[2 * q].wait_recv()
            fwd_up[q].start()
        else:
            y_down[2 * q + 1].wait_recv()
            fwd_down[q].start()

    ctf_copy.wait()
    proj_copy.wait()
    praw_copy.wait_recv()
    half_norms = lax.fori_loop(0, 4, weigh, jnp.zeros((64, 128), F32))
    arrive(1, 0)
    forward(0, 0)
    half_norms = lax.fori_loop(4, 6, weigh, half_norms)
    arrive(1, 1)
    forward(0, 1)

    for copy in meta_copies:
        copy.wait_recv()

    lane2 = lax.broadcasted_iota(jnp.int32, (8, 256), 1)

    def fill_onehot(b, carry):
        classes = smeta[b].astype(F32)[0:8, 8:9].astype(jnp.int32)
        hit = jnp.logical_and(lane2 % 64 == classes, lane2 < 192)
        onehot[pl.ds(pl.multiple_of(b * 8, 8), 8), :] = hit.astype(F32)
        return carry

    lax.fori_loop(0, BLOCKS, fill_onehot, 0)
    lax.fori_loop(0, 3, fill_ctf, 0)

    arrive(2, 0)
    half_norms = lax.fori_loop(6, 9, weigh, half_norms)
    arrive(2, 1)
    forward(1, 0)
    half_norms = lax.fori_loop(9, 11, weigh, half_norms)
    norms[...] = 0.5 * half_norms
    normrows[...] = jnp.dot(
        onehot[:, 0:64], norms[...], precision=HI, preferred_element_type=F32
    )
    forward(1, 1)
    prepare(order[0] * 4 + y, order[1] * 4 + y)
    arrive(3, 0)
    sides(0)
    arrive(3, 1)
    forward(2, 0)
    sides(1)
    forward(2, 1)
    prepare(farthest(0), order[2] * 4 + y)
    sc_copies[0].start()
    forward(3, 0)
    sides(2)
    forward(3, 1)
    prepare(farthest(1), order[3] * 4 + y)
    sc_copies[1].start()
    summarise(0)
    sides(3)
    summarise(1)
    prepare(farthest(2), farthest(3))
    sc_copies[2].start()
    sc_copies[3].start()
    summarise(2)
    summarise(3)

    stat_copies = [
        send(stats.at[own], stats.at[own], stat_s.at[n], stat_r.at[n], target)
        for n, target in enumerate(others)
    ]
    for copy in stat_copies:
        copy.start()
    for copy in stat_copies:
        copy.wait_recv()
    tops = [stats[b, 0:8, :] for b in range(BLOCKS)]
    top = tops[0]
    for b in range(1, BLOCKS):
        top = jnp.maximum(top, tops[b])
    total = jnp.zeros((8, LANES), F32)
    for b in range(BLOCKS):
        total += stats[b, 8:16, :] * jnp.exp(tops[b] - top)
    held = lax.broadcasted_iota(jnp.int32, (8, LANES), 1) % 32

    def turn(value, by):
        inside = pltpu.roll(value, by, 1)
        wrapped = pltpu.roll(value, by + LANES - 32, 1)
        return jnp.where(held >= by, inside, wrapped)

    largest = jnp.maximum(top, turn(top, 8))
    largest = jnp.maximum(largest, turn(largest, 16))
    total = total * jnp.exp(top - largest)
    total = total + turn(total, 8)
    total = total + turn(total, 16)
    evidence = largest + jnp.log(total)
    for i in range(4):
        spot = jnp.logical_and(place == zl, lane == y * 32 + core * 4 + i)
        ev_ref[i] = jnp.sum(jnp.where(spot, evidence, 0.0))
    for g in range(4):
        post[:, g * 128 : (g + 1) * 128] = (
            jnp.exp(pscore[g] - evidence[g : g + 1, :]) * 2048.0
        ).astype(BF16)

    def copy_a(c):
        return send(part[c].at[2 * x2], from_a[c], a_s.at[c], a_r.at[c], right)

    def copy_b(c):
        return send(part[c].at[2 * x2 + 1], from_b[c], b_s.at[c], b_r.at[c], left)

    def copy_p(c):
        return send(part[c].at[pl.ds(2 * xp, 2)], from_p[c], p_s.at[c], p_r.at[c], right)

    def copy_m(c):
        return send(part[c].at[pl.ds(2 * xm, 2)], from_m[c], m_s.at[c], m_r.at[c], left)

    def copy_w(c, k):
        return send(
            zsend[c].at[k], zrecv[c].at[core], w_s.at[c, k], w_r.at[c, core], across[k]
        )

    def arrived_w(c, half):
        return send(zsend[c].at[0], zrecv[c].at[half], w_s.at[c, 0], w_r.at[c, half], across[0])

    def copy_f(c):
        other = pl.ds(pl.multiple_of((1 - core) * 8, 8), 8)
        return send(keep[c].at[other], fin[c], f_s.at[c], f_r.at[c], peer)

    def project(c):
        sums = jnp.dot(
            post[...], prep[:, STARTS[c] * 256 : STARTS[c + 1] * 256], preferred_element_type=F32
        ).astype(BF16)
        for i in range(8):
            part[c][i] = sums[16 * i : 16 * i + 16]
        copy_a(c).start()
        copy_b(c).start()

    def add(into, *others_):
        value = into.astype(F32)
        for other in others_:
            value = value + other.astype(F32)
        return value

    def pass_on(c):
        copy_a(c).wait_recv()
        part[c][2 * xp] = add(part[c][2 * xp], from_a[c][...]).astype(BF16)
        copy_p(c).start()
        copy_b(c).wait_recv()
        part[c][2 * xm + 1] = add(part[c][2 * xm + 1], from_b[c][...]).astype(BF16)
        copy_m(c).start()

    def collect(c):
        half = SIZES[c] * LANES
        copy_p(c).wait_recv()
        copy_m(c).wait_recv()
        far = 1 - zh
        away = add(part[c][2 * x + far], from_p[c][far], from_m[c][far])
        for k in range(2):
            rows = away[8 * k : 8 * k + 8]
            zsend[c][k] = jnp.concatenate([rows[:, :half], rows[:, half:]], axis=0).astype(BF16)
            copy_w(c, k).start()
        keep[c][...] = add(part[c][2 * x + zh], from_p[c][zh], from_m[c][zh])
        copy_f(c).start()

    def complete(c):
        for half in range(2):
            arrived_w(c, half).wait_recv()
        copy_f(c).wait_recv()
        here = keep[c][pl.ds(pl.multiple_of(core * 8, 8), 8), :]
        for half, near in ((core, here), (1 - core, fin[c][...])):
            rows = zrecv[c][half].astype(F32)
            value = near + jnp.concatenate([rows[0:8], rows[8:16]], axis=1)
            for s in range(SIZES[c]):
                at = pl.multiple_of(half * SHIFT + (STARTS[c] + s) * LANES, LANES)
                for k in range(2):
                    out_ref[:, k, pl.ds(at, LANES)] = value[
                        :, s * 256 + k * 128 : s * 256 + k * 128 + 128
                    ]

    for c in range(CHUNKS):
        project(c)
    for c in range(CHUNKS):
        pass_on(c)
    for c in range(CHUNKS):
        collect(c)
        if c >= 2:
            complete(c - 2)
    complete(CHUNKS - 2)
    complete(CHUNKS - 1)

    pmeta_copy.wait_send()
    pair_copy.wait_send()
    praw_copy.wait_send()
    for copy in meta_copies + stat_copies + sc_copies + y_up + y_down + fwd_up + fwd_down:
        copy.wait_send()
    for n in range(8):
        pl.when(goes_right[n // 2])(lambda n=n: z_right[n].wait_send())
        pl.when(goes_left[n // 2])(lambda n=n: z_left[n].wait_send())

    for c in range(CHUNKS):
        for copy in (copy_a, copy_b, copy_p, copy_m, copy_f):
            copy(c).wait_send()
        for k in range(2):
            copy_w(c, k).wait_send()


def per_device(images, projections, ctf_table, noise_weight, shifts, defocus):
    local = images.shape[0]
    pixels = images.shape[2]
    proj = projections.transpose(1, 0, 2).reshape(128, pixels)
    angles = np.arange(KY) * (2.0 * math.pi / KY)
    trig = np.concatenate([np.tile(np.cos(angles), (8, 1)), np.tile(np.sin(angles), (8, 1))])
    trig = jnp.asarray(trig.astype(np.float32))
    vmem = pl.BlockSpec(memory_space=pltpu.VMEM)
    hbm = pl.BlockSpec(memory_space=pl.ANY)
    smem = pl.BlockSpec(memory_space=pltpu.SMEM)
    dma = pltpu.SemaphoreType.DMA
    sems = [dma((2,)), dma((3,)), dma((3,)), dma((15,)), dma((15,)), dma((15,)), dma((15,))]
    sems += [dma((16,)), dma((8,))] + [dma((8,))] * 4 + [dma((4,))] * 6 + [dma((CHUNKS,))] * 8 + [dma((CHUNKS, 2))] * 2 + [dma((CHUNKS,))] * 2
    sums, evidence = pl.pallas_call(
        kernel,
        out_shape=(
            jax.ShapeDtypeStruct((8, 2, pixels), F32),
            jax.ShapeDtypeStruct((local,), F32),
        ),
        in_specs=[vmem, hbm, hbm, vmem, vmem, smem, smem],
        out_specs=(vmem, smem),
        scratch_shapes=[
            pltpu.VMEM((16, 65 * LANES), BF16),
            pltpu.VMEM((16, LANES), BF16),
            pltpu.VMEM((16, HALF), BF16),
            pltpu.VMEM((16, LANES), BF16),
            pltpu.VMEM((BLOCKS, 16, LANES), BF16),
            pltpu.VMEM((BLOCKS, 16, HALF), BF16),
            pltpu.VMEM((2, 128, HALF), BF16),
            pltpu.VMEM((64, HALF), F32),
            pltpu.VMEM((2 * HALF, 128), BF16),
            pltpu.VMEM((64, 128), F32),
            pltpu.VMEM((128, 128), F32),
            pltpu.VMEM((128, 2 * LANES), F32),
            pltpu.VMEM((128, HALF), F32),
            pltpu.VMEM((TILES, 8, LANES), jnp.int32),
            pltpu.VMEM((BLOCKS * 32, 2 * HALF), BF16),
            pltpu.VMEM((4, 128, 128), F32),
            pltpu.VMEM((4, 128, 128), F32),
            pltpu.VMEM((BLOCKS, 16, LANES), F32),
            pltpu.VMEM((128, 512), BF16),
            [pltpu.VMEM((8, 16, 256 * t), BF16) for t in SIZES],
            [pltpu.VMEM((16, 256 * t), BF16) for t in SIZES],
            [pltpu.VMEM((16, 256 * t), BF16) for t in SIZES],
            [pltpu.VMEM((2, 16, 256 * t), BF16) for t in SIZES],
            [pltpu.VMEM((2, 16, 256 * t), BF16) for t in SIZES],
            [pltpu.VMEM((2, 16, 128 * t), BF16) for t in SIZES],
            [pltpu.VMEM((2, 16, 128 * t), BF16) for t in SIZES],
            [pltpu.VMEM((16, 256 * t), F32) for t in SIZES],
            [pltpu.VMEM((8, 256 * t), F32) for t in SIZES],
            *sems,
        ],
        compiler_params=pltpu.CompilerParams(
            collective_id=0, has_side_effects=True, vmem_limit_bytes=34 * 1024 * 1024
        ),
    )(
        images, proj, ctf_table, noise_weight.reshape(65, LANES), trig,
        shifts.transpose(0, 2, 1), defocus,
    )
    return evidence, sums


def solution(mesh):
    in_specs = (
        P(("img", "ori"), None, None),
        P("ori", None, None),
        P(),
        P(),
        P(("img", "ori"), None, None),
        P(("img", "ori")),
    )
    out_specs = (P(("img", "ori")), P(("ori", "img"), None, None))
    return jax.shard_map(
        per_device, mesh=mesh, in_specs=in_specs, out_specs=out_specs, check_vma=False
    )
```

```python
import math

import jax
import jax.numpy as jnp
import numpy as np
from jax import lax
from jax.experimental import pallas as pl
from jax.experimental.pallas import tpu as pltpu
from jax.sharding import PartitionSpec as P

KY = 128
KX = 65
LANES = 128
NX, NZ, NY = 4, 4, 4
BLOCKS = NZ * NY
TRANS = 4
TILES = 33
HALF = TILES * LANES
SHIFT = 32 * LANES
HALF_A = 17 * LANES
SIZES = (5, 7, 8, 8, 5)
STARTS = (0, 5, 12, 20, 28, 33)
CHUNKS = len(SIZES)
OTHERS = [(dz, dy) for dz in range(NZ) for dy in range(NY) if (dz, dy) != (0, 0)]
F32 = jnp.float32
BF16 = jnp.bfloat16


def kernel(
    img_ref, proj_ref, ctf_ref, noise_ref, trig_ref, shift_ref, class_ref,
    out_ref, ev_ref,
    placed, ometa, pair, pmeta, smeta, gath, praw, ctfh, weights, normrows, onehot, ctfrows, vtab, prep,
    score, pscore, stats, post, part, from_a, from_b, from_p, from_m, zsend, zrecv, keep, fin,
    loc_sem, core_s, core_r, meta_s, meta_r, stat_s, stat_r, z_s, z_r,
    yp_s, ym_s, yl_r, yr_r, fa_s, fb_s, fa_r, fb_r, sc_s, sc_r,
    a_s, b_s, a_r, b_r, p_s, m_s, p_r, m_r, w_s, w_r, f_s, f_r,
):
    img = lax.axis_index("img")
    ori = lax.axis_index("ori")
    x, zh = img // 2, img % 2
    core, y, zl = ori % 2, (ori // 2) % 4, ori // 8
    xp, xm, x2 = (x + 1) % 4, (x + 3) % 4, (x + 2) % 4
    yp, ym, y2 = (y + 1) % 4, (y + 3) % 4, (y + 2) % 4
    own = zl * 4 + y

    def dev(x_=x, zh_=zh, zl_=zl, y_=y, core_=core):
        return (x_ * 2 + zh_, (zl_ * 4 + y_) * 2 + core_)

    def send(src, dst, ss, rs, target):
        return pltpu.make_async_remote_copy(
            src_ref=src, dst_ref=dst, send_sem=ss, recv_sem=rs,
            device_id=target, device_id_type=pl.DeviceIdType.MESH,
        )

    peer = dev(core_=1 - core)
    others = [dev(zl_=(zl + dz) % 4, y_=(y + dy) % 4) for dz, dy in OTHERS]
    right, left = dev(x_=xp), dev(x_=xm)
    up, down = dev(y_=yp), dev(y_=ym)
    across = [dev(zh_=1 - zh, core_=k) for k in range(2)]

    barrier = pltpu.get_barrier_semaphore()
    greeted = [peer, *others, right, left, *across]
    for target in greeted:
        pl.semaphore_signal(barrier, inc=1, device_id=target, device_id_type=pl.DeviceIdType.MESH)

    mine = pl.ds(pl.multiple_of(core * SHIFT, LANES), HALF)
    theirs = pl.ds(pl.multiple_of((1 - core) * SHIFT, LANES), HALF)
    ctf_copy = pltpu.make_async_copy(ctf_ref.at[:, mine], ctfh, loc_sem.at[0])
    proj_copy = pltpu.make_async_copy(proj_ref.at[:, mine], praw.at[core], loc_sem.at[1])
    ctf_copy.start()
    proj_copy.start()

    lane = lax.broadcasted_iota(jnp.int32, (8, LANES), 1)
    place = lax.broadcasted_iota(jnp.int32, (8, LANES), 0)

    def lay_out(s, carry):
        cols = pl.ds(pl.multiple_of(s * 5 * LANES, LANES), 5 * LANES)
        at = lax.broadcasted_iota(jnp.int32, (8, 5 * LANES), 0)
        real = jnp.zeros((8, 5 * LANES), F32)
        imag = jnp.zeros((8, 5 * LANES), F32)
        for i in range(4):
            both = img_ref[i, :, cols].astype(F32)
            here = at == i + 4 * core
            real = jnp.where(here, both[0:1], real)
            imag = jnp.where(here, both[1:2], imag)
        placed[:, cols] = jnp.concatenate([real, imag], axis=0).astype(BF16)
        return carry

    lax.fori_loop(0, 13, lay_out, 0)
    meta = jnp.zeros((8, LANES), jnp.int32)
    for i in range(4):
        row = place == i + 4 * core
        for t in range(TRANS):
            for k in range(2):
                spot = jnp.logical_and(row, lane == 2 * t + k)
                meta = jnp.where(spot, shift_ref[i, k, t], meta)
        meta = jnp.where(jnp.logical_and(row, lane == 8), class_ref[i], meta)
    meta = meta.astype(F32)
    ometa[...] = jnp.concatenate([meta, jnp.zeros_like(meta)], axis=0).astype(BF16)

    pl.semaphore_wait(barrier, len(greeted))

    pair_copy = send(placed.at[:, theirs], pair, core_s.at[0], core_r.at[0], peer)
    pmeta_copy = send(ometa, pmeta, core_s.at[1], core_r.at[1], peer)
    praw_copy = send(proj_ref.at[:, theirs], praw.at[core], core_s.at[2], core_r.at[2], peer)
    pmeta_copy.start()
    pair_copy.start()
    praw_copy.start()

    pmeta_copy.wait_recv()
    smeta[own] = ometa[...] + pmeta[...]
    meta_copies = [
        send(smeta.at[own], smeta.at[own], meta_s.at[n], meta_r.at[n], target)
        for n, target in enumerate(others)
    ]
    for copy in meta_copies:
        copy.start()

    pair_copy.wait_recv()
    gath[own] = placed[:, mine] + pair[...]

    b0, b1 = zl % 2, zl // 2

    def pick(table):
        low = (1 - b0) * table[0] + b0 * table[1]
        high = (1 - b0) * table[2] + b0 * table[3]
        return (1 - b1) * low + b1 * high

    order = [zl, pick([1, 0, 3, 2]), pick([2, 2, 1, 1]), pick([3, 3, 0, 0])]

    halves = (pl.ds(0, HALF_A), pl.ds(HALF_A, HALF - HALF_A))

    def same(b, h, ss, rs, target):
        ref = gath.at[b, :, halves[h]]
        return send(ref, ref, ss, rs, target)

    above, below = dev(zl_=zl + 1), dev(zl_=zl - 1)
    goes_right = [zl < 3] + [jnp.logical_and(order[q] < zl, zl < 3) for q in (1, 2, 3)]
    goes_left = [zl > 0] + [jnp.logical_and(order[q] > zl, zl > 0) for q in (1, 2, 3)]
    z_right, z_left, y_up, y_down, fwd_up, fwd_down = [], [], [], [], [], []
    for q in range(4):
        for h in range(2):
            n, came = 2 * q + h, z_r.at[order[q] * 2 + h]
            b = order[q] * 4 + y
            z_right.append(same(b, h, z_s.at[n], came, above))
            z_left.append(same(b, h, z_s.at[8 + n], came, below))
            y_up.append(same(b, h, yp_s.at[n], yl_r.at[n], up))
            y_down.append(same(b, h, ym_s.at[n], yr_r.at[n], down))
        fwd_up.append(same(order[q] * 4 + ym, 0, fa_s.at[q], fa_r.at[q], up))
        fwd_down.append(same(order[q] * 4 + yp, 1, fb_s.at[q], fb_r.at[q], down))

    def launch(q, h):
        n = 2 * q + h
        pl.when(goes_right[q])(lambda: z_right[n].start())
        pl.when(goes_left[q])(lambda: z_left[n].start())
        y_up[n].start()
        y_down[n].start()

    launch(0, 0)
    launch(0, 1)

    def fill_rows(s, carry):
        p = (s + 32 * core) * LANES + lane
        after = lax.shift_right_logical((p + LANES) * 64528, 22)
        vtab[s] = after - lax.shift_right_logical(p * 64528, 22)
        return carry

    lax.fori_loop(0, TILES, fill_rows, 0)
    top_row = lax.shift_right_logical((32 * core * LANES + lane) * 64528, 22)

    def pieces(value):
        one = value.astype(BF16)
        rest = value - one.astype(F32)
        two = rest.astype(BF16)
        three = (rest - two.astype(F32)).astype(BF16)
        return one, two, three

    def fill_ctf(s, carry):
        cols = pl.ds(pl.multiple_of(s * 1408, 1408), 1408)
        one, two, three = pieces(ctfh[:, cols])
        ctfrows[:, cols] = jnp.dot(
            onehot[...].astype(BF16),
            jnp.concatenate([one, two, three, one], axis=0),
            preferred_element_type=F32,
        )
        return carry


    def weigh(n, total):
        wide = pl.ds(pl.multiple_of(n * 384, 384), 384)
        raw = [praw[0, :, wide], praw[1, :, wide]]
        ctfs = ctfh[:, wide]
        noises = [noise_ref[pl.ds(core * 32 + 3 * n + i, 1), :] for i in range(3)]
        counted = 1 - core * (1 - jnp.minimum(n, 1))
        noises[0] = noises[0] * counted.astype(F32)
        turned = []
        for i in range(3):
            tile = slice(i * LANES, (i + 1) * LANES)
            parts = [r[:, tile].astype(F32).reshape(2, 8, 1, 8, LANES) for r in raw]
            both = jnp.concatenate(parts, axis=2).reshape(2, 128, LANES)
            scaled = (both * noises[i][None]).astype(BF16)
            turned += [scaled[0].T, scaled[1].T]
            power = (both[0] * both[0] + both[1] * both[1]).T
            ctf = ctfs[:, tile]
            p1, p2, p3 = pieces(power)
            c1, c2, c3 = pieces(ctf * ctf * noises[i])
            total = total + jnp.dot(
                jnp.concatenate([c1, c1, c1, c2, c2, c3], axis=1),
                jnp.concatenate([p1, p2, p3, p1, p2, p1], axis=0),
                preferred_element_type=F32,
            )
        weights[pl.ds(pl.multiple_of(n * 768, 768), 768), :] = jnp.concatenate(turned, axis=0)
        return total

    def prepare(*bs):
        cosine, sine = trig_ref[0:8, :], trig_ref[8:16, :]

        def wave(steps):
            index = steps & (KY - 1)
            return (
                jnp.take_along_axis(cosine, index, axis=1),
                jnp.take_along_axis(sine, index, axis=1),
            )

        begin, one_row, two_rows = [], [], []
        for b in bs:
            meta = smeta[b].astype(F32)[0:8, :].astype(jnp.int32)
            first_, one, two = [], [], []
            for t in range(TRANS):
                sx = meta[:, 2 * t : 2 * t + 1]
                sy = meta[:, 2 * t + 1 : 2 * t + 2]
                slope = jnp.broadcast_to(sy - KX * sx, (8, LANES))
                first_.append(wave(lane * sx + top_row * slope))
                one.append(wave(slope))
                two.append(wave(2 * slope))
            begin.append(tuple(first_))
            one_row.append(one)
            two_rows.append(two)

        def body(n, carry):
            every, total = carry
            wide = pl.ds(pl.multiple_of(n * 384, 384), 384)
            steps = pl.ds(pl.multiple_of(n * 768, 768), 768)
            singles = [vtab[3 * n + i] == 1 for i in range(3)]
            loaded = [
                (gath[b, :, wide].astype(F32), ctfrows[pl.ds(pl.multiple_of(b * 8, 8), 8), wide])
                for b in bs
            ]
            after, made = [], []
            for k, phases in enumerate(every):
                blocks, ctfs = loaded[k]
                rows = [[], []]
                for i in range(3):
                    tile = slice(i * LANES, (i + 1) * LANES)
                    ctf = ctfs[:, tile]
                    real, imag = blocks[0:8, tile] * ctf, blocks[8:16, tile] * ctf
                    reals, imags, later = [], [], []
                    for t in range(TRANS):
                        c, si = phases[t]
                        reals.append(real * c + imag * si)
                        imags.append(imag * c - real * si)
                        mc = jnp.where(singles[i], one_row[k][t][0], two_rows[k][t][0])
                        ms = jnp.where(singles[i], one_row[k][t][1], two_rows[k][t][1])
                        later.append((c * mc - si * ms, si * mc + c * ms))
                    phases = tuple(later)
                    for h in range(2):
                        for values in (reals, imags):
                            pair_ = jnp.concatenate(values[2 * h : 2 * h + 2], axis=0)
                            rows[h].append(pair_.astype(BF16))
                after.append(phases)
                made += [jnp.concatenate(r, axis=1) for r in rows]
            for k, b in enumerate(bs):
                at = pl.ds(pl.multiple_of(b * 32, 32), 32)
                prep[at, steps] = jnp.concatenate(made[2 * k : 2 * k + 2], axis=0)
            total = total + jnp.dot(
                jnp.concatenate(made, axis=0), weights[steps, :], preferred_element_type=F32
            )
            return tuple(after), total

        start = (tuple(begin), jnp.zeros((32 * len(bs), LANES), F32))
        _, cross = lax.fori_loop(0, TILES // 3, body, start, unroll=11)
        for k, b in enumerate(bs):
            norm = normrows[pl.ds(pl.multiple_of(b * 8, 8), 8), :]
            at = pl.ds(pl.multiple_of((b % 4) * 32, 32), 32)
            score[b // 4, at, :] = cross[32 * k : 32 * k + 32] - jnp.concatenate(
                [norm] * TRANS, axis=0
            )

    sc_copies = [
        send(score.at[order[q]], pscore.at[order[q]], sc_s.at[q], sc_r.at[q], peer)
        for q in range(4)
    ]

    stats[own] = jnp.zeros((16, LANES), F32)

    def summarise(q):
        sc_copies[q].wait_recv()
        g = order[q]
        whole = (score[g] + pscore[g]).T
        pscore[g] = whole
        top = jnp.max(whole, axis=0, keepdims=True)
        stats[own, pl.ds(g, 1), :] = top
        stats[own, pl.ds(8 + g, 1), :] = jnp.sum(jnp.exp(whole - top), axis=0, keepdims=True)

    def sides(q):
        y_up[2 * q + 1].wait_recv()
        y_down[2 * q].wait_recv()
        prepare(order[q] * 4 + ym, order[q] * 4 + yp)

    def farthest(q):
        fwd_up[q].wait_recv()
        fwd_down[q].wait_recv()
        return order[q] * 4 + y2

    def arrive(q, h):
        z_right[2 * q + h].wait_recv()
        launch(q, h)

    def forward(q, h):
        if h == 0:
            y_up[2 * q].wait_recv()
            fwd_up[q].start()
        else:
            y_down[2 * q + 1].wait_recv()
            fwd_down[q].start()

    ctf_copy.wait()
    proj_copy.wait()
    praw_copy.wait_recv()
    half_norms = lax.fori_loop(0, 4, weigh, jnp.zeros((64, 128), F32), unroll=4)
    arrive(1, 0)
    forward(0, 0)
    half_norms = lax.fori_loop(4, 6, weigh, half_norms, unroll=2)
    arrive(1, 1)
    forward(0, 1)

    for copy in meta_copies:
        copy.wait_recv()

    lane2 = lax.broadcasted_iota(jnp.int32, (8, 256), 1)

    def fill_onehot(b, carry):
        classes = smeta[b].astype(F32)[0:8, 8:9].astype(jnp.int32)
        hit = jnp.logical_and(lane2 % 64 == classes, lane2 < 192)
        onehot[pl.ds(pl.multiple_of(b * 8, 8), 8), :] = hit.astype(F32)
        return carry

    lax.fori_loop(0, BLOCKS, fill_onehot, 0)
    lax.fori_loop(0, 3, fill_ctf, 0)

    arrive(2, 0)
    half_norms = lax.fori_loop(6, 9, weigh, half_norms, unroll=3)
    arrive(2, 1)
    forward(1, 0)
    half_norms = lax.fori_loop(9, 11, weigh, half_norms, unroll=2)
    one, two, three = pieces(0.5 * half_norms)
    normrows[...] = jnp.dot(
        onehot[...].astype(BF16),
        jnp.concatenate([one, two, three, one], axis=0),
        preferred_element_type=F32,
    )
    forward(1, 1)
    prepare(order[0] * 4 + y, order[1] * 4 + y)
    arrive(3, 0)
    sides(0)
    arrive(3, 1)
    forward(2, 0)
    sides(1)
    forward(2, 1)
    prepare(farthest(0), order[2] * 4 + y)
    sc_copies[0].start()
    forward(3, 0)
    sides(2)
    forward(3, 1)
    prepare(farthest(1), order[3] * 4 + y)
    sc_copies[1].start()
    summarise(0)
    sides(3)
    summarise(1)
    prepare(farthest(2), farthest(3))
    sc_copies[2].start()
    sc_copies[3].start()
    summarise(2)
    summarise(3)

    stat_copies = [
        send(stats.at[own], stats.at[own], stat_s.at[n], stat_r.at[n], target)
        for n, target in enumerate(others)
    ]
    for copy in stat_copies:
        copy.start()
    for copy in stat_copies:
        copy.wait_recv()
    tops = [stats[b, 0:8, :] for b in range(BLOCKS)]
    top = tops[0]
    for b in range(1, BLOCKS):
        top = jnp.maximum(top, tops[b])
    total = jnp.zeros((8, LANES), F32)
    for b in range(BLOCKS):
        total += stats[b, 8:16, :] * jnp.exp(tops[b] - top)
    held = lax.broadcasted_iota(jnp.int32, (8, LANES), 1) % 32

    def turn(value, by):
        inside = pltpu.roll(value, by, 1)
        wrapped = pltpu.roll(value, by + LANES - 32, 1)
        return jnp.where(held >= by, inside, wrapped)

    largest = jnp.maximum(top, turn(top, 8))
    largest = jnp.maximum(largest, turn(largest, 16))
    total = total * jnp.exp(top - largest)
    total = total + turn(total, 8)
    total = total + turn(total, 16)
    evidence = largest + jnp.log(total)
    for i in range(4):
        spot = jnp.logical_and(place == zl, lane == y * 32 + core * 4 + i)
        ev_ref[i] = jnp.sum(jnp.where(spot, evidence, 0.0))
    for g in range(4):
        post[:, g * 128 : (g + 1) * 128] = (
            jnp.exp(pscore[g] - evidence[g : g + 1, :]) * 2048.0
        ).astype(BF16)

    def copy_a(c):
        return send(part[c].at[2 * x2], from_a[c], a_s.at[c], a_r.at[c], right)

    def copy_b(c):
        return send(part[c].at[2 * x2 + 1], from_b[c], b_s.at[c], b_r.at[c], left)

    def copy_p(c):
        return send(part[c].at[pl.ds(2 * xp, 2)], from_p[c], p_s.at[c], p_r.at[c], right)

    def copy_m(c):
        return send(part[c].at[pl.ds(2 * xm, 2)], from_m[c], m_s.at[c], m_r.at[c], left)

    def copy_w(c, k):
        return send(
            zsend[c].at[k], zrecv[c].at[core], w_s.at[c, k], w_r.at[c, core], across[k]
        )

    def arrived_w(c, half):
        return send(zsend[c].at[0], zrecv[c].at[half], w_s.at[c, 0], w_r.at[c, half], across[0])

    def copy_f(c):
        other = pl.ds(pl.multiple_of((1 - core) * 8, 8), 8)
        return send(keep[c].at[other], fin[c], f_s.at[c], f_r.at[c], peer)

    def project(c):
        sums = jnp.dot(
            post[...], prep[:, STARTS[c] * 256 : STARTS[c + 1] * 256], preferred_element_type=F32
        ).astype(BF16)
        for i in range(8):
            part[c][i] = sums[16 * i : 16 * i + 16]
        copy_a(c).start()
        copy_b(c).start()

    def add(into, *others_):
        value = into.astype(F32)
        for other in others_:
            value = value + other.astype(F32)
        return value

    def pass_on(c):
        copy_a(c).wait_recv()
        part[c][2 * xp] = add(part[c][2 * xp], from_a[c][...]).astype(BF16)
        copy_p(c).start()
        copy_b(c).wait_recv()
        part[c][2 * xm + 1] = add(part[c][2 * xm + 1], from_b[c][...]).astype(BF16)
        copy_m(c).start()

    def collect(c):
        half = SIZES[c] * LANES
        copy_p(c).wait_recv()
        copy_m(c).wait_recv()
        far = 1 - zh
        away = add(part[c][2 * x + far], from_p[c][far], from_m[c][far])
        for k in range(2):
            rows = away[8 * k : 8 * k + 8]
            zsend[c][k] = jnp.concatenate([rows[:, :half], rows[:, half:]], axis=0).astype(BF16)
            copy_w(c, k).start()
        keep[c][...] = add(part[c][2 * x + zh], from_p[c][zh], from_m[c][zh])
        copy_f(c).start()

    def complete(c):
        for half in range(2):
            arrived_w(c, half).wait_recv()
        copy_f(c).wait_recv()
        here = keep[c][pl.ds(pl.multiple_of(core * 8, 8), 8), :]
        for half, near in ((core, here), (1 - core, fin[c][...])):
            rows = zrecv[c][half].astype(F32)
            value = near + jnp.concatenate([rows[0:8], rows[8:16]], axis=1)
            for s in range(SIZES[c]):
                at = pl.multiple_of(half * SHIFT + (STARTS[c] + s) * LANES, LANES)
                for k in range(2):
                    out_ref[:, k, pl.ds(at, LANES)] = value[
                        :, s * 256 + k * 128 : s * 256 + k * 128 + 128
                    ]

    for c in range(CHUNKS):
        project(c)
    for c in range(CHUNKS):
        pass_on(c)
    for c in range(CHUNKS):
        collect(c)
        if c >= 2:
            complete(c - 2)
    complete(CHUNKS - 2)
    complete(CHUNKS - 1)

    pmeta_copy.wait_send()
    pair_copy.wait_send()
    praw_copy.wait_send()
    for copy in meta_copies + stat_copies + sc_copies + y_up + y_down + fwd_up + fwd_down:
        copy.wait_send()
    for n in range(8):
        pl.when(goes_right[n // 2])(lambda n=n: z_right[n].wait_send())
        pl.when(goes_left[n // 2])(lambda n=n: z_left[n].wait_send())

    for c in range(CHUNKS):
        for copy in (copy_a, copy_b, copy_p, copy_m, copy_f):
            copy(c).wait_send()
        for k in range(2):
            copy_w(c, k).wait_send()


def per_device(images, projections, ctf_table, noise_weight, shifts, defocus):
    local = images.shape[0]
    pixels = images.shape[2]
    proj = projections.transpose(1, 0, 2).reshape(128, pixels)
    angles = np.arange(KY) * (2.0 * math.pi / KY)
    trig = np.concatenate([np.tile(np.cos(angles), (8, 1)), np.tile(np.sin(angles), (8, 1))])
    trig = jnp.asarray(trig.astype(np.float32))
    vmem = pl.BlockSpec(memory_space=pltpu.VMEM)
    hbm = pl.BlockSpec(memory_space=pl.ANY)
    smem = pl.BlockSpec(memory_space=pltpu.SMEM)
    dma = pltpu.SemaphoreType.DMA
    sems = [dma((2,)), dma((3,)), dma((3,)), dma((15,)), dma((15,)), dma((15,)), dma((15,))]
    sems += [dma((16,)), dma((8,))] + [dma((8,))] * 4 + [dma((4,))] * 6 + [dma((CHUNKS,))] * 8 + [dma((CHUNKS, 2))] * 2 + [dma((CHUNKS,))] * 2
    sums, evidence = pl.pallas_call(
        kernel,
        out_shape=(
            jax.ShapeDtypeStruct((8, 2, pixels), F32),
            jax.ShapeDtypeStruct((local,), F32),
        ),
        in_specs=[vmem, hbm, hbm, vmem, vmem, smem, smem],
        out_specs=(vmem, smem),
        scratch_shapes=[
            pltpu.VMEM((16, 65 * LANES), BF16),
            pltpu.VMEM((16, LANES), BF16),
            pltpu.VMEM((16, HALF), BF16),
            pltpu.VMEM((16, LANES), BF16),
            pltpu.VMEM((BLOCKS, 16, LANES), BF16),
            pltpu.VMEM((BLOCKS, 16, HALF), BF16),
            pltpu.VMEM((2, 128, HALF), BF16),
            pltpu.VMEM((64, HALF), F32),
            pltpu.VMEM((2 * HALF, 128), BF16),
            pltpu.VMEM((128, 128), F32),
            pltpu.VMEM((128, 2 * LANES), F32),
            pltpu.VMEM((128, HALF), F32),
            pltpu.VMEM((TILES, 8, LANES), jnp.int32),
            pltpu.VMEM((BLOCKS * 32, 2 * HALF), BF16),
            pltpu.VMEM((4, 128, 128), F32),
            pltpu.VMEM((4, 128, 128), F32),
            pltpu.VMEM((BLOCKS, 16, LANES), F32),
            pltpu.VMEM((128, 512), BF16),
            [pltpu.VMEM((8, 16, 256 * t), BF16) for t in SIZES],
            [pltpu.VMEM((16, 256 * t), BF16) for t in SIZES],
            [pltpu.VMEM((16, 256 * t), BF16) for t in SIZES],
            [pltpu.VMEM((2, 16, 256 * t), BF16) for t in SIZES],
            [pltpu.VMEM((2, 16, 256 * t), BF16) for t in SIZES],
            [pltpu.VMEM((2, 16, 128 * t), BF16) for t in SIZES],
            [pltpu.VMEM((2, 16, 128 * t), BF16) for t in SIZES],
            [pltpu.VMEM((16, 256 * t), F32) for t in SIZES],
            [pltpu.VMEM((8, 256 * t), F32) for t in SIZES],
            *sems,
        ],
        compiler_params=pltpu.CompilerParams(
            collective_id=0, has_side_effects=True, vmem_limit_bytes=34 * 1024 * 1024
        ),
    )(
        images, proj, ctf_table, noise_weight.reshape(65, LANES), trig,
        shifts.transpose(0, 2, 1), defocus,
    )
    return evidence, sums


def solution(mesh):
    in_specs = (
        P(("img", "ori"), None, None),
        P("ori", None, None),
        P(),
        P(),
        P(("img", "ori"), None, None),
        P(("img", "ori")),
    )
    out_specs = (P(("img", "ori")), P(("ori", "img"), None, None))
    return jax.shard_map(
        per_device, mesh=mesh, in_specs=in_specs, out_specs=out_specs, check_vma=False
    )
```

```python
import math

import jax
import jax.numpy as jnp
import numpy as np
from jax import lax
from jax.experimental import pallas as pl
from jax.experimental.pallas import tpu as pltpu
from jax.sharding import PartitionSpec as P

KY = 128
KX = 65
LANES = 128
NX, NZ, NY = 4, 4, 4
BLOCKS = NZ * NY
TRANS = 4
TILES = 33
HALF = TILES * LANES
SHIFT = 32 * LANES
HALF_A = 17 * LANES
SIZES = (5, 7, 8, 8, 5)
STARTS = (0, 5, 12, 20, 28, 33)
CHUNKS = len(SIZES)
OTHERS = [(dz, dy) for dz in range(NZ) for dy in range(NY) if (dz, dy) != (0, 0)]
F32 = jnp.float32
BF16 = jnp.bfloat16
HI = lax.Precision.HIGHEST


def kernel(
    img_ref, proj_ref, ctf_ref, noise_ref, trig_ref, shift_ref, class_ref,
    out_ref, ev_ref,
    placed, ometa, pair, pmeta, smeta, gath, praw, weights, norms, normrows, onehot, ctfrows, vtab, prep,
    score, pscore, stats, post, part, from_a, from_b, from_p, from_m, zsend, zrecv, keep, fin,
    core_s, core_r, meta_s, meta_r, stat_s, stat_r, z_s, z_r,
    yp_s, ym_s, yl_r, yr_r, fa_s, fb_s, fa_r, fb_r, sc_s, sc_r,
    a_s, b_s, a_r, b_r, p_s, m_s, p_r, m_r, w_s, w_r, f_s, f_r,
):
    img = lax.axis_index("img")
    ori = lax.axis_index("ori")
    x, zh = img // 2, img % 2
    core, y, zl = ori % 2, (ori // 2) % 4, ori // 8
    xp, xm, x2 = (x + 1) % 4, (x + 3) % 4, (x + 2) % 4
    yp, ym, y2 = (y + 1) % 4, (y + 3) % 4, (y + 2) % 4
    own = zl * 4 + y

    def dev(x_=x, zh_=zh, zl_=zl, y_=y, core_=core):
        return (x_ * 2 + zh_, (zl_ * 4 + y_) * 2 + core_)

    def send(src, dst, ss, rs, target):
        return pltpu.make_async_remote_copy(
            src_ref=src, dst_ref=dst, send_sem=ss, recv_sem=rs,
            device_id=target, device_id_type=pl.DeviceIdType.MESH,
        )

    peer = dev(core_=1 - core)
    others = [dev(zl_=(zl + dz) % 4, y_=(y + dy) % 4) for dz, dy in OTHERS]
    right, left = dev(x_=xp), dev(x_=xm)
    up, down = dev(y_=yp), dev(y_=ym)
    across = [dev(zh_=1 - zh, core_=k) for k in range(2)]

    barrier = pltpu.get_barrier_semaphore()
    greeted = [peer, *others, right, left, *across]
    for target in greeted:
        pl.semaphore_signal(barrier, inc=1, device_id=target, device_id_type=pl.DeviceIdType.MESH)

    mine = pl.ds(pl.multiple_of(core * SHIFT, LANES), HALF)
    theirs = pl.ds(pl.multiple_of((1 - core) * SHIFT, LANES), HALF)

    lane = lax.broadcasted_iota(jnp.int32, (8, LANES), 1)
    place = lax.broadcasted_iota(jnp.int32, (8, LANES), 0)

    def lay_out(s, carry):
        cols = pl.ds(pl.multiple_of(s * 5 * LANES, LANES), 5 * LANES)
        at = lax.broadcasted_iota(jnp.int32, (8, 5 * LANES), 0)
        real = jnp.zeros((8, 5 * LANES), F32)
        imag = jnp.zeros((8, 5 * LANES), F32)
        for i in range(4):
            both = img_ref[i, :, cols].astype(F32)
            here = at == i + 4 * core
            real = jnp.where(here, both[0:1], real)
            imag = jnp.where(here, both[1:2], imag)
        placed[:, cols] = jnp.concatenate([real, imag], axis=0).astype(BF16)
        return carry

    lax.fori_loop(0, 13, lay_out, 0)
    meta = jnp.zeros((8, LANES), jnp.int32)
    for i in range(4):
        row = place == i + 4 * core
        for t in range(TRANS):
            for k in range(2):
                spot = jnp.logical_and(row, lane == 2 * t + k)
                meta = jnp.where(spot, shift_ref[i, k, t], meta)
        meta = jnp.where(jnp.logical_and(row, lane == 8), class_ref[i], meta)
    meta = meta.astype(F32)
    ometa[...] = jnp.concatenate([meta, jnp.zeros_like(meta)], axis=0).astype(BF16)

    pl.semaphore_wait(barrier, len(greeted))

    pair_copy = send(placed.at[:, theirs], pair, core_s.at[0], core_r.at[0], peer)
    pmeta_copy = send(ometa, pmeta, core_s.at[1], core_r.at[1], peer)
    praw_copy = send(proj_ref.at[:, theirs], praw, core_s.at[2], core_r.at[2], peer)
    pmeta_copy.start()
    pair_copy.start()
    praw_copy.start()

    pmeta_copy.wait_recv()
    smeta[own] = ometa[...] + pmeta[...]
    meta_copies = [
        send(smeta.at[own], smeta.at[own], meta_s.at[n], meta_r.at[n], target)
        for n, target in enumerate(others)
    ]
    for copy in meta_copies:
        copy.start()

    pair_copy.wait_recv()
    gath[own] = placed[:, mine] + pair[...]

    b0, b1 = zl % 2, zl // 2

    def pick(table):
        low = (1 - b0) * table[0] + b0 * table[1]
        high = (1 - b0) * table[2] + b0 * table[3]
        return (1 - b1) * low + b1 * high

    order = [zl, pick([1, 0, 3, 2]), pick([2, 2, 1, 1]), pick([3, 3, 0, 0])]

    halves = (pl.ds(0, HALF_A), pl.ds(HALF_A, HALF - HALF_A))

    def same(b, h, ss, rs, target):
        ref = gath.at[b, :, halves[h]]
        return send(ref, ref, ss, rs, target)

    above, below = dev(zl_=zl + 1), dev(zl_=zl - 1)
    goes_right = [zl < 3] + [jnp.logical_and(order[q] < zl, zl < 3) for q in (1, 2, 3)]
    goes_left = [zl > 0] + [jnp.logical_and(order[q] > zl, zl > 0) for q in (1, 2, 3)]
    z_right, z_left, y_up, y_down, fwd_up, fwd_down = [], [], [], [], [], []
    for q in range(4):
        for h in range(2):
            n, came = 2 * q + h, z_r.at[order[q] * 2 + h]
            b = order[q] * 4 + y
            z_right.append(same(b, h, z_s.at[n], came, above))
            z_left.append(same(b, h, z_s.at[8 + n], came, below))
            y_up.append(same(b, h, yp_s.at[n], yl_r.at[n], up))
            y_down.append(same(b, h, ym_s.at[n], yr_r.at[n], down))
        fwd_up.append(same(order[q] * 4 + ym, 0, fa_s.at[q], fa_r.at[q], up))
        fwd_down.append(same(order[q] * 4 + yp, 1, fb_s.at[q], fb_r.at[q], down))

    def launch(q, h):
        n = 2 * q + h
        pl.when(goes_right[q])(lambda: z_right[n].start())
        pl.when(goes_left[q])(lambda: z_left[n].start())
        y_up[n].start()
        y_down[n].start()

    launch(0, 0)
    launch(0, 1)

    def fill_rows(s, carry):
        p = (s + 32 * core) * LANES + lane
        after = lax.shift_right_logical((p + LANES) * 64528, 22)
        vtab[s] = after - lax.shift_right_logical(p * 64528, 22)
        return carry

    lax.fori_loop(0, TILES, fill_rows, 0)
    top_row = lax.shift_right_logical((32 * core * LANES + lane) * 64528, 22)

    def pieces(value):
        one = value.astype(BF16)
        rest = value - one.astype(F32)
        two = rest.astype(BF16)
        three = (rest - two.astype(F32)).astype(BF16)
        return one, two, three

    def fill_ctf(s, carry):
        cols = pl.ds(pl.multiple_of(s * 1408, 1408), 1408)
        there = pl.ds(pl.multiple_of(core * SHIFT + s * 1408, LANES), 1408)
        one, two, three = pieces(ctf_ref[:, there])
        ctfrows[:, cols] = jnp.dot(
            onehot[...].astype(BF16),
            jnp.concatenate([one, two, three, one], axis=0),
            preferred_element_type=F32,
        )
        return carry


    def weigh(n, total):
        wide = pl.ds(pl.multiple_of(n * 384, 384), 384)
        there = pl.ds(pl.multiple_of(core * SHIFT + n * 384, LANES), 384)
        here, far = proj_ref[:, there], praw[:, wide]
        raw = [jnp.where(core == 0, here, far), jnp.where(core == 0, far, here)]
        ctfs = ctf_ref[:, there]
        noises = [noise_ref[pl.ds(core * 32 + 3 * n + i, 1), :] for i in range(3)]
        counted = 1 - core * (1 - jnp.minimum(n, 1))
        noises[0] = noises[0] * counted.astype(F32)
        turned = []
        for i in range(3):
            tile = slice(i * LANES, (i + 1) * LANES)
            parts = [r[:, tile].astype(F32).reshape(2, 8, 1, 8, LANES) for r in raw]
            both = jnp.concatenate(parts, axis=2).reshape(2, 128, LANES)
            scaled = (both * noises[i][None]).astype(BF16)
            turned += [scaled[0].T, scaled[1].T]
            power = (both[0] * both[0] + both[1] * both[1]).T
            ctf = ctfs[:, tile]
            p1, p2, p3 = pieces(power)
            c1, c2, c3 = pieces(ctf * ctf * noises[i])
            total = total + jnp.dot(
                jnp.concatenate([c1, c1, c1, c2, c2, c3], axis=1),
                jnp.concatenate([p1, p2, p3, p1, p2, p1], axis=0),
                preferred_element_type=F32,
            )
        weights[pl.ds(pl.multiple_of(n * 768, 768), 768), :] = jnp.concatenate(turned, axis=0)
        return total

    def prepare(*bs):
        cosine, sine = trig_ref[0:8, :], trig_ref[8:16, :]

        def wave(steps):
            index = steps & (KY - 1)
            return (
                jnp.take_along_axis(cosine, index, axis=1),
                jnp.take_along_axis(sine, index, axis=1),
            )

        begin, one_row, two_rows = [], [], []
        for b in bs:
            meta = smeta[b].astype(F32)[0:8, :].astype(jnp.int32)
            first_, one, two = [], [], []
            for t in range(TRANS):
                sx = meta[:, 2 * t : 2 * t + 1]
                sy = meta[:, 2 * t + 1 : 2 * t + 2]
                slope = jnp.broadcast_to(sy - KX * sx, (8, LANES))
                first_.append(wave(lane * sx + top_row * slope))
                one.append(wave(slope))
                two.append(wave(2 * slope))
            begin.append(tuple(first_))
            one_row.append(one)
            two_rows.append(two)

        def body(n, carry):
            every, total = carry
            wide = pl.ds(pl.multiple_of(n * 384, 384), 384)
            steps = pl.ds(pl.multiple_of(n * 768, 768), 768)
            singles = [vtab[3 * n + i] == 1 for i in range(3)]
            loaded = [
                (gath[b, :, wide].astype(F32), ctfrows[pl.ds(pl.multiple_of(b * 8, 8), 8), wide])
                for b in bs
            ]
            after, made = [], []
            for k, phases in enumerate(every):
                blocks, ctfs = loaded[k]
                rows = [[], []]
                for i in range(3):
                    tile = slice(i * LANES, (i + 1) * LANES)
                    ctf = ctfs[:, tile]
                    real, imag = blocks[0:8, tile] * ctf, blocks[8:16, tile] * ctf
                    reals, imags, later = [], [], []
                    for t in range(TRANS):
                        c, si = phases[t]
                        reals.append(real * c + imag * si)
                        imags.append(imag * c - real * si)
                        mc = jnp.where(singles[i], one_row[k][t][0], two_rows[k][t][0])
                        ms = jnp.where(singles[i], one_row[k][t][1], two_rows[k][t][1])
                        later.append((c * mc - si * ms, si * mc + c * ms))
                    phases = tuple(later)
                    for h in range(2):
                        for values in (reals, imags):
                            pair_ = jnp.concatenate(values[2 * h : 2 * h + 2], axis=0)
                            rows[h].append(pair_.astype(BF16))
                after.append(phases)
                made += [jnp.concatenate(r, axis=1) for r in rows]
            for k, b in enumerate(bs):
                at = pl.ds(pl.multiple_of(b * 32, 32), 32)
                prep[at, steps] = jnp.concatenate(made[2 * k : 2 * k + 2], axis=0)
            total = total + jnp.dot(
                jnp.concatenate(made, axis=0), weights[steps, :], preferred_element_type=F32
            )
            return tuple(after), total

        start = (tuple(begin), jnp.zeros((32 * len(bs), LANES), F32))
        _, cross = lax.fori_loop(0, TILES // 3, body, start, unroll=11)
        for k, b in enumerate(bs):
            norm = normrows[pl.ds(pl.multiple_of(b * 8, 8), 8), :]
            at = pl.ds(pl.multiple_of((b % 4) * 32, 32), 32)
            score[b // 4, at, :] = cross[32 * k : 32 * k + 32] - jnp.concatenate(
                [norm] * TRANS, axis=0
            )

    sc_copies = [
        send(score.at[order[q]], pscore.at[order[q]], sc_s.at[q], sc_r.at[q], peer)
        for q in range(4)
    ]

    stats[own] = jnp.zeros((16, LANES), F32)

    def summarise(q):
        sc_copies[q].wait_recv()
        g = order[q]
        whole = (score[g] + pscore[g]).T
        pscore[g] = whole
        top = jnp.max(whole, axis=0, keepdims=True)
        stats[own, pl.ds(g, 1), :] = top
        stats[own, pl.ds(8 + g, 1), :] = jnp.sum(jnp.exp(whole - top), axis=0, keepdims=True)

    def sides(q):
        y_up[2 * q + 1].wait_recv()
        y_down[2 * q].wait_recv()
        prepare(order[q] * 4 + ym, order[q] * 4 + yp)

    def farthest(q):
        fwd_up[q].wait_recv()
        fwd_down[q].wait_recv()
        return order[q] * 4 + y2

    def arrive(q, h):
        z_right[2 * q + h].wait_recv()
        launch(q, h)

    def forward(q, h):
        if h == 0:
            y_up[2 * q].wait_recv()
            fwd_up[q].start()
        else:
            y_down[2 * q + 1].wait_recv()
            fwd_down[q].start()

    praw_copy.wait_recv()
    half_norms = lax.fori_loop(0, 4, weigh, jnp.zeros((64, 128), F32))
    arrive(1, 0)
    forward(0, 0)
    half_norms = lax.fori_loop(4, 6, weigh, half_norms)
    arrive(1, 1)
    forward(0, 1)

    for copy in meta_copies:
        copy.wait_recv()

    lane2 = lax.broadcasted_iota(jnp.int32, (8, 256), 1)

    def fill_onehot(b, carry):
        classes = smeta[b].astype(F32)[0:8, 8:9].astype(jnp.int32)
        hit = jnp.logical_and(lane2 % 64 == classes, lane2 < 192)
        onehot[pl.ds(pl.multiple_of(b * 8, 8), 8), :] = hit.astype(F32)
        return carry

    lax.fori_loop(0, BLOCKS, fill_onehot, 0)
    lax.fori_loop(0, 3, fill_ctf, 0)

    arrive(2, 0)
    half_norms = lax.fori_loop(6, 9, weigh, half_norms)
    arrive(2, 1)
    forward(1, 0)
    half_norms = lax.fori_loop(9, 11, weigh, half_norms)
    norms[...] = 0.5 * half_norms
    normrows[...] = jnp.dot(
        onehot[:, 0:64], norms[...], precision=HI, preferred_element_type=F32
    )
    forward(1, 1)
    prepare(order[0] * 4 + y, order[1] * 4 + y)
    arrive(3, 0)
    sides(0)
    arrive(3, 1)
    forward(2, 0)
    sides(1)
    forward(2, 1)
    prepare(farthest(0), order[2] * 4 + y)
    sc_copies[0].start()
    forward(3, 0)
    sides(2)
    forward(3, 1)
    prepare(farthest(1), order[3] * 4 + y)
    sc_copies[1].start()
    summarise(0)
    sides(3)
    summarise(1)
    prepare(farthest(2), farthest(3))
    sc_copies[2].start()
    sc_copies[3].start()
    summarise(2)
    summarise(3)

    stat_copies = [
        send(stats.at[own], stats.at[own], stat_s.at[n], stat_r.at[n], target)
        for n, target in enumerate(others)
    ]
    for copy in stat_copies:
        copy.start()
    for copy in stat_copies:
        copy.wait_recv()
    tops = [stats[b, 0:8, :] for b in range(BLOCKS)]
    top = tops[0]
    for b in range(1, BLOCKS):
        top = jnp.maximum(top, tops[b])
    total = jnp.zeros((8, LANES), F32)
    for b in range(BLOCKS):
        total += stats[b, 8:16, :] * jnp.exp(tops[b] - top)
    held = lax.broadcasted_iota(jnp.int32, (8, LANES), 1) % 32

    def turn(value, by):
        inside = pltpu.roll(value, by, 1)
        wrapped = pltpu.roll(value, by + LANES - 32, 1)
        return jnp.where(held >= by, inside, wrapped)

    largest = jnp.maximum(top, turn(top, 8))
    largest = jnp.maximum(largest, turn(largest, 16))
    total = total * jnp.exp(top - largest)
    total = total + turn(total, 8)
    total = total + turn(total, 16)
    evidence = largest + jnp.log(total)
    for i in range(4):
        spot = jnp.logical_and(place == zl, lane == y * 32 + core * 4 + i)
        ev_ref[i] = jnp.sum(jnp.where(spot, evidence, 0.0))
    for g in range(4):
        post[:, g * 128 : (g + 1) * 128] = (
            jnp.exp(pscore[g] - evidence[g : g + 1, :]) * 2048.0
        ).astype(BF16)

    def copy_a(c):
        return send(part[c].at[2 * x2], from_a[c], a_s.at[c], a_r.at[c], right)

    def copy_b(c):
        return send(part[c].at[2 * x2 + 1], from_b[c], b_s.at[c], b_r.at[c], left)

    def copy_p(c):
        return send(part[c].at[pl.ds(2 * xp, 2)], from_p[c], p_s.at[c], p_r.at[c], right)

    def copy_m(c):
        return send(part[c].at[pl.ds(2 * xm, 2)], from_m[c], m_s.at[c], m_r.at[c], left)

    def copy_w(c, k):
        return send(
            zsend[c].at[k], zrecv[c].at[core], w_s.at[c, k], w_r.at[c, core], across[k]
        )

    def arrived_w(c, half):
        return send(zsend[c].at[0], zrecv[c].at[half], w_s.at[c, 0], w_r.at[c, half], across[0])

    def copy_f(c):
        other = pl.ds(pl.multiple_of((1 - core) * 8, 8), 8)
        return send(keep[c].at[other], fin[c], f_s.at[c], f_r.at[c], peer)

    def project(c):
        sums = jnp.dot(
            post[...], prep[:, STARTS[c] * 256 : STARTS[c + 1] * 256], preferred_element_type=F32
        ).astype(BF16)
        for i in range(8):
            part[c][i] = sums[16 * i : 16 * i + 16]
        copy_a(c).start()
        copy_b(c).start()

    def add(into, *others_):
        value = into.astype(F32)
        for other in others_:
            value = value + other.astype(F32)
        return value

    def pass_on(c):
        copy_a(c).wait_recv()
        part[c][2 * xp] = add(part[c][2 * xp], from_a[c][...]).astype(BF16)
        copy_p(c).start()
        copy_b(c).wait_recv()
        part[c][2 * xm + 1] = add(part[c][2 * xm + 1], from_b[c][...]).astype(BF16)
        copy_m(c).start()

    def collect(c):
        half = SIZES[c] * LANES
        copy_p(c).wait_recv()
        copy_m(c).wait_recv()
        far = 1 - zh
        away = add(part[c][2 * x + far], from_p[c][far], from_m[c][far])
        for k in range(2):
            rows = away[8 * k : 8 * k + 8]
            zsend[c][k] = jnp.concatenate([rows[:, :half], rows[:, half:]], axis=0).astype(BF16)
            copy_w(c, k).start()
        keep[c][...] = add(part[c][2 * x + zh], from_p[c][zh], from_m[c][zh])
        copy_f(c).start()

    def complete(c):
        for half in range(2):
            arrived_w(c, half).wait_recv()
        copy_f(c).wait_recv()
        here = keep[c][pl.ds(pl.multiple_of(core * 8, 8), 8), :]
        for half, near in ((core, here), (1 - core, fin[c][...])):
            rows = zrecv[c][half].astype(F32)
            value = near + jnp.concatenate([rows[0:8], rows[8:16]], axis=1)
            for s in range(SIZES[c]):
                at = pl.multiple_of(half * SHIFT + (STARTS[c] + s) * LANES, LANES)
                for k in range(2):
                    out_ref[:, k, pl.ds(at, LANES)] = value[
                        :, s * 256 + k * 128 : s * 256 + k * 128 + 128
                    ]

    for c in range(CHUNKS):
        project(c)
    for c in range(CHUNKS):
        pass_on(c)
    for c in range(CHUNKS):
        collect(c)
        if c >= 2:
            complete(c - 2)
    complete(CHUNKS - 2)
    complete(CHUNKS - 1)

    pmeta_copy.wait_send()
    pair_copy.wait_send()
    praw_copy.wait_send()
    for copy in meta_copies + stat_copies + sc_copies + y_up + y_down + fwd_up + fwd_down:
        copy.wait_send()
    for n in range(8):
        pl.when(goes_right[n // 2])(lambda n=n: z_right[n].wait_send())
        pl.when(goes_left[n // 2])(lambda n=n: z_left[n].wait_send())

    for c in range(CHUNKS):
        for copy in (copy_a, copy_b, copy_p, copy_m, copy_f):
            copy(c).wait_send()
        for k in range(2):
            copy_w(c, k).wait_send()


def per_device(images, projections, ctf_table, noise_weight, shifts, defocus):
    local = images.shape[0]
    pixels = images.shape[2]
    proj = projections.transpose(1, 0, 2).reshape(128, pixels)
    angles = np.arange(KY) * (2.0 * math.pi / KY)
    trig = np.concatenate([np.tile(np.cos(angles), (8, 1)), np.tile(np.sin(angles), (8, 1))])
    trig = jnp.asarray(trig.astype(np.float32))
    vmem = pl.BlockSpec(memory_space=pltpu.VMEM)
    smem = pl.BlockSpec(memory_space=pltpu.SMEM)
    dma = pltpu.SemaphoreType.DMA
    sems = [dma((3,)), dma((3,)), dma((15,)), dma((15,)), dma((15,)), dma((15,))]
    sems += [dma((16,)), dma((8,))] + [dma((8,))] * 4 + [dma((4,))] * 6 + [dma((CHUNKS,))] * 8 + [dma((CHUNKS, 2))] * 2 + [dma((CHUNKS,))] * 2
    sums, evidence = pl.pallas_call(
        kernel,
        out_shape=(
            jax.ShapeDtypeStruct((8, 2, pixels), F32),
            jax.ShapeDtypeStruct((local,), F32),
        ),
        in_specs=[vmem, vmem, vmem, vmem, vmem, smem, smem],
        out_specs=(vmem, smem),
        scratch_shapes=[
            pltpu.VMEM((16, 65 * LANES), BF16),
            pltpu.VMEM((16, LANES), BF16),
            pltpu.VMEM((16, HALF), BF16),
            pltpu.VMEM((16, LANES), BF16),
            pltpu.VMEM((BLOCKS, 16, LANES), BF16),
            pltpu.VMEM((BLOCKS, 16, HALF), BF16),
            pltpu.VMEM((128, HALF), BF16),
            pltpu.VMEM((2 * HALF, 128), BF16),
            pltpu.VMEM((64, 128), F32),
            pltpu.VMEM((128, 128), F32),
            pltpu.VMEM((128, 2 * LANES), F32),
            pltpu.VMEM((128, HALF), F32),
            pltpu.VMEM((TILES, 8, LANES), jnp.int32),
            pltpu.VMEM((BLOCKS * 32, 2 * HALF), BF16),
            pltpu.VMEM((4, 128, 128), F32),
            pltpu.VMEM((4, 128, 128), F32),
            pltpu.VMEM((BLOCKS, 16, LANES), F32),
            pltpu.VMEM((128, 512), BF16),
            [pltpu.VMEM((8, 16, 256 * t), BF16) for t in SIZES],
            [pltpu.VMEM((16, 256 * t), BF16) for t in SIZES],
            [pltpu.VMEM((16, 256 * t), BF16) for t in SIZES],
            [pltpu.VMEM((2, 16, 256 * t), BF16) for t in SIZES],
            [pltpu.VMEM((2, 16, 256 * t), BF16) for t in SIZES],
            [pltpu.VMEM((2, 16, 128 * t), BF16) for t in SIZES],
            [pltpu.VMEM((2, 16, 128 * t), BF16) for t in SIZES],
            [pltpu.VMEM((16, 256 * t), F32) for t in SIZES],
            [pltpu.VMEM((8, 256 * t), F32) for t in SIZES],
            *sems,
        ],
        compiler_params=pltpu.CompilerParams(
            collective_id=0, has_side_effects=True, vmem_limit_bytes=34 * 1024 * 1024
        ),
    )(
        images, proj, ctf_table, noise_weight.reshape(65, LANES), trig,
        shifts.transpose(0, 2, 1), defocus,
    )
    return evidence, sums


def solution(mesh):
    in_specs = (
        P(("img", "ori"), None, None),
        P("ori", None, None),
        P(),
        P(),
        P(("img", "ori"), None, None),
        P(("img", "ori")),
    )
    out_specs = (P(("img", "ori")), P(("ori", "img"), None, None))
    return jax.shard_map(
        per_device, mesh=mesh, in_specs=in_specs, out_specs=out_specs, check_vma=False
    )
```
